32 devices in a mesh: dp: 8 (over z, y), tensor: 4 (over x, core).
Axes of the slice: x: 2, y: 2, z: 4, core: 2. Of those that a mesh axis runs over, the one named last changes fastest.
Arguments:
- tokens: bfloat16 [24576, 768], P(('dp', 'tensor')), may hold values from -6 to 6
- cotangent: bfloat16 [24576, 768], P(('dp', 'tensor')), may hold values from -4.5 to 4.5
- segment_ids: int32 [24576], P('dp'), may hold values from 0 to 15, as said below
- valid: int32 [24576], P(('dp', 'tensor')), may hold values from 0 to 1, as said below
- qkv_weight: float32 [768, 3, 768], P('dp', None, 'tensor'), may hold values from -0.21875 to 0.21875
- qkv_moment1: float32 [768, 3, 768], P('dp', None, 'tensor'), may hold values from -0.0015025384 to 0.0015025384
- qkv_moment2: float32 [768, 3, 768], P('dp', None, 'tensor'), may hold values from 1.4110135e-07 to 5.644054e-07
- out_weight: float32 [768, 768], P('tensor', 'dp'), may hold values from -0.649519 to 0.649519
- out_moment1: float32 [768, 768], P('tensor', 'dp'), may hold values from -0.0015025384 to 0.0015025384
- out_moment2: float32 [768, 768], P('tensor', 'dp'), may hold values from 1.4110135e-07 to 5.644054e-07
- fc_weight: float32 [768, 3072], P('dp', 'tensor'), may hold values from -0.21875 to 0.21875
- fc_moment1: float32 [768, 3072], P('dp', 'tensor'), may hold values from -0.0015025384 to 0.0015025384
- fc_moment2: float32 [768, 3072], P('dp', 'tensor'), may hold values from 1.4110135e-07 to 5.644054e-07
- proj_weight: float32 [3072, 768], P('tensor', 'dp'), may hold values from -0.16237976 to 0.16237976
- proj_moment1: float32 [3072, 768], P('tensor', 'dp'), may hold values from -0.0015025384 to 0.0015025384
- proj_moment2: float32 [3072, 768], P('tensor', 'dp'), may hold values from 1.4110135e-07 to 5.644054e-07
- vector_params: float32 [8, 768], replicated, may hold values from -0.6 to 2.5
- vector_moment1: float32 [8, 768], replicated, may hold values from -0.0015025384 to 0.0015025384
- vector_moment2: float32 [8, 768], replicated, may hold values from 1.4110135e-07 to 5.644054e-07
- fc_bias: float32 [3072], replicated, may hold values from -0.6 to 0.6
- fc_bias_moment1: float32 [3072], replicated, may hold values from -0.0015025384 to 0.0015025384
- fc_bias_moment2: float32 [3072], replicated, may hold values from 1.4110135e-07 to 5.644054e-07
Outputs:
- mixed: bfloat16 [24576, 768], P(('dp', 'tensor'))
- input_grad: bfloat16 [24576, 768], P(('dp', 'tensor'))
- grad_norm: float32 [], replicated
- qkv_weight_new: float32 [768, 3, 768], P('dp', None, 'tensor')
- qkv_moment1_new: float32 [768, 3, 768], P('dp', None, 'tensor')
- qkv_moment2_new: float32 [768, 3, 768], P('dp', None, 'tensor')
- out_weight_new: float32 [768, 768], P('tensor', 'dp')
- out_moment1_new: float32 [768, 768], P('tensor', 'dp')
- out_moment2_new: float32 [768, 768], P('tensor', 'dp')
- fc_weight_new: float32 [768, 3072], P('dp', 'tensor')
- fc_moment1_new: float32 [768, 3072], P('dp', 'tensor')
- fc_moment2_new: float32 [768, 3072], P('dp', 'tensor')
- proj_weight_new: float32 [3072, 768], P('tensor', 'dp')
- proj_moment1_new: float32 [3072, 768], P('tensor', 'dp')
- proj_moment2_new: float32 [3072, 768], P('tensor', 'dp')
- vector_params_new: float32 [8, 768], replicated
- vector_moment1_new: float32 [8, 768], replicated
- vector_moment2_new: float32 [8, 768], replicated
- fc_bias_new: float32 [3072], replicated
- fc_bias_moment1_new: float32 [3072], replicated
- fc_bias_moment2_new: float32 [3072], replicated
The draws below stay inside these ranges and needn't reach their ends.
Inputs may be any that keep to these rules, and one draw needn't show every extreme that they name: `segment_ids`: rows of 1024 slots follow one another. Within a row the ids start at 0 and rise by one at each new sequence; a sequence has 64 to 1023 tokens; the slots whose valid is 0 end the row and share one id. Some row holds 16 sequences. `valid`: 1 on the slots of a row before its padding, 0 on the padding.
All inputs are finite; a program needn't handle non-finite values.
Results may differ from the reference program's by a relative error of at most 0.019.
Values may be sent and summed in bfloat16 or wider, within the bound.
A program may use at most 192 MiB of HBM per device.

```python
import math
import jax
import jax.numpy as jnp
from jax import lax

D = 768
HEADS = 12
HD = 64
FF = 3072
SLOT = 1024
MINLEN = 64
STEP = 10
ROWS = 24
TOKENS = 24576
NPARAM = 7087104


def packing(key):
    candidates = SLOT // MINLEN
    key_level, key_extra, key_row = jax.random.split(key, 3)
    picks = jax.random.randint(key_level, (ROWS, candidates), 1, 16)
    steps_up = (picks >= 2).astype(jnp.int32) + (picks >= 4).astype(jnp.int32) + (picks >= 8).astype(jnp.int32)
    floor_len = MINLEN * jnp.left_shift(jnp.ones_like(picks), 3 - steps_up)
    extra_len = jax.random.randint(key_extra, (ROWS, candidates), 0, 1 << 30) % floor_len
    chosen_row = jax.random.randint(key_row, (), 0, ROWS)
    full_row = (jnp.arange(ROWS, dtype=jnp.int32) == chosen_row)[:, None]
    floor_len = jnp.where(full_row, MINLEN, floor_len)
    extra_len = jnp.where(full_row, 0, extra_len)
    finish = jnp.cumsum(floor_len + extra_len, axis=1)
    inside = finish <= SLOT
    finish = jnp.where(inside, finish, SLOT + 1)
    places = jnp.arange(SLOT, dtype=jnp.int32)
    segment = jnp.sum((finish[:, None, :] <= places[None, :, None]).astype(jnp.int32), axis=2)
    filled = jnp.max(jnp.where(inside, finish, 0), axis=1)
    marks = (places[None, :] < filled[:, None]).astype(jnp.int32)
    return (segment.reshape(ROWS * SLOT), marks.reshape(ROWS * SLOT))


def draw_segment_ids(key, part):
    return packing(key)[0]


def draw_valid(key, part):
    return packing(key)[1]


def ramp(count, low_end):
    return low_end + jnp.arange(count, dtype=jnp.float32) / (count - 1)


def draw_vector_params(key, part):
    key = jax.random.fold_in(key, 5)
    key_gain, key_shift = jax.random.split(key)
    rough = jax.random.uniform(key_gain, (2, D), jnp.float32, 0.8, 1.25)
    rise = ramp(D, 0.5)
    shifts = 0.2 * jax.random.truncated_normal(key_shift, -3.0, 3.0, (6, D), jnp.float32)
    gains = rise[None, :] * rough
    return jnp.stack([gains[0], shifts[0], gains[1], shifts[1], shifts[2], shifts[3], shifts[4], shifts[5]])


def draw_out_weight(key, part):
    key = jax.random.fold_in(key, 7)
    rise = ramp(D, 0.5)
    entries = jax.random.truncated_normal(key, -3.0, 3.0, (D, D), jnp.float32)
    return entries * rise[:, None] * (4.0 / math.sqrt(D))


def draw_proj_weight(key, part):
    key = jax.random.fold_in(key, 9)
    rise = ramp(FF, 0.5)
    entries = jax.random.truncated_normal(key, -3.0, 3.0, (FF, D), jnp.float32)
    return entries * rise[:, None] * (2.0 / math.sqrt(FF))


def draw_cotangent(key, part):
    key = jax.random.fold_in(key, 13)
    rise = ramp(D, 0.5)
    entries = jax.random.truncated_normal(key, -3.0, 3.0, (TOKENS, D), jnp.float32)
    return (entries * rise[None, :]).astype(jnp.bfloat16)


def block_scale(stream_key, dims, cuts, low, top_value):
    factor_of, own = 1.0, jax.random.fold_in(stream_key, 6)
    for position, parts in cuts:
        draws = jnp.exp(jax.random.uniform(jax.random.fold_in(own, position), (parts,), jnp.float32, low / len(cuts), top_value / len(cuts)))
        factor_of = factor_of * jnp.repeat(draws, dims[position] // parts).reshape([-1 if axis == position else 1 for axis in range(len(dims))])
    return factor_of


def scatter_about(rng, dims, width, most, cuts=(), kind=jnp.bfloat16):
    gain = block_scale(rng, dims, cuts, -0.22, 0.18) if cuts else 1.0
    array = jax.random.normal(rng, dims, jnp.float32) * width * gain
    return jnp.minimum(jnp.maximum(array, -most), most).astype(kind)


def setup_inputs(seed: int = 0) -> dict:
    streams_of = jax.random.split(jax.random.key(seed), 23)
    return {
        "tokens": scatter_about(streams_of[0], (TOKENS, D), 1.0, 6.0, ((0, 32),)),
        "cotangent": draw_cotangent(jax.random.fold_in(streams_of[22], 71), 0),
        "segment_ids": draw_segment_ids(jax.random.fold_in(streams_of[22], 71), 0),
        "valid": draw_valid(jax.random.fold_in(streams_of[22], 71), 0),
        "qkv_weight": scatter_about(streams_of[4], (D, 3, D), D ** -0.5, 0.21875, ((0, 8), (2, 4)), jnp.float32),
        "qkv_moment1": scatter_about(streams_of[5], (D, 3, D), (1.0 / NPARAM ** 0.5), 0.0015025384, ((0, 8), (2, 4)), jnp.float32),
        "qkv_moment2": jnp.clip(jnp.exp(math.log(5.644054112963204e-07) - 1.3862944 * jax.random.uniform(streams_of[6], (D, 3, D), jnp.float32) ** block_scale(streams_of[6], (D, 3, D), ((0, 8), (2, 4)), -0.2, 0.2)), 1.411013528240801e-07, 5.644054112963204e-07),
        "out_weight": draw_out_weight(jax.random.fold_in(streams_of[22], 71), 0),
        "out_moment1": scatter_about(streams_of[8], (D, D), (1.0 / NPARAM ** 0.5), 0.0015025384, ((0, 4), (1, 8)), jnp.float32),
        "out_moment2": jnp.clip(jnp.exp(math.log(5.644054112963204e-07) - 1.3862944 * jax.random.uniform(streams_of[9], (D, D), jnp.float32) ** block_scale(streams_of[9], (D, D), ((0, 4), (1, 8)), -0.2, 0.2)), 1.411013528240801e-07, 5.644054112963204e-07),
        "fc_weight": scatter_about(streams_of[10], (D, FF), D ** -0.5, 0.21875, ((0, 8), (1, 4)), jnp.float32),
        "fc_moment1": scatter_about(streams_of[11], (D, FF), (1.0 / NPARAM ** 0.5), 0.0015025384, ((0, 8), (1, 4)), jnp.float32),
        "fc_moment2": jnp.clip(jnp.exp(math.log(5.644054112963204e-07) - 1.3862944 * jax.random.uniform(streams_of[12], (D, FF), jnp.float32) ** block_scale(streams_of[12], (D, FF), ((0, 8), (1, 4)), -0.2, 0.2)), 1.411013528240801e-07, 5.644054112963204e-07),
        "proj_weight": draw_proj_weight(jax.random.fold_in(streams_of[22], 71), 0),
        "proj_moment1": scatter_about(streams_of[14], (FF, D), (1.0 / NPARAM ** 0.5), 0.0015025384, ((0, 4), (1, 8)), jnp.float32),
        "proj_moment2": jnp.clip(jnp.exp(math.log(5.644054112963204e-07) - 1.3862944 * jax.random.uniform(streams_of[15], (FF, D), jnp.float32) ** block_scale(streams_of[15], (FF, D), ((0, 4), (1, 8)), -0.2, 0.2)), 1.411013528240801e-07, 5.644054112963204e-07),
        "vector_params": draw_vector_params(jax.random.fold_in(streams_of[22], 71), 0),
        "vector_moment1": scatter_about(streams_of[17], (8, D), (1.0 / NPARAM ** 0.5), 0.0015025384, (), jnp.float32),
        "vector_moment2": jnp.clip(jnp.exp(jax.random.uniform(streams_of[18], (8, D), jnp.float32, math.log(1.411013528240801e-07), math.log(5.644054112963204e-07))), 1.411013528240801e-07, 5.644054112963204e-07),
        "fc_bias": scatter_about(streams_of[19], (FF,), 0.2, 0.6, (), jnp.float32),
        "fc_bias_moment1": scatter_about(streams_of[20], (FF,), (1.0 / NPARAM ** 0.5), 0.0015025384, (), jnp.float32),
        "fc_bias_moment2": jnp.clip(jnp.exp(jax.random.uniform(streams_of[21], (FF,), jnp.float32, math.log(1.411013528240801e-07), math.log(5.644054112963204e-07))), 1.411013528240801e-07, 5.644054112963204e-07),
    }


NORM_EPSILON = 1e-05
MASK_FILL = -1e+30
DECAY_FIRST = 0.5
DECAY_SECOND = 0.5
ADAM_EPSILON = 1e-08
WEIGHT_DECAY = 0.1
CLIP_NORM = 1.0
RATE_MATRIX = 0.04
RATE_VECTOR = 0.3
HIGHEST = lax.Precision.HIGHEST

@jax.custom_vjp
def low(v):
    return lax.optimization_barrier(v.astype(jnp.bfloat16)).astype(jnp.float32)

@jax.custom_vjp
def low_back(v):
    return v

def low_keep(v):
    return (low(v), None)

def low_pass(kept, grad):
    return (grad,)

def back_keep(v):
    return (v, None)

def back_low(kept, grad):
    return (low(grad),)
low.defvjp(low_keep, low_pass)
low_back.defvjp(back_keep, back_low)

def layer_norm(values, gain_vector, shift_vector):
    centered = values - lax.optimization_barrier(jnp.mean(values, axis=-1, keepdims=True))
    variance = lax.optimization_barrier(jnp.mean(centered * centered, axis=-1, keepdims=True))
    return centered * lax.rsqrt(variance + NORM_EPSILON) * gain_vector + shift_vector

def adamw_update(weight, moment_one, moment_two, gradient, step_rate, decay_rate):
    first_moment = DECAY_FIRST * moment_one + (1.0 - DECAY_FIRST) * gradient
    second_moment = DECAY_SECOND * moment_two + (1.0 - DECAY_SECOND) * gradient * gradient
    first_hat = first_moment / (1.0 - DECAY_FIRST ** STEP)
    second_hat = second_moment / (1.0 - DECAY_SECOND ** STEP)
    fresh_weight = weight - step_rate * (first_hat / (jnp.sqrt(second_hat) + ADAM_EPSILON) + decay_rate * weight)
    return (fresh_weight, first_moment, second_moment)

def attend_row(bundle):
    query_rows, key_rows, value_rows, segment_row = bundle
    places = jnp.arange(segment_row.shape[0])
    allowed = (segment_row[:, None] == segment_row[None, :]) & (places[None, :] <= places[:, None])
    scores = low_back(jnp.einsum('qhe,khe->hqk', query_rows, key_rows, precision=HIGHEST) * HD ** (-0.5))
    scores = jnp.where(allowed[None], scores, MASK_FILL)
    top_score = lax.optimization_barrier(jnp.max(scores, axis=-1, keepdims=True))
    exp_scores = jnp.exp(scores - top_score)
    prob_low = low(exp_scores / lax.optimization_barrier(jnp.sum(exp_scores, axis=-1, keepdims=True)))
    return jnp.einsum('hqk,khe->qhe', prob_low, value_rows, precision=HIGHEST)

def forward(inputs, qkv_weight, out_weight, fc_weight, proj_weight, vector_params, fc_bias, segment_ids):
    model_width = inputs.shape[1]
    normed_one = low(layer_norm(inputs, vector_params[0], vector_params[1]))
    mixed_qkv = jnp.einsum('td,dcj->tcj', normed_one, low(qkv_weight), precision=HIGHEST)
    query_all = low(low_back(mixed_qkv[:, 0] + vector_params[4]))
    key_all = low(low_back(mixed_qkv[:, 1]))
    value_all = low(low_back(mixed_qkv[:, 2] + vector_params[5]))

    def by_rows(values):
        return values.reshape(ROWS, SLOT, HEADS, HD)
    attended = lax.map(jax.checkpoint(attend_row), (by_rows(query_all), by_rows(key_all), by_rows(value_all), segment_ids.reshape(ROWS, SLOT)))
    context = low(low_back(attended.reshape(ROWS * SLOT, model_width)))
    resid = inputs + low_back(jnp.dot(context, low(out_weight), precision=HIGHEST)) + vector_params[6]
    normed_two = low(layer_norm(resid, vector_params[2], vector_params[3]))
    pre_act = low_back(jnp.dot(normed_two, low(fc_weight), precision=HIGHEST) + fc_bias)
    activated = low(jax.nn.gelu(pre_act, approximate=True))
    return resid + low_back(jnp.dot(activated, low(proj_weight), precision=HIGHEST)) + vector_params[7]

def reference(tokens, cotangent, segment_ids, valid, qkv_weight, qkv_moment1, qkv_moment2, out_weight, out_moment1, out_moment2, fc_weight, fc_moment1, fc_moment2, proj_weight, proj_moment1, proj_moment2, vector_params, vector_moment1, vector_moment2, fc_bias, fc_bias_moment1, fc_bias_moment2):
    inputs = tokens.astype(jnp.float32)

    def run(inputs_in, qkv_in, out_in, fc_in, proj_in, vector_in, fc_bias_in):
        return forward(inputs_in, qkv_in, out_in, fc_in, proj_in, vector_in, fc_bias_in, segment_ids)
    result, pullback = jax.vjp(run, inputs, qkv_weight, out_weight, fc_weight, proj_weight, vector_params, fc_bias)
    grad_out = cotangent.astype(jnp.float32) * valid.astype(jnp.float32)[:, None]
    input_grad, qkv_grad, out_grad, fc_grad, proj_grad, vector_grad, fc_bias_grad = pullback(grad_out)
    squares = jnp.sum(qkv_grad * qkv_grad) + jnp.sum(out_grad * out_grad) + jnp.sum(fc_grad * fc_grad) + jnp.sum(proj_grad * proj_grad) + jnp.sum(vector_grad * vector_grad) + jnp.sum(fc_bias_grad * fc_bias_grad)
    grad_norm = jnp.sqrt(squares)
    factor = CLIP_NORM / jnp.maximum(grad_norm, CLIP_NORM)
    qkv_new = adamw_update(qkv_weight, qkv_moment1, qkv_moment2, factor * qkv_grad, RATE_MATRIX, WEIGHT_DECAY)
    out_new = adamw_update(out_weight, out_moment1, out_moment2, factor * out_grad, RATE_MATRIX, WEIGHT_DECAY)
    fc_new = adamw_update(fc_weight, fc_moment1, fc_moment2, factor * fc_grad, RATE_MATRIX, WEIGHT_DECAY)
    proj_new = adamw_update(proj_weight, proj_moment1, proj_moment2, factor * proj_grad, RATE_MATRIX, WEIGHT_DECAY)
    vector_new = adamw_update(vector_params, vector_moment1, vector_moment2, factor * vector_grad, RATE_VECTOR, 0.0)
    fc_bias_new = adamw_update(fc_bias, fc_bias_moment1, fc_bias_moment2, factor * fc_bias_grad, RATE_VECTOR, 0.0)
    return (result.astype(jnp.bfloat16), input_grad.astype(jnp.bfloat16), grad_norm, qkv_new[0], qkv_new[1], qkv_new[2], out_new[0], out_new[1], out_new[2], fc_new[0], fc_new[1], fc_new[2], proj_new[0], proj_new[1], proj_new[2], vector_new[0], vector_new[1], vector_new[2], fc_bias_new[0], fc_bias_new[1], fc_bias_new[2])
```

```python
import functools
import math

import jax
import jax.numpy as jnp
from jax import lax
from jax.experimental import pallas as pl
from jax.experimental.pallas import tpu as pltpu
from jax.sharding import PartitionSpec as P

HD = 64
SLOT = 1024
STEP = 10
NORM_EPSILON = 1e-05
MASK_FILL = -1e30
DECAY_FIRST = 0.5
DECAY_SECOND = 0.5
ADAM_EPSILON = 1e-08
WEIGHT_DECAY = 0.1
CLIP_NORM = 1.0
RATE_MATRIX = 0.04
RATE_VECTOR = 0.3

MESH = pl.DeviceIdType.MESH
BF = jnp.bfloat16
F32 = jnp.float32
HALF = SLOT // 2
BLK = 256
VMEM_LIMIT = 58 * 2**20
LOG2E = math.log2(math.e)
SCORE_SCALE = float(HD) ** (-0.5)
SCORE_SCALE2 = SCORE_SCALE * LOG2E


def dot_nn(a, b):
    return lax.dot_general(a, b, (((1,), (0,)), ((), ())), preferred_element_type=F32)


def dot_nt(a, b):
    return lax.dot_general(a, b, (((1,), (1,)), ((), ())), preferred_element_type=F32)


def dot_tn(a, b):
    return lax.dot_general(a, b, (((0,), (0,)), ((), ())), preferred_element_type=F32)


def dot_tt(a, b):
    return lax.dot_general(a, b, (((0,), (1,)), ((), ())), preferred_element_type=F32)


def params(collective_id=None):
    if collective_id is None:
        return pltpu.CompilerParams(vmem_limit_bytes=VMEM_LIMIT)
    return pltpu.CompilerParams(
        vmem_limit_bytes=VMEM_LIMIT, collective_id=collective_id, has_side_effects=True
    )


VM = pl.BlockSpec(memory_space=pltpu.VMEM)
ANY = pl.BlockSpec(memory_space=pl.ANY)


def sds(shape, dtype):
    return jax.ShapeDtypeStruct(shape, dtype)


def here():
    t = lax.axis_index("tensor")
    return lax.axis_index("dp"), t // 2, t % 2


def greet(ids):
    sem = pltpu.get_barrier_semaphore()
    for one in ids:
        pl.semaphore_signal(sem, inc=1, device_id=one, device_id_type=MESH)
    pl.semaphore_wait(sem, len(ids))


def remote(src, dst, send_sem, recv_sem, target):
    return pltpu.make_async_remote_copy(
        src_ref=src,
        dst_ref=dst,
        send_sem=send_sem,
        recv_sem=recv_sem,
        device_id=target,
        device_id_type=MESH,
    )


def rows_at(start, size):
    return pl.ds(pl.multiple_of(start, size), size)


def norm_parts(values):
    centered = values - jnp.mean(values, axis=-1, keepdims=True)
    variance = jnp.mean(centered * centered, axis=-1, keepdims=True)
    scale = lax.rsqrt(variance + NORM_EPSILON)
    return centered * scale, scale


def share_kernel(tok_ref, grad_ref, tk_ref, gl_ref, loc, ss, rs):
    dp, x, c = here()
    core = (dp, x * 2 + 1 - c)
    across = [(dp, (1 - x) * 2), (dp, (1 - x) * 2 + 1)]
    greet([core] + across)
    rows = tok_ref.shape[0]
    tk_rows = rows_at(x * HALF + c * rows, BLK)
    tk_rows = pl.ds(pl.multiple_of(x * HALF + c * rows, BLK), rows)
    gl_rows = pl.ds(pl.multiple_of(c * rows, BLK), rows)
    mine = [
        pltpu.make_async_copy(tok_ref, tk_ref.at[tk_rows], loc.at[0]),
        pltpu.make_async_copy(grad_ref, gl_ref.at[gl_rows], loc.at[1]),
    ]
    out = [
        remote(tok_ref, tk_ref.at[tk_rows], ss.at[0], rs.at[0], core),
        remote(grad_ref, gl_ref.at[gl_rows], ss.at[1], rs.at[1], core),
    ]
    half_src = tok_ref.at[pl.ds(pl.multiple_of((1 - x) * BLK, BLK), HALF)]
    half_dst = tk_ref.at[pl.ds(pl.multiple_of(x * (SLOT + HALF), HALF), HALF)]
    halves = [
        remote(half_src, half_dst, ss.at[2 + k], rs.at[2], across[k]) for k in range(2)
    ]

    @pl.when(c == 1 - x)
    def _():
        for one in halves:
            one.start()

    for one in mine + out:
        one.start()
    for one in mine + out:
        one.wait()
    halves[0].wait_recv()

    @pl.when(c == 1 - x)
    def _():
        for one in halves:
            one.wait_send()


def share_tokens(tokens, grad_low):
    rows, width = tokens.shape
    return pl.pallas_call(
        share_kernel,
        out_shape=(sds((2 * SLOT, width), BF), sds((2 * rows, width), BF)),
        in_specs=[ANY, ANY],
        out_specs=(ANY, ANY),
        scratch_shapes=[
            pltpu.SemaphoreType.DMA((2,)),
            pltpu.SemaphoreType.DMA((4,)),
            pltpu.SemaphoreType.DMA((3,)),
        ],
        compiler_params=params(1),
        name="share_tokens",
    )(tokens, grad_low)


def gather_kernel(n, *refs):
    shards, outs = refs[:n], refs[n : 2 * n]
    loc, ss, rs = refs[2 * n :]
    dp, x, c = here()
    z, y = dp // 2, dp % 2
    me = x * 2 + c
    z_peers = [(lax.rem(z + k, 4) * 2 + y, me) for k in (1, 2, 3)]
    x_peer = (dp, (1 - x) * 2 + c)
    y_peer = (z * 2 + 1 - y, me)
    greet(z_peers + [x_peer, y_peer])
    owns, zs, xys, fs = [], [], [], []
    for a in range(n):
        block = outs[a].at[x, z, y]
        owns.append(pltpu.make_async_copy(shards[a], block, loc.at[a]))
        zs.append(
            [remote(shards[a], block, ss.at[a, k], rs.at[a, k], z_peers[k]) for k in range(3)]
        )
        column = outs[a].at[x, :, y]
        xys.append(
            [
                remote(column, column, ss.at[a, 3], rs.at[a, 3], x_peer),
                remote(column, column, ss.at[a, 4], rs.at[a, 4], y_peer),
            ]
        )
        from_x = outs[a].at[1 - x, pl.ds(0, 2), y]
        from_y = outs[a].at[x, pl.ds(2, 2), 1 - y]
        fs.append(
            [
                remote(from_x, from_x, ss.at[a, 5], rs.at[a, 5], y_peer),
                remote(from_y, from_y, ss.at[a, 6], rs.at[a, 6], x_peer),
            ]
        )
    for a in range(n):
        owns[a].start()
        for one in zs[a]:
            one.start()
    for a in range(n + 1):
        if a < n:
            owns[a].wait()
            for one in zs[a]:
                one.wait()
            for one in xys[a]:
                one.start()
        if a > 0:
            for one in xys[a - 1]:
                one.wait()
            for one in fs[a - 1]:
                one.start()
    for a in range(n):
        for one in fs[a]:
            one.wait()


def gather_weights(shards):
    n = len(shards)
    if lax.axis_size("dp") != 8:
        slot = lax.axis_index("tensor") // 2
        swap = [(0, 2), (1, 3), (2, 0), (3, 1)]
        result = []
        for shard in shards:
            own = lax.all_gather(shard, "dp", axis=0, tiled=True)
            other = lax.ppermute(own, "tensor", swap)
            result.append(
                jnp.stack([jnp.where(slot == 0, own, other), jnp.where(slot == 0, other, own)])
            )
        return result
    shapes = [(2, 4, 2) + s.shape for s in shards]
    outs = pl.pallas_call(
        functools.partial(gather_kernel, n),
        out_shape=tuple(sds(s, BF) for s in shapes),
        in_specs=[ANY] * n,
        out_specs=(ANY,) * n,
        scratch_shapes=[
            pltpu.SemaphoreType.DMA((n,)),
            pltpu.SemaphoreType.DMA((n, 7)),
            pltpu.SemaphoreType.DMA((n, 7)),
        ],
        compiler_params=params(2),
        name="gather_weights",
    )(*shards)
    return [o.reshape(2, 8 * s.shape[0], s.shape[1]) for o, s in zip(outs, shards, strict=True)]


def qkv_kernel(tk_ref, vec_ref, bias_ref, wq_ref, n1_ref, u_ref):
    _, x, _ = here()
    gain, shift = vec_ref[0:1, :], vec_ref[1:2, :]

    def norm(i, carry):
        rows = rows_at(i * BLK, BLK)
        unit, _ = norm_parts(tk_ref[rows, :].astype(F32))
        n1_ref[rows, :] = (unit * gain + shift).astype(BF)
        return carry

    lax.fori_loop(0, 2 * SLOT // BLK, norm, 0)

    def project(i, carry):
        lanes = rows_at(i * BLK, BLK)
        full = n1_ref[rows_at(x * SLOT + i * BLK, BLK), :]
        u_ref[0, :, lanes] = (dot_tt(wq_ref[0], full) + bias_ref[0]).astype(BF)
        u_ref[1, :, lanes] = (dot_tt(wq_ref[1], full) + bias_ref[1]).astype(BF)
        part = n1_ref[rows_at((1 - x) * SLOT + i * BLK, BLK), :]
        u_ref[2, :, lanes] = (dot_tt(wq_ref[x], part) + bias_ref[x]).astype(BF)
        return carry

    lax.fori_loop(0, SLOT // BLK, project, 0)


def project_qkv(tk, vectors, bias, wq):
    cols = wq.shape[2]
    return pl.pallas_call(
        qkv_kernel,
        out_shape=(sds(tk.shape, BF), sds((3, cols, SLOT), BF)),
        in_specs=[VM] * 4,
        out_specs=(VM, VM),
        compiler_params=params(),
        name="norm_qkv",
    )(tk, vectors, bias, wq)


def allowed_pairs(key_block, query_block, start_row, wide):
    keys = lax.broadcasted_iota(jnp.int32, (BLK, wide), 0) + key_block * BLK
    mask = keys >= start_row
    if key_block == query_block:
        queries = lax.broadcasted_iota(jnp.int32, (BLK, wide), 1) + query_block * BLK
        mask = mask & (keys <= queries)
    return mask


def attend_unit(q, k, v, start):
    blocks = SLOT // BLK
    for i in range(blocks):
        cols = slice(i * BLK, (i + 1) * BLK)
        query = q(cols)
        scores = []
        for j in range(i + 1):
            raw = dot_tn(k(slice(j * BLK, (j + 1) * BLK)), query) * SCORE_SCALE2
            scores.append(jnp.where(allowed_pairs(j, i, start(cols), BLK), raw, MASK_FILL))
        top = functools.reduce(jnp.maximum, [jnp.max(s, axis=0, keepdims=True) for s in scores])
        exps = [jnp.exp2(s - top) for s in scores]
        total = functools.reduce(jnp.add, [jnp.sum(e, axis=0, keepdims=True) for e in exps])
        acc = None
        for j in range(i + 1):
            term = dot_nn(v(slice(j * BLK, (j + 1) * BLK)), exps[j].astype(BF))
            acc = term if acc is None else acc + term
        yield cols, acc / total, top + jnp.log2(total)


def attend_kernel(u_ref, start_ref, ctx_ref, lse_ref):
    for cols, context, log_total in attend_unit(
        lambda s: u_ref[0, 0, 0, :, s],
        lambda s: u_ref[0, 1, 0, :, s],
        lambda s: u_ref[0, 2, 0, :, s],
        lambda s: start_ref[0, :, s],
    ):
        ctx_ref[0, 0, :, cols] = context.astype(BF)
        lse_ref[0, 0, :, cols] = log_total


def attend(units, starts):
    groups, _, heads = units.shape[:3]
    return pl.pallas_call(
        attend_kernel,
        grid=(groups, heads),
        out_shape=(sds((groups, heads, HD, SLOT), BF), sds((groups, heads, 1, SLOT), F32)),
        in_specs=[
            pl.BlockSpec((1, 3, 1, HD, SLOT), lambda g, h: (g, 0, h, 0, 0)),
            pl.BlockSpec((1, 1, SLOT), lambda g, h: (g // 2, 0, 0)),
        ],
        out_specs=(
            pl.BlockSpec((1, 1, HD, SLOT), lambda g, h: (g, h, 0, 0)),
            pl.BlockSpec((1, 1, 1, SLOT), lambda g, h: (g, h, 0, 0)),
        ),
        compiler_params=params(),
        name="attend",
    )(units, starts)


def attend_back_kernel(u_ref, start_ref, ctx_ref, dctx_ref, lse_ref, out_ref, dq_ref):
    blocks = SLOT // BLK
    dctx = dctx_ref[0, 0]
    delta = jnp.sum(dctx.astype(F32) * ctx_ref[0, 0].astype(F32), axis=0, keepdims=True)
    start = start_ref[0]
    lse = lse_ref[0, 0]
    for j in range(blocks):
        keys = slice(j * BLK, (j + 1) * BLK)
        k = u_ref[0, 1, 0, :, keys]
        v = u_ref[0, 2, 0, :, keys]
        probs, dscores = [], []
        for i in range(j, blocks):
            cols = slice(i * BLK, (i + 1) * BLK)
            raw = dot_tn(k, u_ref[0, 0, 0, :, cols]) * SCORE_SCALE2 - lse[:, cols]
            prob = jnp.exp2(jnp.where(allowed_pairs(j, i, start[:, cols], BLK), raw, MASK_FILL))
            dprob = dot_tn(v, dctx[:, cols])
            probs.append(prob.astype(BF))
            dscores.append((prob * (dprob - delta[:, cols])).astype(BF))
        dk, dv = None, None
        for n, i in enumerate(range(j, blocks)):
            cols = slice(i * BLK, (i + 1) * BLK)
            dv_term = dot_nt(dctx[:, cols], probs[n])
            dk_term = dot_nt(u_ref[0, 0, 0, :, cols], dscores[n])
            dv = dv_term if dv is None else dv + dv_term
            dk = dk_term if dk is None else dk + dk_term
            dq_term = dot_nn(k, dscores[n])
            if j == 0:
                dq_ref[:, cols] = dq_term
            else:
                dq_ref[:, cols] += dq_term
        out_ref[0, 1, 0, :, keys] = (dk * SCORE_SCALE).astype(BF)
        out_ref[0, 2, 0, :, keys] = dv.astype(BF)
    out_ref[0, 0, 0] = (dq_ref[...] * SCORE_SCALE).astype(BF)


def attend_back(units, starts, context, dcontext, lse):
    groups, _, heads = units.shape[:3]
    per_unit = pl.BlockSpec((1, 1, HD, SLOT), lambda g, h: (g, h, 0, 0))
    return pl.pallas_call(
        attend_back_kernel,
        grid=(groups, heads),
        out_shape=sds(units.shape, BF),
        in_specs=[
            pl.BlockSpec((1, 3, 1, HD, SLOT), lambda g, h: (g, 0, h, 0, 0)),
            pl.BlockSpec((1, 1, SLOT), lambda g, h: (g // 2, 0, 0)),
            per_unit,
            per_unit,
            pl.BlockSpec((1, 1, 1, SLOT), lambda g, h: (g, h, 0, 0)),
        ],
        out_specs=pl.BlockSpec((1, 3, 1, HD, SLOT), lambda g, h: (g, 0, h, 0, 0)),
        scratch_shapes=[pltpu.VMEM((HD, SLOT), F32)],
        compiler_params=params(),
        name="attend_back",
    )(units, starts, context, dcontext, lse)


def out_kernel(
    ctx_ref, wo_ref, tk_ref, vec_ref, ctxc_ref, resid_ref, n2_ref, half, part, got, xs, cs_s, cs_r
):
    dp, x, c = here()
    core = (dp, x * 2 + 1 - c)
    x_peer = (dp, (1 - x) * 2 + c)
    greet([core, x_peer])
    theirs = pl.ds(pl.multiple_of((1 - x) * HALF, HALF), HALF)
    ours = pl.ds(pl.multiple_of(x * HALF, HALF), HALF)
    cross = remote(ctx_ref.at[2, :, theirs], half, xs.at[0], xs.at[1], x_peer)
    cross.start()
    chunks = []

    def send(chunk, values):
        rows = rows_at(chunk * BLK, BLK)
        part[rows, :] = values.astype(BF)
        copy = remote(part.at[rows], got.at[rows], cs_s.at[chunk], cs_r.at[chunk], core)
        copy.start()
        chunks.append((chunk, copy))

    for i in range(SLOT // BLK):
        lanes = slice(i * BLK, (i + 1) * BLK)
        chunk = x * 2 + i
        out_lanes = rows_at(chunk * BLK, BLK)
        zero, one = ctx_ref[0, :, lanes], ctx_ref[1, :, lanes]
        send(chunk, dot_tt(zero, wo_ref[0]) + dot_tt(one, wo_ref[1]))
        ctxc_ref[0, :, out_lanes] = zero
        ctxc_ref[1, :, out_lanes] = one
    cross.wait()
    for i in range(HALF // BLK):
        chunk = (1 - x) * 4 + i
        out_lanes = rows_at(chunk * BLK, BLK)
        own = ctx_ref[2, :, rows_at(x * HALF + i * BLK, BLK)]
        other = half[:, i * BLK : (i + 1) * BLK]
        send(chunk, dot_tt(own, wo_ref[x]) + dot_tt(other, wo_ref[1 - x]))
        ctxc_ref[x, :, out_lanes] = own
        ctxc_ref[1 - x, :, out_lanes] = other
    for chunk, copy in chunks:
        copy.wait()
        rows = rows_at(chunk * BLK, BLK)
        tok = tk_ref[rows_at(x * HALF + chunk * BLK, BLK), :].astype(F32)
        summed = part[rows, :].astype(F32) + got[rows, :].astype(F32)
        resid = tok + summed + vec_ref[6:7, :]
        resid_ref[rows, :] = resid
        unit, _ = norm_parts(resid)
        n2_ref[rows, :] = (unit * vec_ref[2:3, :] + vec_ref[3:4, :]).astype(BF)


def project_out(ctx, wo, tk, vectors):
    cols = ctx.shape[1]
    width = tk.shape[1]
    rows = SLOT + HALF
    return pl.pallas_call(
        out_kernel,
        out_shape=(sds((2, cols, rows), BF), sds((rows, width), F32), sds((rows, width), BF)),
        in_specs=[VM] * 4,
        out_specs=(VM, VM, VM),
        scratch_shapes=[
            pltpu.VMEM((cols, HALF), BF),
            pltpu.VMEM((rows, width), BF),
            pltpu.VMEM((rows, width), BF),
            pltpu.SemaphoreType.DMA((2,)),
            pltpu.SemaphoreType.DMA((rows // BLK,)),
            pltpu.SemaphoreType.DMA((rows // BLK,)),
        ],
        compiler_params=params(3),
        name="out_norm",
    )(ctx, wo, tk, vectors)


GELU_C = math.sqrt(2.0 / math.pi)
GELU_A = 0.044715


def ffn_kernel(
    n2_ref, gl_ref, wf_ref, wp_ref, fb_ref, br_ref, dn2_ref, gf_ref, gp_ref, gb_ref, act, dpre
):
    rows_all, width = n2_ref.shape
    hidden = wf_ref.shape[2]

    def forward_back(i, carry):
        rows = rows_at(i * BLK, BLK)
        n2, gl = n2_ref[rows, :], gl_ref[rows, :]
        for s in range(2):
            lanes = slice(s * hidden, (s + 1) * hidden)
            u = dot_nn(n2, wf_ref[s]) + fb_ref[s]
            up = dot_nn(gl, wp_ref[s])
            t = jnp.tanh(GELU_C * (u + GELU_A * u * u * u))
            act[rows, lanes] = (0.5 * u * (1.0 + t)).astype(BF)
            slope = 0.5 * (1.0 + t) + 0.5 * u * (1.0 - t * t) * GELU_C * (
                1.0 + 3.0 * GELU_A * u * u
            )
            d = (up * slope).astype(BF)
            dpre[rows, lanes] = d
            gb_ref[s] += jnp.sum(d.astype(F32), axis=0, keepdims=True)
        br = dot_nt(act[rows, :hidden], wp_ref[0]) + dot_nt(act[rows, hidden:], wp_ref[1])
        br_ref[rows, :] = br.astype(BF)
        dn = dot_nt(dpre[rows, :hidden], wf_ref[0]) + dot_nt(dpre[rows, hidden:], wf_ref[1])
        dn2_ref[rows, :] = dn.astype(BF)
        return carry

    gb_ref[...] = jnp.zeros_like(gb_ref)
    lax.fori_loop(0, rows_all // BLK, forward_back, 0)
    for s in range(2):

        def weight_grads(i, carry, s=s):
            lanes = rows_at(i * BLK, BLK)
            wide = rows_at(s * hidden + i * BLK, BLK)
            gp_ref[s, :, lanes] = dot_tn(gl_ref[...], act[:, wide]).astype(BF)
            gf_ref[s, :, lanes] = dot_tn(n2_ref[...], dpre[:, wide]).astype(BF)
            return carry

        lax.fori_loop(0, hidden // BLK, weight_grads, 0)


def feed_forward(n2, gl, wf, wp, fb):
    rows, width = n2.shape
    hidden = wf.shape[2]
    return pl.pallas_call(
        ffn_kernel,
        out_shape=(
            sds((rows, width), BF),
            sds((rows, width), BF),
            sds(wf.shape, BF),
            sds(wp.shape, BF),
            sds((2, 1, hidden), F32),
        ),
        in_specs=[VM] * 5,
        out_specs=(VM,) * 5,
        scratch_shapes=[
            pltpu.VMEM((rows, 2 * hidden), BF),
            pltpu.VMEM((rows, 2 * hidden), BF),
        ],
        compiler_params=params(),
        name="feed_forward",
    )(n2, gl, wf, wp, fb)


def mid_kernel(
    br_ref, dn_ref, resid_ref, gl_ref, ctxc_ref, wo_ref, vec_ref,
    mixed_ref, dres_ref, dctx_ref, go_ref, vg_ref,
    low, got_br, got_dn, outgoing, half, bs, xs, cs_s, cs_r,
):
    dp, x, c = here()
    core = (dp, x * 2 + 1 - c)
    x_peer = (dp, (1 - x) * 2 + c)
    greet([core, x_peer])
    rows_all, width = dn_ref.shape
    own_rows = rows_all // 2
    their = pl.ds(pl.multiple_of((1 - c) * own_rows, BLK), own_rows)
    n_chunks = rows_all // BLK
    copies = []
    for r in range(n_chunks):
        rows = pl.ds(r * BLK, BLK)
        copy = remote(dn_ref.at[rows], got_dn.at[rows], cs_s.at[r], cs_r.at[r], core)
        copy.start()
        copies.append(copy)
    branch = remote(br_ref.at[their], got_br, bs.at[0], bs.at[1], core)
    branch.start()
    vg_ref[...] = jnp.zeros_like(vg_ref)
    gain = vec_ref[2:3, :]
    for r in range(n_chunks):
        copies[r].wait()
        rows = slice(r * BLK, (r + 1) * BLK)
        dn = dn_ref[rows, :].astype(F32) + got_dn[rows, :].astype(F32)
        unit, scale = norm_parts(resid_ref[rows, :])
        e = dn * gain
        dres = gl_ref[rows, :].astype(F32) + scale * (
            e
            - jnp.mean(e, axis=-1, keepdims=True)
            - unit * jnp.mean(e * unit, axis=-1, keepdims=True)
        )
        low[rows, :] = dres.astype(BF)
        dres_ref[rows, :] = dres

        @pl.when(c == r // (n_chunks // 2))
        def _(dn=dn, unit=unit, dres=dres):
            vg_ref[0:1, :] += jnp.sum(dn * unit, axis=0, keepdims=True)
            vg_ref[1:2, :] += jnp.sum(dn, axis=0, keepdims=True)
            vg_ref[2:3, :] += jnp.sum(dres, axis=0, keepdims=True)

    for i in range(HALF // BLK):
        lanes = slice(i * BLK, (i + 1) * BLK)
        rows = rows_at((1 - x) * SLOT + i * BLK, BLK)
        outgoing[:, lanes] = dot_tt(wo_ref[1 - x], low[rows, :]).astype(BF)
        dctx_ref[2, :, rows_at(x * HALF + i * BLK, BLK)] = dot_tt(
            wo_ref[x], low[rows, :]
        ).astype(BF)
    cross = remote(outgoing, half, xs.at[0], xs.at[1], x_peer)
    cross.start()
    for i in range(SLOT // BLK):
        lanes = slice(i * BLK, (i + 1) * BLK)
        rows = rows_at(x * HALF + i * BLK, BLK)
        for s in range(2):
            dctx_ref[s, :, lanes] = dot_tt(wo_ref[s], low[rows, :]).astype(BF)
    for s in range(2):
        go_ref[s] = dot_tt(low[...], ctxc_ref[s]).astype(BF)
    branch.wait()
    for r in range(own_rows // BLK):
        rows = slice(r * BLK, (r + 1) * BLK)
        wide = rows_at(c * own_rows + r * BLK, BLK)
        mixed = (
            resid_ref[wide, :]
            + br_ref[wide, :].astype(F32)
            + got_br[rows, :].astype(F32)
            + vec_ref[7:8, :]
        )
        mixed_ref[rows, :] = mixed.astype(BF)
        vg_ref[3:4, :] += jnp.sum(gl_ref[wide, :].astype(F32), axis=0, keepdims=True)
    cross.wait()
    dctx_ref[2, :, pl.ds(pl.multiple_of((1 - x) * HALF, HALF), HALF)] = half[...]


def middle_back(br, dn, resid, gl, ctxc, wo, vectors):
    rows, width = dn.shape
    cols = ctxc.shape[1]
    return pl.pallas_call(
        mid_kernel,
        out_shape=(
            sds((rows // 2, width), BF),
            sds((rows, width), F32),
            sds((3, cols, SLOT), BF),
            sds((2, width, cols), BF),
            sds((8, width), F32),
        ),
        in_specs=[VM] * 7,
        out_specs=(VM,) * 5,
        scratch_shapes=[
            pltpu.VMEM((rows, width), BF),
            pltpu.VMEM((rows // 2, width), BF),
            pltpu.VMEM((rows, width), BF),
            pltpu.VMEM((cols, HALF), BF),
            pltpu.VMEM((cols, HALF), BF),
            pltpu.SemaphoreType.DMA((2,)),
            pltpu.SemaphoreType.DMA((2,)),
            pltpu.SemaphoreType.DMA((rows // BLK,)),
            pltpu.SemaphoreType.DMA((rows // BLK,)),
        ],
        compiler_params=params(4),
        name="middle_back",
    )(br, dn, resid, gl, ctxc, wo, vectors)


def first_kernel(
    du_ref, n1_ref, wq_ref, dres_ref, tk_ref, vec_ref,
    gq_ref, ig_ref, vg_ref, qb_ref,
    half, part, got, xs, cs_s, cs_r,
):
    dp, x, c = here()
    core = (dp, x * 2 + 1 - c)
    x_peer = (dp, (1 - x) * 2 + c)
    greet([core, x_peer])
    cols = du_ref.shape[1]
    rows_all = SLOT + HALF
    own_chunks = rows_all // BLK // 2
    theirs = pl.ds(pl.multiple_of((1 - x) * HALF, HALF), HALF)
    cross = remote(du_ref.at[2, :, theirs], half, xs.at[0], xs.at[1], x_peer)
    cross.start()
    full_rows = pl.ds(pl.multiple_of(x * SLOT, SLOT), SLOT)
    part_rows = pl.ds(pl.multiple_of((1 - x) * SLOT, SLOT), SLOT)

    def send(chunk, values):
        part[rows_at(chunk * BLK, BLK), :] = values.astype(BF)

    for i in range(SLOT // BLK):
        lanes = slice(i * BLK, (i + 1) * BLK)
        send(
            x * 2 + i,
            dot_tt(du_ref[0, :, lanes], wq_ref[0]) + dot_tt(du_ref[1, :, lanes], wq_ref[1]),
        )
    cross.wait()
    for i in range(HALF // BLK):
        own = du_ref[2, :, rows_at(x * HALF + i * BLK, BLK)]
        send(
            (1 - x) * 4 + i,
            dot_tt(own, wq_ref[x]) + dot_tt(half[:, i * BLK : (i + 1) * BLK], wq_ref[1 - x]),
        )
    their = pl.ds(pl.multiple_of((1 - c) * own_chunks * BLK, BLK), own_chunks * BLK)
    swap = remote(part.at[their], got, cs_s, cs_r, core)
    swap.start()
    ones = jnp.ones((8, SLOT), BF)
    for s in range(2):
        gq_ref[s] = dot_tt(n1_ref[full_rows, :], du_ref[s]).astype(BF)
    gq_ref[x] = (
        gq_ref[x].astype(F32) + dot_tt(n1_ref[part_rows, :], du_ref[2])
    ).astype(BF)
    for g in range(3):
        qb_ref[g] = dot_nt(ones, du_ref[g])
    swap.wait()
    vg_ref[...] = jnp.zeros_like(vg_ref)
    gain = vec_ref[0:1, :]
    for r in range(own_chunks):
        rows = slice(r * BLK, (r + 1) * BLK)
        wide = rows_at((c * own_chunks + r) * BLK, BLK)
        tok_rows = rows_at(x * HALF + (c * own_chunks + r) * BLK, BLK)
        dn = part[wide, :].astype(F32) + got[rows, :].astype(F32)
        unit, scale = norm_parts(tk_ref[tok_rows, :].astype(F32))
        e = dn * gain
        back = scale * (
            e
            - jnp.mean(e, axis=-1, keepdims=True)
            - unit * jnp.mean(e * unit, axis=-1, keepdims=True)
        )
        ig_ref[rows, :] = (dres_ref[wide, :] + back).astype(BF)
        vg_ref[0:1, :] += jnp.sum(dn * unit, axis=0, keepdims=True)
        vg_ref[1:2, :] += jnp.sum(dn, axis=0, keepdims=True)


def first_back(du, n1, wq, dres, tk, vectors):
    cols = du.shape[1]
    width = tk.shape[1]
    rows = SLOT + HALF
    return pl.pallas_call(
        first_kernel,
        out_shape=(
            sds((2, width, cols), BF),
            sds((rows // 2, width), BF),
            sds((8, width), F32),
            sds((3, 8, cols), F32),
        ),
        in_specs=[VM] * 6,
        out_specs=(VM,) * 4,
        scratch_shapes=[
            pltpu.VMEM((cols, HALF), BF),
            pltpu.VMEM((rows, width), BF),
            pltpu.VMEM((rows // 2, width), BF),
            pltpu.SemaphoreType.DMA((2,)),
            pltpu.SemaphoreType.DMA,
            pltpu.SemaphoreType.DMA,
        ],
        compiler_params=params(5),
        name="first_back",
    )(du, n1, wq, dres, tk, vectors)


def reduce_kernel(n, *refs):
    grads = refs[:n]
    vec_ref = refs[n]
    sums = refs[n + 1 : 2 * n + 1]
    vec_out, sq_out = refs[2 * n + 1 : 2 * n + 3]
    rest = refs[2 * n + 3 :]
    r1x, r1y, r2x, r2y, r3, s3, m1, m2 = (rest[i * n : (i + 1) * n] for i in range(8))
    vgot, sgot, ss, rs, vs_s, vs_r, qs_s, qs_r = rest[8 * n :]
    dp, x, c = here()
    z, y = dp // 2, dp % 2
    me = x * 2 + c
    z_peers = [(lax.rem(z + k, 4) * 2 + y, me) for k in (1, 2, 3)]
    x_peer = (dp, (1 - x) * 2 + c)
    y_peer = (z * 2 + 1 - y, me)
    core = (dp, x * 2 + 1 - c)
    greet(z_peers + [x_peer, y_peer, core])
    first, early, second, third = [], [], [], []
    for a in range(n):
        g = grads[a]
        first.append(
            [
                remote(g.at[1 - x, pl.ds(0, 2), 1 - y], r1y[a], ss.at[a, 0], rs.at[a, 0], y_peer),
                remote(g.at[1 - x, pl.ds(2, 2), 1 - y], r1x[a], ss.at[a, 1], rs.at[a, 1], x_peer),
            ]
        )
        early.append(
            [
                remote(
                    g.at[1 - x, pl.ds(2, 2), y],
                    r2x[a].at[pl.ds(2, 2)],
                    ss.at[a, 7],
                    rs.at[a, 7],
                    x_peer,
                ),
                remote(
                    g.at[x, pl.ds(0, 2), 1 - y],
                    r2y[a].at[pl.ds(0, 2)],
                    ss.at[a, 8],
                    rs.at[a, 8],
                    y_peer,
                ),
            ]
        )
        second.append(
            [
                remote(m1[a], r2x[a].at[pl.ds(0, 2)], ss.at[a, 2], rs.at[a, 2], x_peer),
                remote(m2[a], r2y[a].at[pl.ds(2, 2)], ss.at[a, 3], rs.at[a, 3], y_peer),
            ]
        )
        third.append(
            [
                remote(s3[a].at[k], r3[a].at[k], ss.at[a, 4 + k], rs.at[a, 4 + k], z_peers[k])
                for k in range(3)
            ]
        )

    def all_sum(value_ref, got, send, recv):
        for i, peers in enumerate(([core], [x_peer], [y_peer], z_peers)):
            base = i if i < 3 else 3
            copies = [
                remote(value_ref, got.at[base + k], send.at[base + k], recv.at[base + k], peer)
                for k, peer in enumerate(peers)
            ]
            for one in copies:
                one.start()
            for one in copies:
                one.wait()
            if len(peers) == 1:
                value_ref[...] += got[base]
            else:
                blocks = [value_ref[...]] + [got[base + k] for k in range(3)]
                total = None
                for place in range(4):
                    term = blocks[0]
                    for k in range(1, 4):
                        term = jnp.where(lax.rem(z + 4 - k, 4) == place, blocks[k], term)
                    total = term if total is None else total + term
                value_ref[...] = total

    def stage_two(a):
        for one in first[a]:
            one.wait()
        for k in range(2):
            m1[a][k] = (grads[a][1 - x, k, y].astype(F32) + r1y[a][k].astype(F32)).astype(BF)
            m2[a][k] = (grads[a][x, 2 + k, 1 - y].astype(F32) + r1x[a][k].astype(F32)).astype(BF)
        for one in second[a]:
            one.start()

    def column(a, place):
        return (
            grads[a][x, place, y].astype(F32)
            + r2x[a][place].astype(F32)
            + r2y[a][place].astype(F32)
        )

    def stage_three(a):
        for one in early[a] + second[a]:
            one.wait()
        for k in range(3):
            s3[a][k] = column(a, lax.rem(z + k + 1, 4)).astype(BF)
            third[a][k].start()
        sums[a][...] = column(a, z)

    for a in range(n):
        for one in first[a] + early[a]:
            one.start()
    vec_out[...] = vec_ref[...]
    for a in range(n):
        stage_two(a)
        if a > 0:
            stage_three(a - 1)
    stage_three(n - 1)
    all_sum(vec_out, vgot, vs_s, vs_r)
    squares = jnp.zeros((), F32)
    for a in range(n):
        for one in third[a]:
            one.wait()
        total = (
            sums[a][...]
            + r3[a][0].astype(F32)
            + r3[a][1].astype(F32)
            + r3[a][2].astype(F32)
        )
        sums[a][...] = total
        squares = squares + jnp.sum(total * total)
    sq_out[...] = jnp.full(sq_out.shape, squares, F32)
    all_sum(sq_out, sgot, qs_s, qs_r)


def reduce_grads(grads, vec):
    n = len(grads)
    if lax.axis_size("dp") != 8:
        slot = lax.axis_index("tensor") // 2
        swap = [(0, 2), (1, 3), (2, 0), (3, 1)]
        sums = []
        for g in grads:
            mine = jnp.where(slot == 0, g[0], g[1])
            other = jnp.where(slot == 0, g[1], g[0])
            total = mine.astype(F32) + lax.ppermute(other, "tensor", swap).astype(F32)
            sums.append(
                lax.psum_scatter(total.astype(BF), "dp", scatter_dimension=0, tiled=True).astype(F32)
            )
        squares = sum(jnp.sum(s * s) for s in sums)
        vec, squares = lax.psum((vec, squares), ("dp", "tensor"))
        return sums, vec, squares
    shapes = [(g.shape[1] // 8, g.shape[2]) for g in grads]
    wide = [g.reshape((2, 4, 2) + s) for g, s in zip(grads, shapes, strict=True)]
    scratch = []
    for lead in (2, 2, 4, 4, 3, 3, 2, 2):
        scratch += [pltpu.VMEM((lead,) + s, BF) for s in shapes]
    outs = pl.pallas_call(
        functools.partial(reduce_kernel, n),
        out_shape=tuple(sds(s, F32) for s in shapes)
        + (sds(vec.shape, F32), sds((8, 128), F32)),
        in_specs=[VM] * (n + 1),
        out_specs=(VM,) * (n + 2),
        scratch_shapes=scratch
        + [
            pltpu.VMEM((6,) + vec.shape, F32),
            pltpu.VMEM((6, 8, 128), F32),
            pltpu.SemaphoreType.DMA((n, 9)),
            pltpu.SemaphoreType.DMA((n, 9)),
            pltpu.SemaphoreType.DMA((6,)),
            pltpu.SemaphoreType.DMA((6,)),
            pltpu.SemaphoreType.DMA((6,)),
            pltpu.SemaphoreType.DMA((6,)),
        ],
        compiler_params=params(6),
        name="reduce_grads",
    )(*wide, vec)
    return list(outs[:n]), outs[n], outs[n + 1][0, 0]


def adamw_update(weight, moment_one, moment_two, gradient, step_rate, decay_rate):
    first_moment = DECAY_FIRST * moment_one + (1.0 - DECAY_FIRST) * gradient
    second_moment = DECAY_SECOND * moment_two + (1.0 - DECAY_SECOND) * gradient * gradient
    first_hat = first_moment / (1.0 - DECAY_FIRST**STEP)
    second_hat = second_moment / (1.0 - DECAY_SECOND**STEP)
    fresh_weight = weight - step_rate * (
        first_hat / (jnp.sqrt(second_hat) + ADAM_EPSILON) + decay_rate * weight
    )
    return (fresh_weight, first_moment, second_moment)


def on_device(
    tokens,
    cotangent,
    segment_ids,
    valid,
    qkv_weight,
    qkv_moment1,
    qkv_moment2,
    out_weight,
    out_moment1,
    out_moment2,
    fc_weight,
    fc_moment1,
    fc_moment2,
    proj_weight,
    proj_moment1,
    proj_moment2,
    vector_params,
    vector_moment1,
    vector_moment2,
    fc_bias,
    fc_bias_moment1,
    fc_bias_moment2,
):
    tensor_count = lax.axis_size("tensor")
    rank = lax.axis_index("tensor")
    x, c = rank // 2, rank % 2
    width = vector_params.shape[1]
    cols = width // tensor_count
    heads = cols // HD
    hidden = fc_bias.shape[0] // tensor_count
    part_rows = qkv_weight.shape[0]

    wq_s = qkv_weight.reshape(part_rows, 3 * cols).astype(BF)
    wo_s = out_weight.T.astype(BF)
    wf_s = fc_weight.astype(BF)
    wp_s = proj_weight.T.astype(BF)
    grad_low = cotangent * valid.astype(BF)[:, None]

    rows3 = segment_ids.reshape(-1, SLOT)
    starts = jnp.sum((rows3[:, None, :] < rows3[:, :, None]).astype(jnp.int32), axis=-1)
    starts = jnp.stack([lax.dynamic_index_in_dim(starts, 2 * x, 0, False), starts[1]])[:, None, :]

    def of_slots(vector):
        parts = vector.reshape(tensor_count, -1)
        return jnp.stack([lax.dynamic_index_in_dim(parts, c + 2 * s, 0, False) for s in range(2)])

    qb, vb = of_slots(vector_params[4]), of_slots(vector_params[5])
    bias = jnp.concatenate([qb, jnp.zeros_like(qb), vb], axis=1)[:, :, None]
    fb = of_slots(fc_bias)[:, None, :]

    tk, gl = share_tokens(tokens, grad_low)
    wq, wo, wf, wp = gather_weights([wq_s, wo_s, wf_s, wp_s])
    n1, u = project_qkv(tk, vector_params, bias, wq)
    units = u.reshape(3, 3, heads, HD, SLOT)
    ctx, lse = attend(units, starts)
    ctxc, resid, n2 = project_out(ctx.reshape(3, cols, SLOT), wo, tk, vector_params)
    br, dn, gf, gp, gb = feed_forward(n2, gl, wf, wp, fb)
    mixed, dres, dctx, go, vg2 = middle_back(br, dn, resid, gl, ctxc, wo, vector_params)
    du = attend_back(units, starts, ctx, dctx.reshape(ctx.shape), lse)
    gq, input_grad, vg1, qb_sums = first_back(
        du.reshape(u.shape), n1, wq, dres, tk, vector_params
    )
    sums = qb_sums[:, 0, :]
    own_slot = (jnp.arange(2) == x).astype(F32)[:, None]
    per_slot = sums[:2] + own_slot * sums[2:3]

    def to_heads(values):
        return lax.dynamic_update_slice(
            lax.dynamic_update_slice(
                jnp.zeros((tensor_count, values.shape[1]), F32), values[:1], (c, 0)
            ),
            values[1:],
            (c + 2, 0),
        )

    vec = jnp.concatenate(
        [
            vg1[:2],
            vg2[:2],
            to_heads(per_slot[:, :cols]).reshape(1, width),
            to_heads(per_slot[:, 2 * cols :]).reshape(1, width),
            vg2[2:4],
            to_heads(gb[:, 0, :]).reshape(-1, width),
        ],
        axis=0,
    )
    n_vec = vec.shape[0]
    vec = jnp.pad(vec, ((0, -n_vec % 8), (0, 0)))
    (gq, go, gf, gp), vec, squares = reduce_grads([gq, go, gf, gp], vec)
    vec = vec[:n_vec]
    vector_grad, fc_bias_grad = vec[:8], vec[8:].reshape(-1)
    grad_norm = jnp.sqrt(squares + jnp.sum(vec * vec))
    factor = CLIP_NORM / jnp.maximum(grad_norm, CLIP_NORM)
    qkv_new = adamw_update(
        qkv_weight, qkv_moment1, qkv_moment2, factor * gq.reshape(qkv_weight.shape), RATE_MATRIX, WEIGHT_DECAY
    )
    out_new = adamw_update(
        out_weight, out_moment1, out_moment2, factor * go.T, RATE_MATRIX, WEIGHT_DECAY
    )
    fc_new = adamw_update(fc_weight, fc_moment1, fc_moment2, factor * gf, RATE_MATRIX, WEIGHT_DECAY)
    proj_new = adamw_update(
        proj_weight, proj_moment1, proj_moment2, factor * gp.T, RATE_MATRIX, WEIGHT_DECAY
    )
    vector_new = adamw_update(
        vector_params, vector_moment1, vector_moment2, factor * vector_grad, RATE_VECTOR, 0.0
    )
    fc_bias_new = adamw_update(
        fc_bias, fc_bias_moment1, fc_bias_moment2, factor * fc_bias_grad, RATE_VECTOR, 0.0
    )
    return (
        mixed,
        input_grad,
        grad_norm,
        *qkv_new,
        *out_new,
        *fc_new,
        *proj_new,
        *vector_new,
        *fc_bias_new,
    )


def solution(mesh):
    rows = P(("dp", "tensor"), None)
    by_rows = [P("dp", None, "tensor")] * 3
    by_out = [P("tensor", "dp")] * 3
    by_fc = [P("dp", "tensor")] * 3
    weights = by_rows + by_out + by_fc + by_out
    return jax.shard_map(
        on_device,
        mesh=mesh,
        in_specs=(rows, rows, P("dp"), P(("dp", "tensor")), *weights, *[P()] * 6),
        out_specs=(rows, rows, P(), *weights, *[P()] * 6),
        check_vma=False,
    )
```

```python
import functools
import math

import jax
import jax.numpy as jnp
from jax import lax
from jax.experimental import pallas as pl
from jax.experimental.pallas import tpu as pltpu
from jax.sharding import PartitionSpec as P

HD = 64
SLOT = 1024
STEP = 10
NORM_EPSILON = 1e-05
MASK_FILL = -1e30
DECAY_FIRST = 0.5
DECAY_SECOND = 0.5
ADAM_EPSILON = 1e-08
WEIGHT_DECAY = 0.1
CLIP_NORM = 1.0
RATE_MATRIX = 0.04
RATE_VECTOR = 0.3

MESH = pl.DeviceIdType.MESH
BF = jnp.bfloat16
F32 = jnp.float32
HALF = SLOT // 2
BLK = 256
VMEM_LIMIT = 58 * 2**20
LOG2E = math.log2(math.e)
SCORE_SCALE = float(HD) ** (-0.5)
SCORE_SCALE2 = SCORE_SCALE * LOG2E


def dot_nn(a, b):
    return lax.dot_general(a, b, (((1,), (0,)), ((), ())), preferred_element_type=F32)


def dot_nt(a, b):
    return lax.dot_general(a, b, (((1,), (1,)), ((), ())), preferred_element_type=F32)


def dot_tn(a, b):
    return lax.dot_general(a, b, (((0,), (0,)), ((), ())), preferred_element_type=F32)


def dot_tt(a, b):
    return lax.dot_general(a, b, (((0,), (1,)), ((), ())), preferred_element_type=F32)


def params(collective_id=None):
    if collective_id is None:
        return pltpu.CompilerParams(vmem_limit_bytes=VMEM_LIMIT)
    return pltpu.CompilerParams(
        vmem_limit_bytes=VMEM_LIMIT, collective_id=collective_id, has_side_effects=True
    )


VM = pl.BlockSpec(memory_space=pltpu.VMEM)
ANY = pl.BlockSpec(memory_space=pl.ANY)


def sds(shape, dtype):
    return jax.ShapeDtypeStruct(shape, dtype)


def here():
    t = lax.axis_index("tensor")
    return lax.axis_index("dp"), t // 2, t % 2


def greet(ids):
    sem = pltpu.get_barrier_semaphore()
    for one in ids:
        pl.semaphore_signal(sem, inc=1, device_id=one, device_id_type=MESH)
    pl.semaphore_wait(sem, len(ids))


def remote(src, dst, send_sem, recv_sem, target):
    return pltpu.make_async_remote_copy(
        src_ref=src,
        dst_ref=dst,
        send_sem=send_sem,
        recv_sem=recv_sem,
        device_id=target,
        device_id_type=MESH,
    )


def rows_at(start, size):
    return pl.ds(pl.multiple_of(start, size), size)


def norm_parts(values):
    centered = values - jnp.mean(values, axis=-1, keepdims=True)
    variance = jnp.mean(centered * centered, axis=-1, keepdims=True)
    scale = lax.rsqrt(variance + NORM_EPSILON)
    return centered * scale, scale


class Gather:
    def __init__(self, shard, whole, loc, ss, rs):
        dp, x, c = here()
        z, y = dp // 2, dp % 2
        me = x * 2 + c
        x_peer = (dp, (1 - x) * 2 + c)
        y_peer = (z * 2 + 1 - y, me)
        block = whole.at[x, z, y]
        column = whole.at[x, :, y]
        from_x = whole.at[1 - x, pl.ds(0, 2), y]
        from_y = whole.at[x, pl.ds(2, 2), 1 - y]
        self.own = pltpu.make_async_copy(shard, block, loc)
        self.along = [
            remote(shard, block, ss.at[k], rs.at[k], (lax.rem(z + k + 1, 4) * 2 + y, me))
            for k in range(3)
        ]
        self.beside = [
            remote(column, column, ss.at[3], rs.at[3], x_peer),
            remote(column, column, ss.at[4], rs.at[4], y_peer),
        ]
        self.passed = [
            remote(from_x, from_x, ss.at[5], rs.at[5], y_peer),
            remote(from_y, from_y, ss.at[6], rs.at[6], x_peer),
        ]

    def start_along(self):
        self.own.start()
        for one in self.along:
            one.start()

    def start_beside(self):
        self.own.wait()
        for one in self.along:
            one.wait()
        for one in self.beside:
            one.start()

    def start_passed(self):
        for one in self.beside:
            one.wait()
        for one in self.passed:
            one.start()

    def finish(self):
        for one in self.passed:
            one.wait()


def neighbours():
    dp, x, c = here()
    z, y = dp // 2, dp % 2
    me = x * 2 + c
    along = [(lax.rem(z + k, 4) * 2 + y, me) for k in (1, 2, 3)]
    return along, (dp, (1 - x) * 2 + c), (z * 2 + 1 - y, me), (dp, x * 2 + 1 - c)


def whole_weight(ref, slot):
    value = ref[slot]
    return value.reshape(-1, value.shape[-1])


def allowed_pairs(key_block, query_block, start_row, wide):
    keys = lax.broadcasted_iota(jnp.int32, (BLK, wide), 0) + key_block * BLK
    mask = keys >= start_row
    if key_block == query_block:
        queries = lax.broadcasted_iota(jnp.int32, (BLK, wide), 1) + query_block * BLK
        mask = mask & (keys <= queries)
    return mask


def attend_unit(q, k, v, start):
    blocks = SLOT // BLK
    for i in range(blocks):
        cols = slice(i * BLK, (i + 1) * BLK)
        query = q(cols)
        scores = []
        for j in range(i + 1):
            raw = dot_tn(k(slice(j * BLK, (j + 1) * BLK)), query) * SCORE_SCALE2
            scores.append(jnp.where(allowed_pairs(j, i, start(cols), BLK), raw, MASK_FILL))
        top = functools.reduce(jnp.maximum, [jnp.max(s, axis=0, keepdims=True) for s in scores])
        exps = [jnp.exp2(s - top) for s in scores]
        total = functools.reduce(jnp.add, [jnp.sum(e, axis=0, keepdims=True) for e in exps])
        acc = None
        for j in range(i + 1):
            term = dot_nn(v(slice(j * BLK, (j + 1) * BLK)), exps[j].astype(BF))
            acc = term if acc is None else acc + term
        yield cols, acc / total, top + jnp.log2(total)


def forward_kernel(n, custom, *refs):
    tok_ref, grad_ref, vec_ref, bias_ref, start_ref = refs[:5]
    shards, wholes = refs[5 : 5 + n], refs[5 + n : 5 + 2 * n]
    gl_ref, n1_ref, u_ref, ctx_ref, lse_ref, ctxc_ref, resid_ref, n2_ref = refs[
        5 + 2 * n : 13 + 2 * n
    ]
    tk, half, part, got, loc, gs, gr, ts, tr, xs, cs_s, cs_r = refs[13 + 2 * n :]
    dp, x, c = here()
    core = (dp, x * 2 + 1 - c)
    x_peer = (dp, (1 - x) * 2 + c)
    across = [(dp, (1 - x) * 2), (dp, (1 - x) * 2 + 1)]
    if custom:
        along, _, y_peer, _ = neighbours()
        greet([core, *across, *along, y_peer])
        gathers = [
            Gather(shards[a], wholes[a], loc.at[2 + a], gs.at[a], gr.at[a]) for a in range(n)
        ]
    else:
        greet([core, *across])
        gathers = []
    wq, wo = wholes[:3], wholes[3]
    if not custom:
        wq, wo = shards[:3], shards[3]
    rows = tok_ref.shape[0]
    first = x * HALF

    def step(number, what):
        if number < len(gathers):
            getattr(gathers[number], what)()

    own_rows = pl.ds(pl.multiple_of(first + c * rows, BLK), rows)
    gl_rows = pl.ds(pl.multiple_of(c * rows, BLK), rows)
    swap_tok = remote(tok_ref, tk.at[own_rows], ts.at[0], tr.at[0], core)
    swap_grad = remote(grad_ref, gl_ref.at[gl_rows], ts.at[1], tr.at[1], core)
    mine = pltpu.make_async_copy(grad_ref, gl_ref.at[gl_rows], loc.at[0])
    mine_tok = pltpu.make_async_copy(tok_ref, tk.at[own_rows], loc.at[1])
    source = [
        tok_ref.at[pl.ds(pl.multiple_of((1 - x) * BLK + k * BLK, BLK), BLK)] for k in range(2)
    ]
    there = [
        tk.at[pl.ds(pl.multiple_of(x * (SLOT + HALF) + k * BLK, BLK), BLK)] for k in range(2)
    ]
    halves = [remote(source[k], there[k], ts.at[2 + k], tr.at[2], across[k]) for k in range(2)]
    landed = tk.at[pl.ds(pl.multiple_of((1 - x) * (SLOT + HALF) + c * BLK, BLK), BLK)]
    handed = remote(landed, landed, ts.at[4], tr.at[3], core)

    swap_tok.start()
    step(0, "start_along")
    step(1, "start_along")
    mine_tok.start()

    gain, shift = vec_ref[0:1, :], vec_ref[1:2, :]

    def norm_rows(start, count):
        def norm(i, carry):
            at = rows_at(start + i * BLK, BLK)
            unit, _ = norm_parts(tk[at, :].astype(F32))
            n1_ref[at, :] = (unit * gain + shift).astype(BF)
            return carry

        lax.fori_loop(0, count // BLK, norm, 0)

    mine_tok.wait()
    norm_rows(first + c * rows, rows)
    step(0, "start_beside")
    step(2, "start_along")
    swap_tok.wait()
    norm_rows(first + (1 - c) * rows, rows)
    step(1, "start_beside")
    step(3, "start_along")
    step(0, "start_passed")
    step(2, "start_beside")
    step(4, "start_along")
    step(1, "start_passed")

    @pl.when(c == 1 - x)
    def _():
        for one in halves:
            one.start()

    step(0, "finish")
    step(2, "start_passed")

    def project(group, slot, first_row):
        weights = [whole_weight(w, slot) for w in wq]

        def chunk(i, carry):
            lanes = rows_at(i * BLK, BLK)
            values = n1_ref[rows_at(first_row + i * BLK, BLK), :]
            for k in range(3):
                out = dot_tt(weights[k], values) + bias_ref[slot, k]
                u_ref[group, k, :, :, lanes] = out.reshape(-1, HD, BLK).astype(BF)
            return carry

        lax.fori_loop(0, SLOT // BLK, chunk, 0)

    def attend(group, which):
        def unit(h, carry):
            for cols, context, log_total in attend_unit(
                lambda s: u_ref[group, 0, h, :, s],
                lambda s: u_ref[group, 1, h, :, s],
                lambda s: u_ref[group, 2, h, :, s],
                lambda s: start_ref[which, :, s],
            ):
                ctx_ref[group, h, :, cols] = context.astype(BF)
                lse_ref[group, h, :, cols] = log_total
            return carry

        lax.fori_loop(0, u_ref.shape[2], unit, 0)

    project(x, x, x * SLOT)
    step(3, "start_beside")
    step(5, "start_along")
    attend(x, 0)
    step(1, "finish")
    step(2, "finish")
    step(3, "start_passed")
    step(4, "start_beside")
    swap_grad.start()
    mine.start()
    project(1 - x, 1 - x, x * SLOT)
    attend(1 - x, 0)
    step(5, "start_beside")
    halves[0].wait_recv()
    handed.start()
    handed.wait()
    norm_rows((1 - x) * (SLOT + HALF), HALF)
    step(4, "start_passed")
    project(2, x, (1 - x) * SLOT)
    attend(2, 1)
    theirs = pl.ds(pl.multiple_of((1 - x) * HALF, HALF), HALF)
    cross = remote(ctx_ref.at[2, :, :, theirs], half, xs.at[0], xs.at[1], x_peer)
    cross.start()
    step(3, "finish")

    @pl.when(c == 1 - x)
    def _():
        for one in halves:
            one.wait_send()

    chunks = []

    def send(chunk, values):
        at = rows_at(chunk * BLK, BLK)
        part[at, :] = values.astype(BF)
        copy = remote(part.at[at], got.at[at], cs_s.at[chunk], cs_r.at[chunk], core)
        copy.start()
        chunks.append((chunk, copy))

    def context_of(group, lanes):
        value = ctx_ref[group, :, :, lanes]
        return value.reshape(-1, value.shape[-1])

    for i in range(SLOT // BLK):
        lanes = slice(i * BLK, (i + 1) * BLK)
        chunk = x * 2 + i
        at = rows_at(chunk * BLK, BLK)
        zero, one = context_of(0, lanes), context_of(1, lanes)
        send(chunk, dot_tt(zero, whole_weight(wo, 0)) + dot_tt(one, whole_weight(wo, 1)))
        ctxc_ref[0, :, at] = zero
        ctxc_ref[1, :, at] = one
    cross.wait()
    step(5, "start_passed")
    for i in range(HALF // BLK):
        chunk = (1 - x) * 4 + i
        at = rows_at(chunk * BLK, BLK)
        own = context_of(2, rows_at(x * HALF + i * BLK, BLK))
        other = half[:, :, i * BLK : (i + 1) * BLK].reshape(-1, BLK)
        send(chunk, dot_tt(own, whole_weight(wo, x)) + dot_tt(other, whole_weight(wo, 1 - x)))
        ctxc_ref[x, :, at] = own
        ctxc_ref[1 - x, :, at] = other
    for chunk, copy in chunks:
        copy.wait()
        at = rows_at(chunk * BLK, BLK)
        tokens = tk[rows_at(first + chunk * BLK, BLK), :].astype(F32)
        summed = part[at, :].astype(F32) + got[at, :].astype(F32)
        resid = tokens + summed + vec_ref[6:7, :]
        resid_ref[at, :] = resid
        unit, _ = norm_parts(resid)
        n2_ref[at, :] = (unit * vec_ref[2:3, :] + vec_ref[3:4, :]).astype(BF)
    mine.wait()
    swap_grad.wait()
    step(4, "finish")
    step(5, "finish")


def forward(tokens, grad_low, vectors, bias, starts, shards):
    rows, width = tokens.shape
    n = len(shards)
    cols = shards[0].shape[1]
    heads = cols // HD
    chip = 2 * rows
    custom = lax.axis_size("dp") == 8
    if custom:
        wholes = [sds((2, 4, 2) + s.shape, BF) for s in shards]
        places = [VM] * 4 + [ANY] * (n - 4)
        ins = list(shards)
    else:
        slot = lax.axis_index("tensor") // 2
        swap = [(0, 2), (1, 3), (2, 0), (3, 1)]
        ins = []
        for shard in shards:
            own = lax.all_gather(shard, "dp", axis=0, tiled=True)
            other = lax.ppermute(own, "tensor", swap)
            ins.append(
                jnp.stack([jnp.where(slot == 0, own, other), jnp.where(slot == 0, other, own)])
            )
        wholes = [sds((8, 128), BF)] * n
        places = [ANY] * n
    dma = pltpu.SemaphoreType.DMA
    outs = pl.pallas_call(
        functools.partial(forward_kernel, n, custom),
        out_shape=(
            *wholes,
            sds((chip, width), BF),
            sds((2 * SLOT, width), BF),
            sds((3, 3, heads, HD, SLOT), BF),
            sds((3, heads, HD, SLOT), BF),
            sds((3, heads, 1, SLOT), F32),
            sds((2, cols, chip), BF),
            sds((chip, width), F32),
            sds((chip, width), BF),
        ),
        in_specs=[VM] * 5 + ([VM] * n if custom else [VM] * 4 + [ANY] * (n - 4)),
        out_specs=(*places, ANY, *[VM] * 7),
        scratch_shapes=[
            pltpu.VMEM((2 * SLOT, width), BF),
            pltpu.VMEM((heads, HD, HALF), BF),
            pltpu.VMEM((chip, width), BF),
            pltpu.VMEM((chip, width), BF),
            dma((2 + n,)),
            dma((n, 7)),
            dma((n, 7)),
            dma((5,)),
            dma((4,)),
            dma((2,)),
            dma((chip // BLK,)),
            dma((chip // BLK,)),
        ],
        compiler_params=params(1),
        name="forward",
    )(tokens, grad_low, vectors, bias, starts, *ins)
    weights = list(outs[:n])
    if not custom:
        weights = ins
    return weights, outs[n:]


GELU_C = math.sqrt(2.0 / math.pi)
GELU_A = 0.044715


def ffn_kernel(
    n2_ref, gl_ref, wf_ref, wp_ref, fb_ref, br_ref, dn2_ref, gf_ref, gp_ref, gb_ref, act, dpre
):
    rows_all, width = n2_ref.shape
    hidden = wf_ref.shape[2]

    def forward_back(i, carry):
        rows = rows_at(i * BLK, BLK)
        n2, gl = n2_ref[rows, :], gl_ref[rows, :]
        for s in range(2):
            lanes = slice(s * hidden, (s + 1) * hidden)
            u = dot_nn(n2, wf_ref[s]) + fb_ref[s]
            up = dot_nn(gl, wp_ref[s])
            t = jnp.tanh(GELU_C * (u + GELU_A * u * u * u))
            act[rows, lanes] = (0.5 * u * (1.0 + t)).astype(BF)
            slope = 0.5 * (1.0 + t) + 0.5 * u * (1.0 - t * t) * GELU_C * (
                1.0 + 3.0 * GELU_A * u * u
            )
            d = (up * slope).astype(BF)
            dpre[rows, lanes] = d
            gb_ref[s] += jnp.sum(d.astype(F32), axis=0, keepdims=True)
        br = dot_nt(act[rows, :hidden], wp_ref[0]) + dot_nt(act[rows, hidden:], wp_ref[1])
        br_ref[rows, :] = br.astype(BF)
        dn = dot_nt(dpre[rows, :hidden], wf_ref[0]) + dot_nt(dpre[rows, hidden:], wf_ref[1])
        dn2_ref[rows, :] = dn.astype(BF)
        return carry

    gb_ref[...] = jnp.zeros_like(gb_ref)
    lax.fori_loop(0, rows_all // BLK, forward_back, 0)
    for s in range(2):

        def weight_grads(i, carry, s=s):
            lanes = rows_at(i * BLK, BLK)
            wide = rows_at(s * hidden + i * BLK, BLK)
            gp_ref[s, :, lanes] = dot_tn(gl_ref[...], act[:, wide]).astype(BF)
            gf_ref[s, :, lanes] = dot_tn(n2_ref[...], dpre[:, wide]).astype(BF)
            return carry

        lax.fori_loop(0, hidden // BLK, weight_grads, 0)


def feed_forward(n2, gl, wf, wp, fb):
    rows, width = n2.shape
    hidden = wf.shape[2]
    return pl.pallas_call(
        ffn_kernel,
        out_shape=(
            sds((rows, width), BF),
            sds((rows, width), BF),
            sds(wf.shape, BF),
            sds(wp.shape, BF),
            sds((2, 1, hidden), F32),
        ),
        in_specs=[VM] * 5,
        out_specs=(VM,) * 5,
        scratch_shapes=[
            pltpu.VMEM((rows, 2 * hidden), BF),
            pltpu.VMEM((rows, 2 * hidden), BF),
        ],
        compiler_params=params(),
        name="feed_forward",
    )(n2, gl, wf, wp, fb)


def mid_kernel(
    br_ref, dn_ref, resid_ref, gl_ref, ctxc_ref, wo_ref, vec_ref,
    mixed_ref, dres_ref, dctx_ref, go_ref, vg_ref,
    low, got_br, got_dn, outgoing, half, bs, xs, cs_s, cs_r,
):
    dp, x, c = here()
    core = (dp, x * 2 + 1 - c)
    x_peer = (dp, (1 - x) * 2 + c)
    greet([core, x_peer])
    rows_all, width = dn_ref.shape
    own_rows = rows_all // 2
    their = pl.ds(pl.multiple_of((1 - c) * own_rows, BLK), own_rows)
    n_chunks = rows_all // BLK
    copies = []
    for r in range(n_chunks):
        rows = pl.ds(r * BLK, BLK)
        copy = remote(dn_ref.at[rows], got_dn.at[rows], cs_s.at[r], cs_r.at[r], core)
        copy.start()
        copies.append(copy)
    branch = remote(br_ref.at[their], got_br, bs.at[0], bs.at[1], core)
    branch.start()
    vg_ref[...] = jnp.zeros_like(vg_ref)
    gain = vec_ref[2:3, :]
    for r in range(n_chunks):
        copies[r].wait()
        rows = slice(r * BLK, (r + 1) * BLK)
        dn = dn_ref[rows, :].astype(F32) + got_dn[rows, :].astype(F32)
        unit, scale = norm_parts(resid_ref[rows, :])
        e = dn * gain
        dres = gl_ref[rows, :].astype(F32) + scale * (
            e
            - jnp.mean(e, axis=-1, keepdims=True)
            - unit * jnp.mean(e * unit, axis=-1, keepdims=True)
        )
        low[rows, :] = dres.astype(BF)
        mine = r % (n_chunks // 2)

        @pl.when(c == r // (n_chunks // 2))
        def _(dn=dn, unit=unit, dres=dres, mine=mine):
            dres_ref[mine * BLK : (mine + 1) * BLK, :] = dres
            vg_ref[0:1, :] += jnp.sum(dn * unit, axis=0, keepdims=True)
            vg_ref[1:2, :] += jnp.sum(dn, axis=0, keepdims=True)
            vg_ref[2:3, :] += jnp.sum(dres, axis=0, keepdims=True)

    for i in range(HALF // BLK):
        lanes = slice(i * BLK, (i + 1) * BLK)
        rows = rows_at((1 - x) * SLOT + i * BLK, BLK)
        outgoing[:, lanes] = dot_tt(wo_ref[1 - x], low[rows, :]).astype(BF)
        dctx_ref[2, :, rows_at(x * HALF + i * BLK, BLK)] = dot_tt(
            wo_ref[x], low[rows, :]
        ).astype(BF)
    cross = remote(outgoing, half, xs.at[0], xs.at[1], x_peer)
    cross.start()
    for i in range(SLOT // BLK):
        lanes = slice(i * BLK, (i + 1) * BLK)
        rows = rows_at(x * HALF + i * BLK, BLK)
        for s in range(2):
            dctx_ref[s, :, lanes] = dot_tt(wo_ref[s], low[rows, :]).astype(BF)
    for s in range(2):
        go_ref[s] = dot_tt(low[...], ctxc_ref[s]).astype(BF)
    branch.wait()
    for r in range(own_rows // BLK):
        rows = slice(r * BLK, (r + 1) * BLK)
        wide = rows_at(c * own_rows + r * BLK, BLK)
        mixed = (
            resid_ref[wide, :]
            + br_ref[wide, :].astype(F32)
            + got_br[rows, :].astype(F32)
            + vec_ref[7:8, :]
        )
        mixed_ref[rows, :] = mixed.astype(BF)
        vg_ref[3:4, :] += jnp.sum(gl_ref[wide, :].astype(F32), axis=0, keepdims=True)
    cross.wait()
    dctx_ref[2, :, pl.ds(pl.multiple_of((1 - x) * HALF, HALF), HALF)] = half[...]


def middle_back(br, dn, resid, gl, ctxc, wo, vectors):
    rows, width = dn.shape
    cols = ctxc.shape[1]
    return pl.pallas_call(
        mid_kernel,
        out_shape=(
            sds((rows // 2, width), BF),
            sds((rows // 2, width), F32),
            sds((3, cols, SLOT), BF),
            sds((2, width, cols), BF),
            sds((8, width), F32),
        ),
        in_specs=[VM] * 7,
        out_specs=(VM,) * 5,
        scratch_shapes=[
            pltpu.VMEM((rows, width), BF),
            pltpu.VMEM((rows // 2, width), BF),
            pltpu.VMEM((rows, width), BF),
            pltpu.VMEM((cols, HALF), BF),
            pltpu.VMEM((cols, HALF), BF),
            pltpu.SemaphoreType.DMA((2,)),
            pltpu.SemaphoreType.DMA((2,)),
            pltpu.SemaphoreType.DMA((rows // BLK,)),
            pltpu.SemaphoreType.DMA((rows // BLK,)),
        ],
        compiler_params=params(4),
        name="middle_back",
    )(br, dn, resid, gl, ctxc, wo, vectors)


class Reduce:
    def __init__(self, grad, total, bufs, ss, rs):
        dp, x, c = here()
        z, y = dp // 2, dp % 2
        along, x_peer, y_peer, _ = neighbours()
        self.grad, self.total = grad, total
        self.r1x, self.r1y, self.r2x, self.r2y, self.r3, self.s3, self.m1, self.m2 = bufs
        self.place = (x, y, z)
        self.first = [
            remote(grad.at[1 - x, pl.ds(0, 2), 1 - y], self.r1y, ss.at[0], rs.at[0], y_peer),
            remote(grad.at[1 - x, pl.ds(2, 2), 1 - y], self.r1x, ss.at[1], rs.at[1], x_peer),
        ]
        self.early = [
            remote(
                grad.at[1 - x, pl.ds(2, 2), y], self.r2x.at[pl.ds(2, 2)], ss.at[2], rs.at[2], x_peer
            ),
            remote(
                grad.at[x, pl.ds(0, 2), 1 - y], self.r2y.at[pl.ds(0, 2)], ss.at[3], rs.at[3], y_peer
            ),
        ]
        self.second = [
            remote(self.m1, self.r2x.at[pl.ds(0, 2)], ss.at[4], rs.at[4], x_peer),
            remote(self.m2, self.r2y.at[pl.ds(2, 2)], ss.at[5], rs.at[5], y_peer),
        ]
        self.third = [
            remote(self.s3.at[k], self.r3.at[k], ss.at[6 + k], rs.at[6 + k], along[k])
            for k in range(3)
        ]

    def start_first(self):
        for one in self.first:
            one.start()

    def start_early(self):
        for one in self.early:
            one.start()

    def start_second(self):
        x, y, z = self.place
        for one in self.first:
            one.wait()
        for k in range(2):
            self.m1[k] = (self.grad[1 - x, k, y].astype(F32) + self.r1y[k].astype(F32)).astype(BF)
            self.m2[k] = (self.grad[x, 2 + k, 1 - y].astype(F32) + self.r1x[k].astype(F32)).astype(
                BF
            )
        for one in self.second:
            one.start()

    def column(self, place):
        x, y, _ = self.place
        return (
            self.grad[x, place, y].astype(F32)
            + self.r2x[place].astype(F32)
            + self.r2y[place].astype(F32)
        )

    def start_third(self):
        z = self.place[2]
        for one in self.early + self.second:
            one.wait()
        for k in range(3):
            self.s3[k] = self.column(lax.rem(z + k + 1, 4)).astype(BF)
            self.third[k].start()
        self.total[...] = self.column(z)

    def finish(self):
        for one in self.third:
            one.wait()
        total = self.total[...]
        for k in range(3):
            total = total + self.r3[k].astype(F32)
        self.total[...] = total
        return jnp.sum(total * total)


def eight_peers():
    dp, x, c = here()
    z, y = dp // 2, dp % 2
    peers = []
    for k in range(1, 8):
        kx, ky, kc = k // 4, k // 2 % 2, k % 2
        there = ((1 - x if kx else x), (1 - y if ky else y), (1 - c if kc else c))
        peers.append((z * 2 + there[1], there[0] * 2 + there[2]))
    return peers


def sum_over_all(value_ref, near, far, ss, rs):
    dp, x, c = here()
    z, y = dp // 2, dp % 2
    along = neighbours()[0]
    me = x * 4 + y * 2 + c
    near[me] = value_ref[...]
    copies = [
        remote(value_ref, near.at[me], ss.at[k], rs.at[k], peer)
        for k, peer in enumerate(eight_peers())
    ]
    for one in copies:
        one.start()
    for one in copies:
        one.wait()
    value_ref[...] = functools.reduce(jnp.add, [near[k] for k in range(8)])
    far[z] = value_ref[...]
    copies = [
        remote(value_ref, far.at[z], ss.at[7 + k], rs.at[7 + k], along[k]) for k in range(3)
    ]
    for one in copies:
        one.start()
    for one in copies:
        one.wait()
    value_ref[...] = functools.reduce(jnp.add, [far[k] for k in range(4)])


def attend_back_unit(u, out, start, ctx, dctx, lse, dq_ref):
    blocks = SLOT // BLK
    delta = jnp.sum(dctx.astype(F32) * ctx.astype(F32), axis=0, keepdims=True)
    for j in range(blocks):
        keys = slice(j * BLK, (j + 1) * BLK)
        k = u(1, keys)
        v = u(2, keys)
        probs, dscores = [], []
        for i in range(j, blocks):
            cols = slice(i * BLK, (i + 1) * BLK)
            raw = dot_tn(k, u(0, cols)) * SCORE_SCALE2 - lse[:, cols]
            prob = jnp.exp2(jnp.where(allowed_pairs(j, i, start[:, cols], BLK), raw, MASK_FILL))
            dprob = dot_tn(v, dctx[:, cols])
            probs.append(prob.astype(BF))
            dscores.append((prob * (dprob - delta[:, cols])).astype(BF))
        dk, dv = None, None
        for n, i in enumerate(range(j, blocks)):
            cols = slice(i * BLK, (i + 1) * BLK)
            dv_term = dot_nt(dctx[:, cols], probs[n])
            dk_term = dot_nt(u(0, cols), dscores[n])
            dv = dv_term if dv is None else dv + dv_term
            dk = dk_term if dk is None else dk + dk_term
            dq_term = dot_nn(k, dscores[n])
            if j == 0:
                dq_ref[:, cols] = dq_term
            else:
                dq_ref[:, cols] += dq_term
        out(1, keys, (dk * SCORE_SCALE).astype(BF))
        out(2, keys, dv.astype(BF))
    out(0, slice(0, SLOT), (dq_ref[...] * SCORE_SCALE).astype(BF))


def adamw_update(weight, moment_one, moment_two, gradient, step_rate, decay_rate):
    first_moment = DECAY_FIRST * moment_one + (1.0 - DECAY_FIRST) * gradient
    second_moment = DECAY_SECOND * moment_two + (1.0 - DECAY_SECOND) * gradient * gradient
    first_hat = first_moment / (1.0 - DECAY_FIRST**STEP)
    second_hat = second_moment / (1.0 - DECAY_SECOND**STEP)
    fresh_weight = weight - step_rate * (
        first_hat / (jnp.sqrt(second_hat) + ADAM_EPSILON) + decay_rate * weight
    )
    return (fresh_weight, first_moment, second_moment)


VEC_ROWS = 24


def backward_kernel(custom, *refs):
    (u_ref, start_ref, ctx_ref, dctx_ref, lse_ref, n1_ref, wq0, wq1, wq2, dres_ref, tok_ref,
     vec_ref, vg2_ref, gb_ref, gp_in, gf_in, go_in) = refs[:17]
    refs = refs[17:]
    wq = (wq0, wq1, wq2)
    if custom:
        states, refs = refs[:12], refs[12:]
        ig_ref, vs_ref, norm_ref = refs[:3]
        fresh, refs = refs[3:15], refs[15:]
        gq = refs[:3]
        refs = refs[3:]
        totals, refs = refs[:6], refs[6:]
        bufs, refs = [refs[8 * a : 8 * a + 8] for a in range(6)], refs[48:]
        near_v, far_v, near_s, far_s, square, ss, rs, vs, vr, qs, qr = refs[:11]
        refs = refs[11:]
    else:
        ig_ref, vs_ref = refs[:2]
        gq, refs = refs[2:5], refs[5:]
    du, dq, half, part, got, xs, cs = refs
    dp, x, c = here()
    core = (dp, x * 2 + 1 - c)
    x_peer = (dp, (1 - x) * 2 + c)
    reduces = []
    if custom:
        greet(eight_peers() + neighbours()[0])
        grads = [gp_in, gf_in, go_in, *gq]
        reduces = [
            Reduce(grads[a], totals[a], bufs[a], ss.at[a], rs.at[a]) for a in range(6)
        ]
    else:
        greet([core, x_peer])

    def step(number, what):
        if custom:
            getattr(reduces[number], what)()

    step(0, "start_first")
    step(0, "start_early")
    step(1, "start_first")

    def attend_back(group, which):
        def unit(h, carry):
            def put(k, lanes, value):
                du[group, k, h, :, lanes] = value

            attend_back_unit(
                lambda k, lanes: u_ref[group, k, h, :, lanes],
                put,
                start_ref[which],
                ctx_ref[group, h],
                dctx_ref[group, h],
                lse_ref[group, h],
                dq,
            )
            return carry

        lax.fori_loop(0, u_ref.shape[2], unit, 0)

    attend_back(2, 1)
    theirs = pl.ds(pl.multiple_of((1 - x) * HALF, HALF), HALF)
    cross = remote(du.at[2, :, :, :, theirs], half, xs.at[0], xs.at[1], x_peer)
    cross.start()
    step(0, "start_second")
    step(1, "start_early")
    step(2, "start_first")
    attend_back(0, 0)
    step(1, "start_second")
    step(2, "start_early")
    attend_back(1, 0)
    step(0, "start_third")
    step(2, "start_second")

    cols = u_ref.shape[2] * HD
    full_rows = pl.ds(pl.multiple_of(x * SLOT, SLOT), SLOT)
    part_rows = pl.ds(pl.multiple_of((1 - x) * SLOT, SLOT), SLOT)

    def of_group(group, k, lanes):
        value = du[group, k, :, :, lanes]
        return value.reshape(cols, value.shape[-1])

    everything = slice(0, SLOT)
    for k in range(3):
        shape = gq[k].shape[1:]
        for s in range(2):
            gq[k][s] = dot_tt(n1_ref[full_rows, :], of_group(s, k, everything)).astype(BF).reshape(
                shape
            )
        both = gq[k][x].reshape(-1, cols).astype(F32) + dot_tt(
            n1_ref[part_rows, :], of_group(2, k, everything)
        )
        gq[k][x] = both.astype(BF).reshape(shape)
        step(3 + k, "start_first")
        step(3 + k, "start_early")
    step(1, "start_third")

    vs_ref[...] = jnp.zeros_like(vs_ref)
    ones = jnp.ones((8, SLOT), BF)
    for k in (0, 2):
        lanes = slice(k * cols, (k + 1) * cols)
        for g in range(2):
            vs_ref[pl.ds(16 + c + 2 * g, 1), lanes] = dot_nt(ones, of_group(g, k, everything))[0:1]
        vs_ref[pl.ds(16 + c + 2 * x, 1), lanes] += dot_nt(ones, of_group(2, k, everything))[0:1]
    for s in range(2):
        vs_ref[pl.ds(8 + c + 2 * s, 1), :] = gb_ref[s]
    vs_ref[2:4, :] = vg2_ref[0:2, :]
    vs_ref[6:8, :] = vg2_ref[2:4, :]

    def send(chunk, values):
        part[rows_at(chunk * BLK, BLK), :] = values.astype(BF)

    def back_through(pieces):
        total = None
        for value, slot, k in pieces:
            term = dot_tt(value, whole_weight(wq[k], slot))
            total = term if total is None else total + term
        return total

    for i in range(SLOT // BLK):
        lanes = slice(i * BLK, (i + 1) * BLK)
        send(
            x * 2 + i,
            back_through([(of_group(s, k, lanes), s, k) for s in range(2) for k in range(3)]),
        )
    cross.wait()
    for i in range(HALF // BLK):
        lanes = rows_at(x * HALF + i * BLK, BLK)
        send(
            (1 - x) * 4 + i,
            back_through(
                [(of_group(2, k, lanes), x, k) for k in range(3)]
                + [
                    (half[k, :, :, i * BLK : (i + 1) * BLK].reshape(cols, BLK), 1 - x, k)
                    for k in range(3)
                ]
            ),
        )
    own_chunks = (SLOT + HALF) // BLK // 2
    their = pl.ds(pl.multiple_of((1 - c) * own_chunks * BLK, BLK), own_chunks * BLK)
    swap = remote(part.at[their], got, cs.at[0], cs.at[1], core)
    swap.start()
    for k in range(3):
        step(3 + k, "start_second")
    step(2, "start_third")
    swap.wait()
    gain = vec_ref[0:1, :]
    for r in range(own_chunks):
        rows = slice(r * BLK, (r + 1) * BLK)
        wide = rows_at((c * own_chunks + r) * BLK, BLK)
        dn = part[wide, :].astype(F32) + got[rows, :].astype(F32)
        unit, scale = norm_parts(tok_ref[rows, :].astype(F32))
        e = dn * gain
        back = scale * (
            e
            - jnp.mean(e, axis=-1, keepdims=True)
            - unit * jnp.mean(e * unit, axis=-1, keepdims=True)
        )
        ig_ref[rows, :] = (dres_ref[rows, :] + back).astype(BF)
        vs_ref[0:1, :] += jnp.sum(dn * unit, axis=0, keepdims=True)
        vs_ref[1:2, :] += jnp.sum(dn, axis=0, keepdims=True)
    if not custom:
        return
    for k in range(3):
        step(3 + k, "start_third")
    sum_over_all(vs_ref, near_v, far_v, vs, vr)
    squares = functools.reduce(jnp.add, [one.finish() for one in reduces])
    square[...] = jnp.full(square.shape, squares, F32)
    sum_over_all(square, near_s, far_s, qs, qr)
    squares = square[0:1, 0:1] + jnp.sum(vs_ref[...] * vs_ref[...], keepdims=True)
    norm = jnp.sqrt(squares)
    norm_ref[...] = jnp.broadcast_to(norm, norm_ref.shape)
    factor = CLIP_NORM / jnp.maximum(norm, CLIP_NORM)

    def update(number, grad, index):
        old = [states[3 * number + m][index] for m in range(3)]
        new = adamw_update(*old, factor * grad, RATE_MATRIX, WEIGHT_DECAY)
        for m in range(3):
            fresh[3 * number + m][index] = new[m]

    for k in range(3):
        update(0, totals[3 + k][...], (slice(None), slice(k * cols, (k + 1) * cols)))
    update(1, totals[2][...].T, (slice(None), slice(None)))
    update(2, totals[1][...], (slice(None), slice(None)))
    update(3, totals[0][...].T, (slice(None), slice(None)))


def backward(units, starts, ctx, dctx, lse, n1, wq, dres, tokens, vectors, vg2, gb, grads, states):
    rows, width = tokens.shape
    heads = units.shape[2]
    cols = heads * HD
    chip = 2 * rows
    custom = lax.axis_size("dp") == 8
    dma = pltpu.SemaphoreType.DMA
    scratch = [
        pltpu.VMEM(units.shape, BF),
        pltpu.VMEM((HD, SLOT), F32),
        pltpu.VMEM((3, heads, HD, HALF), BF),
        pltpu.VMEM((chip, width), BF),
        pltpu.VMEM((rows, width), BF),
        dma((2,)),
        dma((2,)),
    ]
    ins = [units, starts, ctx, dctx, lse, n1, *wq, dres, tokens, vectors, vg2, gb]
    out_shape = [sds((rows, width), BF), sds((VEC_ROWS, width), F32)]
    if custom:
        shapes = [g.shape[-2:] for g in grads] + [(width // 8, cols)] * 3
        wide = [sds((2, 4, 2) + s, BF) for s in shapes]
        lead = (2, 2, 4, 4, 3, 3, 2, 2)
        scratch = (
            [pltpu.VMEM(w.shape, BF) for w in wide[3:]]
            + [pltpu.VMEM(s, F32) for s in shapes]
            + [pltpu.VMEM((n,) + s, BF) for s in shapes for n in lead]
            + [
                pltpu.VMEM((8, VEC_ROWS, width), F32),
                pltpu.VMEM((4, VEC_ROWS, width), F32),
                pltpu.VMEM((8, 8, 128), F32),
                pltpu.VMEM((4, 8, 128), F32),
                pltpu.VMEM((8, 128), F32),
                dma((6, 9)),
                dma((6, 9)),
                dma((10,)),
                dma((10,)),
                dma((10,)),
                dma((10,)),
            ]
            + scratch
        )
        ins += list(grads) + list(states)
        out_shape += [sds((8, 128), F32)] + [sds(s.shape, F32) for s in states]
    else:
        ins += list(grads)
        out_shape += [sds((2, width, cols), BF)] * 3
    return pl.pallas_call(
        functools.partial(backward_kernel, custom),
        out_shape=tuple(out_shape),
        in_specs=[VM] * 14 + [VM if custom else ANY] * 3 + [VM] * (len(ins) - 17),
        out_specs=(VM,) * len(out_shape),
        scratch_shapes=scratch,
        compiler_params=params(5),
        name="backward",
    )(*ins)


def on_device(
    tokens,
    cotangent,
    segment_ids,
    valid,
    qkv_weight,
    qkv_moment1,
    qkv_moment2,
    out_weight,
    out_moment1,
    out_moment2,
    fc_weight,
    fc_moment1,
    fc_moment2,
    proj_weight,
    proj_moment1,
    proj_moment2,
    vector_params,
    vector_moment1,
    vector_moment2,
    fc_bias,
    fc_bias_moment1,
    fc_bias_moment2,
):
    tensor_count = lax.axis_size("tensor")
    rank = lax.axis_index("tensor")
    x, c = rank // 2, rank % 2
    width = vector_params.shape[1]
    cols = width // tensor_count
    hidden = fc_bias.shape[0] // tensor_count
    part_rows = qkv_weight.shape[0]
    custom = lax.axis_size("dp") == 8

    qkv_low = qkv_weight.astype(BF)
    shards = [qkv_low[:, k] for k in range(3)]
    shards += [out_weight.T.astype(BF), fc_weight.astype(BF), proj_weight.T.astype(BF)]
    grad_low = cotangent * valid.astype(BF)[:, None]

    rows3 = segment_ids.reshape(-1, SLOT)
    starts = jnp.sum((rows3[:, None, :] < rows3[:, :, None]).astype(jnp.int32), axis=-1)
    starts = jnp.stack([lax.dynamic_index_in_dim(starts, 2 * x, 0, False), starts[1]])[:, None, :]

    def of_slots(vector):
        parts = vector.reshape(tensor_count, -1)
        return jnp.stack([lax.dynamic_index_in_dim(parts, c + 2 * s, 0, False) for s in range(2)])

    qb, vb = of_slots(vector_params[4]), of_slots(vector_params[5])
    bias = jnp.stack([qb, jnp.zeros_like(qb), vb], axis=1)[..., None]
    fb = of_slots(fc_bias)[:, None, :]

    weights, rest = forward(tokens, grad_low, vector_params, bias, starts, shards)
    gl, n1, units, ctx, lse, ctxc, resid, n2 = rest
    wo, wf, wp = (w.reshape(2, width, -1) for w in weights[3:])
    br, dn, gf, gp, gb = feed_forward(n2, gl, wf, wp, fb)
    mixed, dres, dctx, go, vg2 = middle_back(br, dn, resid, gl, ctxc, wo, vector_params)
    grads = [gp, gf, go]
    if custom:
        grads = [g.reshape(2, 4, 2, part_rows, -1) for g in grads]
    flat = (part_rows, 3 * cols)
    states = [s.reshape(flat) for s in (qkv_weight, qkv_moment1, qkv_moment2)]
    states += [out_weight, out_moment1, out_moment2, fc_weight, fc_moment1, fc_moment2]
    states += [proj_weight, proj_moment1, proj_moment2]
    outs = backward(
        units, starts, ctx, dctx.reshape(ctx.shape), lse, n1, weights[:3], dres, tokens,
        vector_params, vg2, gb, grads, states,
    )
    input_grad, vec = outs[:2]

    def vector_rows(vec):
        heads = vec[16 : 16 + tensor_count]
        return jnp.concatenate(
            [
                vec[:4],
                heads[:, :cols].reshape(1, width),
                heads[:, 2 * cols : 3 * cols].reshape(1, width),
                vec[6:8],
            ],
            axis=0,
        )

    if custom:
        grad_norm = outs[2][0, 0]
        fresh = list(outs[3:])
        factor = CLIP_NORM / jnp.maximum(grad_norm, CLIP_NORM)
    else:
        slot, swap = x, [(0, 2), (1, 3), (2, 0), (3, 1)]
        sums = []
        for g in [jnp.concatenate(outs[2:5], axis=2), go, gf, gp]:
            mine = jnp.where(slot == 0, g[0], g[1])
            other = jnp.where(slot == 0, g[1], g[0])
            both = mine.astype(F32) + lax.ppermute(other, "tensor", swap).astype(F32)
            both = lax.psum_scatter(both.astype(BF), "dp", scatter_dimension=0, tiled=True)
            sums.append(both.astype(F32))
        squares = sum(jnp.sum(s * s) for s in sums)
        vec, squares = lax.psum((vec, squares), ("dp", "tensor"))
        grad_norm = jnp.sqrt(squares + jnp.sum(vec * vec))
        factor = CLIP_NORM / jnp.maximum(grad_norm, CLIP_NORM)
        sums = [sums[0], sums[1].T, sums[2], sums[3].T]
        fresh = []
        for number, total in enumerate(sums):
            fresh += adamw_update(
                *states[3 * number : 3 * number + 3], factor * total, RATE_MATRIX, WEIGHT_DECAY
            )
    fresh[:3] = [f.reshape(qkv_weight.shape) for f in fresh[:3]]
    vector_new = adamw_update(
        vector_params, vector_moment1, vector_moment2, factor * vector_rows(vec), RATE_VECTOR, 0.0
    )
    fc_bias_new = adamw_update(
        fc_bias,
        fc_bias_moment1,
        fc_bias_moment2,
        factor * vec[8 : 8 + tensor_count, :hidden].reshape(-1),
        RATE_VECTOR,
        0.0,
    )
    return (mixed, input_grad, grad_norm, *fresh, *vector_new, *fc_bias_new)


def solution(mesh):
    rows = P(("dp", "tensor"), None)
    by_rows = [P("dp", None, "tensor")] * 3
    by_out = [P("tensor", "dp")] * 3
    by_fc = [P("dp", "tensor")] * 3
    weights = by_rows + by_out + by_fc + by_out
    return jax.shard_map(
        on_device,
        mesh=mesh,
        in_specs=(rows, rows, P("dp"), P(("dp", "tensor")), *weights, *[P()] * 6),
        out_specs=(rows, rows, P(), *weights, *[P()] * 6),
        check_vma=False,
    )
```

```python
import functools
import math

import jax
import jax.numpy as jnp
from jax import lax
from jax.experimental import pallas as pl
from jax.experimental.pallas import tpu as pltpu
from jax.sharding import PartitionSpec as P

HD = 64
SLOT = 1024
STEP = 10
NORM_EPSILON = 1e-05
MASK_FILL = -1e30
DECAY_FIRST = 0.5
DECAY_SECOND = 0.5
ADAM_EPSILON = 1e-08
WEIGHT_DECAY = 0.1
CLIP_NORM = 1.0
RATE_MATRIX = 0.04
RATE_VECTOR = 0.3

MESH = pl.DeviceIdType.MESH
BF = jnp.bfloat16
F32 = jnp.float32
HALF = SLOT // 2
BLK = 256
VMEM_LIMIT = 58 * 2**20
LOG2E = math.log2(math.e)
SCORE_SCALE = float(HD) ** (-0.5)
SCORE_SCALE2 = SCORE_SCALE * LOG2E


def dot_nn(a, b):
    return lax.dot_general(a, b, (((1,), (0,)), ((), ())), preferred_element_type=F32)


def dot_nt(a, b):
    return lax.dot_general(a, b, (((1,), (1,)), ((), ())), preferred_element_type=F32)


def dot_tn(a, b):
    return lax.dot_general(a, b, (((0,), (0,)), ((), ())), preferred_element_type=F32)


def dot_tt(a, b):
    return lax.dot_general(a, b, (((0,), (1,)), ((), ())), preferred_element_type=F32)


def params(collective_id=None):
    if collective_id is None:
        return pltpu.CompilerParams(vmem_limit_bytes=VMEM_LIMIT)
    return pltpu.CompilerParams(
        vmem_limit_bytes=VMEM_LIMIT, collective_id=collective_id, has_side_effects=True
    )


VM = pl.BlockSpec(memory_space=pltpu.VMEM)
ANY = pl.BlockSpec(memory_space=pl.ANY)


def sds(shape, dtype):
    return jax.ShapeDtypeStruct(shape, dtype)


def here():
    t = lax.axis_index("tensor")
    return lax.axis_index("dp"), t // 2, t % 2


def greet(ids):
    sem = pltpu.get_barrier_semaphore()
    for one in ids:
        pl.semaphore_signal(sem, inc=1, device_id=one, device_id_type=MESH)
    pl.semaphore_wait(sem, len(ids))


def remote(src, dst, send_sem, recv_sem, target):
    return pltpu.make_async_remote_copy(
        src_ref=src,
        dst_ref=dst,
        send_sem=send_sem,
        recv_sem=recv_sem,
        device_id=target,
        device_id_type=MESH,
    )


def rows_at(start, size):
    return pl.ds(pl.multiple_of(start, size), size)


def norm_parts(values):
    centered = values - jnp.mean(values, axis=-1, keepdims=True)
    variance = jnp.mean(centered * centered, axis=-1, keepdims=True)
    scale = lax.rsqrt(variance + NORM_EPSILON)
    return centered * scale, scale


class Gather:
    def __init__(self, shard, whole, part, by_y, ss, rs):
        dp, x, c = here()
        z, y = dp // 2, dp % 2
        along, x_peer, y_peer, _ = neighbours()
        shard = shard.at[part]
        block = whole.at[x, z, y, part]
        column = whole.at[x, :, y, part]
        from_x = whole.at[1 - x, pl.ds(0, by_y), y, part]
        from_y = whole.at[x, pl.ds(by_y, 4 - by_y), 1 - y, part]
        self.along = [remote(shard, block, ss.at[k], rs.at[k], along[k]) for k in range(3)]
        self.beside = [
            remote(column, column, ss.at[3], rs.at[3], x_peer),
            remote(column, column, ss.at[4], rs.at[4], y_peer),
        ]
        self.passed = [
            remote(from_x, from_x, ss.at[5], rs.at[5], y_peer),
            remote(from_y, from_y, ss.at[6], rs.at[6], x_peer),
        ]

    def start_along(self):
        for one in self.along:
            one.start()

    def start_beside(self):
        for one in self.along:
            one.wait()
        for one in self.beside:
            one.start()

    def start_passed(self):
        for one in self.beside:
            one.wait()
        for one in self.passed:
            one.start()

    def finish(self):
        for one in self.passed:
            one.wait()


def neighbours():
    dp, x, c = here()
    z, y = dp // 2, dp % 2
    me = x * 2 + c
    along = [(lax.rem(z + k, 4) * 2 + y, me) for k in (1, 2, 3)]
    return along, (dp, (1 - x) * 2 + c), (z * 2 + 1 - y, me), (dp, x * 2 + 1 - c)


def whole_weight(ref, slot):
    value = ref[slot]
    return value.reshape(-1, value.shape[-1])


def allowed_pairs(key_block, query_block, start_row, wide):
    keys = lax.broadcasted_iota(jnp.int32, (BLK, wide), 0) + key_block * BLK
    mask = keys >= start_row
    if key_block == query_block:
        queries = lax.broadcasted_iota(jnp.int32, (BLK, wide), 1) + query_block * BLK
        mask = mask & (keys <= queries)
    return mask


def attend_unit(q, k, v, start):
    blocks = SLOT // BLK
    for i in range(blocks):
        cols = slice(i * BLK, (i + 1) * BLK)
        query = q(cols)
        scores = []
        for j in range(i + 1):
            raw = dot_tn(k(slice(j * BLK, (j + 1) * BLK)), query) * SCORE_SCALE2
            scores.append(jnp.where(allowed_pairs(j, i, start(cols), BLK), raw, MASK_FILL))
        top = functools.reduce(jnp.maximum, [jnp.max(s, axis=0, keepdims=True) for s in scores])
        exps = [jnp.exp2(s - top) for s in scores]
        total = functools.reduce(jnp.add, [jnp.sum(e, axis=0, keepdims=True) for e in exps])
        acc = None
        for j in range(i + 1):
            term = dot_nn(v(slice(j * BLK, (j + 1) * BLK)), exps[j].astype(BF))
            acc = term if acc is None else acc + term
        yield cols, acc / total, top + jnp.log2(total)


GELU_C = math.sqrt(2.0 / math.pi)
GELU_A = 0.044715


def forward_kernel(custom, *refs):
    (tok_ref, cot_ref, valid_ref, seg_ref, vec_ref, fb_ref), refs = refs[:6], refs[6:]
    shards, refs = refs[:6], refs[6:]
    (gl_out, n1_out, u_out, ctx_out, lse_out, start_out, ctxc_out, resid_out, br_out, dn_out, gp_out, gf_out,
     gb_ref), refs = refs[:13], refs[13:]
    if custom:
        weights_out, refs = refs[:4], refs[4:]
        lows, refs = refs[:6], refs[6:]
        wholes, refs = refs[:6], refs[6:]
        gs, gr, refs = refs[0], refs[1], refs[2:]
    else:
        wholes = shards
    (tk, gl, n1, u, ctx, lse, starts, ctxc, resid, n2, half, part, got, act, dpre, cols, loc, ts, tr, xs, cs_s,
     cs_r) = refs
    wq, wo, wf, wp = wholes[:3], wholes[3], wholes[4], wholes[5]
    dp, x, c = here()
    core = (dp, x * 2 + 1 - c)
    x_peer = (dp, (1 - x) * 2 + c)
    across = [(dp, (1 - x) * 2), (dp, (1 - x) * 2 + 1)]
    rows = tok_ref.shape[0]
    first = x * HALF
    gathers = []
    if custom:
        z, y = dp // 2, dp % 2
        along, _, y_peer, _ = neighbours()
        greet([core, *across, *along, y_peer])
        for k in range(3):
            lows[k][...] = shards[0][k].astype(BF)
        lows[3][...] = shards[1][...].T.astype(BF)
        for k in (4, 5):
            lows[k][...] = shards[k - 2][...].astype(BF)
        pieces = [(0, 0, 1, 2), (1, 0, 1, 2), (2, 0, 1, 2), (3, 0, 1, 2)]
        pieces += [(4, 0, 2, 3), (4, 1, 2, 3), (5, 0, 2, 3), (5, 1, 2, 3)]
        for number, (a, k, parts, by_y) in enumerate(pieces):
            size = lows[a].shape[0] // parts
            gathers.append(
                Gather(
                    lows[a], wholes[a], pl.ds(k * size, size), by_y, gs.at[number], gr.at[number]
                )
            )
    else:
        greet([core, *across])

    def step(number, what):
        if custom:
            getattr(gathers[number], what)()

    own_rows = pl.ds(pl.multiple_of(first + c * rows, BLK), rows)
    gl_rows = pl.ds(pl.multiple_of(c * rows, BLK), rows)
    mine_tok = pltpu.make_async_copy(tok_ref, tk.at[own_rows], loc.at[0])
    swap_tok = remote(tok_ref, tk.at[own_rows], ts.at[0], tr.at[0], core)
    swap_grad = remote(gl.at[gl_rows], gl.at[gl_rows], ts.at[1], tr.at[1], core)
    source = [
        tok_ref.at[pl.ds(pl.multiple_of((1 - x) * BLK + k * BLK, BLK), BLK)] for k in range(2)
    ]
    there = [
        tk.at[pl.ds(pl.multiple_of(x * (SLOT + HALF) + k * BLK, BLK), BLK)] for k in range(2)
    ]
    halves = [remote(source[k], there[k], ts.at[2 + k], tr.at[2], across[k]) for k in range(2)]
    landed = tk.at[pl.ds(pl.multiple_of((1 - x) * (SLOT + HALF) + c * BLK, BLK), BLK)]
    handed = remote(landed, landed, ts.at[4], tr.at[3], core)

    step(0, "start_along")
    mine_tok.start()
    swap_tok.start()
    step(1, "start_along")
    step(2, "start_along")

    def out_copy(number, ref, out):
        copy = pltpu.make_async_copy(ref, out, loc.at[number])
        copy.start()
        return copy

    if custom:
        for a in range(6):
            wholes[a][x, z, y] = lows[a][...]

    cols[...] = vec_ref[...].T
    gain, shift = vec_ref[0:1, :], vec_ref[1:2, :]

    def norm_rows(start, count):
        def norm(i, carry):
            at = rows_at(start + i * BLK, BLK)
            unit, _ = norm_parts(tk[at, :].astype(F32))
            n1[at, :] = (unit * gain + shift).astype(BF)
            return carry

        lax.fori_loop(0, count // BLK, norm, 0)

    mine_tok.wait()
    norm_rows(first + c * rows, rows)
    step(0, "start_beside")
    step(3, "start_along")
    swap_tok.wait()
    norm_rows(first + (1 - c) * rows, rows)
    step(1, "start_beside")
    step(4, "start_along")

    mask = jnp.broadcast_to(valid_ref[...].astype(F32), (8, rows)).T[:, 0:1]
    gl[gl_rows, :] = (cot_ref[...].astype(F32) * mask).astype(BF)
    swap_grad.start()
    for k, row in enumerate((2 * x, 1)):
        segments = seg_ref[pl.ds(row, 1), :].astype(F32)
        column = jnp.broadcast_to(segments, (8, SLOT)).T[:, 0:1]
        for i in range(SLOT // BLK):
            lanes = slice(i * BLK, (i + 1) * BLK)
            below = jnp.where(column < segments[:, lanes], 1.0, 0.0)
            starts[k, :, lanes] = jnp.sum(below, axis=0, keepdims=True).astype(jnp.int32)

    step(0, "start_passed")
    step(2, "start_beside")
    step(5, "start_along")
    step(1, "start_passed")
    step(3, "start_beside")

    @pl.when(c == 1 - x)
    def _():
        for one in halves:
            one.start()

    step(2, "start_passed")
    step(6, "start_along")

    def project(group, slot, first_row):
        bias_rows = rows_at((c + 2 * slot) * wq[0].shape[-1], 64)
        bias_rows = pl.ds(pl.multiple_of((c + 2 * slot) * wq[0].shape[-1], 64), wq[0].shape[-1])
        bias = (cols[bias_rows, 4:5], None, cols[bias_rows, 5:6])

        def chunk(i, carry):
            lanes = rows_at(i * BLK, BLK)
            values = n1[rows_at(first_row + i * BLK, BLK), :]
            for k in range(3):
                out = dot_tt(whole_weight(wq[k], slot), values)
                if k != 1:
                    out = out + bias[k]
                u[group, k, :, :, lanes] = out.reshape(-1, HD, BLK).astype(BF)
            return carry

        lax.fori_loop(0, SLOT // BLK, chunk, 0)

    heads = u.shape[2]

    def attend(group, which, begin, end):
        def unit(h, carry):
            for lanes, context, log_total in attend_unit(
                lambda s: u[group, 0, h, :, s],
                lambda s: u[group, 1, h, :, s],
                lambda s: u[group, 2, h, :, s],
                lambda s: starts[which, :, s],
            ):
                ctx[group, h, :, lanes] = context.astype(BF)
                lse[group, h, :, lanes] = log_total
            return carry

        lax.fori_loop(begin, end, unit, 0)

    project(x, x, x * SLOT)
    step(4, "start_beside")
    step(7, "start_along")
    step(3, "start_passed")
    attend(x, 0, 0, 1)
    step(0, "finish")
    step(5, "start_beside")
    attend(x, 0, 1, heads)
    step(1, "finish")
    step(2, "finish")
    step(4, "start_passed")
    project(1 - x, 1 - x, x * SLOT)
    step(6, "start_beside")
    attend(1 - x, 0, 0, 1)
    step(5, "start_passed")
    attend(1 - x, 0, 1, heads)
    step(7, "start_beside")
    halves[0].wait_recv()
    handed.start()
    handed.wait()
    norm_rows((1 - x) * (SLOT + HALF), HALF)
    project(2, x, (1 - x) * SLOT)
    step(6, "start_passed")
    copies = [out_copy(1, n1, n1_out), out_copy(2, u, u_out)]
    attend(2, 1, 0, heads)
    step(7, "start_passed")
    theirs = pl.ds(pl.multiple_of((1 - x) * HALF, HALF), HALF)
    cross = remote(ctx.at[2, :, :, theirs], half, xs.at[0], xs.at[1], x_peer)
    cross.start()
    step(3, "finish")
    copies += [out_copy(3, ctx, ctx_out), out_copy(4, lse, lse_out), out_copy(5, starts, start_out)]
    if custom:
        copies += [out_copy(6 + a, wholes[a], weights_out[a]) for a in range(4)]

    @pl.when(c == 1 - x)
    def _():
        for one in halves:
            one.wait_send()

    chunks = []

    def send(chunk, values):
        at = rows_at(chunk * BLK, BLK)
        part[at, :] = values.astype(BF)
        copy = remote(part.at[at], got.at[at], cs_s.at[chunk], cs_r.at[chunk], core)
        copy.start()
        chunks.append((chunk, copy))

    def context_of(group, lanes):
        value = ctx[group, :, :, lanes]
        return value.reshape(-1, value.shape[-1])

    for i in range(SLOT // BLK):
        lanes = slice(i * BLK, (i + 1) * BLK)
        chunk = x * 2 + i
        at = rows_at(chunk * BLK, BLK)
        zero, one = context_of(0, lanes), context_of(1, lanes)
        send(chunk, dot_tt(zero, whole_weight(wo, 0)) + dot_tt(one, whole_weight(wo, 1)))
        ctxc[0, :, at] = zero
        ctxc[1, :, at] = one
    cross.wait()
    for i in range(HALF // BLK):
        chunk = (1 - x) * 4 + i
        at = rows_at(chunk * BLK, BLK)
        own = context_of(2, rows_at(x * HALF + i * BLK, BLK))
        other = half[:, :, i * BLK : (i + 1) * BLK].reshape(-1, BLK)
        send(chunk, dot_tt(own, whole_weight(wo, x)) + dot_tt(other, whole_weight(wo, 1 - x)))
        ctxc[x, :, at] = own
        ctxc[1 - x, :, at] = other
    copies.append(out_copy(10, ctxc, ctxc_out))
    swap_grad.wait()
    copies.append(out_copy(11, gl, gl_out))
    for chunk, copy in chunks:
        copy.wait()
        at = rows_at(chunk * BLK, BLK)
        tokens = tk[rows_at(first + chunk * BLK, BLK), :].astype(F32)
        summed = part[at, :].astype(F32) + got[at, :].astype(F32)
        after = tokens + summed + vec_ref[6:7, :]
        resid[at, :] = after
        unit, _ = norm_parts(after)
        n2[at, :] = (unit * vec_ref[2:3, :] + vec_ref[3:4, :]).astype(BF)
    copies.append(out_copy(12, resid, resid_out))
    for number in range(4, 8):
        step(number, "finish")

    hidden = wf.shape[-1]
    gb_ref[...] = jnp.zeros_like(gb_ref)
    bias_of = [
        fb_ref[:, pl.ds(pl.multiple_of((c + 2 * s) * hidden, hidden), hidden)] for s in range(2)
    ]

    def forward_back(i, carry):
        at = rows_at(i * BLK, BLK)
        n2_rows, gl_rows_now = n2[at, :], gl[at, :]
        for s in range(2):
            lanes = slice(s * hidden, (s + 1) * hidden)
            v = dot_nn(n2_rows, whole_weight(wf, s)) + bias_of[s]
            up = dot_nn(gl_rows_now, whole_weight(wp, s))
            square = v * v
            t = jnp.tanh(v * (GELU_C + (GELU_C * GELU_A) * square))
            cdf = 0.5 + 0.5 * t
            act[at, lanes] = (v * cdf).astype(BF)
            slope = cdf + (cdf * (1.0 - t)) * (
                v * (GELU_C + (3.0 * GELU_C * GELU_A) * square)
            )
            d = (up * slope).astype(BF)
            dpre[at, lanes] = d
            gb_ref[s] += jnp.sum(d.astype(F32), axis=0, keepdims=True)
        br = dot_nt(act[at, :hidden], whole_weight(wp, 0))
        br += dot_nt(act[at, hidden:], whole_weight(wp, 1))
        part[at, :] = br.astype(BF)
        dn = dot_nt(dpre[at, :hidden], whole_weight(wf, 0))
        dn += dot_nt(dpre[at, hidden:], whole_weight(wf, 1))
        got[at, :] = dn.astype(BF)
        return carry

    lax.fori_loop(0, 2 * rows // BLK, forward_back, 0)
    copies += [out_copy(13, got, dn_out), out_copy(14, part, br_out)]
    copies[0].wait()
    width = n2.shape[1]
    for number, (base, values, given, out) in enumerate(
        ((n1, gl, act, gp_out), (tk, n2, dpre, gf_out))
    ):
        for s in range(2):

            def weight_grads(i, carry, base=base, values=values, given=given, s=s):
                wide = rows_at(s * hidden + i * BLK, BLK)
                base[pl.ds(s * width, width), rows_at(i * BLK, BLK)] = dot_tn(
                    values[...], given[:, wide]
                ).astype(BF)
                return carry

            lax.fori_loop(0, hidden // BLK, weight_grads, 0)
            copies.append(
                out_copy(15 + 2 * number + s, base.at[pl.ds(s * width, width)], out.at[s])
            )
    for copy in copies[1:]:
        copy.wait()


def forward(tokens, cotangent, valid, segments, vectors, fc_bias, shards):
    rows, width = tokens.shape
    chip = 2 * rows
    custom = lax.axis_size("dp") == 8
    dma = pltpu.SemaphoreType.DMA
    if custom:
        cols = shards[0].shape[2]
        hidden = shards[2].shape[1]
        part_rows = shards[2].shape[0]
        flat = [(part_rows, n) for n in (cols, cols, cols, cols, hidden, hidden)]
        wholes = [(2, 4, 2) + s for s in flat]
        more_out = [sds(w, BF) for w in wholes[:4]]
        more = [pltpu.VMEM(s, BF) for s in flat] + [pltpu.VMEM(w, BF) for w in wholes]
        more += [dma((8, 7)), dma((8, 7))]
        ins = [*shards, shards[3], shards[3]]
    else:
        cols, hidden = shards[0].shape[2], shards[4].shape[2]
        more_out, more = [], []
        ins = list(shards)
    heads = cols // HD
    shapes = [
        ((chip, width), BF),
        ((2 * SLOT, width), BF),
        ((3, 3, heads, HD, SLOT), BF),
        ((3, heads, HD, SLOT), BF),
        ((3, heads, 1, SLOT), F32),
        ((2, 1, SLOT), jnp.int32),
        ((2, cols, chip), BF),
        ((chip, width), F32),
    ]
    out_shape = [sds(*s) for s in shapes]
    out_shape += [sds((chip, width), BF)] * 2 + [sds((2, width, hidden), BF)] * 2
    out_shape += [sds((2, 1, hidden), F32)] + more_out
    outs = pl.pallas_call(
        functools.partial(forward_kernel, custom),
        out_shape=tuple(out_shape),
        in_specs=[ANY] + [VM] * (5 + len(ins)),
        out_specs=(*[ANY] * 12, VM, *[ANY] * len(more_out)),
        scratch_shapes=more
        + [
            pltpu.VMEM((2 * SLOT, width), BF),
            *[pltpu.VMEM(*s) for s in shapes],
            pltpu.VMEM((chip, width), BF),
            pltpu.VMEM((heads, HD, HALF), BF),
            pltpu.VMEM((chip, width), BF),
            pltpu.VMEM((chip, width), BF),
            pltpu.VMEM((chip, 2 * hidden), BF),
            pltpu.VMEM((chip, 2 * hidden), BF),
            pltpu.VMEM((width, 8), F32),
            dma((19,)),
            dma((5,)),
            dma((4,)),
            dma((2,)),
            dma((chip // BLK,)),
            dma((chip // BLK,)),
        ],
        compiler_params=params(1),
        name="forward",
    )(tokens, cotangent, valid, segments, vectors, fc_bias, *ins)
    return outs[:13], (list(outs[13:]) if custom else ins[:4])


class Reduce:
    by_y = 3

    def __init__(self, grad, local, total, bufs, loc, ss, rs):
        dp, x, c = here()
        z, y = dp // 2, dp % 2
        along, x_peer, y_peer, _ = neighbours()
        low, high = pl.ds(0, self.by_y), pl.ds(self.by_y, 4 - self.by_y)
        self.z, self.total = z, total
        self.r1y, self.r1x, self.r2x, self.r2y, self.r3 = bufs
        views = [grad.at[1 - x, low, y], grad.at[x, high, 1 - y], grad.at[x, :, y]]
        self.loads = []
        self.mid_x, self.mid_y, self.own = views
        if local is not None:
            self.loads = [
                pltpu.make_async_copy(views[k], local[k], loc.at[k]) for k in range(3)
            ]
            self.mid_x, self.mid_y, self.own = local
        self.first = [
            remote(grad.at[1 - x, low, 1 - y], self.r1y, ss.at[0], rs.at[0], y_peer),
            remote(grad.at[1 - x, high, 1 - y], self.r1x, ss.at[1], rs.at[1], x_peer),
        ]
        self.early = [
            remote(grad.at[1 - x, high, y], self.r2x.at[high], ss.at[2], rs.at[2], x_peer),
            remote(grad.at[x, low, 1 - y], self.r2y.at[low], ss.at[3], rs.at[3], y_peer),
        ]
        self.second = [
            remote(self.mid_x, self.r2x.at[low], ss.at[4], rs.at[4], x_peer),
            remote(self.mid_y, self.r2y.at[high], ss.at[5], rs.at[5], y_peer),
        ]
        self.third = [
            remote(
                self.own.at[lax.rem(z + k + 1, 4)], self.r3.at[k], ss.at[6 + k], rs.at[6 + k], along[k]
            )
            for k in range(3)
        ]

    def start_first(self):
        for one in self.first:
            one.start()
        for one in self.loads:
            one.start()

    def start_early(self):
        for one in self.early:
            one.start()

    def start_second(self):
        for one in self.first + self.loads:
            one.wait()
        self.mid_x[...] = (self.mid_x[...].astype(F32) + self.r1y[...].astype(F32)).astype(BF)
        self.mid_y[...] = (self.mid_y[...].astype(F32) + self.r1x[...].astype(F32)).astype(BF)
        for one in self.second:
            one.start()

    def start_third(self):
        for one in self.early + self.second:
            one.wait()
        for k in range(4):
            place = lax.rem(self.z + k + 1, 4)
            summed = (
                self.own[place].astype(F32)
                + self.r2x[place].astype(F32)
                + self.r2y[place].astype(F32)
            )
            if k < 3:
                self.own[place] = summed.astype(BF)
                self.third[k].start()
            else:
                self.total[...] = summed

    def finish(self):
        for one in self.third:
            one.wait()
        total = self.total[...]
        for k in range(3):
            total = total + self.r3[k].astype(F32)
        self.total[...] = total
        return jnp.sum(total * total)


def eight_peers():
    dp, x, c = here()
    z, y = dp // 2, dp % 2
    peers = []
    for k in range(1, 8):
        kx, ky, kc = k // 4, k // 2 % 2, k % 2
        there = ((1 - x if kx else x), (1 - y if ky else y), (1 - c if kc else c))
        peers.append((z * 2 + there[1], there[0] * 2 + there[2]))
    return peers


class SumOverAll:
    def __init__(self, value, near, far, ss, rs):
        dp, x, c = here()
        z, y = dp // 2, dp % 2
        self.value, self.near, self.far = value, near, far
        self.me, self.z = x * 4 + y * 2 + c, z
        self.one = [
            remote(value, near.at[self.me], ss.at[k], rs.at[k], peer)
            for k, peer in enumerate(eight_peers())
        ]
        self.two = [
            remote(value, far.at[z], ss.at[7 + k], rs.at[7 + k], peer)
            for k, peer in enumerate(neighbours()[0])
        ]

    def start(self):
        for one in self.one:
            one.start()
        self.near[self.me] = self.value[...]

    def middle(self):
        for one in self.one:
            one.wait()
        self.value[...] = functools.reduce(jnp.add, [self.near[k] for k in range(8)])
        for one in self.two:
            one.start()
        self.far[self.z] = self.value[...]

    def finish(self):
        for one in self.two:
            one.wait()
        return functools.reduce(jnp.add, [self.far[k] for k in range(4)])


def attend_back_unit(u, out, start, ctx, dctx, lse, dq_ref):
    blocks = SLOT // BLK
    delta = jnp.sum(dctx.astype(F32) * ctx.astype(F32), axis=0, keepdims=True)
    for j in range(blocks):
        keys = slice(j * BLK, (j + 1) * BLK)
        k = u(1, keys)
        v = u(2, keys)
        probs, dscores = [], []
        for i in range(j, blocks):
            cols = slice(i * BLK, (i + 1) * BLK)
            raw = dot_tn(k, u(0, cols)) * SCORE_SCALE2 - lse[:, cols]
            prob = jnp.exp2(jnp.where(allowed_pairs(j, i, start[:, cols], BLK), raw, MASK_FILL))
            dprob = dot_tn(v, dctx[:, cols])
            probs.append(prob.astype(BF))
            dscores.append((prob * (dprob - delta[:, cols])).astype(BF))
        dk, dv = None, None
        for n, i in enumerate(range(j, blocks)):
            cols = slice(i * BLK, (i + 1) * BLK)
            dv_term = dot_nt(dctx[:, cols], probs[n])
            dk_term = dot_nt(u(0, cols), dscores[n])
            dv = dv_term if dv is None else dv + dv_term
            dk = dk_term if dk is None else dk + dk_term
            dq_term = dot_nn(k, dscores[n])
            if j == 0:
                dq_ref[:, cols] = dq_term
            else:
                dq_ref[:, cols] += dq_term
        out(1, keys, (dk * SCORE_SCALE).astype(BF))
        out(2, keys, dv.astype(BF))
    out(0, slice(0, SLOT), (dq_ref[...] * SCORE_SCALE).astype(BF))


VEC_ROWS = 24


def norm_back(dn, values, gain):
    unit, scale = norm_parts(values)
    e = dn * gain
    back = scale * (
        e
        - jnp.mean(e, axis=-1, keepdims=True)
        - unit * jnp.mean(e * unit, axis=-1, keepdims=True)
    )
    return back, unit


def backward_kernel(custom, *refs):
    (gl_in, n1_in, u_in, ctx_in, lse_ref, start_ref, ctxc_in, resid_in, br_in, dn_in, gp_in, gf_in, gb_ref, wq0,
     wq1, wq2, wo_in, tok_in, vec_ref), refs = refs[:19], refs[19:]
    (mixed_out, ig_out), refs = refs[:2], refs[2:]
    if custom:
        totals, refs = refs[:6], refs[6:]
        (vs_out, norm_ref), refs = refs[:2], refs[2:]
        go, gq, refs = refs[0], refs[1:4], refs[4:]
        locals_, refs = (refs[:3], refs[3:6]), refs[6:]
        bufs, refs = [refs[5 * a : 5 * a + 5] for a in range(6)], refs[30:]
        (vs, near_v, far_v, near_s, far_s, square, lss, ss, rs, vss, vrs, qss, qrs), refs = (
            refs[:13],
            refs[13:],
        )
    else:
        vs, refs = refs[0], refs[1:]
        go, gq, refs = refs[0], refs[1:4], refs[4:]
    (gl_s, resid_s, dn_s, got_dn, br_s, got_br, mixed, low, dres, dctx, ctxc, wo, half_c, outgoing, u, ctx, n1,
     wqs0, wqs1, wqs2, tok, du, dq, half, got, loc, ld, cs_s, cs_r, bs, xs, ws) = refs
    part = low
    wq = (wqs0, wqs1, wqs2)
    dp, x, c = here()
    core = (dp, x * 2 + 1 - c)
    x_peer = (dp, (1 - x) * 2 + c)
    reduces = []
    if custom:
        greet(eight_peers() + neighbours()[0])
        grads = [gp_in, gf_in, go, *gq]
        for a in range(6):
            local = locals_[a] if a < 2 else None
            loads = lss.at[a] if a < 2 else None
            reduces.append(
                Reduce(grads[a], local, totals[a], bufs[a], loads, ss.at[a], rs.at[a])
            )
    else:
        greet([core, x_peer])

    def step(number, what):
        if custom:
            getattr(reduces[number], what)()

    rows_all, width = low.shape
    own_rows = rows_all // 2
    n_chunks = rows_all // BLK
    order = [(1 - x) * 4 + i for i in range(HALF // BLK)] + [x * 2 + i for i in range(SLOT // BLK)]
    swaps = []
    for chunk in order:
        at = rows_at(chunk * BLK, BLK)
        swaps.append(remote(dn_in.at[at], got_dn.at[at], cs_s.at[chunk], cs_r.at[chunk], core))
    their = pl.ds(pl.multiple_of((1 - c) * own_rows, BLK), own_rows)
    mine = pl.ds(pl.multiple_of(c * own_rows, BLK), own_rows)
    branch = remote(br_in.at[their], got_br, bs.at[0], bs.at[1], core)

    def chunk_loads(n):
        at, slot = rows_at(order[n] * BLK, BLK), n % 2
        return [
            pltpu.make_async_copy(source.at[at], target.at[slot], ld.at[slot, k])
            for k, (source, target) in enumerate(
                ((resid_in, resid_s), (gl_in, gl_s), (dn_in, dn_s))
            )
        ]

    def load(number, source, target):
        copy = pltpu.make_async_copy(source, target, loc.at[number])
        copy.start()
        return copy

    loads = [chunk_loads(n) for n in range(n_chunks)]
    swaps[0].start()
    for n in range(2):
        for one in loads[n]:
            one.start()
    branch.start()
    for one in swaps[1:]:
        one.start()
    step(0, "start_first")
    br_load = load(0, br_in.at[mine], br_s)
    wo_load = load(1, wo_in, wo)
    ctxc_load = load(2, ctxc_in, ctxc)
    step(0, "start_early")
    step(1, "start_first")
    late = [
        load(3, u_in, u),
        load(4, ctx_in, ctx),
        load(5, n1_in, n1),
        load(6, wq0, wqs0),
        load(7, wq1, wqs1),
        load(8, wq2, wqs2),
        load(9, tok_in, tok),
    ]
    vs[...] = jnp.zeros_like(vs)
    branch.wait()
    br_load.wait()
    for n, chunk in enumerate(order):
        slot = n % 2
        for one in loads[n]:
            one.wait()
        swaps[n].wait()
        at = rows_at(chunk * BLK, BLK)
        dn = dn_s[slot].astype(F32) + got_dn[at, :].astype(F32)
        resid = resid_s[slot]
        back, unit = norm_back(dn, resid, vec_ref[2:3, :])
        grad = gl_s[slot].astype(F32)
        after = grad + back
        low[at, :] = after.astype(BF)

        @pl.when(chunk // (n_chunks // 2) == c)
        def _(chunk=chunk, dn=dn, resid=resid, unit=unit, grad=grad, after=after):
            here_at = rows_at((chunk - c * (n_chunks // 2)) * BLK, BLK)
            dres[here_at, :] = after
            branches = br_s[here_at, :].astype(F32) + got_br[here_at, :].astype(F32)
            mixed[here_at, :] = (resid + branches + vec_ref[7:8, :]).astype(BF)
            vs[2:3, :] += jnp.sum(dn * unit, axis=0, keepdims=True)
            vs[3:4, :] += jnp.sum(dn, axis=0, keepdims=True)
            vs[6:7, :] += jnp.sum(after, axis=0, keepdims=True)
            vs[7:8, :] += jnp.sum(grad, axis=0, keepdims=True)

        if n + 2 < n_chunks:
            for one in loads[n + 2]:
                one.start()
        if n == 1:
            wo_load.wait()
            for i in range(HALF // BLK):
                lanes = slice(i * BLK, (i + 1) * BLK)
                rows = low[rows_at((1 - x) * SLOT + i * BLK, BLK), :]
                outgoing[:, :, lanes] = (
                    dot_tt(whole_weight(wo, 1 - x), rows).astype(BF).reshape(-1, HD, BLK)
                )
                dctx[2, :, :, rows_at(x * HALF + i * BLK, BLK)] = (
                    dot_tt(whole_weight(wo, x), rows).astype(BF).reshape(-1, HD, BLK)
                )
            cross_c = remote(outgoing, half_c, xs.at[0], xs.at[1], x_peer)
            cross_c.start()
    mixed_copy = pltpu.make_async_copy(mixed, mixed_out, ws.at[0])
    mixed_copy.start()
    step(0, "start_second")
    step(1, "start_early")
    ctxc_load.wait()
    for s in range(2):
        go[s] = dot_tt(low[...], ctxc[s]).astype(BF).reshape(go.shape[1:])
    step(2, "start_first")
    for i in range(SLOT // BLK):
        lanes = slice(i * BLK, (i + 1) * BLK)
        rows = low[rows_at(x * HALF + i * BLK, BLK), :]
        for s in range(2):
            dctx[s, :, :, lanes] = (
                dot_tt(whole_weight(wo, s), rows).astype(BF).reshape(-1, HD, BLK)
            )
    cross_c.wait()
    dctx[2, :, :, pl.ds(pl.multiple_of((1 - x) * HALF, HALF), HALF)] = half_c[...]
    step(1, "start_second")
    step(2, "start_early")
    late[0].wait()
    late[1].wait()
    heads = u.shape[2]
    cols = heads * HD

    def attend_back(group, which, begin, end):
        def unit(h, carry):
            def put(k, lanes, value):
                du[group, k, h, :, lanes] = value

            attend_back_unit(
                lambda k, lanes: u[group, k, h, :, lanes],
                put,
                start_ref[which],
                ctx[group, h],
                dctx[group, h],
                lse_ref[group, h],
                dq,
            )
            return carry

        lax.fori_loop(begin, end, unit, 0)

    attend_back(2, 1, 0, heads)
    theirs = pl.ds(pl.multiple_of((1 - x) * HALF, HALF), HALF)
    cross = remote(du.at[2, :, :, :, theirs], half, xs.at[2], xs.at[3], x_peer)
    cross.start()
    step(2, "start_second")
    attend_back(0, 0, 0, heads)
    step(0, "start_third")
    attend_back(1, 0, 0, heads)
    for one in late[2:]:
        one.wait()
    full_rows = pl.ds(pl.multiple_of(x * SLOT, SLOT), SLOT)
    part_rows = pl.ds(pl.multiple_of((1 - x) * SLOT, SLOT), SLOT)

    def of_group(group, k, lanes):
        value = du[group, k, :, :, lanes]
        return value.reshape(cols, value.shape[-1])

    everything = slice(0, SLOT)
    for k in range(3):
        shape = gq[k].shape[1:]
        gq[k][1 - x] = (
            dot_tt(n1[full_rows, :], of_group(1 - x, k, everything)).astype(BF).reshape(shape)
        )
        both = dot_tt(n1[full_rows, :], of_group(x, k, everything))
        both += dot_tt(n1[part_rows, :], of_group(2, k, everything))
        gq[k][x] = both.astype(BF).reshape(shape)
        step(3 + k, "start_first")
        step(3 + k, "start_early")
    step(1, "start_third")

    ones = jnp.ones((8, SLOT), BF)
    for k in (0, 2):
        lanes = slice(k * cols, (k + 1) * cols)
        for g in range(2):
            vs[pl.ds(16 + c + 2 * g, 1), lanes] = dot_nt(ones, of_group(g, k, everything))[0:1]
        vs[pl.ds(16 + c + 2 * x, 1), lanes] += dot_nt(ones, of_group(2, k, everything))[0:1]
    for s in range(2):
        vs[pl.ds(8 + c + 2 * s, 1), :] = gb_ref[s]

    def back_through(pieces):
        total = None
        for value, slot, k in pieces:
            term = dot_tt(value, whole_weight(wq[k], slot))
            total = term if total is None else total + term
        return total

    for i in range(SLOT // BLK):
        lanes = slice(i * BLK, (i + 1) * BLK)
        part[rows_at((x * 2 + i) * BLK, BLK), :] = back_through(
            [(of_group(s, k, lanes), s, k) for s in range(2) for k in range(3)]
        ).astype(BF)
    step(3, "start_second")
    cross.wait()
    for i in range(HALF // BLK):
        lanes = rows_at(x * HALF + i * BLK, BLK)
        part[rows_at(((1 - x) * 4 + i) * BLK, BLK), :] = back_through(
            [(of_group(2, k, lanes), x, k) for k in range(3)]
            + [
                (half[k, :, :, i * BLK : (i + 1) * BLK].reshape(cols, BLK), 1 - x, k)
                for k in range(3)
            ]
        ).astype(BF)
    swap = remote(part.at[their], got, bs.at[2], bs.at[3], core)
    swap.start()
    step(4, "start_second")
    step(5, "start_second")
    step(2, "start_third")
    swap.wait()
    for r in range(own_rows // BLK):
        rows = slice(r * BLK, (r + 1) * BLK)
        wide = rows_at(c * own_rows + r * BLK, BLK)
        dn = part[wide, :].astype(F32) + got[rows, :].astype(F32)
        back, unit = norm_back(dn, tok[rows, :].astype(F32), vec_ref[0:1, :])
        mixed_copy.wait() if r == 0 else None
        mixed[rows, :] = (dres[rows, :] + back).astype(BF)
        vs[0:1, :] += jnp.sum(dn * unit, axis=0, keepdims=True)
        vs[1:2, :] += jnp.sum(dn, axis=0, keepdims=True)
    ig_copy = pltpu.make_async_copy(mixed, ig_out, ws.at[1])
    ig_copy.start()
    if custom:
        vectors = SumOverAll(vs, near_v, far_v, vss, vrs)
        vectors.start()
        step(3, "start_third")
        step(4, "start_third")
        vectors.middle()
        step(5, "start_third")
        squares = functools.reduce(jnp.add, [one.finish() for one in reduces])
        square[...] = jnp.full(square.shape, squares, F32)
        norm = SumOverAll(square, near_s, far_s, qss, qrs)
        norm.start()
        summed = vectors.finish()
        vs_out[...] = summed
        vector_squares = jnp.sum(summed * summed, keepdims=True)
        norm.middle()
        norm_ref[...] = jnp.sqrt(norm.finish() + vector_squares)
    ig_copy.wait()


def backward(saved, weights, tokens, vectors):
    (gl, n1, u, ctx, lse, starts, ctxc, resid, br, dn, gp, gf, gb) = saved
    rows, width = tokens.shape
    chip = 2 * rows
    heads = u.shape[2]
    cols = heads * HD
    custom = lax.axis_size("dp") == 8
    dma = pltpu.SemaphoreType.DMA
    out_shape = [sds((rows, width), BF)] * 2
    out_specs = [ANY, ANY]
    if custom:
        hidden = gp.shape[2]
        part_rows = width // 8
        shapes = [(part_rows, n) for n in (hidden, hidden, cols, cols, cols, cols)]
        gp, gf = (g.reshape((2, 4, 2) + shapes[0]) for g in (gp, gf))
        out_shape += [sds(s, F32) for s in shapes] + [sds((VEC_ROWS, width), F32), sds((8, 128), F32)]
        out_specs += [VM] * 8
        by_y = Reduce.by_y
        scratch = [pltpu.VMEM((2, 4, 2) + s, BF) for s in shapes[2:]]
        scratch += [pltpu.VMEM((n,) + shapes[0], BF) for _ in range(2) for n in (by_y, 4 - by_y, 4)]
        scratch += [pltpu.VMEM((n,) + s, BF) for s in shapes for n in (by_y, 4 - by_y, 4, 4, 3)]
        scratch += [
            pltpu.VMEM((VEC_ROWS, width), F32),
            pltpu.VMEM((8, VEC_ROWS, width), F32),
            pltpu.VMEM((4, VEC_ROWS, width), F32),
            pltpu.VMEM((8, 8, 128), F32),
            pltpu.VMEM((4, 8, 128), F32),
            pltpu.VMEM((8, 128), F32),
            dma((2, 3)),
            dma((6, 9)),
            dma((6, 9)),
            dma((10,)),
            dma((10,)),
            dma((10,)),
            dma((10,)),
        ]
    else:
        out_shape += [sds((VEC_ROWS, width), F32)] + [sds((2, width, cols), BF)] * 4
        out_specs += [VM] * 5
        scratch = []
    scratch += [
        pltpu.VMEM((2, BLK, width), BF),
        pltpu.VMEM((2, BLK, width), F32),
        pltpu.VMEM((2, BLK, width), BF),
        pltpu.VMEM((chip, width), BF),
        pltpu.VMEM((rows, width), BF),
        pltpu.VMEM((rows, width), BF),
        pltpu.VMEM((rows, width), BF),
        pltpu.VMEM((chip, width), BF),
        pltpu.VMEM((rows, width), F32),
        pltpu.VMEM(ctx.shape, BF),
        pltpu.VMEM(ctxc.shape, BF),
        pltpu.VMEM(weights[3].shape, BF),
        pltpu.VMEM((heads, HD, HALF), BF),
        pltpu.VMEM((heads, HD, HALF), BF),
        pltpu.VMEM(u.shape, BF),
        pltpu.VMEM(ctx.shape, BF),
        pltpu.VMEM(n1.shape, BF),
        *[pltpu.VMEM(w.shape, BF) for w in weights[:3]],
        pltpu.VMEM((rows, width), BF),
        pltpu.VMEM(u.shape, BF),
        pltpu.VMEM((HD, SLOT), F32),
        pltpu.VMEM((3, heads, HD, HALF), BF),
        pltpu.VMEM((rows, width), BF),
        dma((10,)),
        dma((2, 3)),
        dma((chip // BLK,)),
        dma((chip // BLK,)),
        dma((4,)),
        dma((4,)),
        dma((2,)),
    ]
    return pl.pallas_call(
        functools.partial(backward_kernel, custom),
        out_shape=tuple(out_shape),
        in_specs=[ANY] * 4 + [VM, VM] + [ANY] * 6 + [VM] + [ANY] * 5 + [VM],
        out_specs=tuple(out_specs),
        scratch_shapes=scratch,
        compiler_params=params(2),
        name="backward",
    )(gl, n1, u, ctx, lse, starts, ctxc, resid, br, dn, gp, gf, gb, *weights, tokens, vectors)


def adamw_update(weight, moment_one, moment_two, gradient, step_rate, decay_rate):
    first_moment = DECAY_FIRST * moment_one + (1.0 - DECAY_FIRST) * gradient
    second_moment = DECAY_SECOND * moment_two + (1.0 - DECAY_SECOND) * gradient * gradient
    first_hat = first_moment / (1.0 - DECAY_FIRST**STEP)
    second_hat = second_moment / (1.0 - DECAY_SECOND**STEP)
    fresh_weight = weight - step_rate * (
        first_hat / (jnp.sqrt(second_hat) + ADAM_EPSILON) + decay_rate * weight
    )
    return (fresh_weight, first_moment, second_moment)


def update_kernel(*refs):
    (gp, gf, go, gq0, gq1, gq2, vs_ref, norm_ref), refs = refs[:8], refs[8:]
    old, new = refs[:18], refs[18:]
    factor = CLIP_NORM / jnp.maximum(norm_ref[0:1, 0:1], CLIP_NORM)

    def update(number, grad, index, rate, decay):
        values = [old[3 * number + m][index] for m in range(3)]
        fresh = adamw_update(*values, factor * grad, rate, decay)
        for m in range(3):
            new[3 * number + m][index] = fresh[m]

    for k, grad in enumerate((gq0, gq1, gq2)):
        update(0, grad[...], k, RATE_MATRIX, WEIGHT_DECAY)
    for number, grad in ((1, go[...].T), (2, gf[...]), (3, gp[...])):
        update(number, grad, ..., RATE_MATRIX, WEIGHT_DECAY)
    width = vs_ref.shape[1]
    parts = old[15].shape[1] // width
    cols = gq0.shape[1]

    def heads(k):
        rows = [vs_ref[16 + t : 17 + t, k * cols : (k + 1) * cols] for t in range(parts)]
        return jnp.concatenate(rows, axis=1)

    vector_grad = jnp.concatenate([vs_ref[0:4, :], heads(0), heads(2), vs_ref[6:8, :]], axis=0)
    update(4, vector_grad, ..., RATE_VECTOR, 0.0)
    for t in range(parts):
        lanes = slice(t * width, (t + 1) * width)
        update(5, vs_ref[8 + t : 9 + t, :], (slice(None), lanes), RATE_VECTOR, 0.0)


def update_all(totals, vs, norm, states):
    return pl.pallas_call(
        update_kernel,
        out_shape=tuple(sds(s.shape, F32) for s in states),
        in_specs=[VM] * (8 + len(states)),
        out_specs=(VM,) * len(states),
        compiler_params=params(),
        name="update",
    )(*totals, vs, norm, *states)


def on_device(
    tokens,
    cotangent,
    segment_ids,
    valid,
    qkv_weight,
    qkv_moment1,
    qkv_moment2,
    out_weight,
    out_moment1,
    out_moment2,
    fc_weight,
    fc_moment1,
    fc_moment2,
    proj_weight,
    proj_moment1,
    proj_moment2,
    vector_params,
    vector_moment1,
    vector_moment2,
    fc_bias,
    fc_bias_moment1,
    fc_bias_moment2,
):
    custom = lax.axis_size("dp") == 8
    slot, swap = lax.axis_index("tensor") // 2, [(0, 2), (1, 3), (2, 0), (3, 1)]
    states = [jnp.transpose(s, (1, 0, 2)) for s in (qkv_weight, qkv_moment1, qkv_moment2)]
    states += [out_weight, out_moment1, out_moment2]
    states += [fc_weight, fc_moment1, fc_moment2]
    states += [s.T for s in (proj_weight, proj_moment1, proj_moment2)]
    states += [vector_params, vector_moment1, vector_moment2]
    states += [s[None] for s in (fc_bias, fc_bias_moment1, fc_bias_moment2)]
    shards = [states[0], states[3], states[6], states[9]]
    if not custom:
        parts = [states[0][k] for k in range(3)] + [shards[1].T, *shards[2:]]
        shards = []
        for part in parts:
            own = lax.all_gather(part.astype(BF), "dp", axis=0, tiled=True)
            other = lax.ppermute(own, "tensor", swap)
            shards.append(
                jnp.stack([jnp.where(slot == 0, own, other), jnp.where(slot == 0, other, own)])
            )
    saved, weights = forward(
        tokens,
        cotangent,
        valid[None],
        segment_ids.reshape(-1, SLOT),
        vector_params,
        states[15],
        shards,
    )
    outs = backward(saved, weights, tokens, vector_params)
    mixed, input_grad = outs[:2]
    if custom:
        totals, vs, norm = outs[2:8], outs[8], outs[9]
    else:
        vs, totals = outs[2], []
        for g in [saved[10], saved[11], *outs[3:7]]:
            mine = jnp.where(slot == 0, g[0], g[1])
            other = jnp.where(slot == 0, g[1], g[0])
            both = mine.astype(F32) + lax.ppermute(other, "tensor", swap).astype(F32)
            both = lax.psum_scatter(both.astype(BF), "dp", scatter_dimension=0, tiled=True)
            totals.append(both.astype(F32))
        squares = sum(jnp.sum(t * t) for t in totals)
        vs, squares = lax.psum((vs, squares), ("dp", "tensor"))
        norm = jnp.full((8, 128), jnp.sqrt(squares + jnp.sum(vs * vs)), F32)
    new = list(update_all(totals, vs, norm, states))
    new[:3] = [jnp.transpose(s, (1, 0, 2)) for s in new[:3]]
    new[9:12] = [s.T for s in new[9:12]]
    new[15:18] = [s[0] for s in new[15:18]]
    return (mixed, input_grad, norm[0, 0], *new)


def solution(mesh):
    rows = P(("dp", "tensor"), None)
    by_rows = [P("dp", None, "tensor")] * 3
    by_out = [P("tensor", "dp")] * 3
    by_fc = [P("dp", "tensor")] * 3
    weights = by_rows + by_out + by_fc + by_out
    return jax.shard_map(
        on_device,
        mesh=mesh,
        in_specs=(rows, rows, P("dp"), P(("dp", "tensor")), *weights, *[P()] * 6),
        out_specs=(rows, rows, P(), *weights, *[P()] * 6),
        check_vma=False,
    )
```

```python
import functools
import math

import jax
import jax.numpy as jnp
from jax import lax
from jax.experimental import pallas as pl
from jax.experimental.pallas import tpu as pltpu
from jax.sharding import PartitionSpec as P

HD = 64
SLOT = 1024
STEP = 10
NORM_EPSILON = 1e-05
MASK_FILL = -1e30
DECAY_FIRST = 0.5
DECAY_SECOND = 0.5
ADAM_EPSILON = 1e-08
WEIGHT_DECAY = 0.1
CLIP_NORM = 1.0
RATE_MATRIX = 0.04
RATE_VECTOR = 0.3

MESH = pl.DeviceIdType.MESH
BF = jnp.bfloat16
F32 = jnp.float32
HALF = SLOT // 2
BLK = 256
VMEM_LIMIT = 58 * 2**20
LOG2E = math.log2(math.e)
SCORE_SCALE = float(HD) ** (-0.5)
SCORE_SCALE2 = SCORE_SCALE * LOG2E


def dot_nn(a, b):
    return lax.dot_general(a, b, (((1,), (0,)), ((), ())), preferred_element_type=F32)


def dot_nt(a, b):
    return lax.dot_general(a, b, (((1,), (1,)), ((), ())), preferred_element_type=F32)


def dot_tn(a, b):
    return lax.dot_general(a, b, (((0,), (0,)), ((), ())), preferred_element_type=F32)


def dot_tt(a, b):
    return lax.dot_general(a, b, (((0,), (1,)), ((), ())), preferred_element_type=F32)


def params(collective_id=None):
    if collective_id is None:
        return pltpu.CompilerParams(vmem_limit_bytes=VMEM_LIMIT)
    return pltpu.CompilerParams(
        vmem_limit_bytes=VMEM_LIMIT, collective_id=collective_id, has_side_effects=True
    )


VM = pl.BlockSpec(memory_space=pltpu.VMEM)
ANY = pl.BlockSpec(memory_space=pl.ANY)


def sds(shape, dtype):
    return jax.ShapeDtypeStruct(shape, dtype)


def here():
    t = lax.axis_index("tensor")
    return lax.axis_index("dp"), t // 2, t % 2


def greet(ids):
    sem = pltpu.get_barrier_semaphore()
    for one in ids:
        pl.semaphore_signal(sem, inc=1, device_id=one, device_id_type=MESH)
    pl.semaphore_wait(sem, len(ids))


def remote(src, dst, send_sem, recv_sem, target):
    return pltpu.make_async_remote_copy(
        src_ref=src,
        dst_ref=dst,
        send_sem=send_sem,
        recv_sem=recv_sem,
        device_id=target,
        device_id_type=MESH,
    )


def rows_at(start, size):
    return pl.ds(pl.multiple_of(start, size), size)


def norm_parts(values):
    centered = values - jnp.mean(values, axis=-1, keepdims=True)
    variance = jnp.mean(centered * centered, axis=-1, keepdims=True)
    scale = lax.rsqrt(variance + NORM_EPSILON)
    return centered * scale, scale


class Gather:
    def __init__(self, shard, whole, part, by_y, ss, rs):
        dp, x, c = here()
        z, y = dp // 2, dp % 2
        along, x_peer, y_peer, _ = neighbours()
        shard = shard.at[part]
        block = whole.at[x, z, y, part]
        column = whole.at[x, :, y, part]
        from_x = whole.at[1 - x, pl.ds(0, by_y), y, part]
        from_y = whole.at[x, pl.ds(by_y, 4 - by_y), 1 - y, part]
        self.along = [remote(shard, block, ss.at[k], rs.at[k], along[k]) for k in range(3)]
        self.beside = [
            remote(column, column, ss.at[3], rs.at[3], x_peer),
            remote(column, column, ss.at[4], rs.at[4], y_peer),
        ]
        self.passed = [
            remote(from_x, from_x, ss.at[5], rs.at[5], y_peer),
            remote(from_y, from_y, ss.at[6], rs.at[6], x_peer),
        ]

    def start_along(self):
        for one in self.along:
            one.start()

    def start_beside(self):
        for one in self.along:
            one.wait()
        for one in self.beside:
            one.start()

    def start_passed(self):
        for one in self.beside:
            one.wait()
        for one in self.passed:
            one.start()

    def finish(self):
        for one in self.passed:
            one.wait()


class GatherBeside:
    def __init__(self, shard, whole, start, size, by_y, ss, rs):
        dp, x, c = here()
        z, y = dp // 2, dp % 2
        along, x_peer, y_peer, _ = neighbours()
        part = pl.ds(start, size)
        block = whole.at[x, z, y, part]
        from_x = whole.at[1 - x, z, y, pl.ds(start, by_y)]
        from_y = whole.at[x, z, 1 - y, pl.ds(start + by_y, size - by_y)]
        four = whole.at[:, z, :, part]
        self.beside = [
            remote(shard.at[part], block, ss.at[3], rs.at[3], x_peer),
            remote(shard.at[part], block, ss.at[4], rs.at[4], y_peer),
        ]
        self.passed = [
            remote(from_x, from_x, ss.at[5], rs.at[5], y_peer),
            remote(from_y, from_y, ss.at[6], rs.at[6], x_peer),
        ]
        self.along = [remote(four, four, ss.at[k], rs.at[k], along[k]) for k in range(3)]

    def start_beside(self):
        for one in self.beside:
            one.start()

    def start_passed(self):
        for one in self.beside:
            one.wait()
        for one in self.passed:
            one.start()

    def start_along(self):
        for one in self.passed:
            one.wait()
        for one in self.along:
            one.start()

    def finish(self):
        for one in self.along:
            one.wait()


def neighbours():
    dp, x, c = here()
    z, y = dp // 2, dp % 2
    me = x * 2 + c
    along = [(lax.rem(z + k, 4) * 2 + y, me) for k in (1, 2, 3)]
    return along, (dp, (1 - x) * 2 + c), (z * 2 + 1 - y, me), (dp, x * 2 + 1 - c)


def whole_weight(ref, slot):
    value = ref[slot]
    return value.reshape(-1, value.shape[-1])


def allowed_pairs(key_block, query_block, start_row, wide):
    keys = lax.broadcasted_iota(jnp.int32, (BLK, wide), 0) + key_block * BLK
    mask = keys >= start_row
    if key_block == query_block:
        queries = lax.broadcasted_iota(jnp.int32, (BLK, wide), 1) + query_block * BLK
        mask = mask & (keys <= queries)
    return mask


def attend_unit(q, k, v, start):
    blocks = SLOT // BLK
    for i in range(blocks):
        cols = slice(i * BLK, (i + 1) * BLK)
        query = q(cols)
        scores = []
        for j in range(i + 1):
            raw = dot_tn(k(slice(j * BLK, (j + 1) * BLK)), query) * SCORE_SCALE2
            scores.append(jnp.where(allowed_pairs(j, i, start(cols), BLK), raw, MASK_FILL))
        top = functools.reduce(jnp.maximum, [jnp.max(s, axis=0, keepdims=True) for s in scores])
        exps = [jnp.exp2(s - top) for s in scores]
        total = functools.reduce(jnp.add, [jnp.sum(e, axis=0, keepdims=True) for e in exps])
        acc = None
        for j in range(i + 1):
            term = dot_nn(v(slice(j * BLK, (j + 1) * BLK)), exps[j].astype(BF))
            acc = term if acc is None else acc + term
        yield cols, acc / total, top + jnp.log2(total)


GELU_C = math.sqrt(2.0 / math.pi)
GELU_A = 0.044715


def forward_kernel(custom, *refs):
    (tok_ref, cot_ref, valid_ref, seg_ref, vec_ref, fb_ref), refs = refs[:6], refs[6:]
    shards, refs = refs[:4], refs[4:]
    (gl_out, n1_out, u_out, ctx_out, lse_out, start_out, ctxc_out, resid_out, wo_out, br_out, dn_out, gp_out,
     gf_out, gb_ref), refs = refs[:14], refs[14:]
    if custom:
        weights_out, given, refs = refs[:2], refs[2:6], refs[6:]
        lows, refs = refs[:4], refs[4:]
        wholes, refs = refs[:4], refs[4:]
        gs, gr, ps, pr, refs = *refs[:4], refs[4:]
    else:
        wholes = shards
    (tk, gl, n1, u, ctx, lse, starts, ctxc, resid, wo, n2, half, part, got, act, dpre, gp, cols, loc, ts, tr, xs,
     cs_s, cs_r) = refs
    wqk, wvo, wf, wp = wholes
    dp, x, c = here()
    core = (dp, x * 2 + 1 - c)
    x_peer = (dp, (1 - x) * 2 + c)
    across = [(dp, (1 - x) * 2), (dp, (1 - x) * 2 + 1)]
    rows = tok_ref.shape[0]
    first = x * HALF
    gathers = []
    if custom:
        z, y = dp // 2, dp % 2
        along, _, y_peer, _ = neighbours()
        greet([core, *across, *along, y_peer])
        lows[0][...] = jnp.concatenate([shards[0][0], shards[0][1]], axis=1).astype(BF)
        lows[1][...] = jnp.concatenate([shards[0][2], shards[1][...].T], axis=1).astype(BF)
        lows[2][...] = shards[2][...].astype(BF)
        lows[3][...] = shards[3][...].astype(BF)
        pieces = [(0, 0, 2, 2), (0, 1, 2, 2), (1, 0, 2, 2), (1, 1, 2, 2)]
        pieces += [(2, 0, 2, 3), (2, 1, 2, 3), (3, 0, 2, 3)]
        for number, (a, k, parts, by_y) in enumerate(pieces):
            size = lows[a].shape[0] // parts
            gathers.append(
                Gather(
                    lows[a], wholes[a], pl.ds(k * size, size), by_y, gs.at[number], gr.at[number]
                )
            )
        size = lows[3].shape[0] // 2
        gathers.append(GatherBeside(lows[3], wholes[3], size, size, 32, gs.at[7], gr.at[7]))
    else:
        greet([core, *across])

    def step(number, what):
        if custom:
            getattr(gathers[number], what)()

    own_rows = pl.ds(pl.multiple_of(first + c * rows, BLK), rows)
    gl_rows = pl.ds(pl.multiple_of(c * rows, BLK), rows)
    mine_tok = pltpu.make_async_copy(tok_ref, tk.at[own_rows], loc.at[0])
    swap_tok = remote(tok_ref, tk.at[own_rows], ts.at[0], tr.at[0], core)
    swap_grad = remote(gl.at[gl_rows], gl.at[gl_rows], ts.at[1], tr.at[1], core)
    source = [
        tok_ref.at[pl.ds(pl.multiple_of((1 - x) * BLK + k * BLK, BLK), BLK)] for k in range(2)
    ]
    there = [
        tk.at[pl.ds(pl.multiple_of(x * (SLOT + HALF) + k * BLK, BLK), BLK)] for k in range(2)
    ]
    halves = [remote(source[k], there[k], ts.at[2 + k], tr.at[2], across[k]) for k in range(2)]
    landed = tk.at[pl.ds(pl.multiple_of((1 - x) * (SLOT + HALF) + c * BLK, BLK), BLK)]
    handed = remote(landed, landed, ts.at[4], tr.at[3], core)

    if custom:
        for a in range(4):
            wholes[a][x, z, y] = lows[a][...]
    step(0, "start_along")
    step(7, "start_beside")
    mine_tok.start()
    swap_tok.start()
    step(1, "start_along")

    def out_copy(number, ref, out):
        copy = pltpu.make_async_copy(ref, out, loc.at[number])
        copy.start()
        return copy

    cols[...] = vec_ref[...].T
    gain, shift = vec_ref[0:1, :], vec_ref[1:2, :]

    def norm_rows(start, count):
        def norm(i, carry):
            at = rows_at(start + i * BLK, BLK)
            unit, _ = norm_parts(tk[at, :].astype(F32))
            n1[at, :] = (unit * gain + shift).astype(BF)
            return carry

        lax.fori_loop(0, count // BLK, norm, 0)

    mine_tok.wait()
    norm_rows(first + c * rows, rows)
    swap_tok.wait()
    step(7, "start_passed")
    step(0, "start_beside")
    step(2, "start_along")
    norm_rows(first + (1 - c) * rows, rows)
    step(1, "start_beside")
    step(3, "start_along")

    mask = jnp.broadcast_to(valid_ref[...].astype(F32), (8, rows)).T[:, 0:1]
    gl[gl_rows, :] = (cot_ref[...].astype(F32) * mask).astype(BF)
    swap_grad.start()
    for k, row in enumerate((2 * x, 1)):
        segments = seg_ref[pl.ds(row, 1), :].astype(F32)
        column = jnp.broadcast_to(segments, (8, SLOT)).T[:, 0:1]
        for i in range(SLOT // BLK):
            lanes = slice(i * BLK, (i + 1) * BLK)
            below = jnp.where(column < segments[:, lanes], 1.0, 0.0)
            starts[k, :, lanes] = jnp.sum(below, axis=0, keepdims=True).astype(jnp.int32)

    step(2, "start_beside")
    step(4, "start_along")
    step(3, "start_beside")
    step(5, "start_along")
    for number in range(4):
        step(number, "start_passed")

    @pl.when(c == 1 - x)
    def _():
        for one in halves:
            one.start()

    heads = u.shape[2]
    wide = heads * HD

    def project(group, slot, first_row):
        bias_rows = pl.ds(pl.multiple_of((c + 2 * slot) * wide, HD), wide)
        query_bias, value_bias = cols[bias_rows, 4:5], cols[bias_rows, 5:6]

        def chunk(i, carry):
            lanes = rows_at(i * BLK, BLK)
            values = n1[rows_at(first_row + i * BLK, BLK), :]
            two = dot_tt(whole_weight(wqk, slot), values)
            value = dot_tt(whole_weight(wvo, slot)[:, :wide], values) + value_bias
            for k, out in enumerate((two[:wide] + query_bias, two[wide:], value)):
                u[group, k, :, :, lanes] = out.reshape(-1, HD, BLK).astype(BF)
            return carry

        lax.fori_loop(0, SLOT // BLK, chunk, 0)

    def attend(group, which, begin, end):
        def unit(h, carry):
            for lanes, context, log_total in attend_unit(
                lambda s: u[group, 0, h, :, s],
                lambda s: u[group, 1, h, :, s],
                lambda s: u[group, 2, h, :, s],
                lambda s: starts[which, :, s],
            ):
                ctx[group, h, :, lanes] = context.astype(BF)
                lse[group, h, :, lanes] = log_total
            return carry

        lax.fori_loop(begin, end, unit, 0)

    step(4, "start_beside")
    step(6, "start_along")
    project(x, x, x * SLOT)
    attend(x, 0, 0, 1)
    step(5, "start_beside")
    step(7, "start_along")
    attend(x, 0, 1, heads)
    step(4, "start_passed")
    for number in range(4):
        step(number, "finish")
    project(1 - x, 1 - x, x * SLOT)
    step(6, "start_beside")
    for s in range(2):
        wo[s] = whole_weight(wvo, s)[:, wide:]
    attend(1 - x, 0, 0, heads)
    step(5, "start_passed")
    halves[0].wait_recv()
    handed.start()
    handed.wait()
    norm_rows((1 - x) * (SLOT + HALF), HALF)
    project(2, x, (1 - x) * SLOT)
    copies = [out_copy(1, n1, n1_out), out_copy(2, u, u_out)]
    attend(2, 1, 0, heads)
    step(6, "start_passed")
    theirs = pl.ds(pl.multiple_of((1 - x) * HALF, HALF), HALF)
    cross = remote(ctx.at[2, :, :, theirs], half, xs.at[0], xs.at[1], x_peer)
    cross.start()
    copies += [out_copy(3, ctx, ctx_out), out_copy(4, lse, lse_out), out_copy(5, starts, start_out)]
    copies.append(out_copy(8, wo, wo_out))
    if custom:
        copies += [out_copy(6 + a, wholes[a], weights_out[a]) for a in range(2)]

    @pl.when(c == 1 - x)
    def _():
        for one in halves:
            one.wait_send()

    chunks = []

    def send(chunk, values):
        at = rows_at(chunk * BLK, BLK)
        part[at, :] = values.astype(BF)
        copy = remote(part.at[at], got.at[at], cs_s.at[chunk], cs_r.at[chunk], core)
        copy.start()
        chunks.append((chunk, copy))

    def context_of(group, lanes):
        value = ctx[group, :, :, lanes]
        return value.reshape(-1, value.shape[-1])

    for i in range(SLOT // BLK):
        lanes = slice(i * BLK, (i + 1) * BLK)
        chunk = x * 2 + i
        at = rows_at(chunk * BLK, BLK)
        zero, one = context_of(0, lanes), context_of(1, lanes)
        send(chunk, dot_tt(zero, wo[0]) + dot_tt(one, wo[1]))
        ctxc[0, :, at] = zero
        ctxc[1, :, at] = one
    cross.wait()
    for i in range(HALF // BLK):
        chunk = (1 - x) * 4 + i
        at = rows_at(chunk * BLK, BLK)
        own = context_of(2, rows_at(x * HALF + i * BLK, BLK))
        other = half[:, :, i * BLK : (i + 1) * BLK].reshape(-1, BLK)
        send(chunk, dot_tt(own, wo[x]) + dot_tt(other, wo[1 - x]))
        ctxc[x, :, at] = own
        ctxc[1 - x, :, at] = other
    copies.append(out_copy(10, ctxc, ctxc_out))
    swap_grad.wait()
    copies.append(out_copy(11, gl, gl_out))
    for chunk, copy in chunks:
        copy.wait()
        at = rows_at(chunk * BLK, BLK)
        tokens = tk[rows_at(first + chunk * BLK, BLK), :].astype(F32)
        summed = part[at, :].astype(F32) + got[at, :].astype(F32)
        after = tokens + summed + vec_ref[6:7, :]
        resid[at, :] = after
        unit, _ = norm_parts(after)
        n2[at, :] = (unit * vec_ref[2:3, :] + vec_ref[3:4, :]).astype(BF)
    copies.append(out_copy(12, resid, resid_out))
    step(4, "finish")
    step(5, "finish")

    hidden = wf.shape[-1]
    gb_ref[...] = jnp.zeros_like(gb_ref)
    bias_of = [
        fb_ref[:, pl.ds(pl.multiple_of((c + 2 * s) * hidden, hidden), hidden)] for s in range(2)
    ]
    tile = HALF
    tiles = 2 * rows // tile

    def activate(i, carry):
        at = rows_at(i * tile, tile)
        n2_rows = n2[at, :]
        for s in range(2):
            lanes = slice(s * hidden, (s + 1) * hidden)
            v = dot_nn(n2_rows, whole_weight(wf, s)) + bias_of[s]
            square = v * v
            t = jnp.tanh(v * (GELU_C + (GELU_C * GELU_A) * square))
            cdf = 0.5 + 0.5 * t
            act[at, lanes] = (v * cdf).astype(BF)
            slope = cdf + (cdf * (1.0 - t)) * (v * (GELU_C + (3.0 * GELU_C * GELU_A) * square))
            dpre[at, lanes] = slope.astype(BF)
        return carry

    lax.fori_loop(0, tiles, activate, 0)
    blocks = gp.shape[1:4]

    for s in range(2):
        out = dot_tn(gl[...], act[:, s * hidden : (s + 1) * hidden]).astype(BF)
        gp[s] = out.reshape(*blocks, hidden)
        copies.append(out_copy(15 + s, gp.at[s], gp_out.at[s]))
    passing = []
    if custom:
        low, high = pl.ds(0, 2), pl.ds(2, 2)
        pieces = [
            (gp.at[1 - x, low, 1 - y], y_peer),
            (gp.at[1 - x, high, 1 - y], x_peer),
            (gp.at[1 - x, high, y], x_peer),
            (gp.at[x, low, 1 - y], y_peer),
        ]
        for k, (piece, peer) in enumerate(pieces):
            passing.append(remote(piece, given[k], ps.at[k], pr.at[k], peer))
            passing[-1].start()
    step(6, "finish")
    step(7, "finish")

    def forward_back(i, carry):
        at = rows_at(i * tile, tile)
        gl_now = gl[at, :]
        for s in range(2):
            lanes = slice(s * hidden, (s + 1) * hidden)
            up = dot_nn(gl_now, whole_weight(wp, s))
            d = (up * dpre[at, lanes].astype(F32)).astype(BF)
            dpre[at, lanes] = d
            gb_ref[s] += jnp.sum(d.astype(F32), axis=0, keepdims=True)
        br = dot_nt(act[at, :hidden], whole_weight(wp, 0))
        br += dot_nt(act[at, hidden:], whole_weight(wp, 1))
        part[at, :] = br.astype(BF)
        dn = dot_nt(dpre[at, :hidden], whole_weight(wf, 0))
        dn += dot_nt(dpre[at, hidden:], whole_weight(wf, 1))
        got[at, :] = dn.astype(BF)
        return carry

    lax.fori_loop(0, tiles, forward_back, 0)
    copies += [out_copy(13, got, dn_out), out_copy(14, part, br_out)]
    width = n2.shape[1]

    for s in range(2):
        at = slice(s * width, (s + 1) * width)
        tk[at, :] = dot_tn(n2[...], dpre[:, s * hidden : (s + 1) * hidden]).astype(BF)
        copies.append(out_copy(17 + s, tk.at[at], gf_out.at[s]))
    for copy in copies + passing:
        copy.wait()


def forward(tokens, cotangent, valid, segments, vectors, fc_bias, shards):
    rows, width = tokens.shape
    chip = 2 * rows
    custom = lax.axis_size("dp") == 8
    dma = pltpu.SemaphoreType.DMA
    if custom:
        cols = shards[0].shape[2]
        hidden = shards[2].shape[1]
        part_rows = shards[2].shape[0]
        flat = [(part_rows, n) for n in (2 * cols, 2 * cols, hidden, hidden)]
        wholes = [(2, 4, 2) + s for s in flat]
        more_out = [sds(w, BF) for w in wholes[:2]] + [sds((2, part_rows, hidden), BF)] * 4
        more = [pltpu.VMEM(s, BF) for s in flat] + [pltpu.VMEM(w, BF) for w in wholes]
        more += [dma((8, 7)), dma((8, 7)), dma((4,)), dma((4,))]
        grad_shape = wholes[3]
    else:
        cols, hidden = shards[0].shape[2] // 2, shards[2].shape[2]
        more_out, more = [], []
        grad_shape = (2, 1, 1, width, hidden)
    heads = cols // HD
    shapes = [
        ((chip, width), BF),
        ((2 * SLOT, width), BF),
        ((3, 3, heads, HD, SLOT), BF),
        ((3, heads, HD, SLOT), BF),
        ((3, heads, 1, SLOT), F32),
        ((2, 1, SLOT), jnp.int32),
        ((2, cols, chip), BF),
        ((chip, width), F32),
        ((2, width, cols), BF),
    ]
    out_shape = [sds(*s) for s in shapes]
    out_shape += [sds((chip, width), BF)] * 2 + [sds(grad_shape, BF), sds((2, width, hidden), BF)]
    out_shape += [sds((2, 1, hidden), F32)] + more_out
    outs = pl.pallas_call(
        functools.partial(forward_kernel, custom),
        out_shape=tuple(out_shape),
        in_specs=[ANY] + [VM] * (5 + len(shards)),
        out_specs=(*[ANY] * 13, VM, *[ANY] * len(more_out)),
        scratch_shapes=more
        + [
            pltpu.VMEM((2 * SLOT, width), BF),
            *[pltpu.VMEM(*s) for s in shapes],
            pltpu.VMEM((chip, width), BF),
            pltpu.VMEM((heads, HD, HALF), BF),
            pltpu.VMEM((chip, width), BF),
            pltpu.VMEM((chip, width), BF),
            pltpu.VMEM((chip, 2 * hidden), BF),
            pltpu.VMEM((chip, 2 * hidden), BF),
            pltpu.VMEM(grad_shape, BF),
            pltpu.VMEM((width, 8), F32),
            dma((19,)),
            dma((5,)),
            dma((4,)),
            dma((2,)),
            dma((chip // BLK,)),
            dma((chip // BLK,)),
        ],
        compiler_params=params(1),
        name="forward",
    )(tokens, cotangent, valid, segments, vectors, fc_bias, *shards)
    if custom:
        return outs[:14], outs[14:16], outs[16:]
    return outs[:14], shards[:2], []


class Reduce:
    def __init__(self, grad, by_y, local, given, total, bufs, loc, ss, rs):
        dp, x, c = here()
        z, y = dp // 2, dp % 2
        along, x_peer, y_peer, _ = neighbours()
        low, high = pl.ds(0, by_y), pl.ds(by_y, 4 - by_y)
        self.z, self.total = z, total
        self.r1y, self.r1x, self.r2x, self.r2y, self.r3 = bufs
        views = [grad.at[1 - x, low, y], grad.at[x, high, 1 - y], grad.at[x, :, y]]
        self.loads = []
        self.mid_x, self.mid_y, self.own = views
        if local is not None:
            self.loads = [
                pltpu.make_async_copy(views[k], local[k], loc.at[k]) for k in range(3)
            ]
            self.mid_x, self.mid_y, self.own = local
        if given is None:
            self.first = [
                remote(grad.at[1 - x, low, 1 - y], self.r1y, ss.at[0], rs.at[0], y_peer),
                remote(grad.at[1 - x, high, 1 - y], self.r1x, ss.at[1], rs.at[1], x_peer),
            ]
            self.early = [
                remote(grad.at[1 - x, high, y], self.r2x.at[high], ss.at[2], rs.at[2], x_peer),
                remote(grad.at[x, low, 1 - y], self.r2y.at[low], ss.at[3], rs.at[3], y_peer),
            ]
        else:
            targets = (self.r1y, self.r1x, self.r2x.at[high], self.r2y.at[low])
            copies = [
                pltpu.make_async_copy(given[k], targets[k], rs.at[k]) for k in range(4)
            ]
            self.first, self.early = copies[:2], copies[2:]
        self.second = [
            remote(self.mid_x, self.r2x.at[low], ss.at[4], rs.at[4], x_peer),
            remote(self.mid_y, self.r2y.at[high], ss.at[5], rs.at[5], y_peer),
        ]
        self.third = [
            remote(
                self.own.at[lax.rem(z + k + 1, 4)], self.r3.at[k], ss.at[6 + k], rs.at[6 + k], along[k]
            )
            for k in range(3)
        ]

    def start_first(self):
        for one in self.loads:
            one.start()
        for one in self.first:
            one.start()

    def start_early(self, which):
        self.early[which].start()

    def start_second(self, which):
        self.first[which].wait()
        if self.loads:
            self.loads[which].wait()
        mid, came = ((self.mid_x, self.r1y), (self.mid_y, self.r1x))[which]
        mid[...] = (mid[...].astype(F32) + came[...].astype(F32)).astype(BF)
        self.second[which].start()

    def start_third(self):
        for one in self.early + self.second + self.loads[2:]:
            one.wait()
        for k in range(4):
            place = lax.rem(self.z + k + 1, 4)
            summed = (
                self.own[place].astype(F32)
                + self.r2x[place].astype(F32)
                + self.r2y[place].astype(F32)
            )
            if k < 3:
                self.own[place] = summed.astype(BF)
                self.third[k].start()
            else:
                self.total[...] = summed

    def finish(self):
        for one in self.third:
            one.wait()
        total = self.total[...]
        for k in range(3):
            total = total + self.r3[k].astype(F32)
        self.total[...] = total
        return jnp.sum(total * total)


def eight_peers():
    dp, x, c = here()
    z, y = dp // 2, dp % 2
    peers = []
    for k in range(1, 8):
        kx, ky, kc = k // 4, k // 2 % 2, k % 2
        there = ((1 - x if kx else x), (1 - y if ky else y), (1 - c if kc else c))
        peers.append((z * 2 + there[1], there[0] * 2 + there[2]))
    return peers


class SumOverAll:
    def __init__(self, value, near, far, ss, rs):
        dp, x, c = here()
        z, y = dp // 2, dp % 2
        self.value, self.near, self.far = value, near, far
        self.me, self.z = x * 4 + y * 2 + c, z
        self.one = [
            remote(value, near.at[self.me], ss.at[k], rs.at[k], peer)
            for k, peer in enumerate(eight_peers())
        ]
        self.two = [
            remote(value, far.at[z], ss.at[7 + k], rs.at[7 + k], peer)
            for k, peer in enumerate(neighbours()[0])
        ]

    def start(self):
        for one in self.one:
            one.start()
        self.near[self.me] = self.value[...]

    def middle(self):
        for one in self.one:
            one.wait()
        self.value[...] = functools.reduce(jnp.add, [self.near[k] for k in range(8)])
        for one in self.two:
            one.start()
        self.far[self.z] = self.value[...]

    def finish(self):
        for one in self.two:
            one.wait()
        return functools.reduce(jnp.add, [self.far[k] for k in range(4)])


def attend_back_unit(u, out, start, ctx, dctx, lse, dq_ref):
    blocks = SLOT // BLK
    delta = jnp.sum(dctx.astype(F32) * ctx.astype(F32), axis=0, keepdims=True)
    for j in range(blocks):
        keys = slice(j * BLK, (j + 1) * BLK)
        k = u(1, keys)
        v = u(2, keys)
        probs, dscores = [], []
        for i in range(j, blocks):
            cols = slice(i * BLK, (i + 1) * BLK)
            raw = dot_tn(k, u(0, cols)) * SCORE_SCALE2 - lse[:, cols]
            prob = jnp.exp2(jnp.where(allowed_pairs(j, i, start[:, cols], BLK), raw, MASK_FILL))
            dprob = dot_tn(v, dctx[:, cols])
            probs.append(prob.astype(BF))
            dscores.append((prob * (dprob - delta[:, cols])).astype(BF))
        dk, dv = None, None
        for n, i in enumerate(range(j, blocks)):
            cols = slice(i * BLK, (i + 1) * BLK)
            dv_term = dot_nt(dctx[:, cols], probs[n])
            dk_term = dot_nt(u(0, cols), dscores[n])
            dv = dv_term if dv is None else dv + dv_term
            dk = dk_term if dk is None else dk + dk_term
            dq_term = dot_nn(k, dscores[n])
            if j == 0:
                dq_ref[:, cols] = dq_term
            else:
                dq_ref[:, cols] += dq_term
        out(1, keys, (dk * SCORE_SCALE).astype(BF))
        out(2, keys, dv.astype(BF))
    out(0, slice(0, SLOT), (dq_ref[...] * SCORE_SCALE).astype(BF))


BY_Y = (2, 3, 3, 3)


def norm_back(dn, values, gain):
    unit, scale = norm_parts(values)
    e = dn * gain
    back = scale * (
        e
        - jnp.mean(e, axis=-1, keepdims=True)
        - unit * jnp.mean(e * unit, axis=-1, keepdims=True)
    )
    return back, unit


def backward_kernel(custom, *refs):
    (gl_in, n1_in, u_in, ctx_in, lse_ref, start_ref, ctxc_in, resid_in, wo_in, br_in, dn_in, gp_in, gf_in, gb_ref,
     wqk_in, wvo_in, tok_in, vec_ref), refs = refs[:18], refs[18:]
    given = None
    if custom:
        given, refs = refs[:4], refs[4:]
    (mixed_out, ig_out), refs = refs[:2], refs[2:]
    if custom:
        totals, refs = refs[:4], refs[4:]
        (va_out, vb_out, norm_ref), refs = refs[:3], refs[3:]
        gvo, gqk, refs = refs[0], refs[1], refs[2:]
        locals_, refs = (refs[:3], refs[3:6]), refs[6:]
        bufs, refs = [refs[5 * a : 5 * a + 5] for a in range(4)], refs[20:]
        (va, vb, near_a, far_a, near_b, far_b, near_s, far_s, square, lss, ss, rs, ass, ars, bss, brs, qss,
         qrs), refs = refs[:18], refs[18:]
    else:
        va, vb, gvo, gqk, refs = *refs[:4], refs[4:]
    (gl_s, resid_s, dn_s, got_dn, br_s, got_br, mixed, low, dres, dctx, ctxc, wo, half_c, outgoing, u, ctx, n1,
     wqk, wvo, tok, du, dq, half, got, loc, ld, cs_s, cs_r, bs, xs, ws) = refs
    part = low
    dp, x, c = here()
    core = (dp, x * 2 + 1 - c)
    x_peer = (dp, (1 - x) * 2 + c)
    reduces = []
    if custom:
        greet(eight_peers() + neighbours()[0])
        for a, grad in enumerate((gp_in, gf_in, gvo, gqk)):
            local = locals_[a] if a < 2 else None
            loads = lss.at[a] if a < 2 else None
            came = given if a == 0 else None
            reduces.append(
                Reduce(
                    grad, BY_Y[a], local, came, totals[a], bufs[a], loads, ss.at[a], rs.at[a]
                )
            )
    else:
        greet([core, x_peer])

    def step(number, what, *which):
        if custom:
            getattr(reduces[number], what)(*which)

    rows_all, width = low.shape
    own_rows = rows_all // 2
    n_chunks = rows_all // BLK
    order = [(1 - x) * 4 + i for i in range(HALF // BLK)] + [x * 2 + i for i in range(SLOT // BLK)]
    swaps = []
    for chunk in order:
        at = rows_at(chunk * BLK, BLK)
        swaps.append(remote(dn_in.at[at], got_dn.at[at], cs_s.at[chunk], cs_r.at[chunk], core))
    their = pl.ds(pl.multiple_of((1 - c) * own_rows, BLK), own_rows)
    mine = pl.ds(pl.multiple_of(c * own_rows, BLK), own_rows)
    branch = remote(br_in.at[their], got_br, bs.at[0], bs.at[1], core)

    def chunk_loads(n):
        at, slot = rows_at(order[n] * BLK, BLK), n % 2
        return [
            pltpu.make_async_copy(source.at[at], target.at[slot], ld.at[slot, k])
            for k, (source, target) in enumerate(
                ((resid_in, resid_s), (gl_in, gl_s), (dn_in, dn_s))
            )
        ]

    def load(number, source, target):
        copy = pltpu.make_async_copy(source, target, loc.at[number])
        copy.start()
        return copy

    loads = [chunk_loads(n) for n in range(n_chunks)]
    swaps[0].start()
    for n in range(2):
        for one in loads[n]:
            one.start()
    branch.start()
    for one in swaps[1:]:
        one.start()
    step(0, "start_first")
    step(0, "start_early", 0)
    step(0, "start_early", 1)
    step(1, "start_first")
    br_load = load(0, br_in.at[mine], br_s)
    wo_load = load(1, wo_in, wo)
    ctxc_load = load(2, ctxc_in, ctxc)
    step(1, "start_early", 0)
    step(1, "start_early", 1)
    late = [
        load(3, u_in, u),
        load(4, ctx_in, ctx),
        load(5, n1_in, n1),
        load(6, wqk_in, wqk),
        load(7, wvo_in, wvo),
        load(8, tok_in, tok),
    ]
    va[...] = jnp.zeros_like(va)
    vb[...] = jnp.zeros_like(vb)
    for s in range(2):
        va[pl.ds(4 + c + 2 * s, 1), :] = gb_ref[s]
    branch.wait()
    br_load.wait()
    for n, chunk in enumerate(order):
        slot = n % 2
        for one in loads[n]:
            one.wait()
        swaps[n].wait()
        at = rows_at(chunk * BLK, BLK)
        dn = dn_s[slot].astype(F32) + got_dn[at, :].astype(F32)
        resid = resid_s[slot]
        back, unit = norm_back(dn, resid, vec_ref[2:3, :])
        grad = gl_s[slot].astype(F32)
        after = grad + back
        low[at, :] = after.astype(BF)

        @pl.when(chunk // (n_chunks // 2) == c)
        def _(chunk=chunk, dn=dn, resid=resid, unit=unit, grad=grad, after=after):
            here_at = rows_at((chunk - c * (n_chunks // 2)) * BLK, BLK)
            dres[here_at, :] = after
            branches = br_s[here_at, :].astype(F32) + got_br[here_at, :].astype(F32)
            mixed[here_at, :] = (resid + branches + vec_ref[7:8, :]).astype(BF)
            va[0:1, :] += jnp.sum(dn * unit, axis=0, keepdims=True)
            va[1:2, :] += jnp.sum(dn, axis=0, keepdims=True)
            va[2:3, :] += jnp.sum(after, axis=0, keepdims=True)
            va[3:4, :] += jnp.sum(grad, axis=0, keepdims=True)

        if n + 2 < n_chunks:
            for one in loads[n + 2]:
                one.start()
        if n == 1:
            wo_load.wait()
            for i in range(HALF // BLK):
                lanes = slice(i * BLK, (i + 1) * BLK)
                rows = low[rows_at((1 - x) * SLOT + i * BLK, BLK), :]
                outgoing[:, :, lanes] = (
                    dot_tt(wo[1 - x], rows).astype(BF).reshape(-1, HD, BLK)
                )
                dctx[2, :, :, rows_at(x * HALF + i * BLK, BLK)] = (
                    dot_tt(wo[x], rows).astype(BF).reshape(-1, HD, BLK)
                )
            cross_c = remote(outgoing, half_c, xs.at[0], xs.at[1], x_peer)
            cross_c.start()
            step(0, "start_second", 0)
            step(0, "start_second", 1)
    mixed_copy = pltpu.make_async_copy(mixed, mixed_out, ws.at[0])
    mixed_copy.start()
    if custom:
        early_sum = SumOverAll(va, near_a, far_a, ass, ars)
        early_sum.start()
    heads = u.shape[2]
    cols = heads * HD
    blocks = gvo.shape[1:4]
    ctxc_load.wait()
    for s in range(2):
        gvo[s, :, :, :, cols:] = dot_tt(low[...], ctxc[s]).astype(BF).reshape(*blocks, cols)
    for i in range(SLOT // BLK):
        lanes = slice(i * BLK, (i + 1) * BLK)
        rows = low[rows_at(x * HALF + i * BLK, BLK), :]
        for s in range(2):
            dctx[s, :, :, lanes] = dot_tt(wo[s], rows).astype(BF).reshape(-1, HD, BLK)
    step(0, "start_third")
    step(1, "start_second", 0)
    step(1, "start_second", 1)
    late[0].wait()
    late[1].wait()

    def attend_back(group, which, begin, end):
        def unit(h, carry):
            def put(k, lanes, value):
                du[group, k, h, :, lanes] = value

            attend_back_unit(
                lambda k, lanes: u[group, k, h, :, lanes],
                put,
                start_ref[which],
                ctx[group, h],
                dctx[group, h],
                lse_ref[group, h],
                dq,
            )
            return carry

        lax.fori_loop(begin, end, unit, 0)

    full_rows = pl.ds(pl.multiple_of(x * SLOT, SLOT), SLOT)
    part_rows = pl.ds(pl.multiple_of((1 - x) * SLOT, SLOT), SLOT)
    everything = slice(0, SLOT)

    def of_group(group, k, lanes):
        value = du[group, k, :, :, lanes]
        return value.reshape(cols, value.shape[-1])

    def weight_grad(slot, which, with_part):
        def rows_of(group):
            if which == 1:
                return of_group(group, 2, everything)
            return du[group, 0:2].reshape(2 * cols, SLOT)

        out = dot_tt(n1[full_rows, :], rows_of(slot))
        if with_part:
            out += dot_tt(n1[part_rows, :], rows_of(2))
        if which == 1:
            gvo[slot, :, :, :, :cols] = out.astype(BF).reshape(*blocks, cols)
        else:
            gqk[slot] = out.astype(BF).reshape(*blocks, 2 * cols)

    attend_back(1 - x, 0, 0, heads)
    for one in late[2:]:
        one.wait()
    for number, which in ((2, 1), (3, 0)):
        weight_grad(1 - x, which, False)
        step(number, "start_first")
        step(number, "start_early", 0)
    if custom:
        early_sum.middle()
    cross_c.wait()
    dctx[2, :, :, pl.ds(pl.multiple_of((1 - x) * HALF, HALF), HALF)] = half_c[...]
    attend_back(2, 1, 0, heads)
    theirs = pl.ds(pl.multiple_of((1 - x) * HALF, HALF), HALF)
    cross = remote(du.at[2, :, :, :, theirs], half, xs.at[2], xs.at[3], x_peer)
    cross.start()
    step(1, "start_third")
    step(2, "start_second", 0)
    step(3, "start_second", 0)
    attend_back(x, 0, 0, heads)
    for number, which in ((2, 1), (3, 0)):
        weight_grad(x, which, True)
        step(number, "start_early", 1)
        step(number, "start_second", 1)

    def bias_sums(group):
        sums = [
            jnp.sum(of_group(group, k, everything).astype(F32), axis=1, keepdims=True)
            for k in (0, 2)
        ]
        return jnp.concatenate(sums, axis=0)

    columns = [bias_sums(x) + bias_sums(2), bias_sums(1 - x)]
    as_rows = jnp.concatenate(columns + [jnp.zeros((2 * cols, 6), F32)], axis=1).T
    for n, slot in enumerate((x, 1 - x)):
        vb[pl.ds(2 + c + 2 * slot, 1), : 2 * cols] = as_rows[n : n + 1, :]

    def back_through(two, value, slot):
        return dot_tt(two, whole_weight(wqk, slot)) + dot_tt(
            value, whole_weight(wvo, slot)[:, :cols]
        )

    def pair_of(group, lanes):
        value = du[group, 0:2, :, :, lanes]
        return value.reshape(2 * cols, value.shape[-1])

    for i in range(SLOT // BLK):
        lanes = slice(i * BLK, (i + 1) * BLK)
        back = [back_through(pair_of(s, lanes), of_group(s, 2, lanes), s) for s in range(2)]
        part[rows_at((x * 2 + i) * BLK, BLK), :] = (back[0] + back[1]).astype(BF)
    cross.wait()
    for i in range(HALF // BLK):
        lanes = rows_at(x * HALF + i * BLK, BLK)
        back = back_through(pair_of(2, lanes), of_group(2, 2, lanes), x)
        lanes = slice(i * BLK, (i + 1) * BLK)
        back += back_through(
            half[0:2, :, :, lanes].reshape(2 * cols, BLK),
            half[2, :, :, lanes].reshape(cols, BLK),
            1 - x,
        )
        part[rows_at(((1 - x) * 4 + i) * BLK, BLK), :] = back.astype(BF)
    swap = remote(part.at[their], got, bs.at[2], bs.at[3], core)
    swap.start()
    step(2, "start_third")
    swap.wait()
    for r in range(own_rows // BLK):
        rows = slice(r * BLK, (r + 1) * BLK)
        wide = rows_at(c * own_rows + r * BLK, BLK)
        dn = part[wide, :].astype(F32) + got[rows, :].astype(F32)
        back, unit = norm_back(dn, tok[rows, :].astype(F32), vec_ref[0:1, :])
        mixed_copy.wait() if r == 0 else None
        mixed[rows, :] = (dres[rows, :] + back).astype(BF)
        vb[0:1, :] += jnp.sum(dn * unit, axis=0, keepdims=True)
        vb[1:2, :] += jnp.sum(dn, axis=0, keepdims=True)
    ig_copy = pltpu.make_async_copy(mixed, ig_out, ws.at[1])
    ig_copy.start()
    if custom:
        late_sum = SumOverAll(vb, near_b, far_b, bss, brs)
        late_sum.start()
        va_out[...] = early_sum.finish()
        step(3, "start_third")
        late_sum.middle()
        squares = functools.reduce(jnp.add, [one.finish() for one in reduces])
        square[...] = jnp.full(square.shape, squares, F32)
        norm = SumOverAll(square, near_s, far_s, qss, qrs)
        norm.start()
        vb_out[...] = late_sum.finish()
        vector_squares = jnp.sum(va_out[...] * va_out[...], keepdims=True)
        vector_squares += jnp.sum(vb_out[...] * vb_out[...], keepdims=True)
        norm.middle()
        norm_ref[...] = jnp.sqrt(norm.finish() + vector_squares)
    ig_copy.wait()


def backward(saved, weights, given, tokens, vectors):
    (gl, n1, u, ctx, lse, starts, ctxc, resid, wo, br, dn, gp, gf, gb) = saved
    rows, width = tokens.shape
    chip = 2 * rows
    heads = u.shape[2]
    cols = heads * HD
    custom = lax.axis_size("dp") == 8
    dma = pltpu.SemaphoreType.DMA
    out_shape = [sds((rows, width), BF)] * 2
    out_specs = [ANY, ANY]
    if custom:
        hidden = gp.shape[-1]
        part_rows = width // 8
        shapes = [(part_rows, n) for n in (hidden, hidden, 2 * cols, 2 * cols)]
        gf = gf.reshape(gp.shape)
        out_shape += [sds(s, F32) for s in shapes]
        out_shape += [sds((8, width), F32)] * 2 + [sds((8, 128), F32)]
        out_specs += [VM] * 7
        scratch = [pltpu.VMEM((2, 4, 2) + s, BF) for s in shapes[2:]]
        scratch += [
            pltpu.VMEM((n,) + shapes[a], BF) for a in range(2) for n in (BY_Y[a], 4 - BY_Y[a], 4)
        ]
        scratch += [
            pltpu.VMEM((n,) + shapes[a], BF)
            for a in range(4)
            for n in (BY_Y[a], 4 - BY_Y[a], 4, 4, 3)
        ]
        scratch += [
            *[pltpu.VMEM((8, width), F32)] * 2,
            *[pltpu.VMEM((8, 8, width), F32), pltpu.VMEM((4, 8, width), F32)] * 2,
            pltpu.VMEM((8, 8, 128), F32),
            pltpu.VMEM((4, 8, 128), F32),
            pltpu.VMEM((8, 128), F32),
            dma((2, 3)),
            dma((4, 9)),
            dma((4, 9)),
            *[dma((10,))] * 6,
        ]
    else:
        out_shape += [sds((8, width), F32)] * 2 + [sds((2, 1, 1, width, 2 * cols), BF)] * 2
        out_specs += [VM] * 4
        scratch = []
    scratch += [
        pltpu.VMEM((2, BLK, width), BF),
        pltpu.VMEM((2, BLK, width), F32),
        pltpu.VMEM((2, BLK, width), BF),
        pltpu.VMEM((chip, width), BF),
        pltpu.VMEM((rows, width), BF),
        pltpu.VMEM((rows, width), BF),
        pltpu.VMEM((rows, width), BF),
        pltpu.VMEM((chip, width), BF),
        pltpu.VMEM((rows, width), F32),
        pltpu.VMEM(ctx.shape, BF),
        pltpu.VMEM(ctxc.shape, BF),
        pltpu.VMEM(wo.shape, BF),
        pltpu.VMEM((heads, HD, HALF), BF),
        pltpu.VMEM((heads, HD, HALF), BF),
        pltpu.VMEM(u.shape, BF),
        pltpu.VMEM(ctx.shape, BF),
        pltpu.VMEM(n1.shape, BF),
        *[pltpu.VMEM(w.shape, BF) for w in weights],
        pltpu.VMEM((rows, width), BF),
        pltpu.VMEM(u.shape, BF),
        pltpu.VMEM((HD, SLOT), F32),
        pltpu.VMEM((3, heads, HD, HALF), BF),
        pltpu.VMEM((rows, width), BF),
        dma((9,)),
        dma((2, 3)),
        dma((chip // BLK,)),
        dma((chip // BLK,)),
        dma((4,)),
        dma((4,)),
        dma((2,)),
    ]
    return pl.pallas_call(
        functools.partial(backward_kernel, custom),
        out_shape=tuple(out_shape),
        in_specs=[ANY] * 4 + [VM, VM] + [ANY] * 7 + [VM] + [ANY] * 3 + [VM] + [ANY] * len(given),
        out_specs=tuple(out_specs),
        scratch_shapes=scratch,
        compiler_params=params(2),
        name="backward",
    )(gl, n1, u, ctx, lse, starts, ctxc, resid, wo, br, dn, gp, gf, gb, *weights, tokens, vectors, *given)


def adamw_update(weight, moment_one, moment_two, gradient, step_rate, decay_rate):
    first_moment = DECAY_FIRST * moment_one + (1.0 - DECAY_FIRST) * gradient
    second_moment = DECAY_SECOND * moment_two + (1.0 - DECAY_SECOND) * gradient * gradient
    first_hat = first_moment / (1.0 - DECAY_FIRST**STEP)
    second_hat = second_moment / (1.0 - DECAY_SECOND**STEP)
    fresh_weight = weight - step_rate * (
        first_hat / (jnp.sqrt(second_hat) + ADAM_EPSILON) + decay_rate * weight
    )
    return (fresh_weight, first_moment, second_moment)


def update_kernel(*refs):
    (gp, gf, gvo, gqk, va, vb, norm_ref), refs = refs[:7], refs[7:]
    cols = gvo.shape[1] // 2
    old, new = refs[:18], refs[18:]
    factor = CLIP_NORM / jnp.maximum(norm_ref[0:1, 0:1], CLIP_NORM)

    def update(number, grad, index, rate, decay):
        values = [old[3 * number + m][index] for m in range(3)]
        fresh = adamw_update(*values, factor * grad, rate, decay)
        for m in range(3):
            new[3 * number + m][index] = fresh[m]

    for k, grad in enumerate((gqk[:, :cols], gqk[:, cols:], gvo[:, :cols])):
        update(0, grad, k, RATE_MATRIX, WEIGHT_DECAY)
    for number, grad in ((1, gvo[:, cols:].T), (2, gf[...]), (3, gp[...])):
        update(number, grad, ..., RATE_MATRIX, WEIGHT_DECAY)
    width = va.shape[1]
    parts = old[15].shape[1] // width

    def heads(k):
        rows = [vb[2 + t : 3 + t, k * cols : (k + 1) * cols] for t in range(parts)]
        return jnp.concatenate(rows, axis=1)

    vector_grad = jnp.concatenate(
        [vb[0:2, :], va[0:2, :], heads(0), heads(1), va[2:4, :]], axis=0
    )
    update(4, vector_grad, ..., RATE_VECTOR, 0.0)
    for t in range(parts):
        lanes = slice(t * width, (t + 1) * width)
        update(5, va[4 + t : 5 + t, :], (slice(None), lanes), RATE_VECTOR, 0.0)


def update_all(totals, va, vb, norm, states):
    return pl.pallas_call(
        update_kernel,
        out_shape=tuple(sds(s.shape, F32) for s in states),
        in_specs=[VM] * (7 + len(states)),
        out_specs=(VM,) * len(states),
        compiler_params=params(),
        name="update",
    )(*totals, va, vb, norm, *states)


def on_device(
    tokens,
    cotangent,
    segment_ids,
    valid,
    qkv_weight,
    qkv_moment1,
    qkv_moment2,
    out_weight,
    out_moment1,
    out_moment2,
    fc_weight,
    fc_moment1,
    fc_moment2,
    proj_weight,
    proj_moment1,
    proj_moment2,
    vector_params,
    vector_moment1,
    vector_moment2,
    fc_bias,
    fc_bias_moment1,
    fc_bias_moment2,
):
    custom = lax.axis_size("dp") == 8
    slot, swap = lax.axis_index("tensor") // 2, [(0, 2), (1, 3), (2, 0), (3, 1)]
    states = [jnp.transpose(s, (1, 0, 2)) for s in (qkv_weight, qkv_moment1, qkv_moment2)]
    states += [out_weight, out_moment1, out_moment2]
    states += [fc_weight, fc_moment1, fc_moment2]
    states += [s.T for s in (proj_weight, proj_moment1, proj_moment2)]
    states += [vector_params, vector_moment1, vector_moment2]
    states += [s[None] for s in (fc_bias, fc_bias_moment1, fc_bias_moment2)]
    shards = [states[0], states[3], states[6], states[9]]
    if not custom:
        parts = [
            jnp.concatenate([states[0][0], states[0][1]], axis=1),
            jnp.concatenate([states[0][2], shards[1].T], axis=1),
            *shards[2:],
        ]
        shards = []
        for part in parts:
            own = lax.all_gather(part.astype(BF), "dp", axis=0, tiled=True)
            other = lax.ppermute(own, "tensor", swap)
            shards.append(
                jnp.stack([jnp.where(slot == 0, own, other), jnp.where(slot == 0, other, own)])
            )
    saved, weights, given = forward(
        tokens,
        cotangent,
        valid[None],
        segment_ids.reshape(-1, SLOT),
        vector_params,
        states[15],
        shards,
    )
    outs = backward(saved, weights, given, tokens, vector_params)
    mixed, input_grad = outs[:2]
    if custom:
        totals, (va, vb, norm) = outs[2:6], outs[6:]
    else:
        va, vb, totals = *outs[2:4], []
        for g in [saved[11], saved[12], *outs[4:6]]:
            g = g.reshape(2, -1, g.shape[-1])
            mine = jnp.where(slot == 0, g[0], g[1])
            other = jnp.where(slot == 0, g[1], g[0])
            both = mine.astype(F32) + lax.ppermute(other, "tensor", swap).astype(F32)
            both = lax.psum_scatter(both.astype(BF), "dp", scatter_dimension=0, tiled=True)
            totals.append(both.astype(F32))
        squares = sum(jnp.sum(t * t) for t in totals)
        va, vb, squares = lax.psum((va, vb, squares), ("dp", "tensor"))
        squares += jnp.sum(va * va) + jnp.sum(vb * vb)
        norm = jnp.full((8, 128), jnp.sqrt(squares), F32)
    new = list(update_all(totals, va, vb, norm, states))
    new[:3] = [jnp.transpose(s, (1, 0, 2)) for s in new[:3]]
    new[9:12] = [s.T for s in new[9:12]]
    new[15:18] = [s[0] for s in new[15:18]]
    return (mixed, input_grad, norm[0, 0], *new)


def solution(mesh):
    rows = P(("dp", "tensor"), None)
    by_rows = [P("dp", None, "tensor")] * 3
    by_out = [P("tensor", "dp")] * 3
    by_fc = [P("dp", "tensor")] * 3
    weights = by_rows + by_out + by_fc + by_out
    return jax.shard_map(
        on_device,
        mesh=mesh,
        in_specs=(rows, rows, P("dp"), P(("dp", "tensor")), *weights, *[P()] * 6),
        out_specs=(rows, rows, P(), *weights, *[P()] * 6),
        check_vma=False,
    )
```

```python
import functools
import math

import jax
import jax.numpy as jnp
from jax import lax
from jax.experimental import pallas as pl
from jax.experimental.pallas import tpu as pltpu
from jax.sharding import PartitionSpec as P

HD = 64
SLOT = 1024
STEP = 10
NORM_EPSILON = 1e-05
MASK_FILL = -1e30
DECAY_FIRST = 0.5
DECAY_SECOND = 0.5
ADAM_EPSILON = 1e-08
WEIGHT_DECAY = 0.1
CLIP_NORM = 1.0
RATE_MATRIX = 0.04
RATE_VECTOR = 0.3

MESH = pl.DeviceIdType.MESH
BF = jnp.bfloat16
F32 = jnp.float32
HALF = SLOT // 2
BLK = 256
VMEM_LIMIT = 58 * 2**20
LOG2E = math.log2(math.e)
SCORE_SCALE = float(HD) ** (-0.5)
SCORE_SCALE2 = SCORE_SCALE * LOG2E


def dot_nn(a, b):
    return lax.dot_general(a, b, (((1,), (0,)), ((), ())), preferred_element_type=F32)


def dot_nt(a, b):
    return lax.dot_general(a, b, (((1,), (1,)), ((), ())), preferred_element_type=F32)


def dot_tn(a, b):
    return lax.dot_general(a, b, (((0,), (0,)), ((), ())), preferred_element_type=F32)


def dot_tt(a, b):
    return lax.dot_general(a, b, (((0,), (1,)), ((), ())), preferred_element_type=F32)


def params(collective_id=None):
    if collective_id is None:
        return pltpu.CompilerParams(vmem_limit_bytes=VMEM_LIMIT)
    return pltpu.CompilerParams(
        vmem_limit_bytes=VMEM_LIMIT, collective_id=collective_id, has_side_effects=True
    )


VM = pl.BlockSpec(memory_space=pltpu.VMEM)
ANY = pl.BlockSpec(memory_space=pl.ANY)


def sds(shape, dtype):
    return jax.ShapeDtypeStruct(shape, dtype)


def here():
    t = lax.axis_index("tensor")
    return lax.axis_index("dp"), t // 2, t % 2


def greet(ids):
    sem = pltpu.get_barrier_semaphore()
    for one in ids:
        pl.semaphore_signal(sem, inc=1, device_id=one, device_id_type=MESH)
    pl.semaphore_wait(sem, len(ids))


def remote(src, dst, send_sem, recv_sem, target):
    return pltpu.make_async_remote_copy(
        src_ref=src,
        dst_ref=dst,
        send_sem=send_sem,
        recv_sem=recv_sem,
        device_id=target,
        device_id_type=MESH,
    )


def rows_at(start, size):
    return pl.ds(pl.multiple_of(start, size), size)


def norm_parts(values):
    centered = values - jnp.mean(values, axis=-1, keepdims=True)
    variance = jnp.mean(centered * centered, axis=-1, keepdims=True)
    scale = lax.rsqrt(variance + NORM_EPSILON)
    return centered * scale, scale


class Gather:
    def __init__(self, shard, whole, part, by_y, ss, rs):
        dp, x, c = here()
        z, y = dp // 2, dp % 2
        along, x_peer, y_peer, _ = neighbours()
        shard = shard.at[part]
        block = whole.at[x, z, y, part]
        column = whole.at[x, :, y, part]
        from_x = whole.at[1 - x, pl.ds(0, by_y), y, part]
        from_y = whole.at[x, pl.ds(by_y, 4 - by_y), 1 - y, part]
        self.along = [remote(shard, block, ss.at[k], rs.at[k], along[k]) for k in range(3)]
        self.beside = [
            remote(column, column, ss.at[3], rs.at[3], x_peer),
            remote(column, column, ss.at[4], rs.at[4], y_peer),
        ]
        self.passed = [
            remote(from_x, from_x, ss.at[5], rs.at[5], y_peer),
            remote(from_y, from_y, ss.at[6], rs.at[6], x_peer),
        ]

    def start_along(self):
        for one in self.along:
            one.start()

    def start_beside(self):
        for one in self.along:
            one.wait()
        for one in self.beside:
            one.start()

    def start_passed(self):
        for one in self.beside:
            one.wait()
        for one in self.passed:
            one.start()

    def finish(self):
        for one in self.passed:
            one.wait()


class GatherBeside:
    def __init__(self, shard, whole, start, size, by_y, ss, rs):
        dp, x, c = here()
        z, y = dp // 2, dp % 2
        along, x_peer, y_peer, _ = neighbours()
        part = pl.ds(start, size)
        block = whole.at[x, z, y, part]
        from_x = whole.at[1 - x, z, y, pl.ds(start, by_y)]
        from_y = whole.at[x, z, 1 - y, pl.ds(start + by_y, size - by_y)]
        four = whole.at[:, z, :, part]
        self.beside = [
            remote(shard.at[part], block, ss.at[3], rs.at[3], x_peer),
            remote(shard.at[part], block, ss.at[4], rs.at[4], y_peer),
        ]
        self.passed = [
            remote(from_x, from_x, ss.at[5], rs.at[5], y_peer),
            remote(from_y, from_y, ss.at[6], rs.at[6], x_peer),
        ]
        self.along = [remote(four, four, ss.at[k], rs.at[k], along[k]) for k in range(3)]

    def start_beside(self):
        for one in self.beside:
            one.start()

    def start_passed(self):
        for one in self.beside:
            one.wait()
        for one in self.passed:
            one.start()

    def start_along(self):
        for one in self.passed:
            one.wait()
        for one in self.along:
            one.start()

    def finish(self):
        for one in self.along:
            one.wait()


def neighbours():
    dp, x, c = here()
    z, y = dp // 2, dp % 2
    me = x * 2 + c
    along = [(lax.rem(z + k, 4) * 2 + y, me) for k in (1, 2, 3)]
    return along, (dp, (1 - x) * 2 + c), (z * 2 + 1 - y, me), (dp, x * 2 + 1 - c)


def whole_weight(ref, slot):
    value = ref[slot]
    return value.reshape(-1, value.shape[-1])


def allowed_pairs(key_block, query_block, start_row, wide):
    keys = lax.broadcasted_iota(jnp.int32, (BLK, wide), 0) + key_block * BLK
    mask = keys >= start_row
    if key_block == query_block:
        queries = lax.broadcasted_iota(jnp.int32, (BLK, wide), 1) + query_block * BLK
        mask = mask & (keys <= queries)
    return mask


def attend_unit(q, k, v, start):
    blocks = SLOT // BLK
    for i in range(blocks):
        cols = slice(i * BLK, (i + 1) * BLK)
        query = q(cols)
        scores = []
        for j in range(i + 1):
            raw = dot_tn(k(slice(j * BLK, (j + 1) * BLK)), query) * SCORE_SCALE2
            scores.append(jnp.where(allowed_pairs(j, i, start(cols), BLK), raw, MASK_FILL))
        top = functools.reduce(jnp.maximum, [jnp.max(s, axis=0, keepdims=True) for s in scores])
        exps = [jnp.exp2(s - top) for s in scores]
        total = functools.reduce(jnp.add, [jnp.sum(e, axis=0, keepdims=True) for e in exps])
        acc = None
        for j in range(i + 1):
            term = dot_nn(v(slice(j * BLK, (j + 1) * BLK)), exps[j].astype(BF))
            acc = term if acc is None else acc + term
        yield cols, acc / total, top + jnp.log2(total)


GELU_C = math.sqrt(2.0 / math.pi)
GELU_A = 0.044715


def forward_kernel(custom, *refs):
    (tok_ref, cot_ref, valid_ref, seg_ref, vec_ref, fb_ref), refs = refs[:6], refs[6:]
    shards, refs = refs[:4], refs[4:]
    (gl_out, n1_out, u_out, ctx_out, lse_out, start_out, ctxc_out, resid_out, wo_out, br_out, dn_out, gp_out,
     gf_out, gb_ref), refs = refs[:14], refs[14:]
    if custom:
        weights_out, given, refs = refs[:2], refs[2:6], refs[6:]
        lows, refs = refs[:4], refs[4:]
        wholes, refs = refs[:4], refs[4:]
        gs, gr, ps, pr, refs = *refs[:4], refs[4:]
    else:
        wholes = shards
    (tk, gl, n1, u, ctx, lse, starts, ctxc, resid, wo, n2, half, part, got, act, dpre, gp, cols, loc, ts, tr, xs,
     cs_s, cs_r) = refs
    wqk, wvo, wf, wp = wholes
    dp, x, c = here()
    core = (dp, x * 2 + 1 - c)
    x_peer = (dp, (1 - x) * 2 + c)
    across = [(dp, (1 - x) * 2), (dp, (1 - x) * 2 + 1)]
    rows = tok_ref.shape[0]
    first = x * HALF
    gathers = []
    if custom:
        z, y = dp // 2, dp % 2
        along, _, y_peer, _ = neighbours()
        greet([core, *across, *along, y_peer])
        lows[0][...] = jnp.concatenate([shards[0][0], shards[0][1]], axis=1).astype(BF)
        lows[1][...] = jnp.concatenate([shards[0][2], shards[1][...].T], axis=1).astype(BF)
        lows[2][...] = shards[2][...].astype(BF)
        lows[3][...] = shards[3][...].astype(BF)
        pieces = [(0, 0, 2, 2), (0, 1, 2, 2), (1, 0, 2, 2), (1, 1, 2, 2)]
        pieces += [(2, 0, 2, 3), (2, 1, 2, 3), (3, 0, 2, 3)]
        for number, (a, k, parts, by_y) in enumerate(pieces):
            size = lows[a].shape[0] // parts
            gathers.append(
                Gather(
                    lows[a], wholes[a], pl.ds(k * size, size), by_y, gs.at[number], gr.at[number]
                )
            )
        size = lows[3].shape[0] // 2
        gathers.append(GatherBeside(lows[3], wholes[3], size, size, 32, gs.at[7], gr.at[7]))
    else:
        greet([core, *across])

    def step(number, what):
        if custom:
            getattr(gathers[number], what)()

    own_rows = pl.ds(pl.multiple_of(first + c * rows, BLK), rows)
    gl_rows = pl.ds(pl.multiple_of(c * rows, BLK), rows)
    mine_tok = pltpu.make_async_copy(tok_ref, tk.at[own_rows], loc.at[0])
    swap_tok = remote(tok_ref, tk.at[own_rows], ts.at[0], tr.at[0], core)
    swap_grad = remote(gl.at[gl_rows], gl.at[gl_rows], ts.at[1], tr.at[1], core)
    source = [
        tok_ref.at[pl.ds(pl.multiple_of((1 - x) * BLK + k * BLK, BLK), BLK)] for k in range(2)
    ]
    there = [
        tk.at[pl.ds(pl.multiple_of(x * (SLOT + HALF) + k * BLK, BLK), BLK)] for k in range(2)
    ]
    halves = [remote(source[k], there[k], ts.at[2 + k], tr.at[2], across[k]) for k in range(2)]
    landed = tk.at[pl.ds(pl.multiple_of((1 - x) * (SLOT + HALF) + c * BLK, BLK), BLK)]
    handed = remote(landed, landed, ts.at[4], tr.at[3], core)

    if custom:
        for a in range(4):
            wholes[a][x, z, y] = lows[a][...]
    step(0, "start_along")
    step(7, "start_beside")
    mine_tok.start()
    swap_tok.start()

    @pl.when(c == 1 - x)
    def _():
        for one in halves:
            one.start()

    step(1, "start_along")

    def out_copy(number, ref, out):
        copy = pltpu.make_async_copy(ref, out, loc.at[number])
        copy.start()
        return copy

    cols[...] = vec_ref[...].T
    gain, shift = vec_ref[0:1, :], vec_ref[1:2, :]

    def norm_rows(start, count):
        def norm(i, carry):
            at = rows_at(start + i * BLK, BLK)
            unit, _ = norm_parts(tk[at, :].astype(F32))
            n1[at, :] = (unit * gain + shift).astype(BF)
            return carry

        lax.fori_loop(0, count // BLK, norm, 0)

    mine_tok.wait()
    norm_rows(first + c * rows, rows)
    swap_tok.wait()
    step(7, "start_passed")
    step(0, "start_beside")
    step(2, "start_along")
    norm_rows(first + (1 - c) * rows, rows)
    step(1, "start_beside")
    step(3, "start_along")

    mask = jnp.broadcast_to(valid_ref[...].reshape(1, rows).astype(F32), (8, rows)).T[:, 0:1]
    gl[gl_rows, :] = (cot_ref[...].astype(F32) * mask).astype(BF)
    swap_grad.start()
    for k, row in enumerate((2 * x, 1)):
        segments = seg_ref[pl.ds(pl.multiple_of(row * SLOT, SLOT), SLOT)].reshape(1, SLOT).astype(F32)
        column = jnp.broadcast_to(segments, (8, SLOT)).T[:, 0:1]
        for i in range(SLOT // BLK):
            lanes = slice(i * BLK, (i + 1) * BLK)
            below = jnp.where(column < segments[:, lanes], 1.0, 0.0)
            starts[k, :, lanes] = jnp.sum(below, axis=0, keepdims=True).astype(jnp.int32)

    step(2, "start_beside")
    step(4, "start_along")
    step(3, "start_beside")
    step(5, "start_along")
    for number in range(4):
        step(number, "start_passed")

    heads = u.shape[2]
    wide = heads * HD

    def project(group, slot, first_row):
        bias_rows = pl.ds(pl.multiple_of((c + 2 * slot) * wide, HD), wide)
        query_bias, value_bias = cols[bias_rows, 4:5], cols[bias_rows, 5:6]

        def chunk(i, carry):
            lanes = rows_at(i * BLK, BLK)
            values = n1[rows_at(first_row + i * BLK, BLK), :]
            two = dot_tt(whole_weight(wqk, slot), values)
            value = dot_tt(whole_weight(wvo, slot)[:, :wide], values) + value_bias
            for k, out in enumerate((two[:wide] + query_bias, two[wide:], value)):
                u[group, k, :, :, lanes] = out.reshape(-1, HD, BLK).astype(BF)
            return carry

        lax.fori_loop(0, SLOT // BLK, chunk, 0)

    def attend(group, which, begin, end):
        def unit(h, carry):
            for lanes, context, log_total in attend_unit(
                lambda s: u[group, 0, h, :, s],
                lambda s: u[group, 1, h, :, s],
                lambda s: u[group, 2, h, :, s],
                lambda s: starts[which, :, s],
            ):
                ctx[group, h, :, lanes] = context.astype(BF)
                lse[group, h, :, lanes] = log_total
            return carry

        lax.fori_loop(begin, end, unit, 0)

    step(4, "start_beside")
    step(6, "start_along")
    project(x, x, x * SLOT)
    attend(x, 0, 0, 1)
    step(5, "start_beside")
    step(7, "start_along")
    attend(x, 0, 1, heads)
    halves[0].wait_recv()
    handed.start()
    handed.wait()
    norm_rows((1 - x) * (SLOT + HALF), HALF)
    project(2, x, (1 - x) * SLOT)
    step(4, "start_passed")
    attend(2, 1, 0, heads)
    theirs = pl.ds(pl.multiple_of((1 - x) * HALF, HALF), HALF)
    cross = remote(ctx.at[2, :, :, theirs], half, xs.at[0], xs.at[1], x_peer)
    cross.start()
    step(6, "start_beside")
    for number in range(4):
        step(number, "finish")
    project(1 - x, 1 - x, x * SLOT)
    copies = [out_copy(1, n1, n1_out), out_copy(2, u, u_out)]
    step(5, "start_passed")
    for s in range(2):
        wo[s] = whole_weight(wvo, s)[:, wide:]
    attend(1 - x, 0, 0, heads)
    step(6, "start_passed")
    copies += [out_copy(3, ctx, ctx_out), out_copy(4, lse, lse_out), out_copy(5, starts, start_out)]
    copies.append(out_copy(8, wo, wo_out))
    if custom:
        copies += [out_copy(6 + a, wholes[a], weights_out[a]) for a in range(2)]

    @pl.when(c == 1 - x)
    def _():
        for one in halves:
            one.wait_send()

    chunks = []

    def send(chunk, values):
        at = rows_at(chunk * BLK, BLK)
        part[at, :] = values.astype(BF)
        copy = remote(part.at[at], got.at[at], cs_s.at[chunk], cs_r.at[chunk], core)
        copy.start()
        chunks.append((chunk, copy))

    def context_of(group, lanes):
        value = ctx[group, :, :, lanes]
        return value.reshape(-1, value.shape[-1])

    for i in range(SLOT // BLK):
        lanes = slice(i * BLK, (i + 1) * BLK)
        chunk = x * 2 + i
        at = rows_at(chunk * BLK, BLK)
        zero, one = context_of(0, lanes), context_of(1, lanes)
        send(chunk, dot_tt(zero, wo[0]) + dot_tt(one, wo[1]))
        ctxc[0, :, at] = zero
        ctxc[1, :, at] = one
    cross.wait()
    for i in range(HALF // BLK):
        chunk = (1 - x) * 4 + i
        at = rows_at(chunk * BLK, BLK)
        own = context_of(2, rows_at(x * HALF + i * BLK, BLK))
        other = half[:, :, i * BLK : (i + 1) * BLK].reshape(-1, BLK)
        send(chunk, dot_tt(own, wo[x]) + dot_tt(other, wo[1 - x]))
        ctxc[x, :, at] = own
        ctxc[1 - x, :, at] = other
    copies.append(out_copy(10, ctxc, ctxc_out))
    swap_grad.wait()
    copies.append(out_copy(11, gl, gl_out))
    for chunk, copy in chunks:
        copy.wait()
        at = rows_at(chunk * BLK, BLK)
        tokens = tk[rows_at(first + chunk * BLK, BLK), :].astype(F32)
        summed = part[at, :].astype(F32) + got[at, :].astype(F32)
        after = tokens + summed + vec_ref[6:7, :]
        resid[at, :] = after
        unit, _ = norm_parts(after)
        n2[at, :] = (unit * vec_ref[2:3, :] + vec_ref[3:4, :]).astype(BF)
    copies.append(out_copy(12, resid, resid_out))
    step(4, "finish")
    step(5, "finish")

    hidden = wf.shape[-1]
    gb_ref[...] = jnp.zeros_like(gb_ref)
    bias_of = [
        fb_ref[:, pl.ds(pl.multiple_of((c + 2 * s) * hidden, hidden), hidden)] for s in range(2)
    ]
    tile = HALF
    tiles = 2 * rows // tile

    def activate(i, carry):
        at = rows_at(i * tile, tile)
        n2_rows = n2[at, :]
        for s in range(2):
            lanes = slice(s * hidden, (s + 1) * hidden)
            v = dot_nn(n2_rows, whole_weight(wf, s)) + bias_of[s]
            square = v * v
            t = jnp.tanh(v * (GELU_C + (GELU_C * GELU_A) * square))
            cdf = 0.5 + 0.5 * t
            act[at, lanes] = (v * cdf).astype(BF)
            slope = cdf + (cdf * (1.0 - t)) * (v * (GELU_C + (3.0 * GELU_C * GELU_A) * square))
            dpre[at, lanes] = slope.astype(BF)
        return carry

    lax.fori_loop(0, tiles, activate, 0)
    blocks = gp.shape[1:4]

    for s in range(2):
        out = dot_tn(gl[...], act[:, s * hidden : (s + 1) * hidden]).astype(BF)
        gp[s] = out.reshape(*blocks, hidden)
        copies.append(out_copy(15 + s, gp.at[s], gp_out.at[s]))
    passing = []
    if custom:
        low, high = pl.ds(0, 2), pl.ds(2, 2)
        pieces = [
            (gp.at[1 - x, low, 1 - y], y_peer),
            (gp.at[1 - x, high, 1 - y], x_peer),
            (gp.at[1 - x, high, y], x_peer),
            (gp.at[x, low, 1 - y], y_peer),
        ]
        for k, (piece, peer) in enumerate(pieces):
            passing.append(remote(piece, given[k], ps.at[k], pr.at[k], peer))
            passing[-1].start()
    step(6, "finish")
    step(7, "finish")

    def forward_back(i, carry):
        at = rows_at(i * tile, tile)
        gl_now = gl[at, :]
        for s in range(2):
            lanes = slice(s * hidden, (s + 1) * hidden)
            up = dot_nn(gl_now, whole_weight(wp, s))
            d = (up * dpre[at, lanes].astype(F32)).astype(BF)
            dpre[at, lanes] = d
            gb_ref[s] += jnp.sum(d.astype(F32), axis=0, keepdims=True)
        br = dot_nt(act[at, :hidden], whole_weight(wp, 0))
        br += dot_nt(act[at, hidden:], whole_weight(wp, 1))
        part[at, :] = br.astype(BF)
        dn = dot_nt(dpre[at, :hidden], whole_weight(wf, 0))
        dn += dot_nt(dpre[at, hidden:], whole_weight(wf, 1))
        got[at, :] = dn.astype(BF)
        return carry

    lax.fori_loop(0, tiles, forward_back, 0)
    copies += [out_copy(13, got, dn_out), out_copy(14, part, br_out)]
    width = n2.shape[1]

    for s in range(2):
        at = slice(s * width, (s + 1) * width)
        tk[at, :] = dot_tn(n2[...], dpre[:, s * hidden : (s + 1) * hidden]).astype(BF)
        copies.append(out_copy(17 + s, tk.at[at], gf_out.at[s]))
    for copy in copies + passing:
        copy.wait()


def forward(tokens, cotangent, valid, segments, vectors, fc_bias, shards):
    rows, width = tokens.shape
    chip = 2 * rows
    custom = lax.axis_size("dp") == 8
    dma = pltpu.SemaphoreType.DMA
    if custom:
        cols = shards[0].shape[2]
        hidden = shards[2].shape[1]
        part_rows = shards[2].shape[0]
        flat = [(part_rows, n) for n in (2 * cols, 2 * cols, hidden, hidden)]
        wholes = [(2, 4, 2) + s for s in flat]
        more_out = [sds(w, BF) for w in wholes[:2]] + [sds((2, part_rows, hidden), BF)] * 4
        more = [pltpu.VMEM(s, BF) for s in flat] + [pltpu.VMEM(w, BF) for w in wholes]
        more += [dma((8, 7)), dma((8, 7)), dma((4,)), dma((4,))]
        grad_shape = wholes[3]
    else:
        cols, hidden = shards[0].shape[2] // 2, shards[2].shape[2]
        more_out, more = [], []
        grad_shape = (2, 1, 1, width, hidden)
    heads = cols // HD
    shapes = [
        ((chip, width), BF),
        ((2 * SLOT, width), BF),
        ((3, 3, heads, HD, SLOT), BF),
        ((3, heads, HD, SLOT), BF),
        ((3, heads, 1, SLOT), F32),
        ((2, 1, SLOT), jnp.int32),
        ((2, cols, chip), BF),
        ((chip, width), F32),
        ((2, width, cols), BF),
    ]
    out_shape = [sds(*s) for s in shapes]
    out_shape += [sds((chip, width), BF)] * 2 + [sds(grad_shape, BF), sds((2, width, hidden), BF)]
    out_shape += [sds((2, 1, hidden), F32)] + more_out
    outs = pl.pallas_call(
        functools.partial(forward_kernel, custom),
        out_shape=tuple(out_shape),
        in_specs=[ANY] + [VM] * (5 + len(shards)),
        out_specs=(*[ANY] * 13, VM, *[ANY] * len(more_out)),
        scratch_shapes=more
        + [
            pltpu.VMEM((2 * SLOT, width), BF),
            *[pltpu.VMEM(*s) for s in shapes],
            pltpu.VMEM((chip, width), BF),
            pltpu.VMEM((heads, HD, HALF), BF),
            pltpu.VMEM((chip, width), BF),
            pltpu.VMEM((chip, width), BF),
            pltpu.VMEM((chip, 2 * hidden), BF),
            pltpu.VMEM((chip, 2 * hidden), BF),
            pltpu.VMEM(grad_shape, BF),
            pltpu.VMEM((width, 8), F32),
            dma((19,)),
            dma((5,)),
            dma((4,)),
            dma((2,)),
            dma((chip // BLK,)),
            dma((chip // BLK,)),
        ],
        compiler_params=params(1),
        name="forward",
    )(tokens, cotangent, valid, segments, vectors, fc_bias, *shards)
    if custom:
        return outs[:14], outs[14:16], outs[16:]
    return outs[:14], shards[:2], []


class Reduce:
    def __init__(self, grad, by_y, local, given, total, bufs, loc, ss, rs):
        dp, x, c = here()
        z, y = dp // 2, dp % 2
        along, x_peer, y_peer, _ = neighbours()
        low, high = pl.ds(0, by_y), pl.ds(by_y, 4 - by_y)
        self.z, self.total = z, total
        self.r1y, self.r1x, self.r2x, self.r2y, self.r3 = bufs
        views = [grad.at[1 - x, low, y], grad.at[x, high, 1 - y], grad.at[x, :, y]]
        self.loads = []
        self.mid_x, self.mid_y, self.own = views
        if local is not None:
            self.loads = [
                pltpu.make_async_copy(views[k], local[k], loc.at[k]) for k in range(3)
            ]
            self.mid_x, self.mid_y, self.own = local
        if given is None:
            self.first = [
                remote(grad.at[1 - x, low, 1 - y], self.r1y, ss.at[0], rs.at[0], y_peer),
                remote(grad.at[1 - x, high, 1 - y], self.r1x, ss.at[1], rs.at[1], x_peer),
            ]
            self.early = [
                remote(grad.at[1 - x, high, y], self.r2x.at[high], ss.at[2], rs.at[2], x_peer),
                remote(grad.at[x, low, 1 - y], self.r2y.at[low], ss.at[3], rs.at[3], y_peer),
            ]
        else:
            targets = (self.r1y, self.r1x, self.r2x.at[high], self.r2y.at[low])
            copies = [
                pltpu.make_async_copy(given[k], targets[k], rs.at[k]) for k in range(4)
            ]
            self.first, self.early = copies[:2], copies[2:]
        self.second = [
            remote(self.mid_x, self.r2x.at[low], ss.at[4], rs.at[4], x_peer),
            remote(self.mid_y, self.r2y.at[high], ss.at[5], rs.at[5], y_peer),
        ]
        self.third = [
            remote(
                self.own.at[lax.rem(z + k + 1, 4)], self.r3.at[k], ss.at[6 + k], rs.at[6 + k], along[k]
            )
            for k in range(3)
        ]

    def start_first(self):
        for one in self.loads:
            one.start()
        for one in self.first:
            one.start()

    def start_early(self, which):
        self.early[which].start()

    def start_second(self, which):
        self.first[which].wait()
        if self.loads:
            self.loads[which].wait()
        mid, came = ((self.mid_x, self.r1y), (self.mid_y, self.r1x))[which]
        mid[...] = (mid[...].astype(F32) + came[...].astype(F32)).astype(BF)
        self.second[which].start()

    def start_third(self):
        for one in self.early + self.second + self.loads[2:]:
            one.wait()
        for k in range(4):
            place = lax.rem(self.z + k + 1, 4)
            summed = (
                self.own[place].astype(F32)
                + self.r2x[place].astype(F32)
                + self.r2y[place].astype(F32)
            )
            if k < 3:
                self.own[place] = summed.astype(BF)
                self.third[k].start()
            else:
                self.total[...] = summed

    def finish(self):
        for one in self.third:
            one.wait()
        total = self.total[...]
        for k in range(3):
            total = total + self.r3[k].astype(F32)
        self.total[...] = total
        return jnp.sum(total * total)


def eight_peers():
    dp, x, c = here()
    z, y = dp // 2, dp % 2
    peers = []
    for k in range(1, 8):
        kx, ky, kc = k // 4, k // 2 % 2, k % 2
        there = ((1 - x if kx else x), (1 - y if ky else y), (1 - c if kc else c))
        peers.append((z * 2 + there[1], there[0] * 2 + there[2]))
    return peers


class SumOverAll:
    def __init__(self, value, near, far, ss, rs):
        dp, x, c = here()
        z, y = dp // 2, dp % 2
        self.value, self.near, self.far = value, near, far
        self.me, self.z = x * 4 + y * 2 + c, z
        self.one = [
            remote(value, near.at[self.me], ss.at[k], rs.at[k], peer)
            for k, peer in enumerate(eight_peers())
        ]
        self.two = [
            remote(value, far.at[z], ss.at[7 + k], rs.at[7 + k], peer)
            for k, peer in enumerate(neighbours()[0])
        ]

    def start(self):
        for one in self.one:
            one.start()
        self.near[self.me] = self.value[...]

    def middle(self):
        for one in self.one:
            one.wait()
        self.value[...] = functools.reduce(jnp.add, [self.near[k] for k in range(8)])
        for one in self.two:
            one.start()
        self.far[self.z] = self.value[...]

    def finish(self):
        for one in self.two:
            one.wait()
        return functools.reduce(jnp.add, [self.far[k] for k in range(4)])


def attend_back_unit(u, out, start, ctx, dctx, lse, dq_ref):
    blocks = SLOT // BLK
    delta = jnp.sum(dctx.astype(F32) * ctx.astype(F32), axis=0, keepdims=True)
    for j in range(blocks):
        keys = slice(j * BLK, (j + 1) * BLK)
        k = u(1, keys)
        v = u(2, keys)
        probs, dscores = [], []
        for i in range(j, blocks):
            cols = slice(i * BLK, (i + 1) * BLK)
            raw = dot_tn(k, u(0, cols)) * SCORE_SCALE2 - lse[:, cols]
            prob = jnp.exp2(jnp.where(allowed_pairs(j, i, start[:, cols], BLK), raw, MASK_FILL))
            dprob = dot_tn(v, dctx[:, cols])
            probs.append(prob.astype(BF))
            dscores.append((prob * (dprob - delta[:, cols])).astype(BF))
        dk, dv = None, None
        for n, i in enumerate(range(j, blocks)):
            cols = slice(i * BLK, (i + 1) * BLK)
            dv_term = dot_nt(dctx[:, cols], probs[n])
            dk_term = dot_nt(u(0, cols), dscores[n])
            dv = dv_term if dv is None else dv + dv_term
            dk = dk_term if dk is None else dk + dk_term
            dq_term = dot_nn(k, dscores[n])
            if j == 0:
                dq_ref[:, cols] = dq_term
            else:
                dq_ref[:, cols] += dq_term
        out(1, keys, (dk * SCORE_SCALE).astype(BF))
        out(2, keys, dv.astype(BF))
    out(0, slice(0, SLOT), (dq_ref[...] * SCORE_SCALE).astype(BF))


BY_Y = (2, 3, 3, 3)


def norm_back(dn, values, gain):
    unit, scale = norm_parts(values)
    e = dn * gain
    back = scale * (
        e
        - jnp.mean(e, axis=-1, keepdims=True)
        - unit * jnp.mean(e * unit, axis=-1, keepdims=True)
    )
    return back, unit


def backward_kernel(custom, *refs):
    (gl_in, n1_in, u_in, ctx_in, lse_ref, start_ref, ctxc_in, resid_in, wo_in, br_in, dn_in, gp_in, gf_in, gb_ref,
     wqk_in, wvo_in, tok_in, vec_ref), refs = refs[:18], refs[18:]
    given = None
    if custom:
        given, refs = refs[:4], refs[4:]
    (mixed_out, ig_out), refs = refs[:2], refs[2:]
    if custom:
        totals, refs = refs[:4], refs[4:]
        (va_out, vb_out, norm_ref), refs = refs[:3], refs[3:]
        gvo, gqk, refs = refs[0], refs[1], refs[2:]
        locals_, refs = (refs[:3], refs[3:6]), refs[6:]
        bufs, refs = [refs[5 * a : 5 * a + 5] for a in range(4)], refs[20:]
        (va, vb, near_a, far_a, near_b, far_b, near_s, far_s, square, lss, ss, rs, ass, ars, bss, brs, qss,
         qrs), refs = refs[:18], refs[18:]
    else:
        va, vb, gvo, gqk, refs = *refs[:4], refs[4:]
    (gl_s, resid_s, dn_s, got_dn, br_s, got_br, mixed, low, dres, dctx, ctxc, wo, half_c, outgoing, u, ctx, n1,
     wqk, wvo, tok, du, dq, away, away_got, half, got, loc, ld, cs_s, cs_r, bs, xs, ws) = refs
    part = low
    dp, x, c = here()
    core = (dp, x * 2 + 1 - c)
    x_peer = (dp, (1 - x) * 2 + c)
    reduces = []
    if custom:
        greet(eight_peers() + neighbours()[0])
        for a, grad in enumerate((gp_in, gf_in, gvo, gqk)):
            local = locals_[a] if a < 2 else None
            loads = lss.at[a] if a < 2 else None
            came = given if a == 0 else None
            reduces.append(
                Reduce(
                    grad, BY_Y[a], local, came, totals[a], bufs[a], loads, ss.at[a], rs.at[a]
                )
            )
    else:
        greet([core, x_peer, (dp, (1 - x) * 2 + 1 - c)])

    def step(number, what, *which):
        if custom:
            getattr(reduces[number], what)(*which)

    rows_all, width = low.shape
    own_rows = rows_all // 2
    n_chunks = rows_all // BLK
    order = [(1 - x) * 4 + i for i in range(HALF // BLK)] + [x * 2 + i for i in range(SLOT // BLK)]
    swaps = []
    for chunk in order:
        at = rows_at(chunk * BLK, BLK)
        swaps.append(remote(dn_in.at[at], got_dn.at[at], cs_s.at[chunk], cs_r.at[chunk], core))
    their = pl.ds(pl.multiple_of((1 - c) * own_rows, BLK), own_rows)
    mine = pl.ds(pl.multiple_of(c * own_rows, BLK), own_rows)
    branch = remote(br_in.at[their], got_br, bs.at[0], bs.at[1], core)

    def chunk_loads(n):
        at, slot = rows_at(order[n] * BLK, BLK), n % 2
        return [
            pltpu.make_async_copy(source.at[at], target.at[slot], ld.at[slot, k])
            for k, (source, target) in enumerate(
                ((resid_in, resid_s), (gl_in, gl_s), (dn_in, dn_s))
            )
        ]

    def load(number, source, target):
        copy = pltpu.make_async_copy(source, target, loc.at[number])
        copy.start()
        return copy

    loads = [chunk_loads(n) for n in range(n_chunks)]
    swaps[0].start()
    for n in range(2):
        for one in loads[n]:
            one.start()
    branch.start()
    for one in swaps[1:]:
        one.start()
    step(0, "start_first")
    step(0, "start_early", 0)
    step(0, "start_early", 1)
    step(1, "start_first")
    br_load = load(0, br_in.at[mine], br_s)
    wo_load = load(1, wo_in, wo)
    ctxc_load = load(2, ctxc_in, ctxc)
    step(1, "start_early", 0)
    step(1, "start_early", 1)
    late = [
        load(3, u_in, u),
        load(4, ctx_in, ctx),
        load(5, n1_in, n1),
        load(6, wqk_in, wqk),
        load(7, wvo_in, wvo),
        load(8, tok_in, tok),
    ]

    @pl.when(c == x)
    def _():
        half[...] = jnp.zeros_like(half)

    va[...] = jnp.zeros_like(va)
    vb[...] = jnp.zeros_like(vb)
    for s in range(2):
        va[pl.ds(4 + c + 2 * s, 1), :] = gb_ref[s]
    branch.wait()
    br_load.wait()
    for n, chunk in enumerate(order):
        slot = n % 2
        for one in loads[n]:
            one.wait()
        swaps[n].wait()
        at = rows_at(chunk * BLK, BLK)
        dn = dn_s[slot].astype(F32) + got_dn[at, :].astype(F32)
        resid = resid_s[slot]
        back, unit = norm_back(dn, resid, vec_ref[2:3, :])
        grad = gl_s[slot].astype(F32)
        after = grad + back
        low[at, :] = after.astype(BF)

        @pl.when(chunk // (n_chunks // 2) == c)
        def _(chunk=chunk, dn=dn, resid=resid, unit=unit, grad=grad, after=after):
            here_at = rows_at((chunk - c * (n_chunks // 2)) * BLK, BLK)
            dres[here_at, :] = after
            branches = br_s[here_at, :].astype(F32) + got_br[here_at, :].astype(F32)
            mixed[here_at, :] = (resid + branches + vec_ref[7:8, :]).astype(BF)
            va[0:1, :] += jnp.sum(dn * unit, axis=0, keepdims=True)
            va[1:2, :] += jnp.sum(dn, axis=0, keepdims=True)
            va[2:3, :] += jnp.sum(after, axis=0, keepdims=True)
            va[3:4, :] += jnp.sum(grad, axis=0, keepdims=True)

        if n + 2 < n_chunks:
            for one in loads[n + 2]:
                one.start()
        if n == 1:
            wo_load.wait()
            for i in range(HALF // BLK):
                lanes = slice(i * BLK, (i + 1) * BLK)
                rows = low[rows_at((1 - x) * SLOT + i * BLK, BLK), :]
                outgoing[:, :, lanes] = (
                    dot_tt(wo[1 - x], rows).astype(BF).reshape(-1, HD, BLK)
                )
                dctx[2, :, :, rows_at(x * HALF + i * BLK, BLK)] = (
                    dot_tt(wo[x], rows).astype(BF).reshape(-1, HD, BLK)
                )
            cross_c = remote(outgoing, half_c, xs.at[0], xs.at[1], x_peer)
            cross_c.start()
            step(0, "start_second", 0)
            step(0, "start_second", 1)
    mixed_copy = pltpu.make_async_copy(mixed, mixed_out, ws.at[0])
    mixed_copy.start()
    if custom:
        early_sum = SumOverAll(va, near_a, far_a, ass, ars)
        early_sum.start()
    heads = u.shape[2]
    cols = heads * HD
    blocks = gvo.shape[1:4]
    ctxc_load.wait()
    for s in range(2):
        gvo[s, :, :, :, cols:] = dot_tt(low[...], ctxc[s]).astype(BF).reshape(*blocks, cols)
    for i in range(SLOT // BLK):
        lanes = slice(i * BLK, (i + 1) * BLK)
        rows = low[rows_at(x * HALF + i * BLK, BLK), :]
        for s in range(2):
            dctx[s, :, :, lanes] = dot_tt(wo[s], rows).astype(BF).reshape(-1, HD, BLK)
    step(1, "start_second", 0)
    step(1, "start_second", 1)
    late[0].wait()
    late[1].wait()

    def attend_back(group, which, begin, end):
        def unit(h, carry):
            def put(k, lanes, value):
                du[group, k, h, :, lanes] = value

            attend_back_unit(
                lambda k, lanes: u[group, k, h, :, lanes],
                put,
                start_ref[which],
                ctx[group, h],
                dctx[group, h],
                lse_ref[group, h],
                dq,
            )
            return carry

        lax.fori_loop(begin, end, unit, 0)

    full_rows = pl.ds(pl.multiple_of(x * SLOT, SLOT), SLOT)
    part_rows = pl.ds(pl.multiple_of((1 - x) * SLOT, SLOT), SLOT)
    everything = slice(0, SLOT)

    def of_group(group, k, lanes):
        value = du[group, k, :, :, lanes]
        return value.reshape(cols, value.shape[-1])

    def weight_grad(slot, which, with_part):
        def rows_of(group):
            if which == 1:
                return of_group(group, 2, everything)
            return du[group, 0:2].reshape(2 * cols, SLOT)

        out = dot_tt(n1[full_rows, :], rows_of(slot))
        if with_part:
            out += dot_tt(n1[part_rows, :], rows_of(2))
        if which == 1:
            gvo[slot, :, :, :, :cols] = out.astype(BF).reshape(*blocks, cols)
        else:
            gqk[slot] = out.astype(BF).reshape(*blocks, 2 * cols)

    attend_back(1 - x, 0, 0, heads)
    for one in late[2:]:
        one.wait()
    for number, which in ((2, 1), (3, 0)):
        weight_grad(1 - x, which, False)
        step(number, "start_first")
        step(number, "start_early", 0)
    if custom:
        early_sum.middle()
    step(0, "start_third")
    cross_c.wait()
    dctx[2, :, :, pl.ds(pl.multiple_of((1 - x) * HALF, HALF), HALF)] = half_c[...]
    attend_back(2, 1, 0, heads)

    def back_through(group, lanes, slot):
        two = du[group, 0:2, :, :, lanes]
        two = two.reshape(2 * cols, two.shape[-1])
        out = dot_tt(two, whole_weight(wqk, slot))
        return out + dot_tt(of_group(group, 2, lanes), whole_weight(wvo, slot)[:, :cols])

    theirs = pl.ds(pl.multiple_of((1 - x) * HALF, HALF), HALF)
    away[...] = back_through(2, theirs, x).astype(BF).reshape(away.shape)
    swap_away = remote(away.at[1 - c], away_got, bs.at[4], bs.at[5], core)
    swap_away.start()
    step(2, "start_second", 0)
    step(3, "start_second", 0)
    swap_away.wait()
    away[c] = (away[c].astype(F32) + away_got[...].astype(F32)).astype(BF)
    cross = remote(away.at[c], half.at[c], xs.at[2], xs.at[3 + c], (dp, (1 - x) * 2 + x))
    cross.start()
    other = remote(away.at[1 - c], half.at[1 - c], xs.at[2], xs.at[4 - c], (dp, (1 - x) * 2 + x))
    step(1, "start_third")
    attend_back(x, 0, 0, heads)
    for number, which in ((2, 1), (3, 0)):
        weight_grad(x, which, True)
        step(number, "start_early", 1)
        step(number, "start_second", 1)

    def bias_sums(group):
        sums = [
            jnp.sum(of_group(group, k, everything).astype(F32), axis=1, keepdims=True)
            for k in (0, 2)
        ]
        return jnp.concatenate(sums, axis=0)

    columns = [bias_sums(x) + bias_sums(2), bias_sums(1 - x)]
    as_rows = jnp.concatenate(columns + [jnp.zeros((2 * cols, 6), F32)], axis=1).T
    for n, slot in enumerate((x, 1 - x)):
        vb[pl.ds(2 + c + 2 * slot, 1), : 2 * cols] = as_rows[n : n + 1, :]

    def back_rows(start, count):
        return pl.ds(pl.multiple_of(start, HALF), count)

    for i in range(SLOT // HALF):
        lanes = slice(i * HALF, (i + 1) * HALF)
        back = back_through(0, lanes, 0) + back_through(1, lanes, 1)
        part[back_rows(x * HALF + i * HALF, HALF), :] = back.astype(BF)
    back = back_through(2, back_rows(x * HALF, HALF), x)
    part[back_rows((1 - x) * SLOT, HALF), :] = back.astype(BF)
    swap = remote(part.at[their], got, bs.at[2], bs.at[3], core)
    swap.start()
    step(2, "start_third")
    swap.wait()
    cross.wait_send()

    @pl.when(c == 1 - x)
    def _():
        cross.wait_recv()
        other.wait_recv()

    for r in range(own_rows // BLK):
        rows = slice(r * BLK, (r + 1) * BLK)
        wide = rows_at(c * own_rows + r * BLK, BLK)
        dn = part[wide, :].astype(F32) + got[rows, :].astype(F32)
        place = r - (1 - x)
        also = (c == 1 - x) & (place >= 0) & (place < 2)
        dn += jnp.where(also, half[jnp.clip(place, 0, 1)].astype(F32), 0.0)
        back, unit = norm_back(dn, tok[rows, :].astype(F32), vec_ref[0:1, :])
        mixed_copy.wait() if r == 0 else None
        mixed[rows, :] = (dres[rows, :] + back).astype(BF)
        vb[0:1, :] += jnp.sum(dn * unit, axis=0, keepdims=True)
        vb[1:2, :] += jnp.sum(dn, axis=0, keepdims=True)
    ig_copy = pltpu.make_async_copy(mixed, ig_out, ws.at[1])
    ig_copy.start()
    if custom:
        late_sum = SumOverAll(vb, near_b, far_b, bss, brs)
        late_sum.start()
        va_out[...] = early_sum.finish()
        step(3, "start_third")
        late_sum.middle()
        squares = functools.reduce(jnp.add, [one.finish() for one in reduces])
        square[...] = jnp.full(square.shape, squares, F32)
        norm = SumOverAll(square, near_s, far_s, qss, qrs)
        norm.start()
        vb_out[...] = late_sum.finish()
        vector_squares = jnp.sum(va_out[...] * va_out[...], keepdims=True)
        vector_squares += jnp.sum(vb_out[...] * vb_out[...], keepdims=True)
        norm.middle()
        norm_ref[...] = jnp.sqrt(norm.finish() + vector_squares)
    ig_copy.wait()


def backward(saved, weights, given, tokens, vectors):
    (gl, n1, u, ctx, lse, starts, ctxc, resid, wo, br, dn, gp, gf, gb) = saved
    rows, width = tokens.shape
    chip = 2 * rows
    heads = u.shape[2]
    cols = heads * HD
    custom = lax.axis_size("dp") == 8
    dma = pltpu.SemaphoreType.DMA
    out_shape = [sds((rows, width), BF)] * 2
    out_specs = [ANY, ANY]
    if custom:
        hidden = gp.shape[-1]
        part_rows = width // 8
        shapes = [(part_rows, n) for n in (hidden, hidden, 2 * cols, 2 * cols)]
        gf = gf.reshape(gp.shape)
        out_shape += [sds(s, F32) for s in shapes]
        out_shape += [sds((8, width), F32)] * 2 + [sds((8, 128), F32)]
        out_specs += [VM] * 7
        scratch = [pltpu.VMEM((2, 4, 2) + s, BF) for s in shapes[2:]]
        scratch += [
            pltpu.VMEM((n,) + shapes[a], BF) for a in range(2) for n in (BY_Y[a], 4 - BY_Y[a], 4)
        ]
        scratch += [
            pltpu.VMEM((n,) + shapes[a], BF)
            for a in range(4)
            for n in (BY_Y[a], 4 - BY_Y[a], 4, 4, 3)
        ]
        scratch += [
            *[pltpu.VMEM((8, width), F32)] * 2,
            *[pltpu.VMEM((8, 8, width), F32), pltpu.VMEM((4, 8, width), F32)] * 2,
            pltpu.VMEM((8, 8, 128), F32),
            pltpu.VMEM((4, 8, 128), F32),
            pltpu.VMEM((8, 128), F32),
            dma((2, 3)),
            dma((4, 9)),
            dma((4, 9)),
            *[dma((10,))] * 6,
        ]
    else:
        out_shape += [sds((8, width), F32)] * 2 + [sds((2, 1, 1, width, 2 * cols), BF)] * 2
        out_specs += [VM] * 4
        scratch = []
    scratch += [
        pltpu.VMEM((2, BLK, width), BF),
        pltpu.VMEM((2, BLK, width), F32),
        pltpu.VMEM((2, BLK, width), BF),
        pltpu.VMEM((chip, width), BF),
        pltpu.VMEM((rows, width), BF),
        pltpu.VMEM((rows, width), BF),
        pltpu.VMEM((rows, width), BF),
        pltpu.VMEM((chip, width), BF),
        pltpu.VMEM((rows, width), F32),
        pltpu.VMEM(ctx.shape, BF),
        pltpu.VMEM(ctxc.shape, BF),
        pltpu.VMEM(wo.shape, BF),
        pltpu.VMEM((heads, HD, HALF), BF),
        pltpu.VMEM((heads, HD, HALF), BF),
        pltpu.VMEM(u.shape, BF),
        pltpu.VMEM(ctx.shape, BF),
        pltpu.VMEM(n1.shape, BF),
        *[pltpu.VMEM(w.shape, BF) for w in weights],
        pltpu.VMEM((rows, width), BF),
        pltpu.VMEM(u.shape, BF),
        pltpu.VMEM((HD, SLOT), F32),
        pltpu.VMEM((2, BLK, width), BF),
        pltpu.VMEM((BLK, width), BF),
        pltpu.VMEM((2, BLK, width), BF),
        pltpu.VMEM((rows, width), BF),
        dma((9,)),
        dma((2, 3)),
        dma((chip // BLK,)),
        dma((chip // BLK,)),
        dma((6,)),
        dma((5,)),
        dma((2,)),
    ]
    return pl.pallas_call(
        functools.partial(backward_kernel, custom),
        out_shape=tuple(out_shape),
        in_specs=[ANY] * 4 + [VM, VM] + [ANY] * 7 + [VM] + [ANY] * 3 + [VM] + [ANY] * len(given),
        out_specs=tuple(out_specs),
        scratch_shapes=scratch,
        compiler_params=params(2),
        name="backward",
    )(gl, n1, u, ctx, lse, starts, ctxc, resid, wo, br, dn, gp, gf, gb, *weights, tokens, vectors, *given)


def adamw_update(weight, moment_one, moment_two, gradient, step_rate, decay_rate):
    first_moment = DECAY_FIRST * moment_one + (1.0 - DECAY_FIRST) * gradient
    second_moment = DECAY_SECOND * moment_two + (1.0 - DECAY_SECOND) * gradient * gradient
    first_hat = first_moment / (1.0 - DECAY_FIRST**STEP)
    second_hat = second_moment / (1.0 - DECAY_SECOND**STEP)
    fresh_weight = weight - step_rate * (
        first_hat / (jnp.sqrt(second_hat) + ADAM_EPSILON) + decay_rate * weight
    )
    return (fresh_weight, first_moment, second_moment)


def update_kernel(*refs):
    (gp, gf, gvo, gqk, va, vb, norm_ref), refs = refs[:7], refs[7:]
    cols = gvo.shape[1] // 2
    old, new, norm_out = refs[:18], refs[18:36], refs[36]
    norm_out[0, 0] = norm_ref[0, 0]
    factor = CLIP_NORM / jnp.maximum(norm_ref[0:1, 0:1], CLIP_NORM)

    def update(number, grad, index, rate, decay):
        values = [old[3 * number + m][index] for m in range(3)]
        fresh = adamw_update(*values, factor * grad, rate, decay)
        for m in range(3):
            new[3 * number + m][index] = fresh[m]

    for k, grad in enumerate((gqk[:, :cols], gqk[:, cols:], gvo[:, :cols])):
        update(0, grad, k, RATE_MATRIX, WEIGHT_DECAY)
    for number, grad in ((1, gvo[:, cols:].T), (2, gf[...]), (3, gp[...])):
        update(number, grad, ..., RATE_MATRIX, WEIGHT_DECAY)
    width = va.shape[1]
    parts = old[15].shape[1] // width

    def heads(k):
        rows = [vb[2 + t : 3 + t, k * cols : (k + 1) * cols] for t in range(parts)]
        return jnp.concatenate(rows, axis=1)

    vector_grad = jnp.concatenate(
        [vb[0:2, :], va[0:2, :], heads(0), heads(1), va[2:4, :]], axis=0
    )
    update(4, vector_grad, ..., RATE_VECTOR, 0.0)
    for t in range(parts):
        lanes = slice(t * width, (t + 1) * width)
        update(5, va[4 + t : 5 + t, :], (slice(None), lanes), RATE_VECTOR, 0.0)


def update_all(totals, va, vb, norm, states):
    return pl.pallas_call(
        update_kernel,
        out_shape=(*[sds(s.shape, F32) for s in states], sds((1, 1), F32)),
        in_specs=[VM] * (7 + len(states)),
        out_specs=(*[VM] * len(states), pl.BlockSpec(memory_space=pltpu.SMEM)),
        compiler_params=params(),
        name="update",
    )(*totals, va, vb, norm, *states)


def on_device(
    tokens,
    cotangent,
    segment_ids,
    valid,
    qkv_weight,
    qkv_moment1,
    qkv_moment2,
    out_weight,
    out_moment1,
    out_moment2,
    fc_weight,
    fc_moment1,
    fc_moment2,
    proj_weight,
    proj_moment1,
    proj_moment2,
    vector_params,
    vector_moment1,
    vector_moment2,
    fc_bias,
    fc_bias_moment1,
    fc_bias_moment2,
):
    custom = lax.axis_size("dp") == 8
    slot, swap = lax.axis_index("tensor") // 2, [(0, 2), (1, 3), (2, 0), (3, 1)]
    states = [jnp.transpose(s, (1, 0, 2)) for s in (qkv_weight, qkv_moment1, qkv_moment2)]
    states += [out_weight, out_moment1, out_moment2]
    states += [fc_weight, fc_moment1, fc_moment2]
    states += [s.T for s in (proj_weight, proj_moment1, proj_moment2)]
    states += [vector_params, vector_moment1, vector_moment2]
    states += [s[None] for s in (fc_bias, fc_bias_moment1, fc_bias_moment2)]
    shards = [states[0], states[3], states[6], states[9]]
    if not custom:
        parts = [
            jnp.concatenate([states[0][0], states[0][1]], axis=1),
            jnp.concatenate([states[0][2], shards[1].T], axis=1),
            *shards[2:],
        ]
        shards = []
        for part in parts:
            own = lax.all_gather(part.astype(BF), "dp", axis=0, tiled=True)
            other = lax.ppermute(own, "tensor", swap)
            shards.append(
                jnp.stack([jnp.where(slot == 0, own, other), jnp.where(slot == 0, other, own)])
            )
    saved, weights, given = forward(
        tokens,
        cotangent,
        valid,
        segment_ids,
        vector_params,
        states[15],
        shards,
    )
    outs = backward(saved, weights, given, tokens, vector_params)
    mixed, input_grad = outs[:2]
    if custom:
        totals, (va, vb, norm) = outs[2:6], outs[6:]
    else:
        va, vb, totals = *outs[2:4], []
        for g in [saved[11], saved[12], *outs[4:6]]:
            g = g.reshape(2, -1, g.shape[-1])
            mine = jnp.where(slot == 0, g[0], g[1])
            other = jnp.where(slot == 0, g[1], g[0])
            both = mine.astype(F32) + lax.ppermute(other, "tensor", swap).astype(F32)
            both = lax.psum_scatter(both.astype(BF), "dp", scatter_dimension=0, tiled=True)
            totals.append(both.astype(F32))
        squares = sum(jnp.sum(t * t) for t in totals)
        va, vb, squares = lax.psum((va, vb, squares), ("dp", "tensor"))
        squares += jnp.sum(va * va) + jnp.sum(vb * vb)
        norm = jnp.full((8, 128), jnp.sqrt(squares), F32)
    *new, grad_norm = update_all(totals, va, vb, norm, states)
    new[:3] = [jnp.transpose(s, (1, 0, 2)) for s in new[:3]]
    new[9:12] = [s.T for s in new[9:12]]
    new[15:18] = [s[0] for s in new[15:18]]
    return (mixed, input_grad, grad_norm.reshape(()), *new)


def solution(mesh):
    rows = P(("dp", "tensor"), None)
    by_rows = [P("dp", None, "tensor")] * 3
    by_out = [P("tensor", "dp")] * 3
    by_fc = [P("dp", "tensor")] * 3
    weights = by_rows + by_out + by_fc + by_out
    return jax.shard_map(
        on_device,
        mesh=mesh,
        in_specs=(rows, rows, P("dp"), P(("dp", "tensor")), *weights, *[P()] * 6),
        out_specs=(rows, rows, P(), *weights, *[P()] * 6),
        check_vma=False,
    )
```

```python
import functools
import math

import jax
import jax.numpy as jnp
from jax import lax
from jax.experimental import pallas as pl
from jax.experimental.pallas import tpu as pltpu
from jax.sharding import PartitionSpec as P

HD = 64
SLOT = 1024
STEP = 10
NORM_EPSILON = 1e-05
MASK_FILL = -1e30
DECAY_FIRST = 0.5
DECAY_SECOND = 0.5
ADAM_EPSILON = 1e-08
WEIGHT_DECAY = 0.1
CLIP_NORM = 1.0
RATE_MATRIX = 0.04
RATE_VECTOR = 0.3

MESH = pl.DeviceIdType.MESH
BF = jnp.bfloat16
F32 = jnp.float32
HALF = SLOT // 2
BLK = 256
VMEM_LIMIT = 58 * 2**20
LOG2E = math.log2(math.e)
SCORE_SCALE = float(HD) ** (-0.5)
SCORE_SCALE2 = SCORE_SCALE * LOG2E


def dot_nn(a, b):
    return lax.dot_general(a, b, (((1,), (0,)), ((), ())), preferred_element_type=F32)


def dot_nt(a, b):
    return lax.dot_general(a, b, (((1,), (1,)), ((), ())), preferred_element_type=F32)


def dot_tn(a, b):
    return lax.dot_general(a, b, (((0,), (0,)), ((), ())), preferred_element_type=F32)


def dot_tt(a, b):
    return lax.dot_general(a, b, (((0,), (1,)), ((), ())), preferred_element_type=F32)


def params(collective_id=None):
    if collective_id is None:
        return pltpu.CompilerParams(vmem_limit_bytes=VMEM_LIMIT)
    return pltpu.CompilerParams(
        vmem_limit_bytes=VMEM_LIMIT, collective_id=collective_id, has_side_effects=True
    )


VM = pl.BlockSpec(memory_space=pltpu.VMEM)
ANY = pl.BlockSpec(memory_space=pl.ANY)


def sds(shape, dtype):
    return jax.ShapeDtypeStruct(shape, dtype)


def here():
    t = lax.axis_index("tensor")
    return lax.axis_index("dp"), t // 2, t % 2


def announce(ids):
    sem = pltpu.get_barrier_semaphore()
    for one in ids:
        pl.semaphore_signal(sem, inc=1, device_id=one, device_id_type=MESH)


def await_others(ids):
    pl.semaphore_wait(pltpu.get_barrier_semaphore(), len(ids))


def greet(ids):
    announce(ids)
    await_others(ids)


def remote(src, dst, send_sem, recv_sem, target):
    return pltpu.make_async_remote_copy(
        src_ref=src,
        dst_ref=dst,
        send_sem=send_sem,
        recv_sem=recv_sem,
        device_id=target,
        device_id_type=MESH,
    )


def rows_at(start, size):
    return pl.ds(pl.multiple_of(start, size), size)


def norm_parts(values):
    centered = values - jnp.mean(values, axis=-1, keepdims=True)
    variance = jnp.mean(centered * centered, axis=-1, keepdims=True)
    scale = lax.rsqrt(variance + NORM_EPSILON)
    return centered * scale, scale


class Gather:
    def __init__(self, shard, whole, part, by_y, ss, rs):
        dp, x, c = here()
        z, y = dp // 2, dp % 2
        along, x_peer, y_peer, _ = neighbours()
        shard = shard.at[part]
        block = whole.at[x, z, y, part]
        column = whole.at[x, :, y, part]
        from_x = whole.at[1 - x, pl.ds(0, by_y), y, part]
        from_y = whole.at[x, pl.ds(by_y, 4 - by_y), 1 - y, part]
        self.along = [remote(shard, block, ss.at[k], rs.at[k], along[k]) for k in range(3)]
        self.beside = [
            remote(column, column, ss.at[3], rs.at[3], x_peer),
            remote(column, column, ss.at[4], rs.at[4], y_peer),
        ]
        self.passed = [
            remote(from_x, from_x, ss.at[5], rs.at[5], y_peer),
            remote(from_y, from_y, ss.at[6], rs.at[6], x_peer),
        ]

    def start_along(self):
        for one in self.along:
            one.start()

    def start_beside(self):
        for one in self.along:
            one.wait()
        for one in self.beside:
            one.start()

    def start_passed(self):
        for one in self.beside:
            one.wait()
        for one in self.passed:
            one.start()

    def finish(self):
        for one in self.passed:
            one.wait()


class GatherBeside:
    def __init__(self, shard, whole, start, size, by_y, ss, rs):
        dp, x, c = here()
        z, y = dp // 2, dp % 2
        along, x_peer, y_peer, _ = neighbours()
        part = pl.ds(start, size)
        block = whole.at[x, z, y, part]
        from_x = whole.at[1 - x, z, y, pl.ds(start, by_y)]
        from_y = whole.at[x, z, 1 - y, pl.ds(start + by_y, size - by_y)]
        four = whole.at[:, z, :, part]
        self.beside = [
            remote(shard.at[part], block, ss.at[3], rs.at[3], x_peer),
            remote(shard.at[part], block, ss.at[4], rs.at[4], y_peer),
        ]
        self.passed = [
            remote(from_x, from_x, ss.at[5], rs.at[5], y_peer),
            remote(from_y, from_y, ss.at[6], rs.at[6], x_peer),
        ]
        self.along = [remote(four, four, ss.at[k], rs.at[k], along[k]) for k in range(3)]

    def start_beside(self):
        for one in self.beside:
            one.start()

    def start_passed(self):
        for one in self.beside:
            one.wait()
        for one in self.passed:
            one.start()

    def start_along(self):
        for one in self.passed:
            one.wait()
        for one in self.along:
            one.start()

    def finish(self):
        for one in self.along:
            one.wait()


def neighbours():
    dp, x, c = here()
    z, y = dp // 2, dp % 2
    me = x * 2 + c
    along = [(lax.rem(z + k, 4) * 2 + y, me) for k in (1, 2, 3)]
    return along, (dp, (1 - x) * 2 + c), (z * 2 + 1 - y, me), (dp, x * 2 + 1 - c)


def whole_weight(ref, slot):
    value = ref[slot]
    return value.reshape(-1, value.shape[-1])


MASKED = -(2.0**100)
ATT = 512


def segment_features(segments):
    numbers = lax.broadcasted_iota(jnp.int32, (16, segments.shape[1]), 0).astype(F32) + 1.0
    query = jnp.where(segments >= numbers, 1.0, 0.0)
    key = jnp.where(segments < numbers, MASKED, 0.0)
    return query.astype(BF), key.astype(BF)


def causal(scores):
    keys = lax.broadcasted_iota(jnp.int32, scores.shape, 0)
    queries = lax.broadcasted_iota(jnp.int32, scores.shape, 1)
    return jnp.where(keys <= queries, scores, MASK_FILL)


def attend_unit(q, k, v):
    for i in range(SLOT // ATT):
        cols = slice(i * ATT, (i + 1) * ATT)
        query = q(cols)
        scores = []
        for j in range(i + 1):
            raw = dot_tn(k(slice(j * ATT, (j + 1) * ATT)), query) * SCORE_SCALE2
            scores.append(causal(raw) if j == i else raw)
        top = functools.reduce(jnp.maximum, [jnp.max(s, axis=0, keepdims=True) for s in scores])
        exps = [jnp.exp2(s - top) for s in scores]
        total = functools.reduce(jnp.add, [jnp.sum(e, axis=0, keepdims=True) for e in exps])
        low = jnp.concatenate([e.astype(BF) for e in exps], axis=0)
        yield cols, dot_nn(v(slice(0, (i + 1) * ATT)), low) / total, top + jnp.log2(total)


GELU_C = math.sqrt(2.0 / math.pi)
GELU_A = 0.044715


def forward_kernel(custom, *refs):
    (tok_ref, cot_ref, valid_ref, seg_ref, vec_ref, fb_ref), refs = refs[:6], refs[6:]
    shards, refs = refs[:4], refs[4:]
    (gl_out, n1_out, u_out, ctx_out, lse_out, feat_out, ctxc_out, resid_out, wo_out, br_out, dn_out, gp_out,
     gf_out, gb_ref), refs = refs[:14], refs[14:]
    if custom:
        weights_out, given, refs = refs[:2], refs[2:6], refs[6:]
        lows, refs = refs[:4], refs[4:]
        wholes, refs = refs[:4], refs[4:]
        gs, gr, ps, pr, refs = *refs[:4], refs[4:]
    else:
        wholes = shards
    (tk, gl, n1, u, ctx, lse, features, ctxc, resid, wo, n2, half, part, got, act, dpre, gp, cols, loc, ts, tr, xs,
     cs_s, cs_r) = refs
    wqk, wvo, wf, wp = wholes
    dp, x, c = here()
    core = (dp, x * 2 + 1 - c)
    x_peer = (dp, (1 - x) * 2 + c)
    across = [(dp, (1 - x) * 2), (dp, (1 - x) * 2 + 1)]
    rows = tok_ref.shape[0]
    first = x * HALF
    gathers = []
    if custom:
        z, y = dp // 2, dp % 2
        along, _, y_peer, _ = neighbours()
        others = [core, *across, *along, y_peer]
        announce(others)
        lows[0][...] = jnp.concatenate([shards[0][0], shards[0][1]], axis=1).astype(BF)
        lows[1][...] = jnp.concatenate([shards[0][2], shards[1][...].T], axis=1).astype(BF)
        lows[2][...] = shards[2][...].astype(BF)
        lows[3][...] = shards[3][...].astype(BF)
        await_others(others)
        pieces = [(a, k, 2, 2) for a in range(2) for k in range(2)]
        pieces += [(2, 0, 2, 3), (2, 1, 2, 3), (3, 0, 2, 3)]
        for number, (a, k, parts, by_y) in enumerate(pieces):
            size = lows[a].shape[0] // parts
            gathers.append(
                Gather(
                    lows[a], wholes[a], pl.ds(k * size, size), by_y, gs.at[number], gr.at[number]
                )
            )
        size = lows[3].shape[0] // 2
        gathers.append(GatherBeside(lows[3], wholes[3], size, size, 32, gs.at[7], gr.at[7]))
    else:
        greet([core, *across])

    def step(number, what):
        if custom:
            getattr(gathers[number], what)()

    own_rows = pl.ds(pl.multiple_of(first + c * rows, BLK), rows)
    gl_rows = pl.ds(pl.multiple_of(c * rows, BLK), rows)
    mine_tok = pltpu.make_async_copy(tok_ref, tk.at[own_rows], loc.at[0])
    cot_load = pltpu.make_async_copy(cot_ref, part.at[pl.ds(0, rows)], loc.at[9])
    swap_tok = remote(tok_ref, tk.at[own_rows], ts.at[0], tr.at[0], core)
    swap_grad = remote(gl.at[gl_rows], gl.at[gl_rows], ts.at[1], tr.at[1], core)
    source = [
        tok_ref.at[pl.ds(pl.multiple_of((1 - x) * BLK + k * BLK, BLK), BLK)] for k in range(2)
    ]
    there = [
        tk.at[pl.ds(pl.multiple_of(x * (SLOT + HALF) + k * BLK, BLK), BLK)] for k in range(2)
    ]
    halves = [remote(source[k], there[k], ts.at[2 + k], tr.at[2], across[k]) for k in range(2)]
    landed = tk.at[pl.ds(pl.multiple_of((1 - x) * (SLOT + HALF) + c * BLK, BLK), BLK)]
    handed = remote(landed, landed, ts.at[4], tr.at[3], core)

    step(0, "start_along")
    step(7, "start_beside")
    step(1, "start_along")
    mine_tok.start()
    swap_tok.start()
    cot_load.start()

    @pl.when(c == 1 - x)
    def _():
        for one in halves:
            one.start()

    if custom:
        for a in range(4):
            wholes[a][x, z, y] = lows[a][...]

    def out_copy(number, ref, out):
        copy = pltpu.make_async_copy(ref, out, loc.at[number])
        copy.start()
        return copy

    cols[...] = vec_ref[...].T
    gain, shift = vec_ref[0:1, :], vec_ref[1:2, :]

    def norm_rows(start, count):
        def norm(i, carry):
            at = rows_at(start + i * BLK, BLK)
            unit, _ = norm_parts(tk[at, :].astype(F32))
            n1[at, :] = (unit * gain + shift).astype(BF)
            return carry

        lax.fori_loop(0, count // BLK, norm, 0)

    mine_tok.wait()
    norm_rows(first + c * rows, rows)
    swap_tok.wait()
    step(0, "start_beside")
    step(2, "start_along")
    norm_rows(first + (1 - c) * rows, rows)
    step(1, "start_beside")
    step(3, "start_along")

    mask = jnp.broadcast_to(valid_ref[...].reshape(1, rows).astype(F32), (8, rows)).T[:, 0:1]
    cot_load.wait()
    gl[gl_rows, :] = (part[:rows, :].astype(F32) * mask).astype(BF)
    swap_grad.start()
    for k, row in enumerate((2 * x, 1)):
        at = pl.ds(pl.multiple_of(row * SLOT, SLOT), SLOT)
        query, key = segment_features(seg_ref[at].reshape(1, SLOT).astype(F32))
        features[k, 0] = query
        features[k, 1] = key

    halves[0].wait_recv()
    handed.start()
    step(2, "start_beside")
    step(4, "start_along")
    handed.wait()
    norm_rows((1 - x) * (SLOT + HALF), HALF)
    step(3, "start_beside")
    step(5, "start_along")
    step(7, "start_passed")
    for number in range(4):
        step(number, "start_passed")

    heads = u.shape[2]
    wide = heads * HD

    def project(group, slot, first_row):
        bias_rows = pl.ds(pl.multiple_of((c + 2 * slot) * wide, HD), wide)
        query_bias, value_bias = cols[bias_rows, 4:5], cols[bias_rows, 5:6]

        def chunk(i, carry):
            lanes = rows_at(i * BLK, BLK)
            values = n1[rows_at(first_row + i * BLK, BLK), :]
            two = dot_tt(whole_weight(wqk, slot), values)
            value = dot_tt(whole_weight(wvo, slot)[:, :wide], values) + value_bias
            for k, out in enumerate((two[:wide] + query_bias, two[wide:], value)):
                u[group, k, :, :, lanes] = out.reshape(-1, HD, BLK).astype(BF)
            return carry

        lax.fori_loop(0, SLOT // BLK, chunk, 0)

    def attend(group, which, begin, end):
        def unit(h, carry):
            for lanes, context, log_total in attend_unit(
                lambda s: jnp.concatenate([u[group, 0, h, :, s], features[which, 0, :, s]], axis=0),
                lambda s: jnp.concatenate([u[group, 1, h, :, s], features[which, 1, :, s]], axis=0),
                lambda s: u[group, 2, h, :, s],
            ):
                ctx[group, h, :, lanes] = context.astype(BF)
                lse[group, h, :, lanes] = log_total
            return carry

        lax.fori_loop(begin, end, unit, 0)

    project(x, x, x * SLOT)
    step(4, "start_beside")
    step(6, "start_along")
    attend(x, 0, 0, 1)
    step(5, "start_beside")
    step(7, "start_along")
    attend(x, 0, 1, heads)
    step(4, "start_passed")
    project(2, x, (1 - x) * SLOT)
    step(6, "start_beside")
    attend(2, 1, 0, heads)
    theirs = pl.ds(pl.multiple_of((1 - x) * HALF, HALF), HALF)
    cross = remote(ctx.at[2, :, :, theirs], half, xs.at[0], xs.at[1], x_peer)
    cross.start()
    for number in range(4):
        step(number, "finish")
    step(5, "start_passed")
    project(1 - x, 1 - x, x * SLOT)
    copies = [out_copy(1, n1, n1_out), out_copy(2, u, u_out)]
    for s in range(2):
        wo[s] = whole_weight(wvo, s)[:, wide:]
    attend(1 - x, 0, 0, 1)
    step(6, "start_passed")
    attend(1 - x, 0, 1, heads)
    copies += [out_copy(3, ctx, ctx_out), out_copy(4, lse, lse_out), out_copy(5, features, feat_out)]
    copies.append(out_copy(8, wo, wo_out))
    if custom:
        copies += [out_copy(6 + a, wholes[a], weights_out[a]) for a in range(2)]

    @pl.when(c == 1 - x)
    def _():
        for one in halves:
            one.wait_send()

    chunks = []

    def send(chunk, values):
        at = rows_at(chunk * BLK, BLK)
        part[at, :] = values.astype(BF)
        copy = remote(part.at[at], got.at[at], cs_s.at[chunk], cs_r.at[chunk], core)
        copy.start()
        chunks.append((chunk, copy))

    def context_of(group, lanes):
        value = ctx[group, :, :, lanes]
        return value.reshape(-1, value.shape[-1])

    for i in range(SLOT // BLK):
        lanes = slice(i * BLK, (i + 1) * BLK)
        chunk = x * 2 + i
        at = rows_at(chunk * BLK, BLK)
        zero, one = context_of(0, lanes), context_of(1, lanes)
        send(chunk, dot_tt(zero, wo[0]) + dot_tt(one, wo[1]))
        ctxc[0, :, at] = zero
        ctxc[1, :, at] = one
    cross.wait()
    for i in range(HALF // BLK):
        chunk = (1 - x) * 4 + i
        at = rows_at(chunk * BLK, BLK)
        own = context_of(2, rows_at(x * HALF + i * BLK, BLK))
        other = half[:, :, i * BLK : (i + 1) * BLK].reshape(-1, BLK)
        send(chunk, dot_tt(own, wo[x]) + dot_tt(other, wo[1 - x]))
        ctxc[x, :, at] = own
        ctxc[1 - x, :, at] = other
    copies.append(out_copy(10, ctxc, ctxc_out))
    swap_grad.wait()
    copies.append(out_copy(11, gl, gl_out))
    for chunk, copy in chunks:
        copy.wait()
        at = rows_at(chunk * BLK, BLK)
        tokens = tk[rows_at(first + chunk * BLK, BLK), :].astype(F32)
        summed = part[at, :].astype(F32) + got[at, :].astype(F32)
        after = tokens + summed + vec_ref[6:7, :]
        resid[at, :] = after
        unit, _ = norm_parts(after)
        n2[at, :] = (unit * vec_ref[2:3, :] + vec_ref[3:4, :]).astype(BF)
    copies.append(out_copy(12, resid, resid_out))
    step(4, "finish")
    step(5, "finish")

    hidden = wf.shape[-1]
    gb_ref[...] = jnp.zeros_like(gb_ref)
    bias_of = [
        fb_ref[:, pl.ds(pl.multiple_of((c + 2 * s) * hidden, hidden), hidden)] for s in range(2)
    ]
    tile = HALF
    tiles = 2 * rows // tile

    def activate(i, carry):
        at = rows_at(i * tile, tile)
        n2_rows = n2[at, :]
        for s in range(2):
            lanes = slice(s * hidden, (s + 1) * hidden)
            v = dot_nn(n2_rows, whole_weight(wf, s)) + bias_of[s]
            square = v * v
            t = jnp.tanh(v * (GELU_C + (GELU_C * GELU_A) * square))
            cdf = 0.5 + 0.5 * t
            act[at, lanes] = (v * cdf).astype(BF)
            slope = cdf + (cdf * (1.0 - t)) * (v * (GELU_C + (3.0 * GELU_C * GELU_A) * square))
            dpre[at, lanes] = slope.astype(BF)
        return carry

    lax.fori_loop(0, tiles, activate, 0)
    blocks = gp.shape[1:4]

    for s in range(2):
        out = dot_tn(gl[...], act[:, s * hidden : (s + 1) * hidden]).astype(BF)
        gp[s] = out.reshape(*blocks, hidden)
        copies.append(out_copy(15 + s, gp.at[s], gp_out.at[s]))
    passing = []
    if custom:
        low, high = pl.ds(0, 2), pl.ds(2, 2)
        pieces = [
            (gp.at[1 - x, low, 1 - y], y_peer),
            (gp.at[1 - x, high, 1 - y], x_peer),
            (gp.at[1 - x, high, y], x_peer),
            (gp.at[x, low, 1 - y], y_peer),
        ]
        for k, (piece, peer) in enumerate(pieces):
            passing.append(remote(piece, given[k], ps.at[k], pr.at[k], peer))
            passing[-1].start()
    step(6, "finish")
    step(7, "finish")

    def forward_back(i, carry):
        at = rows_at(i * tile, tile)
        gl_now = gl[at, :]
        for s in range(2):
            lanes = slice(s * hidden, (s + 1) * hidden)
            up = dot_nn(gl_now, whole_weight(wp, s))
            d = (up * dpre[at, lanes].astype(F32)).astype(BF)
            dpre[at, lanes] = d
            gb_ref[s] += jnp.sum(d.astype(F32), axis=0, keepdims=True)
        br = dot_nt(act[at, :hidden], whole_weight(wp, 0))
        br += dot_nt(act[at, hidden:], whole_weight(wp, 1))
        part[at, :] = br.astype(BF)
        dn = dot_nt(dpre[at, :hidden], whole_weight(wf, 0))
        dn += dot_nt(dpre[at, hidden:], whole_weight(wf, 1))
        got[at, :] = dn.astype(BF)
        return carry

    lax.fori_loop(0, tiles, forward_back, 0)
    copies += [out_copy(13, got, dn_out), out_copy(14, part, br_out)]
    width = n2.shape[1]

    for s in range(2):
        at = slice(s * width, (s + 1) * width)
        tk[at, :] = dot_tn(n2[...], dpre[:, s * hidden : (s + 1) * hidden]).astype(BF)
        copies.append(out_copy(17 + s, tk.at[at], gf_out.at[s]))
    for copy in copies + passing:
        copy.wait()


def forward(tokens, cotangent, valid, segments, vectors, fc_bias, shards):
    rows, width = tokens.shape
    chip = 2 * rows
    custom = lax.axis_size("dp") == 8
    dma = pltpu.SemaphoreType.DMA
    if custom:
        cols = shards[0].shape[2]
        hidden = shards[2].shape[1]
        part_rows = shards[2].shape[0]
        flat = [(part_rows, n) for n in (2 * cols, 2 * cols, hidden, hidden)]
        wholes = [(2, 4, 2) + s for s in flat]
        more_out = [sds(w, BF) for w in wholes[:2]] + [sds((2, part_rows, hidden), BF)] * 4
        more = [pltpu.VMEM(s, BF) for s in flat] + [pltpu.VMEM(w, BF) for w in wholes]
        more += [dma((8, 7)), dma((8, 7)), dma((4,)), dma((4,))]
        grad_shape = wholes[3]
    else:
        cols, hidden = shards[0].shape[2] // 2, shards[2].shape[2]
        more_out, more = [], []
        grad_shape = (2, 1, 1, width, hidden)
    heads = cols // HD
    shapes = [
        ((chip, width), BF),
        ((2 * SLOT, width), BF),
        ((3, 3, heads, HD, SLOT), BF),
        ((3, heads, HD, SLOT), BF),
        ((3, heads, 1, SLOT), F32),
        ((2, 2, 16, SLOT), BF),
        ((2, cols, chip), BF),
        ((chip, width), F32),
        ((2, width, cols), BF),
    ]
    out_shape = [sds(*s) for s in shapes]
    out_shape += [sds((chip, width), BF)] * 2 + [sds(grad_shape, BF), sds((2, width, hidden), BF)]
    out_shape += [sds((2, 1, hidden), F32)] + more_out
    outs = pl.pallas_call(
        functools.partial(forward_kernel, custom),
        out_shape=tuple(out_shape),
        in_specs=[ANY, ANY] + [VM] * (4 + len(shards)),
        out_specs=(*[ANY] * 13, VM, *[ANY] * len(more_out)),
        scratch_shapes=more
        + [
            pltpu.VMEM((2 * SLOT, width), BF),
            *[pltpu.VMEM(*s) for s in shapes],
            pltpu.VMEM((chip, width), BF),
            pltpu.VMEM((heads, HD, HALF), BF),
            pltpu.VMEM((chip, width), BF),
            pltpu.VMEM((chip, width), BF),
            pltpu.VMEM((chip, 2 * hidden), BF),
            pltpu.VMEM((chip, 2 * hidden), BF),
            pltpu.VMEM(grad_shape, BF),
            pltpu.VMEM((width, 8), F32),
            dma((19,)),
            dma((5,)),
            dma((4,)),
            dma((2,)),
            dma((chip // BLK,)),
            dma((chip // BLK,)),
        ],
        compiler_params=params(1),
        name="forward",
    )(tokens, cotangent, valid, segments, vectors, fc_bias, *shards)
    if custom:
        return outs[:14], outs[14:16], outs[16:]
    return outs[:14], shards[:2], []


class Reduce:
    def __init__(self, grad, by_y, local, given, total, bufs, loc, ss, rs):
        dp, x, c = here()
        z, y = dp // 2, dp % 2
        along, x_peer, y_peer, _ = neighbours()
        low, high = pl.ds(0, by_y), pl.ds(by_y, 4 - by_y)
        self.z, self.total = z, total
        self.r1y, self.r1x, self.r2x, self.r2y, self.r3 = bufs
        views = [grad.at[1 - x, low, y], grad.at[x, high, 1 - y], grad.at[x, :, y]]
        self.loads = []
        self.mid_x, self.mid_y, self.own = views
        if local is not None:
            self.loads = [
                pltpu.make_async_copy(views[k], local[k], loc.at[k]) for k in range(3)
            ]
            self.mid_x, self.mid_y, self.own = local
        self.first = [
            remote(grad.at[1 - x, low, 1 - y], self.r1y, ss.at[0], rs.at[0], y_peer),
            remote(grad.at[1 - x, high, 1 - y], self.r1x, ss.at[1], rs.at[1], x_peer),
        ]
        self.early = [
            remote(grad.at[1 - x, high, y], self.r2x.at[high], ss.at[2], rs.at[2], x_peer),
            remote(grad.at[x, low, 1 - y], self.r2y.at[low], ss.at[3], rs.at[3], y_peer),
        ]
        targets = (self.r1y, self.r1x, self.r2x.at[high], self.r2y.at[low])
        for k, came in enumerate(given or ()):
            copies = (self.first, self.early)[k // 2]
            copies[k % 2] = pltpu.make_async_copy(came, targets[k], rs.at[k])
        self.second = [
            remote(self.mid_x, self.r2x.at[low], ss.at[4], rs.at[4], x_peer),
            remote(self.mid_y, self.r2y.at[high], ss.at[5], rs.at[5], y_peer),
        ]
        self.third = [
            remote(
                self.own.at[lax.rem(z + k + 1, 4)], self.r3.at[k], ss.at[6 + k], rs.at[6 + k], along[k]
            )
            for k in range(3)
        ]

    def start_first(self):
        for one in self.loads:
            one.start()
        for one in self.first:
            one.start()

    def start_early(self, which):
        self.early[which].start()

    def start_second(self, which):
        self.first[which].wait()
        if self.loads:
            self.loads[which].wait()
        mid, came = ((self.mid_x, self.r1y), (self.mid_y, self.r1x))[which]
        mid[...] = (mid[...].astype(F32) + came[...].astype(F32)).astype(BF)
        self.second[which].start()

    def start_third(self):
        for one in self.early + self.second + self.loads[2:]:
            one.wait()
        for k in range(4):
            place = lax.rem(self.z + k + 1, 4)
            summed = (
                self.own[place].astype(F32)
                + self.r2x[place].astype(F32)
                + self.r2y[place].astype(F32)
            )
            if k < 3:
                self.own[place] = summed.astype(BF)
                self.third[k].start()
            else:
                self.total[...] = summed

    def finish(self):
        for one in self.third:
            one.wait()
        total = self.total[...]
        for k in range(3):
            total = total + self.r3[k].astype(F32)
        self.total[...] = total
        return jnp.sum(total * total)


def eight_peers():
    dp, x, c = here()
    z, y = dp // 2, dp % 2
    peers = []
    for k in range(1, 8):
        kx, ky, kc = k // 4, k // 2 % 2, k % 2
        there = ((1 - x if kx else x), (1 - y if ky else y), (1 - c if kc else c))
        peers.append((z * 2 + there[1], there[0] * 2 + there[2]))
    return peers


class SumOverAll:
    def __init__(self, value, near, far, ss, rs):
        dp, x, c = here()
        z, y = dp // 2, dp % 2
        self.value, self.near, self.far = value, near, far
        self.me, self.z = x * 4 + y * 2 + c, z
        self.one = [
            remote(value, near.at[self.me], ss.at[k], rs.at[k], peer)
            for k, peer in enumerate(eight_peers())
        ]
        self.two = [
            remote(value, far.at[z], ss.at[7 + k], rs.at[7 + k], peer)
            for k, peer in enumerate(neighbours()[0])
        ]

    def start(self):
        for one in self.one:
            one.start()
        self.near[self.me] = self.value[...]

    def middle(self):
        for one in self.one:
            one.wait()
        self.value[...] = functools.reduce(jnp.add, [self.near[k] for k in range(8)])
        for one in self.two:
            one.start()
        self.far[self.z] = self.value[...]

    def finish(self):
        for one in self.two:
            one.wait()
        return functools.reduce(jnp.add, [self.far[k] for k in range(4)])


def attend_back_unit(u, out, features, ctx, dctx, lse, dq_ref):
    blocks = SLOT // BLK
    delta = jnp.sum(dctx.astype(F32) * ctx.astype(F32), axis=0, keepdims=True)
    for j in range(blocks):
        keys = slice(j * BLK, (j + 1) * BLK)
        after = slice(j * BLK, SLOT)
        k, v = u(1, keys), u(2, keys)
        wide = jnp.concatenate([k, features(1, keys)], axis=0)
        probs, dscores = [], []
        for i in range(j, blocks):
            cols = slice(i * BLK, (i + 1) * BLK)
            query = jnp.concatenate([u(0, cols), features(0, cols)], axis=0)
            raw = dot_tn(wide, query) * SCORE_SCALE2 - lse[:, cols]
            prob = jnp.exp2(causal(raw) if i == j else raw)
            dprob = dot_tn(v, dctx[:, cols])
            probs.append(prob.astype(BF))
            dscores.append((prob * (dprob - delta[:, cols])).astype(BF))
        probs, dscores = jnp.concatenate(probs, axis=1), jnp.concatenate(dscores, axis=1)
        dq = dot_nn(k, dscores)
        if j == 0:
            dq_ref[...] = dq
        else:
            dq_ref[:, after] += dq
        out(1, keys, (dot_nt(u(0, after), dscores) * SCORE_SCALE).astype(BF))
        out(2, keys, dot_nt(dctx[:, after], probs).astype(BF))
    out(0, slice(0, SLOT), (dq_ref[...] * SCORE_SCALE).astype(BF))


BY_Y = (2, 2, 3, 3)


def norm_back(dn, values, gain):
    unit, scale = norm_parts(values)
    e = dn * gain
    back = scale * (
        e
        - jnp.mean(e, axis=-1, keepdims=True)
        - unit * jnp.mean(e * unit, axis=-1, keepdims=True)
    )
    return back, unit


def backward_kernel(custom, *refs):
    (gl_in, n1_in, u_in, ctx_in, lse_ref, feat_ref, ctxc_in, resid_in, wo_in, br_in, dn_in, gp_in, gf_in, gb_ref,
     wqk_in, wvo_in, tok_in, vec_ref), refs = refs[:18], refs[18:]
    given = None
    if custom:
        given, refs = (refs[:4], None, None, None), refs[4:]
    (mixed_out, ig_out), refs = refs[:2], refs[2:]
    if custom:
        totals, refs = refs[:4], refs[4:]
        (va_out, vb_out, norm_ref), refs = refs[:3], refs[3:]
        g01, g2o, refs = refs[0], refs[1], refs[2:]
        locals_, refs = (refs[:3], refs[3:6]), refs[6:]
        bufs, refs = [refs[5 * a : 5 * a + 5] for a in range(4)], refs[20:]
        (va, vb, near_a, far_a, near_b, far_b, near_s, far_s, square, lss, ss, rs, ass, ars, bss, brs, qss,
         qrs), refs = refs[:18], refs[18:]
    else:
        va, vb, g01, g2o, refs = *refs[:4], refs[4:]
    (gl_s, resid_s, dn_s, got_dn, br_s, got_br, mixed, low, dres, dctx, ctxc, wo, half_c, outgoing, u, ctx, n1,
     wqk, wvo, tok, du, dq, away, away_got, half, got, loc, ld, cs_s, cs_r, bs, xs, ws) = refs
    part = low
    dp, x, c = here()
    core = (dp, x * 2 + 1 - c)
    x_peer = (dp, (1 - x) * 2 + c)
    reduces = []
    if custom:
        greet(eight_peers() + neighbours()[0])
        for a, grad in enumerate((gp_in, gf_in, g01, g2o)):
            local = locals_[a] if a < 2 else None
            loads = lss.at[a] if a < 2 else None
            came = given[a]
            reduces.append(
                Reduce(
                    grad, BY_Y[a], local, came, totals[a], bufs[a], loads, ss.at[a], rs.at[a]
                )
            )
    else:
        greet([core, x_peer, (dp, (1 - x) * 2 + 1 - c)])

    def step(number, what, *which):
        if custom:
            getattr(reduces[number], what)(*which)

    rows_all, width = low.shape
    own_rows = rows_all // 2
    n_chunks = rows_all // BLK
    order = [(1 - x) * 4 + i for i in range(HALF // BLK)] + [x * 2 + i for i in range(SLOT // BLK)]
    swaps = []
    for chunk in order:
        at = rows_at(chunk * BLK, BLK)
        swaps.append(remote(dn_in.at[at], got_dn.at[at], cs_s.at[chunk], cs_r.at[chunk], core))
    their = pl.ds(pl.multiple_of((1 - c) * own_rows, BLK), own_rows)
    mine = pl.ds(pl.multiple_of(c * own_rows, BLK), own_rows)
    branch = remote(br_in.at[their], got_br, bs.at[0], bs.at[1], core)

    def chunk_loads(n):
        at, slot = rows_at(order[n] * BLK, BLK), n % 2
        return [
            pltpu.make_async_copy(source.at[at], target.at[slot], ld.at[slot, k])
            for k, (source, target) in enumerate(
                ((resid_in, resid_s), (gl_in, gl_s), (dn_in, dn_s))
            )
        ]

    def load(number, source, target):
        copy = pltpu.make_async_copy(source, target, loc.at[number])
        copy.start()
        return copy

    loads = [chunk_loads(n) for n in range(n_chunks)]
    swaps[0].start()
    for n in range(2):
        for one in loads[n]:
            one.start()
    branch.start()
    for one in swaps[1:]:
        one.start()
    step(0, "start_first")
    step(0, "start_early", 0)
    step(0, "start_early", 1)
    step(1, "start_first")
    br_load = load(0, br_in.at[mine], br_s)
    wo_load = load(1, wo_in, wo)
    ctxc_load = load(2, ctxc_in, ctxc)
    step(1, "start_early", 0)
    step(1, "start_early", 1)
    late = [
        load(3, u_in, u),
        load(4, ctx_in, ctx),
        load(5, n1_in, n1),
        load(6, wqk_in, wqk),
        load(7, wvo_in, wvo),
        load(8, tok_in, tok),
    ]

    @pl.when(c == x)
    def _():
        half[...] = jnp.zeros_like(half)

    va[...] = jnp.zeros_like(va)
    vb[...] = jnp.zeros_like(vb)
    for s in range(2):
        va[pl.ds(4 + c + 2 * s, 1), :] = gb_ref[s]
    branch.wait()
    br_load.wait()
    for n, chunk in enumerate(order):
        slot = n % 2
        for one in loads[n]:
            one.wait()
        swaps[n].wait()
        at = rows_at(chunk * BLK, BLK)
        dn = dn_s[slot].astype(F32) + got_dn[at, :].astype(F32)
        resid = resid_s[slot]
        back, unit = norm_back(dn, resid, vec_ref[2:3, :])
        grad = gl_s[slot].astype(F32)
        after = grad + back
        low[at, :] = after.astype(BF)

        @pl.when(chunk // (n_chunks // 2) == c)
        def _(chunk=chunk, dn=dn, resid=resid, unit=unit, grad=grad, after=after):
            here_at = rows_at((chunk - c * (n_chunks // 2)) * BLK, BLK)
            dres[here_at, :] = after
            branches = br_s[here_at, :].astype(F32) + got_br[here_at, :].astype(F32)
            mixed[here_at, :] = (resid + branches + vec_ref[7:8, :]).astype(BF)
            va[0:1, :] += jnp.sum(dn * unit, axis=0, keepdims=True)
            va[1:2, :] += jnp.sum(dn, axis=0, keepdims=True)
            va[2:3, :] += jnp.sum(after, axis=0, keepdims=True)
            va[3:4, :] += jnp.sum(grad, axis=0, keepdims=True)

        if n + 2 < n_chunks:
            for one in loads[n + 2]:
                one.start()
        if n == 1:
            wo_load.wait()
            for i in range(HALF // BLK):
                lanes = slice(i * BLK, (i + 1) * BLK)
                rows = low[rows_at((1 - x) * SLOT + i * BLK, BLK), :]
                outgoing[:, :, lanes] = (
                    dot_tt(wo[1 - x], rows).astype(BF).reshape(-1, HD, BLK)
                )
                dctx[2, :, :, rows_at(x * HALF + i * BLK, BLK)] = (
                    dot_tt(wo[x], rows).astype(BF).reshape(-1, HD, BLK)
                )
            cross_c = remote(outgoing, half_c, xs.at[0], xs.at[1], x_peer)
            cross_c.start()
            step(0, "start_second", 0)
            step(0, "start_second", 1)
    mixed_copy = pltpu.make_async_copy(mixed, mixed_out, ws.at[0])
    mixed_copy.start()
    if custom:
        early_sum = SumOverAll(va, near_a, far_a, ass, ars)
        early_sum.start()
    heads = u.shape[2]
    cols = heads * HD
    blocks = g2o.shape[1:4]
    ctxc_load.wait()
    for s in range(2):
        g2o[s, :, :, :, cols:] = dot_tt(low[...], ctxc[s]).astype(BF).reshape(*blocks, cols)
    for i in range(SLOT // BLK):
        lanes = slice(i * BLK, (i + 1) * BLK)
        rows = low[rows_at(x * HALF + i * BLK, BLK), :]
        for s in range(2):
            dctx[s, :, :, lanes] = dot_tt(wo[s], rows).astype(BF).reshape(-1, HD, BLK)
    step(1, "start_second", 0)
    step(1, "start_second", 1)
    late[0].wait()
    late[1].wait()

    def attend_back(group, which, begin, end):
        def unit(h, carry):
            def put(k, lanes, value):
                du[group, k, h, :, lanes] = value

            attend_back_unit(
                lambda k, lanes: u[group, k, h, :, lanes],
                put,
                lambda k, lanes: feat_ref[which, k, :, lanes],
                ctx[group, h],
                dctx[group, h],
                lse_ref[group, h],
                dq,
            )
            return carry

        lax.fori_loop(begin, end, unit, 0)

    full_rows = pl.ds(pl.multiple_of(x * SLOT, SLOT), SLOT)
    part_rows = pl.ds(pl.multiple_of((1 - x) * SLOT, SLOT), SLOT)
    everything = slice(0, SLOT)

    def of_group(group, k, lanes):
        value = du[group, k, :, :, lanes]
        return value.reshape(cols, value.shape[-1])

    def weight_grad(slot, which, with_part):
        def rows_of(group):
            value = du[group, :, heads - 1 :] if which else du[group, :, : heads - 1]
            return value.reshape(-1, SLOT)

        out = dot_tt(n1[full_rows, :], rows_of(slot))
        if with_part:
            out += dot_tt(n1[part_rows, :], rows_of(2))
        out = out.astype(BF)
        if which:
            g2o[slot, :, :, :, :cols] = out.reshape(*blocks, cols)
        else:
            g01[slot] = out.reshape(*blocks, 2 * cols)

    attend_back(1 - x, 0, 0, heads)
    for one in late[2:]:
        one.wait()
    for which in range(2):
        weight_grad(1 - x, which, False)
        step(2 + which, "start_first")
        step(2 + which, "start_early", 0)
    step(0, "start_third")
    cross_c.wait()
    dctx[2, :, :, pl.ds(pl.multiple_of((1 - x) * HALF, HALF), HALF)] = half_c[...]
    attend_back(2, 1, 0, heads)

    def back_through(group, lanes, slot):
        two = du[group, 0:2, :, :, lanes]
        two = two.reshape(2 * cols, two.shape[-1])
        out = dot_tt(two, whole_weight(wqk, slot))
        return out + dot_tt(of_group(group, 2, lanes), whole_weight(wvo, slot)[:, :cols])

    theirs = pl.ds(pl.multiple_of((1 - x) * HALF, HALF), HALF)
    away[...] = back_through(2, theirs, x).astype(BF).reshape(away.shape)
    swap_away = remote(away.at[1 - c], away_got, bs.at[4], bs.at[5], core)
    swap_away.start()
    step(1, "start_third")
    swap_away.wait()
    away[c] = (away[c].astype(F32) + away_got[...].astype(F32)).astype(BF)
    cross = remote(away.at[c], half.at[c], xs.at[2], xs.at[3 + c], (dp, (1 - x) * 2 + x))
    cross.start()
    other = remote(away.at[1 - c], half.at[1 - c], xs.at[2], xs.at[4 - c], (dp, (1 - x) * 2 + x))
    attend_back(x, 0, 0, heads - 1)
    weight_grad(x, 0, True)
    step(2, "start_early", 1)
    step(2, "start_second", 1)
    step(2, "start_second", 0)
    attend_back(x, 0, heads - 1, heads)
    weight_grad(x, 1, True)
    step(3, "start_early", 1)
    step(3, "start_second", 1)
    step(3, "start_second", 0)
    if custom:
        early_sum.middle()

    def bias_sums(group):
        sums = [
            jnp.sum(of_group(group, k, everything).astype(F32), axis=1, keepdims=True)
            for k in (0, 2)
        ]
        return jnp.concatenate(sums, axis=0)

    columns = [bias_sums(x) + bias_sums(2), bias_sums(1 - x)]
    as_rows = jnp.concatenate(columns + [jnp.zeros((2 * cols, 6), F32)], axis=1).T
    for n, slot in enumerate((x, 1 - x)):
        vb[pl.ds(2 + c + 2 * slot, 1), : 2 * cols] = as_rows[n : n + 1, :]

    def back_rows(start, count):
        return pl.ds(pl.multiple_of(start, HALF), count)

    for i in range(SLOT // HALF):
        lanes = slice(i * HALF, (i + 1) * HALF)
        back = back_through(0, lanes, 0) + back_through(1, lanes, 1)
        part[back_rows(x * HALF + i * HALF, HALF), :] = back.astype(BF)
    back = back_through(2, back_rows(x * HALF, HALF), x)
    part[back_rows((1 - x) * SLOT, HALF), :] = back.astype(BF)
    swap = remote(part.at[their], got, bs.at[2], bs.at[3], core)
    swap.start()
    step(2, "start_third")
    swap.wait()
    cross.wait_send()

    @pl.when(c == 1 - x)
    def _():
        cross.wait_recv()
        other.wait_recv()

    for r in range(own_rows // BLK):
        rows = slice(r * BLK, (r + 1) * BLK)
        wide = rows_at(c * own_rows + r * BLK, BLK)
        dn = part[wide, :].astype(F32) + got[rows, :].astype(F32)
        place = r - (1 - x)
        also = (c == 1 - x) & (place >= 0) & (place < 2)
        dn += jnp.where(also, half[jnp.clip(place, 0, 1)].astype(F32), 0.0)
        back, unit = norm_back(dn, tok[rows, :].astype(F32), vec_ref[0:1, :])
        mixed_copy.wait() if r == 0 else None
        mixed[rows, :] = (dres[rows, :] + back).astype(BF)
        vb[0:1, :] += jnp.sum(dn * unit, axis=0, keepdims=True)
        vb[1:2, :] += jnp.sum(dn, axis=0, keepdims=True)
    ig_copy = pltpu.make_async_copy(mixed, ig_out, ws.at[1])
    ig_copy.start()
    if custom:
        late_sum = SumOverAll(vb, near_b, far_b, bss, brs)
        late_sum.start()
        va_out[...] = early_sum.finish()
        step(3, "start_third")
        late_sum.middle()
        squares = functools.reduce(jnp.add, [one.finish() for one in reduces])
        square[...] = jnp.full(square.shape, squares, F32)
        norm = SumOverAll(square, near_s, far_s, qss, qrs)
        norm.start()
        vb_out[...] = late_sum.finish()
        vector_squares = jnp.sum(va_out[...] * va_out[...], keepdims=True)
        vector_squares += jnp.sum(vb_out[...] * vb_out[...], keepdims=True)
        norm.middle()
        norm_ref[...] = jnp.sqrt(norm.finish() + vector_squares)
    ig_copy.wait()


def backward(saved, weights, given, tokens, vectors):
    (gl, n1, u, ctx, lse, features, ctxc, resid, wo, br, dn, gp, gf, gb) = saved
    rows, width = tokens.shape
    chip = 2 * rows
    heads = u.shape[2]
    cols = heads * HD
    custom = lax.axis_size("dp") == 8
    dma = pltpu.SemaphoreType.DMA
    out_shape = [sds((rows, width), BF)] * 2
    out_specs = [ANY, ANY]
    if custom:
        hidden = gp.shape[-1]
        part_rows = width // 8
        shapes = [(part_rows, n) for n in (hidden, hidden, 2 * cols, 2 * cols)]
        gf = gf.reshape(gp.shape)
        out_shape += [sds(s, F32) for s in shapes]
        out_shape += [sds((8, width), F32)] * 2 + [sds((8, 128), F32)]
        out_specs += [VM] * 7
        scratch = [pltpu.VMEM((2, 4, 2) + s, BF) for s in shapes[2:]]
        scratch += [
            pltpu.VMEM((n,) + shapes[a], BF) for a in range(2) for n in (BY_Y[a], 4 - BY_Y[a], 4)
        ]
        scratch += [
            pltpu.VMEM((n,) + shapes[a], BF)
            for a in range(4)
            for n in (BY_Y[a], 4 - BY_Y[a], 4, 4, 3)
        ]
        scratch += [
            *[pltpu.VMEM((8, width), F32)] * 2,
            *[pltpu.VMEM((8, 8, width), F32), pltpu.VMEM((4, 8, width), F32)] * 2,
            pltpu.VMEM((8, 8, 128), F32),
            pltpu.VMEM((4, 8, 128), F32),
            pltpu.VMEM((8, 128), F32),
            dma((2, 3)),
            dma((4, 9)),
            dma((4, 9)),
            *[dma((10,))] * 6,
        ]
    else:
        out_shape += [sds((8, width), F32)] * 2 + [sds((2, 1, 1, width, 2 * cols), BF)] * 2
        out_specs += [VM] * 4
        scratch = []
    scratch += [
        pltpu.VMEM((2, BLK, width), BF),
        pltpu.VMEM((2, BLK, width), F32),
        pltpu.VMEM((2, BLK, width), BF),
        pltpu.VMEM((chip, width), BF),
        pltpu.VMEM((rows, width), BF),
        pltpu.VMEM((rows, width), BF),
        pltpu.VMEM((rows, width), BF),
        pltpu.VMEM((chip, width), BF),
        pltpu.VMEM((rows, width), F32),
        pltpu.VMEM(ctx.shape, BF),
        pltpu.VMEM(ctxc.shape, BF),
        pltpu.VMEM(wo.shape, BF),
        pltpu.VMEM((heads, HD, HALF), BF),
        pltpu.VMEM((heads, HD, HALF), BF),
        pltpu.VMEM(u.shape, BF),
        pltpu.VMEM(ctx.shape, BF),
        pltpu.VMEM(n1.shape, BF),
        *[pltpu.VMEM(w.shape, BF) for w in weights],
        pltpu.VMEM((rows, width), BF),
        pltpu.VMEM(u.shape, BF),
        pltpu.VMEM((HD, SLOT), F32),
        pltpu.VMEM((2, BLK, width), BF),
        pltpu.VMEM((BLK, width), BF),
        pltpu.VMEM((2, BLK, width), BF),
        pltpu.VMEM((rows, width), BF),
        dma((9,)),
        dma((2, 3)),
        dma((chip // BLK,)),
        dma((chip // BLK,)),
        dma((6,)),
        dma((5,)),
        dma((2,)),
    ]
    return pl.pallas_call(
        functools.partial(backward_kernel, custom),
        out_shape=tuple(out_shape),
        in_specs=[ANY] * 4 + [VM, VM] + [ANY] * 7 + [VM] + [ANY] * 3 + [VM] + [ANY] * len(given),
        out_specs=tuple(out_specs),
        scratch_shapes=scratch,
        compiler_params=params(2),
        name="backward",
    )(gl, n1, u, ctx, lse, features, ctxc, resid, wo, br, dn, gp, gf, gb, *weights, tokens, vectors, *given)


def adamw_update(weight, moment_one, moment_two, gradient, step_rate, decay_rate):
    first_moment = DECAY_FIRST * moment_one + (1.0 - DECAY_FIRST) * gradient
    second_moment = DECAY_SECOND * moment_two + (1.0 - DECAY_SECOND) * gradient * gradient
    first_hat = first_moment / (1.0 - DECAY_FIRST**STEP)
    second_hat = second_moment / (1.0 - DECAY_SECOND**STEP)
    fresh_weight = weight - step_rate * (
        first_hat / (jnp.sqrt(second_hat) + ADAM_EPSILON) + decay_rate * weight
    )
    return (fresh_weight, first_moment, second_moment)


def update_kernel(*refs):
    (gp, gf, g01, g2o, va, vb, norm_ref), refs = refs[:7], refs[7:]
    cols = g2o.shape[1] // 2
    most = cols - HD
    old, new, norm_out = refs[:18], refs[18:36], refs[36]
    norm_out[0, 0] = norm_ref[0, 0]
    factor = CLIP_NORM / jnp.maximum(norm_ref[0:1, 0:1], CLIP_NORM)

    def update(number, grad, index, rate, decay):
        values = [old[3 * number + m][index] for m in range(3)]
        fresh = adamw_update(*values, factor * grad, rate, decay)
        for m in range(3):
            new[3 * number + m][index] = fresh[m]

    for k in range(3):
        grad = [g01[:, k * most : (k + 1) * most], g2o[:, k * HD : (k + 1) * HD]]
        update(0, jnp.concatenate(grad, axis=1), k, RATE_MATRIX, WEIGHT_DECAY)
    for number, grad in ((1, g2o[:, cols:].T), (2, gf[...]), (3, gp[...])):
        update(number, grad, ..., RATE_MATRIX, WEIGHT_DECAY)
    width = va.shape[1]
    parts = old[15].shape[1] // width

    def heads(k):
        rows = [vb[2 + t : 3 + t, k * cols : (k + 1) * cols] for t in range(parts)]
        return jnp.concatenate(rows, axis=1)

    vector_grad = jnp.concatenate(
        [vb[0:2, :], va[0:2, :], heads(0), heads(1), va[2:4, :]], axis=0
    )
    update(4, vector_grad, ..., RATE_VECTOR, 0.0)
    for t in range(parts):
        lanes = slice(t * width, (t + 1) * width)
        update(5, va[4 + t : 5 + t, :], (slice(None), lanes), RATE_VECTOR, 0.0)


def update_all(totals, va, vb, norm, states):
    return pl.pallas_call(
        update_kernel,
        out_shape=(*[sds(s.shape, F32) for s in states], sds((1, 1), F32)),
        in_specs=[VM] * (7 + len(states)),
        out_specs=(*[VM] * len(states), pl.BlockSpec(memory_space=pltpu.SMEM)),
        compiler_params=params(),
        name="update",
    )(*totals, va, vb, norm, *states)


def on_device(
    tokens,
    cotangent,
    segment_ids,
    valid,
    qkv_weight,
    qkv_moment1,
    qkv_moment2,
    out_weight,
    out_moment1,
    out_moment2,
    fc_weight,
    fc_moment1,
    fc_moment2,
    proj_weight,
    proj_moment1,
    proj_moment2,
    vector_params,
    vector_moment1,
    vector_moment2,
    fc_bias,
    fc_bias_moment1,
    fc_bias_moment2,
):
    custom = lax.axis_size("dp") == 8
    slot, swap = lax.axis_index("tensor") // 2, [(0, 2), (1, 3), (2, 0), (3, 1)]
    states = [jnp.transpose(s, (1, 0, 2)) for s in (qkv_weight, qkv_moment1, qkv_moment2)]
    states += [out_weight, out_moment1, out_moment2]
    states += [fc_weight, fc_moment1, fc_moment2]
    states += [s.T for s in (proj_weight, proj_moment1, proj_moment2)]
    states += [vector_params, vector_moment1, vector_moment2]
    states += [s[None] for s in (fc_bias, fc_bias_moment1, fc_bias_moment2)]
    shards = [states[0], states[3], states[6], states[9]]
    if not custom:
        parts = [
            jnp.concatenate([states[0][0], states[0][1]], axis=1),
            jnp.concatenate([states[0][2], shards[1].T], axis=1),
            *shards[2:],
        ]
        shards = []
        for part in parts:
            own = lax.all_gather(part.astype(BF), "dp", axis=0, tiled=True)
            other = lax.ppermute(own, "tensor", swap)
            shards.append(
                jnp.stack([jnp.where(slot == 0, own, other), jnp.where(slot == 0, other, own)])
            )
    saved, weights, given = forward(
        tokens,
        cotangent,
        valid,
        segment_ids,
        vector_params,
        states[15],
        shards,
    )
    outs = backward(saved, weights, given, tokens, vector_params)
    mixed, input_grad = outs[:2]
    if custom:
        totals, (va, vb, norm) = outs[2:6], outs[6:]
    else:
        va, vb, totals = *outs[2:4], []
        for g in [saved[11], saved[12], *outs[4:6]]:
            g = g.reshape(2, -1, g.shape[-1])
            mine = jnp.where(slot == 0, g[0], g[1])
            other = jnp.where(slot == 0, g[1], g[0])
            both = mine.astype(F32) + lax.ppermute(other, "tensor", swap).astype(F32)
            both = lax.psum_scatter(both.astype(BF), "dp", scatter_dimension=0, tiled=True)
            totals.append(both.astype(F32))
        squares = sum(jnp.sum(t * t) for t in totals)
        va, vb, squares = lax.psum((va, vb, squares), ("dp", "tensor"))
        squares += jnp.sum(va * va) + jnp.sum(vb * vb)
        norm = jnp.full((8, 128), jnp.sqrt(squares), F32)
    *new, grad_norm = update_all(totals, va, vb, norm, states)
    new[:3] = [jnp.transpose(s, (1, 0, 2)) for s in new[:3]]
    new[9:12] = [s.T for s in new[9:12]]
    new[15:18] = [s[0] for s in new[15:18]]
    return (mixed, input_grad, grad_norm.reshape(()), *new)


def solution(mesh):
    rows = P(("dp", "tensor"), None)
    by_rows = [P("dp", None, "tensor")] * 3
    by_out = [P("tensor", "dp")] * 3
    by_fc = [P("dp", "tensor")] * 3
    weights = by_rows + by_out + by_fc + by_out
    return jax.shard_map(
        on_device,
        mesh=mesh,
        in_specs=(rows, rows, P("dp"), P(("dp", "tensor")), *weights, *[P()] * 6),
        out_specs=(rows, rows, P(), *weights, *[P()] * 6),
        check_vma=False,
    )
```

```python
import functools
import math

import jax
import jax.numpy as jnp
from jax import lax
from jax.experimental import pallas as pl
from jax.experimental.pallas import tpu as pltpu
from jax.sharding import PartitionSpec as P

HD = 64
SLOT = 1024
STEP = 10
NORM_EPSILON = 1e-05
MASK_FILL = -1e30
DECAY_FIRST = 0.5
DECAY_SECOND = 0.5
ADAM_EPSILON = 1e-08
WEIGHT_DECAY = 0.1
CLIP_NORM = 1.0
RATE_MATRIX = 0.04
RATE_VECTOR = 0.3

MESH = pl.DeviceIdType.MESH
BF = jnp.bfloat16
F32 = jnp.float32
HALF = SLOT // 2
BLK = 256
VMEM_LIMIT = 58 * 2**20
LOG2E = math.log2(math.e)
SCORE_SCALE = float(HD) ** (-0.5)
SCORE_SCALE2 = SCORE_SCALE * LOG2E


def dot_nn(a, b):
    return lax.dot_general(a, b, (((1,), (0,)), ((), ())), preferred_element_type=F32)


def dot_nt(a, b):
    return lax.dot_general(a, b, (((1,), (1,)), ((), ())), preferred_element_type=F32)


def dot_tn(a, b):
    return lax.dot_general(a, b, (((0,), (0,)), ((), ())), preferred_element_type=F32)


def dot_tt(a, b):
    return lax.dot_general(a, b, (((0,), (1,)), ((), ())), preferred_element_type=F32)


def params(collective_id=None):
    if collective_id is None:
        return pltpu.CompilerParams(vmem_limit_bytes=VMEM_LIMIT)
    return pltpu.CompilerParams(
        vmem_limit_bytes=VMEM_LIMIT, collective_id=collective_id, has_side_effects=True
    )


VM = pl.BlockSpec(memory_space=pltpu.VMEM)
ANY = pl.BlockSpec(memory_space=pl.ANY)


def sds(shape, dtype):
    return jax.ShapeDtypeStruct(shape, dtype)


def here():
    t = lax.axis_index("tensor")
    return lax.axis_index("dp"), t // 2, t % 2


def announce(ids):
    sem = pltpu.get_barrier_semaphore()
    for one in ids:
        pl.semaphore_signal(sem, inc=1, device_id=one, device_id_type=MESH)


def await_others(ids):
    pl.semaphore_wait(pltpu.get_barrier_semaphore(), len(ids))


def greet(ids):
    announce(ids)
    await_others(ids)


def remote(src, dst, send_sem, recv_sem, target):
    return pltpu.make_async_remote_copy(
        src_ref=src,
        dst_ref=dst,
        send_sem=send_sem,
        recv_sem=recv_sem,
        device_id=target,
        device_id_type=MESH,
    )


def rows_at(start, size):
    return pl.ds(pl.multiple_of(start, size), size)


def norm_parts(values):
    centered = values - jnp.mean(values, axis=-1, keepdims=True)
    variance = jnp.mean(centered * centered, axis=-1, keepdims=True)
    scale = lax.rsqrt(variance + NORM_EPSILON)
    return centered * scale, scale


class Gather:
    def __init__(self, shard, whole, part, by_y, ss, rs):
        dp, x, c = here()
        z, y = dp // 2, dp % 2
        along, x_peer, y_peer, _ = neighbours()
        shard = shard.at[part]
        block = whole.at[x, z, y, part]
        column = whole.at[x, :, y, part]
        from_x = whole.at[1 - x, pl.ds(0, by_y), y, part]
        from_y = whole.at[x, pl.ds(by_y, 4 - by_y), 1 - y, part]
        self.along = [remote(shard, block, ss.at[k], rs.at[k], along[k]) for k in range(3)]
        self.beside = [
            remote(column, column, ss.at[3], rs.at[3], x_peer),
            remote(column, column, ss.at[4], rs.at[4], y_peer),
        ]
        self.passed = [
            remote(from_x, from_x, ss.at[5], rs.at[5], y_peer),
            remote(from_y, from_y, ss.at[6], rs.at[6], x_peer),
        ]

    def start_along(self):
        for one in self.along:
            one.start()

    def start_beside(self):
        for one in self.along:
            one.wait()
        for one in self.beside:
            one.start()

    def start_passed(self):
        for one in self.beside:
            one.wait()
        for one in self.passed:
            one.start()

    def finish(self):
        for one in self.passed:
            one.wait()


class GatherBeside:
    def __init__(self, shard, whole, start, size, by_y, ss, rs):
        dp, x, c = here()
        z, y = dp // 2, dp % 2
        along, x_peer, y_peer, _ = neighbours()
        part = pl.ds(start, size)
        block = whole.at[x, z, y, part]
        from_x = whole.at[1 - x, z, y, pl.ds(start, by_y)]
        from_y = whole.at[x, z, 1 - y, pl.ds(start + by_y, size - by_y)]
        four = whole.at[:, z, :, part]
        self.beside = [
            remote(shard.at[part], block, ss.at[3], rs.at[3], x_peer),
            remote(shard.at[part], block, ss.at[4], rs.at[4], y_peer),
        ]
        self.passed = [
            remote(from_x, from_x, ss.at[5], rs.at[5], y_peer),
            remote(from_y, from_y, ss.at[6], rs.at[6], x_peer),
        ]
        self.along = [remote(four, four, ss.at[k], rs.at[k], along[k]) for k in range(3)]

    def start_beside(self):
        for one in self.beside:
            one.start()

    def start_passed(self):
        for one in self.beside:
            one.wait()
        for one in self.passed:
            one.start()

    def start_along(self):
        for one in self.passed:
            one.wait()
        for one in self.along:
            one.start()

    def finish(self):
        for one in self.along:
            one.wait()


def neighbours():
    dp, x, c = here()
    z, y = dp // 2, dp % 2
    me = x * 2 + c
    along = [(lax.rem(z + k, 4) * 2 + y, me) for k in (1, 2, 3)]
    return along, (dp, (1 - x) * 2 + c), (z * 2 + 1 - y, me), (dp, x * 2 + 1 - c)


def whole_weight(ref, slot):
    value = ref[slot]
    return value.reshape(-1, value.shape[-1])


MASKED = -(2.0**100)
ATT = 512


def segment_features(segments):
    numbers = lax.broadcasted_iota(jnp.int32, (16, segments.shape[1]), 0).astype(F32) + 1.0
    query = jnp.where(segments >= numbers, 1.0, 0.0)
    key = jnp.where(segments < numbers, MASKED, 0.0)
    return query.astype(BF), key.astype(BF)


def causal(scores):
    keys = lax.broadcasted_iota(jnp.int32, scores.shape, 0)
    queries = lax.broadcasted_iota(jnp.int32, scores.shape, 1)
    return jnp.where(keys <= queries, scores, MASK_FILL)


def attend_unit(q, k, v):
    for i in range(SLOT // ATT):
        cols = slice(i * ATT, (i + 1) * ATT)
        query = q(cols)
        scores = []
        for j in range(i + 1):
            raw = dot_tn(k(slice(j * ATT, (j + 1) * ATT)), query) * SCORE_SCALE2
            scores.append(causal(raw) if j == i else raw)
        top = functools.reduce(jnp.maximum, [jnp.max(s, axis=0, keepdims=True) for s in scores])
        exps = [jnp.exp2(s - top) for s in scores]
        total = functools.reduce(jnp.add, [jnp.sum(e, axis=0, keepdims=True) for e in exps])
        low = jnp.concatenate([e.astype(BF) for e in exps], axis=0)
        yield cols, dot_nn(v(slice(0, (i + 1) * ATT)), low) / total, top + jnp.log2(total)


GELU_C = math.sqrt(2.0 / math.pi)
GELU_A = 0.044715


def forward_kernel(custom, *refs):
    (tok_ref, cot_ref, valid_ref, seg_ref, vec_ref, fb_ref), refs = refs[:6], refs[6:]
    shards, refs = refs[:4], refs[4:]
    (gl_out, n1_out, u_out, ctx_out, lse_out, feat_out, ctxc_out, resid_out, wo_out, br_out, dn_out, gp_out,
     gf_out, gb_ref), refs = refs[:14], refs[14:]
    if custom:
        weights_out, given, refs = refs[:2], refs[2:6], refs[6:]
        lows, refs = refs[:4], refs[4:]
        wholes, refs = refs[:4], refs[4:]
        gs, gr, ps, pr, refs = *refs[:4], refs[4:]
    else:
        wholes = shards
    (tk, gl, n1, u, ctx, lse, features, ctxc, resid, wo, n2, half, part, got, act, dpre, gp, cols, loc, ts, tr, xs,
     cs_s, cs_r) = refs
    wqk, wvo, wf, wp = wholes
    dp, x, c = here()
    core = (dp, x * 2 + 1 - c)
    x_peer = (dp, (1 - x) * 2 + c)
    across = [(dp, (1 - x) * 2), (dp, (1 - x) * 2 + 1)]
    rows = tok_ref.shape[0]
    first = x * HALF
    gathers = []
    if custom:
        z, y = dp // 2, dp % 2
        along, _, y_peer, _ = neighbours()
        others = [core, *across, *along, y_peer]
        announce(others)
        lows[0][...] = jnp.concatenate([shards[0][0], shards[0][1]], axis=1).astype(BF)
        lows[1][...] = jnp.concatenate([shards[0][2], shards[1][...].T], axis=1).astype(BF)
        lows[2][...] = shards[2][...].astype(BF)
        lows[3][...] = shards[3][...].astype(BF)
        await_others(others)
        pieces = [(a, k, 2, 2) for a in range(2) for k in range(2)]
        pieces += [(2, 0, 2, 3), (2, 1, 2, 3), (3, 0, 2, 3)]
        for number, (a, k, parts, by_y) in enumerate(pieces):
            size = lows[a].shape[0] // parts
            gathers.append(
                Gather(
                    lows[a], wholes[a], pl.ds(k * size, size), by_y, gs.at[number], gr.at[number]
                )
            )
        size = lows[3].shape[0] // 2
        gathers.append(GatherBeside(lows[3], wholes[3], size, size, 32, gs.at[7], gr.at[7]))
    else:
        greet([core, *across])

    def step(number, what):
        if custom:
            getattr(gathers[number], what)()

    own_rows = pl.ds(pl.multiple_of(first + c * rows, BLK), rows)
    gl_rows = pl.ds(pl.multiple_of(c * rows, BLK), rows)
    mine_tok = pltpu.make_async_copy(tok_ref, tk.at[own_rows], loc.at[0])
    cot_load = pltpu.make_async_copy(cot_ref, part.at[pl.ds(0, rows)], loc.at[9])
    swap_tok = remote(tok_ref, tk.at[own_rows], ts.at[0], tr.at[0], core)
    swap_grad = remote(gl.at[gl_rows], gl.at[gl_rows], ts.at[1], tr.at[1], core)
    source = [
        tok_ref.at[pl.ds(pl.multiple_of((1 - x) * BLK + k * BLK, BLK), BLK)] for k in range(2)
    ]
    there = [
        tk.at[pl.ds(pl.multiple_of(x * (SLOT + HALF) + k * BLK, BLK), BLK)] for k in range(2)
    ]
    halves = [remote(source[k], there[k], ts.at[2 + k], tr.at[2], across[k]) for k in range(2)]
    landed = tk.at[pl.ds(pl.multiple_of((1 - x) * (SLOT + HALF) + c * BLK, BLK), BLK)]
    handed = remote(landed, landed, ts.at[4], tr.at[3], core)

    step(0, "start_along")
    step(7, "start_beside")
    step(1, "start_along")
    mine_tok.start()
    swap_tok.start()
    cot_load.start()

    @pl.when(c == 1 - x)
    def _():
        for one in halves:
            one.start()

    if custom:
        for a in range(4):
            wholes[a][x, z, y] = lows[a][...]

    def out_copy(number, ref, out):
        copy = pltpu.make_async_copy(ref, out, loc.at[number])
        copy.start()
        return copy

    cols[...] = vec_ref[...].T
    gain, shift = vec_ref[0:1, :], vec_ref[1:2, :]

    def norm_rows(start, count):
        def norm(i, carry):
            at = rows_at(start + i * BLK, BLK)
            unit, _ = norm_parts(tk[at, :].astype(F32))
            n1[at, :] = (unit * gain + shift).astype(BF)
            return carry

        lax.fori_loop(0, count // BLK, norm, 0)

    mine_tok.wait()
    norm_rows(first + c * rows, rows)
    swap_tok.wait()
    step(0, "start_beside")
    step(2, "start_along")
    norm_rows(first + (1 - c) * rows, rows)
    step(1, "start_beside")
    step(3, "start_along")

    mask = jnp.broadcast_to(valid_ref[...].reshape(1, rows).astype(F32), (8, rows)).T[:, 0:1]
    cot_load.wait()
    gl[gl_rows, :] = (part[:rows, :].astype(F32) * mask).astype(BF)
    swap_grad.start()
    for k, row in enumerate((2 * x, 1)):
        at = pl.ds(pl.multiple_of(row * SLOT, SLOT), SLOT)
        query, key = segment_features(seg_ref[at].reshape(1, SLOT).astype(F32))
        features[k, 0] = query
        features[k, 1] = key

    halves[0].wait_recv()
    handed.start()
    step(2, "start_beside")
    step(4, "start_along")
    handed.wait()
    norm_rows((1 - x) * (SLOT + HALF), HALF)
    step(3, "start_beside")
    step(5, "start_along")
    step(7, "start_passed")
    for number in range(4):
        step(number, "start_passed")

    heads = u.shape[2]
    wide = heads * HD

    def project(group, slot, first_row):
        bias_rows = pl.ds(pl.multiple_of((c + 2 * slot) * wide, HD), wide)
        query_bias, value_bias = cols[bias_rows, 4:5], cols[bias_rows, 5:6]

        def chunk(i, carry):
            lanes = rows_at(i * BLK, BLK)
            values = n1[rows_at(first_row + i * BLK, BLK), :]
            two = dot_tt(whole_weight(wqk, slot), values)
            value = dot_tt(whole_weight(wvo, slot)[:, :wide], values) + value_bias
            for k, out in enumerate((two[:wide] + query_bias, two[wide:], value)):
                u[group, k, :, :, lanes] = out.reshape(-1, HD, BLK).astype(BF)
            return carry

        lax.fori_loop(0, SLOT // BLK, chunk, 0)

    def attend(group, which, begin, end):
        def unit(h, carry):
            for lanes, context, log_total in attend_unit(
                lambda s: jnp.concatenate([u[group, 0, h, :, s], features[which, 0, :, s]], axis=0),
                lambda s: jnp.concatenate([u[group, 1, h, :, s], features[which, 1, :, s]], axis=0),
                lambda s: u[group, 2, h, :, s],
            ):
                ctx[group, h, :, lanes] = context.astype(BF)
                lse[group, h, :, lanes] = log_total
            return carry

        lax.fori_loop(begin, end, unit, 0)

    project(x, x, x * SLOT)
    step(4, "start_beside")
    step(6, "start_along")
    attend(x, 0, 0, 1)
    step(5, "start_beside")
    step(7, "start_along")
    attend(x, 0, 1, heads)
    step(4, "start_passed")
    project(2, x, (1 - x) * SLOT)
    step(6, "start_beside")
    attend(2, 1, 0, heads)
    theirs = pl.ds(pl.multiple_of((1 - x) * HALF, HALF), HALF)
    cross = remote(ctx.at[2, :, :, theirs], half, xs.at[0], xs.at[1], x_peer)
    cross.start()
    for number in range(4):
        step(number, "finish")
    step(5, "start_passed")
    project(1 - x, 1 - x, x * SLOT)
    copies = [out_copy(1, n1, n1_out), out_copy(2, u, u_out)]
    for s in range(2):
        wo[s] = whole_weight(wvo, s)[:, wide:]
    attend(1 - x, 0, 0, 1)
    step(6, "start_passed")
    attend(1 - x, 0, 1, heads)
    copies += [out_copy(3, ctx, ctx_out), out_copy(4, lse, lse_out), out_copy(5, features, feat_out)]
    copies.append(out_copy(8, wo, wo_out))
    if custom:
        copies += [out_copy(6 + a, wholes[a], weights_out[a]) for a in range(2)]

    @pl.when(c == 1 - x)
    def _():
        for one in halves:
            one.wait_send()

    chunks = []

    def send(chunk, values):
        at = rows_at(chunk * BLK, BLK)
        part[at, :] = values.astype(BF)
        copy = remote(part.at[at], got.at[at], cs_s.at[chunk], cs_r.at[chunk], core)
        copy.start()
        chunks.append((chunk, copy))

    def context_of(group, lanes):
        value = ctx[group, :, :, lanes]
        return value.reshape(-1, value.shape[-1])

    for i in range(SLOT // BLK):
        lanes = slice(i * BLK, (i + 1) * BLK)
        chunk = x * 2 + i
        at = rows_at(chunk * BLK, BLK)
        zero, one = context_of(0, lanes), context_of(1, lanes)
        send(chunk, dot_tt(zero, wo[0]) + dot_tt(one, wo[1]))
        ctxc[0, :, at] = zero
        ctxc[1, :, at] = one
    cross.wait()
    for i in range(HALF // BLK):
        chunk = (1 - x) * 4 + i
        at = rows_at(chunk * BLK, BLK)
        own = context_of(2, rows_at(x * HALF + i * BLK, BLK))
        other = half[:, :, i * BLK : (i + 1) * BLK].reshape(-1, BLK)
        send(chunk, dot_tt(own, wo[x]) + dot_tt(other, wo[1 - x]))
        ctxc[x, :, at] = own
        ctxc[1 - x, :, at] = other
    copies.append(out_copy(10, ctxc, ctxc_out))
    swap_grad.wait()
    copies.append(out_copy(11, gl, gl_out))
    for chunk, copy in chunks:
        copy.wait()
        at = rows_at(chunk * BLK, BLK)
        tokens = tk[rows_at(first + chunk * BLK, BLK), :].astype(F32)
        summed = part[at, :].astype(F32) + got[at, :].astype(F32)
        after = tokens + summed + vec_ref[6:7, :]
        resid[at, :] = after
        unit, _ = norm_parts(after)
        n2[at, :] = (unit * vec_ref[2:3, :] + vec_ref[3:4, :]).astype(BF)
    copies.append(out_copy(12, resid, resid_out))
    step(4, "finish")
    step(5, "finish")

    hidden = wf.shape[-1]
    gb_ref[...] = jnp.zeros_like(gb_ref)
    bias_of = [
        fb_ref[:, pl.ds(pl.multiple_of((c + 2 * s) * hidden, hidden), hidden)] for s in range(2)
    ]
    tile = HALF
    tiles = 2 * rows // tile

    def activate(i, carry):
        at = rows_at(i * tile, tile)
        n2_rows = n2[at, :]
        for s in range(2):
            lanes = slice(s * hidden, (s + 1) * hidden)
            v = dot_nn(n2_rows, whole_weight(wf, s)) + bias_of[s]
            square = v * v
            t = jnp.tanh(v * (GELU_C + (GELU_C * GELU_A) * square))
            cdf = 0.5 + 0.5 * t
            act[at, lanes] = (v * cdf).astype(BF)
            slope = cdf + (cdf * (1.0 - t)) * (v * (GELU_C + (3.0 * GELU_C * GELU_A) * square))
            dpre[at, lanes] = slope.astype(BF)
        return carry

    lax.fori_loop(0, tiles, activate, 0)
    blocks = gp.shape[1:4]

    for s in range(2):
        out = dot_tn(gl[...], act[:, s * hidden : (s + 1) * hidden]).astype(BF)
        gp[s] = out.reshape(*blocks, hidden)
        copies.append(out_copy(15 + s, gp.at[s], gp_out.at[s]))
    passing = []
    if custom:
        low, high = pl.ds(0, 2), pl.ds(2, 2)
        pieces = [
            (gp.at[1 - x, low, 1 - y], y_peer),
            (gp.at[1 - x, high, 1 - y], x_peer),
            (gp.at[1 - x, high, y], x_peer),
            (gp.at[x, low, 1 - y], y_peer),
        ]
        for k, (piece, peer) in enumerate(pieces):
            passing.append(remote(piece, given[k], ps.at[k], pr.at[k], peer))
            passing[-1].start()
    step(6, "finish")
    step(7, "finish")

    def forward_back(i, carry):
        at = rows_at(i * tile, tile)
        gl_now = gl[at, :]
        for s in range(2):
            lanes = slice(s * hidden, (s + 1) * hidden)
            up = dot_nn(gl_now, whole_weight(wp, s))
            d = (up * dpre[at, lanes].astype(F32)).astype(BF)
            dpre[at, lanes] = d
            gb_ref[s] += jnp.sum(d.astype(F32), axis=0, keepdims=True)
        br = dot_nt(act[at, :hidden], whole_weight(wp, 0))
        br += dot_nt(act[at, hidden:], whole_weight(wp, 1))
        part[at, :] = br.astype(BF)
        dn = dot_nt(dpre[at, :hidden], whole_weight(wf, 0))
        dn += dot_nt(dpre[at, hidden:], whole_weight(wf, 1))
        got[at, :] = dn.astype(BF)
        return carry

    lax.fori_loop(0, tiles, forward_back, 0)
    copies += [out_copy(13, got, dn_out), out_copy(14, part, br_out)]
    width = n2.shape[1]

    for s in range(2):
        at = slice(s * width, (s + 1) * width)
        tk[at, :] = dot_tn(n2[...], dpre[:, s * hidden : (s + 1) * hidden]).astype(BF)
        copies.append(out_copy(17 + s, tk.at[at], gf_out.at[s]))
    for copy in copies + passing:
        copy.wait()


def forward(tokens, cotangent, valid, segments, vectors, fc_bias, shards):
    rows, width = tokens.shape
    chip = 2 * rows
    custom = lax.axis_size("dp") == 8
    dma = pltpu.SemaphoreType.DMA
    if custom:
        cols = shards[0].shape[2]
        hidden = shards[2].shape[1]
        part_rows = shards[2].shape[0]
        flat = [(part_rows, n) for n in (2 * cols, 2 * cols, hidden, hidden)]
        wholes = [(2, 4, 2) + s for s in flat]
        more_out = [sds(w, BF) for w in wholes[:2]] + [sds((2, part_rows, hidden), BF)] * 4
        more = [pltpu.VMEM(s, BF) for s in flat] + [pltpu.VMEM(w, BF) for w in wholes]
        more += [dma((8, 7)), dma((8, 7)), dma((4,)), dma((4,))]
        grad_shape = wholes[3]
    else:
        cols, hidden = shards[0].shape[2] // 2, shards[2].shape[2]
        more_out, more = [], []
        grad_shape = (2, 1, 1, width, hidden)
    heads = cols // HD
    shapes = [
        ((chip, width), BF),
        ((2 * SLOT, width), BF),
        ((3, 3, heads, HD, SLOT), BF),
        ((3, heads, HD, SLOT), BF),
        ((3, heads, 1, SLOT), F32),
        ((2, 2, 16, SLOT), BF),
        ((2, cols, chip), BF),
        ((chip, width), F32),
        ((2, width, cols), BF),
    ]
    out_shape = [sds(*s) for s in shapes]
    out_shape += [sds((chip, width), BF)] * 2 + [sds(grad_shape, BF), sds((2, width, hidden), BF)]
    out_shape += [sds((2, 1, hidden), F32)] + more_out
    outs = pl.pallas_call(
        functools.partial(forward_kernel, custom),
        out_shape=tuple(out_shape),
        in_specs=[ANY, ANY] + [VM] * (4 + len(shards)),
        out_specs=(*[ANY] * 13, VM, *[ANY] * len(more_out)),
        scratch_shapes=more
        + [
            pltpu.VMEM((2 * SLOT, width), BF),
            *[pltpu.VMEM(*s) for s in shapes],
            pltpu.VMEM((chip, width), BF),
            pltpu.VMEM((heads, HD, HALF), BF),
            pltpu.VMEM((chip, width), BF),
            pltpu.VMEM((chip, width), BF),
            pltpu.VMEM((chip, 2 * hidden), BF),
            pltpu.VMEM((chip, 2 * hidden), BF),
            pltpu.VMEM(grad_shape, BF),
            pltpu.VMEM((width, 8), F32),
            dma((19,)),
            dma((5,)),
            dma((4,)),
            dma((2,)),
            dma((chip // BLK,)),
            dma((chip // BLK,)),
        ],
        compiler_params=params(1),
        name="forward",
    )(tokens, cotangent, valid, segments, vectors, fc_bias, *shards)
    if custom:
        return outs[:14], outs[14:16], outs[16:]
    return outs[:14], shards[:2], []


class Reduce:
    def __init__(self, grad, part, by_y, local, given, total, bufs, loc, ss, rs):
        dp, x, c = here()
        z, y = dp // 2, dp % 2
        along, x_peer, y_peer, _ = neighbours()
        low, high = pl.ds(0, by_y), pl.ds(by_y, 4 - by_y)
        self.z, self.total = z, total
        self.r1y, self.r1x, self.r2x, self.r2y, self.r3 = bufs
        views = [
            grad.at[1 - x, low, y, part],
            grad.at[x, high, 1 - y, part],
            grad.at[x, :, y, part],
        ]
        self.loads = []
        self.mid_x, self.mid_y, self.own = views
        if local is not None:
            self.loads = [
                pltpu.make_async_copy(views[k], local[k], loc.at[k]) for k in range(3)
            ]
            self.mid_x, self.mid_y, self.own = local
        self.first = [
            remote(grad.at[1 - x, low, 1 - y, part], self.r1y, ss.at[0], rs.at[0], y_peer),
            remote(grad.at[1 - x, high, 1 - y, part], self.r1x, ss.at[1], rs.at[1], x_peer),
        ]
        self.early = [
            remote(grad.at[1 - x, high, y, part], self.r2x.at[high], ss.at[2], rs.at[2], x_peer),
            remote(grad.at[x, low, 1 - y, part], self.r2y.at[low], ss.at[3], rs.at[3], y_peer),
        ]
        targets = (self.r1y, self.r1x, self.r2x.at[high], self.r2y.at[low])
        for k, came in enumerate(given or ()):
            copies = (self.first, self.early)[k // 2]
            copies[k % 2] = pltpu.make_async_copy(came, targets[k], rs.at[k])
        self.second = [
            remote(self.mid_x, self.r2x.at[low], ss.at[4], rs.at[4], x_peer),
            remote(self.mid_y, self.r2y.at[high], ss.at[5], rs.at[5], y_peer),
        ]
        self.third = [
            remote(
                self.own.at[lax.rem(z + k + 1, 4)], self.r3.at[k], ss.at[6 + k], rs.at[6 + k], along[k]
            )
            for k in range(3)
        ]

    def start_first(self):
        for one in self.loads:
            one.start()
        for one in self.first:
            one.start()

    def start_early(self, which):
        self.early[which].start()

    def start_second(self, which):
        self.first[which].wait()
        if self.loads:
            self.loads[which].wait()
        mid, came = ((self.mid_x, self.r1y), (self.mid_y, self.r1x))[which]
        mid[...] = (mid[...].astype(F32) + came[...].astype(F32)).astype(BF)
        self.second[which].start()

    def start_third(self):
        for one in self.early + self.second + self.loads[2:]:
            one.wait()
        for k in range(4):
            place = lax.rem(self.z + k + 1, 4)
            summed = (
                self.own[place].astype(F32)
                + self.r2x[place].astype(F32)
                + self.r2y[place].astype(F32)
            )
            if k < 3:
                self.own[place] = summed.astype(BF)
                self.third[k].start()
            else:
                self.total[...] = summed

    def finish(self):
        for one in self.third:
            one.wait()
        total = self.total[...]
        for k in range(3):
            total = total + self.r3[k].astype(F32)
        self.total[...] = total
        return jnp.sum(total * total)


class ReduceAlong:
    def __init__(self, grad, start, by_y, total, bufs, loc, ss, rs):
        dp, x, c = here()
        z, y = dp // 2, dp % 2
        along, x_peer, y_peer, _ = neighbours()
        self.place, self.total = (x, y), total
        self.own, self.rz, self.r1y, self.r1x, self.r2x, self.r2y = bufs
        size = self.own.shape[2]
        part = pl.ds(start, size)
        low, high = pl.ds(0, by_y), pl.ds(by_y, size - by_y)
        own = self.own
        self.load = pltpu.make_async_copy(grad.at[:, z, :, part], own, loc)
        self.along = [
            remote(
                grad.at[:, lax.rem(z + k + 1, 4), :, part], self.rz.at[k], ss.at[k], rs.at[k], along[k]
            )
            for k in range(3)
        ]
        self.first = [
            remote(own.at[1 - x, 1 - y, low], self.r1y, ss.at[3], rs.at[3], y_peer),
            remote(own.at[1 - x, 1 - y, high], self.r1x, ss.at[4], rs.at[4], x_peer),
        ]
        self.early = [
            remote(own.at[1 - x, y, high], self.r2x.at[high], ss.at[5], rs.at[5], x_peer),
            remote(own.at[x, 1 - y, low], self.r2y.at[low], ss.at[6], rs.at[6], y_peer),
        ]
        self.mid = (own.at[1 - x, y, low], own.at[x, 1 - y, high])
        self.second = [
            remote(self.mid[0], self.r2x.at[low], ss.at[7], rs.at[7], x_peer),
            remote(self.mid[1], self.r2y.at[high], ss.at[8], rs.at[8], y_peer),
        ]

    def start_along(self):
        self.load.start()
        for one in self.along:
            one.start()

    def start_first(self):
        self.load.wait()
        for one in self.along:
            one.wait()
        for a in range(2):
            for b in range(2):
                total = self.own[a, b].astype(F32)
                for k in range(3):
                    total += self.rz[k, a, b].astype(F32)
                self.own[a, b] = total.astype(BF)
        for one in self.first + self.early:
            one.start()

    def start_second(self):
        for k, came in enumerate((self.r1y, self.r1x)):
            self.first[k].wait()
            mid = self.mid[k]
            mid[...] = (mid[...].astype(F32) + came[...].astype(F32)).astype(BF)
            self.second[k].start()

    def finish(self):
        for one in self.early + self.second:
            one.wait()
        x, y = self.place
        total = self.own[x, y].astype(F32) + self.r2x[...].astype(F32) + self.r2y[...].astype(F32)
        self.total[...] = total
        return jnp.sum(total * total)


def eight_peers():
    dp, x, c = here()
    z, y = dp // 2, dp % 2
    peers = []
    for k in range(1, 8):
        kx, ky, kc = k // 4, k // 2 % 2, k % 2
        there = ((1 - x if kx else x), (1 - y if ky else y), (1 - c if kc else c))
        peers.append((z * 2 + there[1], there[0] * 2 + there[2]))
    return peers


class SumOverAll:
    def __init__(self, value, near, far, ss, rs):
        dp, x, c = here()
        z, y = dp // 2, dp % 2
        self.value, self.near, self.far = value, near, far
        self.me, self.z = x * 4 + y * 2 + c, z
        self.one = [
            remote(value, near.at[self.me], ss.at[k], rs.at[k], peer)
            for k, peer in enumerate(eight_peers())
        ]
        self.two = [
            remote(value, far.at[z], ss.at[7 + k], rs.at[7 + k], peer)
            for k, peer in enumerate(neighbours()[0])
        ]

    def start(self):
        for one in self.one:
            one.start()
        self.near[self.me] = self.value[...]

    def middle(self):
        for one in self.one:
            one.wait()
        self.value[...] = functools.reduce(jnp.add, [self.near[k] for k in range(8)])
        for one in self.two:
            one.start()
        self.far[self.z] = self.value[...]

    def finish(self):
        for one in self.two:
            one.wait()
        return functools.reduce(jnp.add, [self.far[k] for k in range(4)])


def attend_back_unit(u, out, features, ctx, dctx, lse, dq_ref):
    blocks = SLOT // BLK
    delta = jnp.sum(dctx.astype(F32) * ctx.astype(F32), axis=0, keepdims=True)
    for j in range(blocks):
        keys = slice(j * BLK, (j + 1) * BLK)
        after = slice(j * BLK, SLOT)
        k, v = u(1, keys), u(2, keys)
        wide = jnp.concatenate([k, features(1, keys)], axis=0)
        probs, dscores = [], []
        for i in range(j, blocks):
            cols = slice(i * BLK, (i + 1) * BLK)
            query = jnp.concatenate([u(0, cols), features(0, cols)], axis=0)
            raw = dot_tn(wide, query) * SCORE_SCALE2 - lse[:, cols]
            prob = jnp.exp2(causal(raw) if i == j else raw)
            dprob = dot_tn(v, dctx[:, cols])
            probs.append(prob.astype(BF))
            dscores.append((prob * (dprob - delta[:, cols])).astype(BF))
        probs, dscores = jnp.concatenate(probs, axis=1), jnp.concatenate(dscores, axis=1)
        dq = dot_nn(k, dscores)
        if j == 0:
            dq_ref[...] = dq
        else:
            dq_ref[:, after] += dq
        out(1, keys, (dot_nt(u(0, after), dscores) * SCORE_SCALE).astype(BF))
        out(2, keys, dot_nt(dctx[:, after], probs).astype(BF))
    out(0, slice(0, SLOT), (dq_ref[...] * SCORE_SCALE).astype(BF))


BY_Y = (2, 2, 3, 3)


def norm_back(dn, values, gain):
    unit, scale = norm_parts(values)
    e = dn * gain
    back = scale * (
        e
        - jnp.mean(e, axis=-1, keepdims=True)
        - unit * jnp.mean(e * unit, axis=-1, keepdims=True)
    )
    return back, unit


def backward_kernel(custom, *refs):
    (gl_in, n1_in, u_in, ctx_in, lse_ref, feat_ref, ctxc_in, resid_in, wo_in, br_in, dn_in, gp_in, gf_in, gb_ref,
     wqk_in, wvo_in, tok_in, vec_ref), refs = refs[:18], refs[18:]
    given = None
    if custom:
        given, refs = (refs[:4], None, None, None), refs[4:]
    (mixed_out, ig_out), refs = refs[:2], refs[2:]
    if custom:
        totals, refs = refs[:4], refs[4:]
        (va_out, vb_out, norm_ref), refs = refs[:3], refs[3:]
        g01, g2o, refs = refs[0], refs[1], refs[2:]
        locals_, refs = (refs[:3], refs[3:6]), refs[6:]
        bufs, refs = [refs[5 * a : 5 * a + 5] for a in range(4)], refs[20:]
        last_bufs, last_loc, last_ss, last_rs, refs = refs[:6], *refs[6:9], refs[9:]
        (va, vb, near_a, far_a, near_b, far_b, near_s, far_s, square, lss, ss, rs, ass, ars, bss, brs, qss,
         qrs), refs = refs[:18], refs[18:]
    else:
        va, vb, g01, g2o, refs = *refs[:4], refs[4:]
    (gl_s, resid_s, dn_s, got_dn, br_s, got_br, mixed, low, dres, dctx, ctxc, wo, half_c, outgoing, u, ctx, n1,
     wqk, wvo, tok, du, dq, away, away_got, half, got, loc, ld, cs_s, cs_r, bs, xs, ws) = refs
    part = low
    dp, x, c = here()
    core = (dp, x * 2 + 1 - c)
    x_peer = (dp, (1 - x) * 2 + c)
    reduces = []
    if custom:
        greet(eight_peers() + neighbours()[0])
        shard_rows = totals[1].shape[0]
        half_rows = shard_rows // 2
        for a, grad in enumerate((gp_in, gf_in, g01, g2o)):
            rows = half_rows if a == 1 else shard_rows
            total = totals[1].at[pl.ds(0, half_rows)] if a == 1 else totals[a]
            local = locals_[a] if a < 2 else None
            loads = lss.at[a] if a < 2 else None
            came = given[a]
            reduces.append(
                Reduce(
                    grad, pl.ds(0, rows), BY_Y[a], local, came, total, bufs[a], loads, ss.at[a], rs.at[a]
                )
            )
        reduces.append(
            ReduceAlong(
                gf_in, half_rows, 32, totals[1].at[pl.ds(half_rows, half_rows)], last_bufs, last_loc, last_ss,
                last_rs,
            )
        )
    else:
        greet([core, x_peer, (dp, (1 - x) * 2 + 1 - c)])

    def step(number, what, *which):
        if custom:
            getattr(reduces[number], what)(*which)

    rows_all, width = low.shape
    own_rows = rows_all // 2
    n_chunks = rows_all // BLK
    order = [(1 - x) * 4 + i for i in range(HALF // BLK)] + [x * 2 + i for i in range(SLOT // BLK)]
    swaps = []
    for chunk in order:
        at = rows_at(chunk * BLK, BLK)
        swaps.append(remote(dn_in.at[at], got_dn.at[at], cs_s.at[chunk], cs_r.at[chunk], core))
    their = pl.ds(pl.multiple_of((1 - c) * own_rows, BLK), own_rows)
    mine = pl.ds(pl.multiple_of(c * own_rows, BLK), own_rows)
    branch = remote(br_in.at[their], got_br, bs.at[0], bs.at[1], core)

    def chunk_loads(n):
        at, slot = rows_at(order[n] * BLK, BLK), n % 2
        return [
            pltpu.make_async_copy(source.at[at], target.at[slot], ld.at[slot, k])
            for k, (source, target) in enumerate(
                ((resid_in, resid_s), (gl_in, gl_s), (dn_in, dn_s))
            )
        ]

    def load(number, source, target):
        copy = pltpu.make_async_copy(source, target, loc.at[number])
        copy.start()
        return copy

    loads = [chunk_loads(n) for n in range(n_chunks)]
    swaps[0].start()
    for n in range(2):
        for one in loads[n]:
            one.start()
    branch.start()
    for one in swaps[1:]:
        one.start()
    step(4, "start_along")
    step(0, "start_first")
    step(0, "start_early", 0)
    step(0, "start_early", 1)
    step(1, "start_first")
    br_load = load(0, br_in.at[mine], br_s)
    wo_load = load(1, wo_in, wo)
    ctxc_load = load(2, ctxc_in, ctxc)
    step(1, "start_early", 0)
    step(1, "start_early", 1)
    late = [
        load(3, u_in, u),
        load(4, ctx_in, ctx),
        load(5, n1_in, n1),
        load(6, wqk_in, wqk),
        load(7, wvo_in, wvo),
        load(8, tok_in, tok),
    ]

    @pl.when(c == x)
    def _():
        half[...] = jnp.zeros_like(half)

    va[...] = jnp.zeros_like(va)
    vb[...] = jnp.zeros_like(vb)
    for s in range(2):
        va[pl.ds(4 + c + 2 * s, 1), :] = gb_ref[s]
    branch.wait()
    br_load.wait()
    for n, chunk in enumerate(order):
        slot = n % 2
        for one in loads[n]:
            one.wait()
        swaps[n].wait()
        at = rows_at(chunk * BLK, BLK)
        dn = dn_s[slot].astype(F32) + got_dn[at, :].astype(F32)
        resid = resid_s[slot]
        back, unit = norm_back(dn, resid, vec_ref[2:3, :])
        grad = gl_s[slot].astype(F32)
        after = grad + back
        low[at, :] = after.astype(BF)

        @pl.when(chunk // (n_chunks // 2) == c)
        def _(chunk=chunk, dn=dn, resid=resid, unit=unit, grad=grad, after=after):
            here_at = rows_at((chunk - c * (n_chunks // 2)) * BLK, BLK)
            dres[here_at, :] = after
            branches = br_s[here_at, :].astype(F32) + got_br[here_at, :].astype(F32)
            mixed[here_at, :] = (resid + branches + vec_ref[7:8, :]).astype(BF)
            va[0:1, :] += jnp.sum(dn * unit, axis=0, keepdims=True)
            va[1:2, :] += jnp.sum(dn, axis=0, keepdims=True)
            va[2:3, :] += jnp.sum(after, axis=0, keepdims=True)
            va[3:4, :] += jnp.sum(grad, axis=0, keepdims=True)

        if n + 2 < n_chunks:
            for one in loads[n + 2]:
                one.start()
        if n == 1:
            wo_load.wait()
            for i in range(HALF // BLK):
                lanes = slice(i * BLK, (i + 1) * BLK)
                rows = low[rows_at((1 - x) * SLOT + i * BLK, BLK), :]
                outgoing[:, :, lanes] = (
                    dot_tt(wo[1 - x], rows).astype(BF).reshape(-1, HD, BLK)
                )
                dctx[2, :, :, rows_at(x * HALF + i * BLK, BLK)] = (
                    dot_tt(wo[x], rows).astype(BF).reshape(-1, HD, BLK)
                )
            cross_c = remote(outgoing, half_c, xs.at[0], xs.at[1], x_peer)
            cross_c.start()
            step(0, "start_second", 0)
            step(0, "start_second", 1)
    mixed_copy = pltpu.make_async_copy(mixed, mixed_out, ws.at[0])
    mixed_copy.start()
    if custom:
        early_sum = SumOverAll(va, near_a, far_a, ass, ars)
        early_sum.start()
    heads = u.shape[2]
    cols = heads * HD
    blocks = g2o.shape[1:4]
    ctxc_load.wait()
    for s in range(2):
        g2o[s, :, :, :, cols:] = dot_tt(low[...], ctxc[s]).astype(BF).reshape(*blocks, cols)
    for i in range(SLOT // BLK):
        lanes = slice(i * BLK, (i + 1) * BLK)
        rows = low[rows_at(x * HALF + i * BLK, BLK), :]
        for s in range(2):
            dctx[s, :, :, lanes] = dot_tt(wo[s], rows).astype(BF).reshape(-1, HD, BLK)
    step(1, "start_second", 0)
    step(1, "start_second", 1)
    late[0].wait()
    late[1].wait()

    def attend_back(group, which, begin, end):
        def unit(h, carry):
            def put(k, lanes, value):
                du[group, k, h, :, lanes] = value

            attend_back_unit(
                lambda k, lanes: u[group, k, h, :, lanes],
                put,
                lambda k, lanes: feat_ref[which, k, :, lanes],
                ctx[group, h],
                dctx[group, h],
                lse_ref[group, h],
                dq,
            )
            return carry

        lax.fori_loop(begin, end, unit, 0)

    full_rows = pl.ds(pl.multiple_of(x * SLOT, SLOT), SLOT)
    part_rows = pl.ds(pl.multiple_of((1 - x) * SLOT, SLOT), SLOT)
    everything = slice(0, SLOT)

    def of_group(group, k, lanes):
        value = du[group, k, :, :, lanes]
        return value.reshape(cols, value.shape[-1])

    def weight_grad(slot, which, with_part):
        def rows_of(group):
            value = du[group, :, heads - 1 :] if which else du[group, :, : heads - 1]
            return value.reshape(-1, SLOT)

        out = dot_tt(n1[full_rows, :], rows_of(slot))
        if with_part:
            out += dot_tt(n1[part_rows, :], rows_of(2))
        out = out.astype(BF)
        if which:
            g2o[slot, :, :, :, :cols] = out.reshape(*blocks, cols)
        else:
            g01[slot] = out.reshape(*blocks, 2 * cols)

    attend_back(1 - x, 0, 0, heads)
    for one in late[2:]:
        one.wait()
    for which in range(2):
        weight_grad(1 - x, which, False)
        step(2 + which, "start_first")
        step(2 + which, "start_early", 0)
    step(0, "start_third")
    cross_c.wait()
    dctx[2, :, :, pl.ds(pl.multiple_of((1 - x) * HALF, HALF), HALF)] = half_c[...]
    attend_back(2, 1, 0, heads)

    def back_through(group, lanes, slot):
        two = du[group, 0:2, :, :, lanes]
        two = two.reshape(2 * cols, two.shape[-1])
        out = dot_tt(two, whole_weight(wqk, slot))
        return out + dot_tt(of_group(group, 2, lanes), whole_weight(wvo, slot)[:, :cols])

    theirs = pl.ds(pl.multiple_of((1 - x) * HALF, HALF), HALF)
    away[...] = back_through(2, theirs, x).astype(BF).reshape(away.shape)
    swap_away = remote(away.at[1 - c], away_got, bs.at[4], bs.at[5], core)
    swap_away.start()
    step(1, "start_third")
    step(4, "start_first")
    swap_away.wait()
    away[c] = (away[c].astype(F32) + away_got[...].astype(F32)).astype(BF)
    cross = remote(away.at[c], half.at[c], xs.at[2], xs.at[3 + c], (dp, (1 - x) * 2 + x))
    cross.start()
    other = remote(away.at[1 - c], half.at[1 - c], xs.at[2], xs.at[4 - c], (dp, (1 - x) * 2 + x))
    attend_back(x, 0, 0, heads - 1)
    weight_grad(x, 0, True)
    step(2, "start_early", 1)
    step(2, "start_second", 1)
    step(2, "start_second", 0)
    step(4, "start_second")
    attend_back(x, 0, heads - 1, heads)
    weight_grad(x, 1, True)
    step(3, "start_early", 1)
    step(3, "start_second", 1)
    step(3, "start_second", 0)
    if custom:
        early_sum.middle()

    def bias_sums(group):
        sums = [
            jnp.sum(of_group(group, k, everything).astype(F32), axis=1, keepdims=True)
            for k in (0, 2)
        ]
        return jnp.concatenate(sums, axis=0)

    columns = [bias_sums(x) + bias_sums(2), bias_sums(1 - x)]
    as_rows = jnp.concatenate(columns + [jnp.zeros((2 * cols, 6), F32)], axis=1).T
    for n, slot in enumerate((x, 1 - x)):
        vb[pl.ds(2 + c + 2 * slot, 1), : 2 * cols] = as_rows[n : n + 1, :]

    def back_rows(start, count):
        return pl.ds(pl.multiple_of(start, HALF), count)

    for i in range(SLOT // HALF):
        lanes = slice(i * HALF, (i + 1) * HALF)
        back = back_through(0, lanes, 0) + back_through(1, lanes, 1)
        part[back_rows(x * HALF + i * HALF, HALF), :] = back.astype(BF)
    back = back_through(2, back_rows(x * HALF, HALF), x)
    part[back_rows((1 - x) * SLOT, HALF), :] = back.astype(BF)
    swap = remote(part.at[their], got, bs.at[2], bs.at[3], core)
    swap.start()
    step(2, "start_third")
    swap.wait()
    cross.wait_send()

    @pl.when(c == 1 - x)
    def _():
        cross.wait_recv()
        other.wait_recv()

    for r in range(own_rows // BLK):
        rows = slice(r * BLK, (r + 1) * BLK)
        wide = rows_at(c * own_rows + r * BLK, BLK)
        dn = part[wide, :].astype(F32) + got[rows, :].astype(F32)
        place = r - (1 - x)
        also = (c == 1 - x) & (place >= 0) & (place < 2)
        dn += jnp.where(also, half[jnp.clip(place, 0, 1)].astype(F32), 0.0)
        back, unit = norm_back(dn, tok[rows, :].astype(F32), vec_ref[0:1, :])
        mixed_copy.wait() if r == 0 else None
        mixed[rows, :] = (dres[rows, :] + back).astype(BF)
        vb[0:1, :] += jnp.sum(dn * unit, axis=0, keepdims=True)
        vb[1:2, :] += jnp.sum(dn, axis=0, keepdims=True)
    ig_copy = pltpu.make_async_copy(mixed, ig_out, ws.at[1])
    ig_copy.start()
    if custom:
        late_sum = SumOverAll(vb, near_b, far_b, bss, brs)
        late_sum.start()
        va_out[...] = early_sum.finish()
        step(3, "start_third")
        late_sum.middle()
        squares = functools.reduce(jnp.add, [one.finish() for one in reduces])
        square[...] = jnp.full(square.shape, squares, F32)
        norm = SumOverAll(square, near_s, far_s, qss, qrs)
        norm.start()
        vb_out[...] = late_sum.finish()
        vector_squares = jnp.sum(va_out[...] * va_out[...], keepdims=True)
        vector_squares += jnp.sum(vb_out[...] * vb_out[...], keepdims=True)
        norm.middle()
        norm_ref[...] = jnp.sqrt(norm.finish() + vector_squares)
    ig_copy.wait()


def backward(saved, weights, given, tokens, vectors):
    (gl, n1, u, ctx, lse, features, ctxc, resid, wo, br, dn, gp, gf, gb) = saved
    rows, width = tokens.shape
    chip = 2 * rows
    heads = u.shape[2]
    cols = heads * HD
    custom = lax.axis_size("dp") == 8
    dma = pltpu.SemaphoreType.DMA
    out_shape = [sds((rows, width), BF)] * 2
    out_specs = [ANY, ANY]
    if custom:
        hidden = gp.shape[-1]
        part_rows = width // 8
        shapes = [(part_rows, n) for n in (hidden, hidden, 2 * cols, 2 * cols)]
        gf = gf.reshape(gp.shape)
        out_shape += [sds(s, F32) for s in shapes]
        out_shape += [sds((8, width), F32)] * 2 + [sds((8, 128), F32)]
        out_specs += [VM] * 7
        scratch = [pltpu.VMEM((2, 4, 2) + s, BF) for s in shapes[2:]]
        half_rows = part_rows // 2
        pieces = [shapes[0], (half_rows, hidden), *shapes[2:]]
        scratch += [
            pltpu.VMEM((n,) + pieces[a], BF) for a in range(2) for n in (BY_Y[a], 4 - BY_Y[a], 4)
        ]
        scratch += [
            pltpu.VMEM((n,) + pieces[a], BF)
            for a in range(4)
            for n in (BY_Y[a], 4 - BY_Y[a], 4, 4, 3)
        ]
        scratch += [
            pltpu.VMEM((2, 2, half_rows, hidden), BF),
            pltpu.VMEM((3, 2, 2, half_rows, hidden), BF),
            pltpu.VMEM((32, hidden), BF),
            pltpu.VMEM((half_rows - 32, hidden), BF),
            pltpu.VMEM((half_rows, hidden), BF),
            pltpu.VMEM((half_rows, hidden), BF),
            dma,
            dma((9,)),
            dma((9,)),
        ]
        scratch += [
            *[pltpu.VMEM((8, width), F32)] * 2,
            *[pltpu.VMEM((8, 8, width), F32), pltpu.VMEM((4, 8, width), F32)] * 2,
            pltpu.VMEM((8, 8, 128), F32),
            pltpu.VMEM((4, 8, 128), F32),
            pltpu.VMEM((8, 128), F32),
            dma((2, 3)),
            dma((4, 9)),
            dma((4, 9)),
            *[dma((10,))] * 6,
        ]
    else:
        out_shape += [sds((8, width), F32)] * 2 + [sds((2, 1, 1, width, 2 * cols), BF)] * 2
        out_specs += [VM] * 4
        scratch = []
    scratch += [
        pltpu.VMEM((2, BLK, width), BF),
        pltpu.VMEM((2, BLK, width), F32),
        pltpu.VMEM((2, BLK, width), BF),
        pltpu.VMEM((chip, width), BF),
        pltpu.VMEM((rows, width), BF),
        pltpu.VMEM((rows, width), BF),
        pltpu.VMEM((rows, width), BF),
        pltpu.VMEM((chip, width), BF),
        pltpu.VMEM((rows, width), F32),
        pltpu.VMEM(ctx.shape, BF),
        pltpu.VMEM(ctxc.shape, BF),
        pltpu.VMEM(wo.shape, BF),
        pltpu.VMEM((heads, HD, HALF), BF),
        pltpu.VMEM((heads, HD, HALF), BF),
        pltpu.VMEM(u.shape, BF),
        pltpu.VMEM(ctx.shape, BF),
        pltpu.VMEM(n1.shape, BF),
        *[pltpu.VMEM(w.shape, BF) for w in weights],
        pltpu.VMEM((rows, width), BF),
        pltpu.VMEM(u.shape, BF),
        pltpu.VMEM((HD, SLOT), F32),
        pltpu.VMEM((2, BLK, width), BF),
        pltpu.VMEM((BLK, width), BF),
        pltpu.VMEM((2, BLK, width), BF),
        pltpu.VMEM((rows, width), BF),
        dma((9,)),
        dma((2, 3)),
        dma((chip // BLK,)),
        dma((chip // BLK,)),
        dma((6,)),
        dma((5,)),
        dma((2,)),
    ]
    return pl.pallas_call(
        functools.partial(backward_kernel, custom),
        out_shape=tuple(out_shape),
        in_specs=[ANY] * 4 + [VM, VM] + [ANY] * 7 + [VM] + [ANY] * 3 + [VM] + [ANY] * len(given),
        out_specs=tuple(out_specs),
        scratch_shapes=scratch,
        compiler_params=params(2),
        name="backward",
    )(gl, n1, u, ctx, lse, features, ctxc, resid, wo, br, dn, gp, gf, gb, *weights, tokens, vectors, *given)


def adamw_update(weight, moment_one, moment_two, gradient, step_rate, decay_rate):
    first_moment = DECAY_FIRST * moment_one + (1.0 - DECAY_FIRST) * gradient
    second_moment = DECAY_SECOND * moment_two + (1.0 - DECAY_SECOND) * gradient * gradient
    first_hat = first_moment / (1.0 - DECAY_FIRST**STEP)
    second_hat = second_moment / (1.0 - DECAY_SECOND**STEP)
    fresh_weight = weight - step_rate * (
        first_hat / (jnp.sqrt(second_hat) + ADAM_EPSILON) + decay_rate * weight
    )
    return (fresh_weight, first_moment, second_moment)


def update_kernel(*refs):
    (gp, gf, g01, g2o, va, vb, norm_ref), refs = refs[:7], refs[7:]
    cols = g2o.shape[1] // 2
    most = cols - HD
    old, new, norm_out = refs[:18], refs[18:36], refs[36]
    norm_out[0, 0] = norm_ref[0, 0]
    factor = CLIP_NORM / jnp.maximum(norm_ref[0:1, 0:1], CLIP_NORM)

    def update(number, grad, index, rate, decay):
        values = [old[3 * number + m][index] for m in range(3)]
        fresh = adamw_update(*values, factor * grad, rate, decay)
        for m in range(3):
            new[3 * number + m][index] = fresh[m]

    for k in range(3):
        grad = [g01[:, k * most : (k + 1) * most], g2o[:, k * HD : (k + 1) * HD]]
        update(0, jnp.concatenate(grad, axis=1), k, RATE_MATRIX, WEIGHT_DECAY)
    for number, grad in ((1, g2o[:, cols:].T), (2, gf[...]), (3, gp[...])):
        update(number, grad, ..., RATE_MATRIX, WEIGHT_DECAY)
    width = va.shape[1]
    parts = old[15].shape[1] // width

    def heads(k):
        rows = [vb[2 + t : 3 + t, k * cols : (k + 1) * cols] for t in range(parts)]
        return jnp.concatenate(rows, axis=1)

    vector_grad = jnp.concatenate(
        [vb[0:2, :], va[0:2, :], heads(0), heads(1), va[2:4, :]], axis=0
    )
    update(4, vector_grad, ..., RATE_VECTOR, 0.0)
    for t in range(parts):
        lanes = slice(t * width, (t + 1) * width)
        update(5, va[4 + t : 5 + t, :], (slice(None), lanes), RATE_VECTOR, 0.0)


def update_all(totals, va, vb, norm, states):
    return pl.pallas_call(
        update_kernel,
        out_shape=(*[sds(s.shape, F32) for s in states], sds((1, 1), F32)),
        in_specs=[VM] * (7 + len(states)),
        out_specs=(*[VM] * len(states), pl.BlockSpec(memory_space=pltpu.SMEM)),
        compiler_params=params(),
        name="update",
    )(*totals, va, vb, norm, *states)


def on_device(
    tokens,
    cotangent,
    segment_ids,
    valid,
    qkv_weight,
    qkv_moment1,
    qkv_moment2,
    out_weight,
    out_moment1,
    out_moment2,
    fc_weight,
    fc_moment1,
    fc_moment2,
    proj_weight,
    proj_moment1,
    proj_moment2,
    vector_params,
    vector_moment1,
    vector_moment2,
    fc_bias,
    fc_bias_moment1,
    fc_bias_moment2,
):
    custom = lax.axis_size("dp") == 8
    slot, swap = lax.axis_index("tensor") // 2, [(0, 2), (1, 3), (2, 0), (3, 1)]
    states = [jnp.transpose(s, (1, 0, 2)) for s in (qkv_weight, qkv_moment1, qkv_moment2)]
    states += [out_weight, out_moment1, out_moment2]
    states += [fc_weight, fc_moment1, fc_moment2]
    states += [s.T for s in (proj_weight, proj_moment1, proj_moment2)]
    states += [vector_params, vector_moment1, vector_moment2]
    states += [s[None] for s in (fc_bias, fc_bias_moment1, fc_bias_moment2)]
    shards = [states[0], states[3], states[6], states[9]]
    if not custom:
        parts = [
            jnp.concatenate([states[0][0], states[0][1]], axis=1),
            jnp.concatenate([states[0][2], shards[1].T], axis=1),
            *shards[2:],
        ]
        shards = []
        for part in parts:
            own = lax.all_gather(part.astype(BF), "dp", axis=0, tiled=True)
            other = lax.ppermute(own, "tensor", swap)
            shards.append(
                jnp.stack([jnp.where(slot == 0, own, other), jnp.where(slot == 0, other, own)])
            )
    saved, weights, given = forward(
        tokens,
        cotangent,
        valid,
        segment_ids,
        vector_params,
        states[15],
        shards,
    )
    outs = backward(saved, weights, given, tokens, vector_params)
    mixed, input_grad = outs[:2]
    if custom:
        totals, (va, vb, norm) = outs[2:6], outs[6:]
    else:
        va, vb, totals = *outs[2:4], []
        for g in [saved[11], saved[12], *outs[4:6]]:
            g = g.reshape(2, -1, g.shape[-1])
            mine = jnp.where(slot == 0, g[0], g[1])
            other = jnp.where(slot == 0, g[1], g[0])
            both = mine.astype(F32) + lax.ppermute(other, "tensor", swap).astype(F32)
            both = lax.psum_scatter(both.astype(BF), "dp", scatter_dimension=0, tiled=True)
            totals.append(both.astype(F32))
        squares = sum(jnp.sum(t * t) for t in totals)
        va, vb, squares = lax.psum((va, vb, squares), ("dp", "tensor"))
        squares += jnp.sum(va * va) + jnp.sum(vb * vb)
        norm = jnp.full((8, 128), jnp.sqrt(squares), F32)
    *new, grad_norm = update_all(totals, va, vb, norm, states)
    new[:3] = [jnp.transpose(s, (1, 0, 2)) for s in new[:3]]
    new[9:12] = [s.T for s in new[9:12]]
    new[15:18] = [s[0] for s in new[15:18]]
    return (mixed, input_grad, grad_norm.reshape(()), *new)


def solution(mesh):
    rows = P(("dp", "tensor"), None)
    by_rows = [P("dp", None, "tensor")] * 3
    by_out = [P("tensor", "dp")] * 3
    by_fc = [P("dp", "tensor")] * 3
    weights = by_rows + by_out + by_fc + by_out
    return jax.shard_map(
        on_device,
        mesh=mesh,
        in_specs=(rows, rows, P("dp"), P(("dp", "tensor")), *weights, *[P()] * 6),
        out_specs=(rows, rows, P(), *weights, *[P()] * 6),
        check_vma=False,
    )
```

```python
import functools
import math

import jax
import jax.numpy as jnp
from jax import lax
from jax.experimental import pallas as pl
from jax.experimental.pallas import tpu as pltpu
from jax.sharding import PartitionSpec as P

HD = 64
SLOT = 1024
STEP = 10
NORM_EPSILON = 1e-05
MASK_FILL = -1e30
DECAY_FIRST = 0.5
DECAY_SECOND = 0.5
ADAM_EPSILON = 1e-08
WEIGHT_DECAY = 0.1
CLIP_NORM = 1.0
RATE_MATRIX = 0.04
RATE_VECTOR = 0.3

MESH = pl.DeviceIdType.MESH
BF = jnp.bfloat16
F32 = jnp.float32
HALF = SLOT // 2
BLK = 256
VMEM_LIMIT = 58 * 2**20
LOG2E = math.log2(math.e)
SCORE_SCALE = float(HD) ** (-0.5)
SCORE_SCALE2 = SCORE_SCALE * LOG2E


def dot_nn(a, b):
    return lax.dot_general(a, b, (((1,), (0,)), ((), ())), preferred_element_type=F32)


def dot_nt(a, b):
    return lax.dot_general(a, b, (((1,), (1,)), ((), ())), preferred_element_type=F32)


def dot_tn(a, b):
    return lax.dot_general(a, b, (((0,), (0,)), ((), ())), preferred_element_type=F32)


def dot_tt(a, b):
    return lax.dot_general(a, b, (((0,), (1,)), ((), ())), preferred_element_type=F32)


def params(collective_id=None):
    if collective_id is None:
        return pltpu.CompilerParams(vmem_limit_bytes=VMEM_LIMIT)
    return pltpu.CompilerParams(
        vmem_limit_bytes=VMEM_LIMIT, collective_id=collective_id, has_side_effects=True
    )


VM = pl.BlockSpec(memory_space=pltpu.VMEM)
ANY = pl.BlockSpec(memory_space=pl.ANY)


def sds(shape, dtype):
    return jax.ShapeDtypeStruct(shape, dtype)


def here():
    t = lax.axis_index("tensor")
    return lax.axis_index("dp"), t // 2, t % 2


def announce(ids):
    sem = pltpu.get_barrier_semaphore()
    for one in ids:
        pl.semaphore_signal(sem, inc=1, device_id=one, device_id_type=MESH)


def await_others(ids):
    pl.semaphore_wait(pltpu.get_barrier_semaphore(), len(ids))


def greet(ids):
    announce(ids)
    await_others(ids)


def remote(src, dst, send_sem, recv_sem, target):
    return pltpu.make_async_remote_copy(
        src_ref=src,
        dst_ref=dst,
        send_sem=send_sem,
        recv_sem=recv_sem,
        device_id=target,
        device_id_type=MESH,
    )


def rows_at(start, size):
    return pl.ds(pl.multiple_of(start, size), size)


def norm_parts(values):
    centered = values - jnp.mean(values, axis=-1, keepdims=True)
    variance = jnp.mean(centered * centered, axis=-1, keepdims=True)
    scale = lax.rsqrt(variance + NORM_EPSILON)
    return centered * scale, scale


class Gather:
    def __init__(self, shard, whole, part, by_y, ss, rs):
        dp, x, c = here()
        z, y = dp // 2, dp % 2
        along, x_peer, y_peer, _ = neighbours()
        shard = shard.at[part]
        block = whole.at[x, z, y, part]
        column = whole.at[x, :, y, part]
        from_x = whole.at[1 - x, pl.ds(0, by_y), y, part]
        from_y = whole.at[x, pl.ds(by_y, 4 - by_y), 1 - y, part]
        self.along = [remote(shard, block, ss.at[k], rs.at[k], along[k]) for k in range(3)]
        self.beside = [
            remote(column, column, ss.at[3], rs.at[3], x_peer),
            remote(column, column, ss.at[4], rs.at[4], y_peer),
        ]
        self.passed = [
            remote(from_x, from_x, ss.at[5], rs.at[5], y_peer),
            remote(from_y, from_y, ss.at[6], rs.at[6], x_peer),
        ]

    def start_along(self):
        for one in self.along:
            one.start()

    def start_beside(self):
        for one in self.along:
            one.wait()
        for one in self.beside:
            one.start()

    def start_passed(self):
        for one in self.beside:
            one.wait()
        for one in self.passed:
            one.start()

    def finish(self):
        for one in self.passed:
            one.wait()


class GatherBeside:
    def __init__(self, shard, whole, start, size, by_y, ss, rs):
        dp, x, c = here()
        z, y = dp // 2, dp % 2
        along, x_peer, y_peer, _ = neighbours()
        part = pl.ds(start, size)
        block = whole.at[x, z, y, part]
        from_x = whole.at[1 - x, z, y, pl.ds(start, by_y)]
        from_y = whole.at[x, z, 1 - y, pl.ds(start + by_y, size - by_y)]
        four = whole.at[:, z, :, part]
        self.beside = [
            remote(shard.at[part], block, ss.at[3], rs.at[3], x_peer),
            remote(shard.at[part], block, ss.at[4], rs.at[4], y_peer),
        ]
        self.passed = [
            remote(from_x, from_x, ss.at[5], rs.at[5], y_peer),
            remote(from_y, from_y, ss.at[6], rs.at[6], x_peer),
        ]
        self.along = [remote(four, four, ss.at[k], rs.at[k], along[k]) for k in range(3)]

    def start_beside(self):
        for one in self.beside:
            one.start()

    def start_passed(self):
        for one in self.beside:
            one.wait()
        for one in self.passed:
            one.start()

    def start_along(self):
        for one in self.passed:
            one.wait()
        for one in self.along:
            one.start()

    def finish(self):
        for one in self.along:
            one.wait()


def neighbours():
    dp, x, c = here()
    z, y = dp // 2, dp % 2
    me = x * 2 + c
    along = [(lax.rem(z + k, 4) * 2 + y, me) for k in (1, 2, 3)]
    return along, (dp, (1 - x) * 2 + c), (z * 2 + 1 - y, me), (dp, x * 2 + 1 - c)


def whole_weight(ref, slot):
    value = ref[slot]
    return value.reshape(-1, value.shape[-1])


MASKED = -(2.0**100)
ATT = 512


def segment_features(segments):
    numbers = lax.broadcasted_iota(jnp.int32, (16, segments.shape[1]), 0).astype(F32) + 1.0
    query = jnp.where(segments >= numbers, 1.0, 0.0)
    key = jnp.where(segments < numbers, MASKED, 0.0)
    return query.astype(BF), key.astype(BF)


def causal(scores):
    keys = lax.broadcasted_iota(jnp.int32, scores.shape, 0)
    queries = lax.broadcasted_iota(jnp.int32, scores.shape, 1)
    return jnp.where(keys <= queries, scores, MASK_FILL)


def attend_unit(q, k, v):
    for i in range(SLOT // ATT):
        cols = slice(i * ATT, (i + 1) * ATT)
        query = q(cols)
        scores = []
        for j in range(i + 1):
            raw = dot_tn(k(slice(j * ATT, (j + 1) * ATT)), query) * SCORE_SCALE2
            scores.append(causal(raw) if j == i else raw)
        top = functools.reduce(jnp.maximum, [jnp.max(s, axis=0, keepdims=True) for s in scores])
        exps = [jnp.exp2(s - top) for s in scores]
        total = functools.reduce(jnp.add, [jnp.sum(e, axis=0, keepdims=True) for e in exps])
        low = jnp.concatenate([e.astype(BF) for e in exps], axis=0)
        yield cols, dot_nn(v(slice(0, (i + 1) * ATT)), low) / total, top + jnp.log2(total)


GELU_C = math.sqrt(2.0 / math.pi)
GELU_A = 0.044715


def forward_kernel(custom, *refs):
    (tok_ref, cot_ref, valid_ref, seg_ref, vec_ref, fb_ref), refs = refs[:6], refs[6:]
    shards, refs = refs[:4], refs[4:]
    (gl_out, n1_out, u_out, ctx_out, lse_out, feat_out, ctxc_out, resid_out, wo_out, br_out, dn_out, gp_out,
     gf_out, gb_ref), refs = refs[:14], refs[14:]
    if custom:
        weights_out, given, refs = refs[:2], refs[2:6], refs[6:]
        lows, refs = refs[:4], refs[4:]
        wholes, refs = refs[:4], refs[4:]
        gs, gr, ps, pr, refs = *refs[:4], refs[4:]
    else:
        wholes = shards
    (tk, gl, n1, u, ctx, lse, features, ctxc, resid, wo, n2, half, part, got, act, dpre, gp, cols, loc, ts, tr, xs,
     cs_s, cs_r) = refs
    wqk, wvo, wf, wp = wholes
    dp, x, c = here()
    core = (dp, x * 2 + 1 - c)
    x_peer = (dp, (1 - x) * 2 + c)
    across = [(dp, (1 - x) * 2), (dp, (1 - x) * 2 + 1)]
    rows = tok_ref.shape[0]
    first = x * HALF
    gathers = []
    if custom:
        z, y = dp // 2, dp % 2
        along, _, y_peer, _ = neighbours()
        others = [core, *across, *along, y_peer]
        announce(others)
        lows[0][...] = jnp.concatenate([shards[0][0], shards[0][1]], axis=1).astype(BF)
        lows[1][...] = jnp.concatenate([shards[0][2], shards[1][...].T], axis=1).astype(BF)
        lows[2][...] = shards[2][...].astype(BF)
        lows[3][...] = shards[3][...].astype(BF)
        await_others(others)
        pieces = [(a, k, 2, 2) for a in range(2) for k in range(2)]
        pieces += [(2, 0, 2, 3), (2, 1, 2, 3), (3, 0, 2, 3)]
        for number, (a, k, parts, by_y) in enumerate(pieces):
            size = lows[a].shape[0] // parts
            gathers.append(
                Gather(
                    lows[a], wholes[a], pl.ds(k * size, size), by_y, gs.at[number], gr.at[number]
                )
            )
        size = lows[3].shape[0] // 2
        gathers.append(GatherBeside(lows[3], wholes[3], size, size, 32, gs.at[7], gr.at[7]))
    else:
        greet([core, *across])

    def step(number, what):
        if custom:
            getattr(gathers[number], what)()

    own_rows = pl.ds(pl.multiple_of(first + c * rows, BLK), rows)
    gl_rows = pl.ds(pl.multiple_of(c * rows, BLK), rows)
    mine_tok = pltpu.make_async_copy(tok_ref, tk.at[own_rows], loc.at[0])
    cot_load = pltpu.make_async_copy(cot_ref, part.at[pl.ds(0, rows)], loc.at[9])
    swap_tok = remote(tok_ref, tk.at[own_rows], ts.at[0], tr.at[0], core)
    swap_grad = remote(gl.at[gl_rows], gl.at[gl_rows], ts.at[1], tr.at[1], core)
    source = [
        tok_ref.at[pl.ds(pl.multiple_of((1 - x) * BLK + k * BLK, BLK), BLK)] for k in range(2)
    ]
    there = [
        tk.at[pl.ds(pl.multiple_of(x * (SLOT + HALF) + k * BLK, BLK), BLK)] for k in range(2)
    ]
    halves = [remote(source[k], there[k], ts.at[2 + k], tr.at[2], across[k]) for k in range(2)]
    landed = tk.at[pl.ds(pl.multiple_of((1 - x) * (SLOT + HALF) + c * BLK, BLK), BLK)]
    handed = remote(landed, landed, ts.at[4], tr.at[3], core)

    step(0, "start_along")
    step(7, "start_beside")
    step(1, "start_along")
    mine_tok.start()
    swap_tok.start()
    cot_load.start()

    @pl.when(c == 1 - x)
    def _():
        for one in halves:
            one.start()

    if custom:
        for a in range(4):
            wholes[a][x, z, y] = lows[a][...]

    def out_copy(number, ref, out):
        copy = pltpu.make_async_copy(ref, out, loc.at[number])
        copy.start()
        return copy

    cols[...] = vec_ref[...].T
    gain, shift = vec_ref[0:1, :], vec_ref[1:2, :]

    def norm_rows(start, count):
        def norm(i, carry):
            at = rows_at(start + i * BLK, BLK)
            unit, _ = norm_parts(tk[at, :].astype(F32))
            n1[at, :] = (unit * gain + shift).astype(BF)
            return carry

        lax.fori_loop(0, count // BLK, norm, 0)

    mine_tok.wait()
    norm_rows(first + c * rows, rows)
    swap_tok.wait()
    step(0, "start_beside")
    step(2, "start_along")
    norm_rows(first + (1 - c) * rows, rows)
    step(1, "start_beside")
    step(3, "start_along")

    mask = jnp.broadcast_to(valid_ref[...].reshape(1, rows).astype(F32), (8, rows)).T[:, 0:1]
    cot_load.wait()
    gl[gl_rows, :] = (part[:rows, :].astype(F32) * mask).astype(BF)
    swap_grad.start()
    for k, row in enumerate((2 * x, 1)):
        at = pl.ds(pl.multiple_of(row * SLOT, SLOT), SLOT)
        query, key = segment_features(seg_ref[at].reshape(1, SLOT).astype(F32))
        features[k, 0] = query
        features[k, 1] = key

    halves[0].wait_recv()
    handed.start()
    step(2, "start_beside")
    step(4, "start_along")
    handed.wait()
    norm_rows((1 - x) * (SLOT + HALF), HALF)
    step(3, "start_beside")
    step(5, "start_along")
    step(7, "start_passed")
    for number in range(4):
        step(number, "start_passed")

    heads = u.shape[2]
    wide = heads * HD

    def project(group, slot, first_row):
        bias_rows = pl.ds(pl.multiple_of((c + 2 * slot) * wide, HD), wide)
        query_bias, value_bias = cols[bias_rows, 4:5], cols[bias_rows, 5:6]

        def chunk(i, carry):
            lanes = rows_at(i * BLK, BLK)
            values = n1[rows_at(first_row + i * BLK, BLK), :]
            two = dot_tt(whole_weight(wqk, slot), values)
            value = dot_tt(whole_weight(wvo, slot)[:, :wide], values) + value_bias
            for k, out in enumerate((two[:wide] + query_bias, two[wide:], value)):
                u[group, k, :, :, lanes] = out.reshape(-1, HD, BLK).astype(BF)
            return carry

        lax.fori_loop(0, SLOT // BLK, chunk, 0)

    def attend(group, which, begin, end):
        def unit(h, carry):
            for lanes, context, log_total in attend_unit(
                lambda s: jnp.concatenate([u[group, 0, h, :, s], features[which, 0, :, s]], axis=0),
                lambda s: jnp.concatenate([u[group, 1, h, :, s], features[which, 1, :, s]], axis=0),
                lambda s: u[group, 2, h, :, s],
            ):
                ctx[group, h, :, lanes] = context.astype(BF)
                lse[group, h, :, lanes] = log_total
            return carry

        lax.fori_loop(begin, end, unit, 0)

    project(x, x, x * SLOT)
    step(4, "start_beside")
    step(6, "start_along")
    attend(x, 0, 0, 1)
    step(5, "start_beside")
    step(7, "start_along")
    attend(x, 0, 1, heads)
    step(4, "start_passed")
    project(2, x, (1 - x) * SLOT)
    step(6, "start_beside")
    attend(2, 1, 0, heads)
    theirs = pl.ds(pl.multiple_of((1 - x) * HALF, HALF), HALF)
    cross = remote(ctx.at[2, :, :, theirs], half, xs.at[0], xs.at[1], x_peer)
    cross.start()
    for number in range(4):
        step(number, "finish")
    step(5, "start_passed")
    project(1 - x, 1 - x, x * SLOT)
    copies = [out_copy(1, n1, n1_out), out_copy(2, u, u_out)]
    for s in range(2):
        wo[s] = whole_weight(wvo, s)[:, wide:]
    attend(1 - x, 0, 0, 1)
    step(6, "start_passed")
    attend(1 - x, 0, 1, heads)
    copies += [out_copy(3, ctx, ctx_out), out_copy(4, lse, lse_out), out_copy(5, features, feat_out)]
    copies.append(out_copy(8, wo, wo_out))
    if custom:
        copies += [out_copy(6 + a, wholes[a], weights_out[a]) for a in range(2)]

    @pl.when(c == 1 - x)
    def _():
        for one in halves:
            one.wait_send()

    chunks = []

    def send(chunk, values):
        at = rows_at(chunk * BLK, BLK)
        part[at, :] = values.astype(BF)
        copy = remote(part.at[at], got.at[at], cs_s.at[chunk], cs_r.at[chunk], core)
        copy.start()
        chunks.append((chunk, copy))

    def context_of(group, lanes):
        value = ctx[group, :, :, lanes]
        return value.reshape(-1, value.shape[-1])

    for i in range(SLOT // BLK):
        lanes = slice(i * BLK, (i + 1) * BLK)
        chunk = x * 2 + i
        at = rows_at(chunk * BLK, BLK)
        zero, one = context_of(0, lanes), context_of(1, lanes)
        send(chunk, dot_tt(zero, wo[0]) + dot_tt(one, wo[1]))
        ctxc[0, :, at] = zero
        ctxc[1, :, at] = one
    cross.wait()
    for i in range(HALF // BLK):
        chunk = (1 - x) * 4 + i
        at = rows_at(chunk * BLK, BLK)
        own = context_of(2, rows_at(x * HALF + i * BLK, BLK))
        other = half[:, :, i * BLK : (i + 1) * BLK].reshape(-1, BLK)
        send(chunk, dot_tt(own, wo[x]) + dot_tt(other, wo[1 - x]))
        ctxc[x, :, at] = own
        ctxc[1 - x, :, at] = other
    copies.append(out_copy(10, ctxc, ctxc_out))
    swap_grad.wait()
    copies.append(out_copy(11, gl, gl_out))
    for chunk, copy in chunks:
        copy.wait()
        at = rows_at(chunk * BLK, BLK)
        tokens = tk[rows_at(first + chunk * BLK, BLK), :].astype(F32)
        summed = part[at, :].astype(F32) + got[at, :].astype(F32)
        after = tokens + summed + vec_ref[6:7, :]
        resid[at, :] = after
        unit, _ = norm_parts(after)
        n2[at, :] = (unit * vec_ref[2:3, :] + vec_ref[3:4, :]).astype(BF)
    copies.append(out_copy(12, resid, resid_out))
    step(4, "finish")
    step(5, "finish")

    hidden = wf.shape[-1]
    gb_ref[...] = jnp.zeros_like(gb_ref)
    bias_of = [
        fb_ref[:, pl.ds(pl.multiple_of((c + 2 * s) * hidden, hidden), hidden)] for s in range(2)
    ]
    tile = HALF
    tiles = 2 * rows // tile

    def activate(i, carry):
        at = rows_at(i * tile, tile)
        n2_rows = n2[at, :]
        for s in range(2):
            lanes = slice(s * hidden, (s + 1) * hidden)
            v = dot_nn(n2_rows, whole_weight(wf, s)) + bias_of[s]
            square = v * v
            t = jnp.tanh(v * (GELU_C + (GELU_C * GELU_A) * square))
            cdf = 0.5 + 0.5 * t
            act[at, lanes] = (v * cdf).astype(BF)
            slope = cdf + (cdf * (1.0 - t)) * (v * (GELU_C + (3.0 * GELU_C * GELU_A) * square))
            dpre[at, lanes] = slope.astype(BF)
        return carry

    lax.fori_loop(0, tiles, activate, 0)
    blocks = gp.shape[1:4]

    for s in range(2):
        out = dot_tn(gl[...], act[:, s * hidden : (s + 1) * hidden]).astype(BF)
        gp[s] = out.reshape(*blocks, hidden)
        copies.append(out_copy(15 + s, gp.at[s], gp_out.at[s]))
    passing = []
    if custom:
        low, high = pl.ds(0, 2), pl.ds(2, 2)
        pieces = [
            (gp.at[1 - x, low, 1 - y], y_peer),
            (gp.at[1 - x, high, 1 - y], x_peer),
            (gp.at[1 - x, high, y], x_peer),
            (gp.at[x, low, 1 - y], y_peer),
        ]
        for k, (piece, peer) in enumerate(pieces):
            passing.append(remote(piece, given[k], ps.at[k], pr.at[k], peer))
            passing[-1].start()
    step(6, "finish")
    step(7, "finish")

    def forward_back(i, carry):
        at = rows_at(i * tile, tile)
        gl_now = gl[at, :]
        for s in range(2):
            lanes = slice(s * hidden, (s + 1) * hidden)
            up = dot_nn(gl_now, whole_weight(wp, s))
            d = (up * dpre[at, lanes].astype(F32)).astype(BF)
            dpre[at, lanes] = d
            gb_ref[s] += jnp.sum(d.astype(F32), axis=0, keepdims=True)
        br = dot_nt(act[at, :hidden], whole_weight(wp, 0))
        br += dot_nt(act[at, hidden:], whole_weight(wp, 1))
        part[at, :] = br.astype(BF)
        dn = dot_nt(dpre[at, :hidden], whole_weight(wf, 0))
        dn += dot_nt(dpre[at, hidden:], whole_weight(wf, 1))
        got[at, :] = dn.astype(BF)
        return carry

    lax.fori_loop(0, tiles, forward_back, 0)
    copies += [out_copy(13, got, dn_out), out_copy(14, part, br_out)]
    width = n2.shape[1]

    for s in range(2):
        at = slice(s * width, (s + 1) * width)
        tk[at, :] = dot_tn(n2[...], dpre[:, s * hidden : (s + 1) * hidden]).astype(BF)
        copies.append(out_copy(17 + s, tk.at[at], gf_out.at[s]))
    for copy in copies + passing:
        copy.wait()


def forward(tokens, cotangent, valid, segments, vectors, fc_bias, shards):
    rows, width = tokens.shape
    chip = 2 * rows
    custom = lax.axis_size("dp") == 8
    dma = pltpu.SemaphoreType.DMA
    if custom:
        cols = shards[0].shape[2]
        hidden = shards[2].shape[1]
        part_rows = shards[2].shape[0]
        flat = [(part_rows, n) for n in (2 * cols, 2 * cols, hidden, hidden)]
        wholes = [(2, 4, 2) + s for s in flat]
        more_out = [sds(w, BF) for w in wholes[:2]] + [sds((2, part_rows, hidden), BF)] * 4
        more = [pltpu.VMEM(s, BF) for s in flat] + [pltpu.VMEM(w, BF) for w in wholes]
        more += [dma((8, 7)), dma((8, 7)), dma((4,)), dma((4,))]
        grad_shape = wholes[3]
    else:
        cols, hidden = shards[0].shape[2] // 2, shards[2].shape[2]
        more_out, more = [], []
        grad_shape = (2, 1, 1, width, hidden)
    heads = cols // HD
    shapes = [
        ((chip, width), BF),
        ((2 * SLOT, width), BF),
        ((3, 3, heads, HD, SLOT), BF),
        ((3, heads, HD, SLOT), BF),
        ((3, heads, 1, SLOT), F32),
        ((2, 2, 16, SLOT), BF),
        ((2, cols, chip), BF),
        ((chip, width), F32),
        ((2, width, cols), BF),
    ]
    out_shape = [sds(*s) for s in shapes]
    out_shape += [sds((chip, width), BF)] * 2 + [sds(grad_shape, BF), sds((2, width, hidden), BF)]
    out_shape += [sds((2, 1, hidden), F32)] + more_out
    outs = pl.pallas_call(
        functools.partial(forward_kernel, custom),
        out_shape=tuple(out_shape),
        in_specs=[ANY, ANY] + [VM] * (4 + len(shards)),
        out_specs=(*[ANY] * 13, VM, *[ANY] * len(more_out)),
        scratch_shapes=more
        + [
            pltpu.VMEM((2 * SLOT, width), BF),
            *[pltpu.VMEM(*s) for s in shapes],
            pltpu.VMEM((chip, width), BF),
            pltpu.VMEM((heads, HD, HALF), BF),
            pltpu.VMEM((chip, width), BF),
            pltpu.VMEM((chip, width), BF),
            pltpu.VMEM((chip, 2 * hidden), BF),
            pltpu.VMEM((chip, 2 * hidden), BF),
            pltpu.VMEM(grad_shape, BF),
            pltpu.VMEM((width, 8), F32),
            dma((19,)),
            dma((5,)),
            dma((4,)),
            dma((2,)),
            dma((chip // BLK,)),
            dma((chip // BLK,)),
        ],
        compiler_params=params(1),
        name="forward",
    )(tokens, cotangent, valid, segments, vectors, fc_bias, *shards)
    if custom:
        return outs[:14], outs[14:16], outs[16:]
    return outs[:14], shards[:2], []


class Reduce:
    def __init__(self, grad, part, by_y, local, given, total, bufs, loc, ss, rs):
        dp, x, c = here()
        z, y = dp // 2, dp % 2
        along, x_peer, y_peer, _ = neighbours()
        low, high = pl.ds(0, by_y), pl.ds(by_y, 4 - by_y)
        self.z, self.total = z, total
        self.r1y, self.r1x, self.r2x, self.r2y, self.r3 = bufs
        views = [
            grad.at[1 - x, low, y, part],
            grad.at[x, high, 1 - y, part],
            grad.at[x, :, y, part],
        ]
        self.loads = []
        self.mid_x, self.mid_y, self.own = views
        if local is not None:
            self.loads = [
                pltpu.make_async_copy(views[k], local[k], loc.at[k]) for k in range(3)
            ]
            self.mid_x, self.mid_y, self.own = local
        self.first = [
            remote(grad.at[1 - x, low, 1 - y, part], self.r1y, ss.at[0], rs.at[0], y_peer),
            remote(grad.at[1 - x, high, 1 - y, part], self.r1x, ss.at[1], rs.at[1], x_peer),
        ]
        self.early = [
            remote(grad.at[1 - x, high, y, part], self.r2x.at[high], ss.at[2], rs.at[2], x_peer),
            remote(grad.at[x, low, 1 - y, part], self.r2y.at[low], ss.at[3], rs.at[3], y_peer),
        ]
        targets = (self.r1y, self.r1x, self.r2x.at[high], self.r2y.at[low])
        for k, came in enumerate(given or ()):
            copies = (self.first, self.early)[k // 2]
            copies[k % 2] = pltpu.make_async_copy(came, targets[k], rs.at[k])
        self.second = [
            remote(self.mid_x, self.r2x.at[low], ss.at[4], rs.at[4], x_peer),
            remote(self.mid_y, self.r2y.at[high], ss.at[5], rs.at[5], y_peer),
        ]
        self.third = [
            remote(
                self.own.at[lax.rem(z + k + 1, 4)], self.r3.at[k], ss.at[6 + k], rs.at[6 + k], along[k]
            )
            for k in range(3)
        ]

    def start_first(self):
        for one in self.loads:
            one.start()
        for one in self.first:
            one.start()

    def start_early(self, which):
        self.early[which].start()

    def start_second(self, which):
        self.first[which].wait()
        if self.loads:
            self.loads[which].wait()
        mid, came = ((self.mid_x, self.r1y), (self.mid_y, self.r1x))[which]
        mid[...] = (mid[...].astype(F32) + came[...].astype(F32)).astype(BF)
        self.second[which].start()

    def start_third(self):
        for one in self.early + self.second + self.loads[2:]:
            one.wait()
        for k in range(4):
            place = lax.rem(self.z + k + 1, 4)
            summed = (
                self.own[place].astype(F32)
                + self.r2x[place].astype(F32)
                + self.r2y[place].astype(F32)
            )
            if k < 3:
                self.own[place] = summed.astype(BF)
                self.third[k].start()
            else:
                self.total[...] = summed

    def finish(self):
        for one in self.third:
            one.wait()
        total = self.total[...]
        for k in range(3):
            total = total + self.r3[k].astype(F32)
        self.total[...] = total
        return jnp.sum(total * total)


class ReduceAlong:
    def __init__(self, grad, start, by_y, total, bufs, loc, ss, rs):
        dp, x, c = here()
        z, y = dp // 2, dp % 2
        along, x_peer, y_peer, _ = neighbours()
        self.place, self.total = (x, y), total
        self.own, self.rz, self.r1y, self.r1x, self.r2x, self.r2y = bufs
        size = self.own.shape[2]
        part = pl.ds(start, size)
        low, high = pl.ds(0, by_y), pl.ds(by_y, size - by_y)
        own = self.own
        self.load = pltpu.make_async_copy(grad.at[:, z, :, part], own, loc)
        self.along = [
            remote(
                grad.at[:, lax.rem(z + k + 1, 4), :, part], self.rz.at[k], ss.at[k], rs.at[k], along[k]
            )
            for k in range(3)
        ]
        self.first = [
            remote(own.at[1 - x, 1 - y, low], self.r1y, ss.at[3], rs.at[3], y_peer),
            remote(own.at[1 - x, 1 - y, high], self.r1x, ss.at[4], rs.at[4], x_peer),
        ]
        self.early = [
            remote(own.at[1 - x, y, high], self.r2x.at[high], ss.at[5], rs.at[5], x_peer),
            remote(own.at[x, 1 - y, low], self.r2y.at[low], ss.at[6], rs.at[6], y_peer),
        ]
        self.mid = (own.at[1 - x, y, low], own.at[x, 1 - y, high])
        self.second = [
            remote(self.mid[0], self.r2x.at[low], ss.at[7], rs.at[7], x_peer),
            remote(self.mid[1], self.r2y.at[high], ss.at[8], rs.at[8], y_peer),
        ]

    def start_along(self):
        self.load.start()
        for one in self.along:
            one.start()

    def start_first(self):
        self.load.wait()
        for one in self.along:
            one.wait()
        for a in range(2):
            for b in range(2):
                total = self.own[a, b].astype(F32)
                for k in range(3):
                    total += self.rz[k, a, b].astype(F32)
                self.own[a, b] = total.astype(BF)
        for one in self.first + self.early:
            one.start()

    def start_second(self):
        for k, came in enumerate((self.r1y, self.r1x)):
            self.first[k].wait()
            mid = self.mid[k]
            mid[...] = (mid[...].astype(F32) + came[...].astype(F32)).astype(BF)
            self.second[k].start()

    def finish(self):
        for one in self.early + self.second:
            one.wait()
        x, y = self.place
        total = self.own[x, y].astype(F32) + self.r2x[...].astype(F32) + self.r2y[...].astype(F32)
        self.total[...] = total
        return jnp.sum(total * total)


def eight_peers():
    dp, x, c = here()
    z, y = dp // 2, dp % 2
    peers = []
    for k in range(1, 8):
        kx, ky, kc = k // 4, k // 2 % 2, k % 2
        there = ((1 - x if kx else x), (1 - y if ky else y), (1 - c if kc else c))
        peers.append((z * 2 + there[1], there[0] * 2 + there[2]))
    return peers


class SumOverAll:
    def __init__(self, value, near, far, ss, rs):
        dp, x, c = here()
        z, y = dp // 2, dp % 2
        self.value, self.near, self.far = value, near, far
        self.me, self.z = x * 4 + y * 2 + c, z
        self.one = [
            remote(value, near.at[self.me], ss.at[k], rs.at[k], peer)
            for k, peer in enumerate(eight_peers())
        ]
        self.two = [
            remote(value, far.at[z], ss.at[7 + k], rs.at[7 + k], peer)
            for k, peer in enumerate(neighbours()[0])
        ]

    def start(self):
        for one in self.one:
            one.start()
        self.near[self.me] = self.value[...]

    def middle(self):
        for one in self.one:
            one.wait()
        self.value[...] = functools.reduce(jnp.add, [self.near[k] for k in range(8)])
        for one in self.two:
            one.start()
        self.far[self.z] = self.value[...]

    def finish(self):
        for one in self.two:
            one.wait()
        return functools.reduce(jnp.add, [self.far[k] for k in range(4)])


def attend_back_unit(u, out, features, ctx, dctx, lse, dq_ref):
    blocks = SLOT // BLK
    delta = jnp.sum(dctx.astype(F32) * ctx.astype(F32), axis=0, keepdims=True)
    for j in range(blocks):
        keys = slice(j * BLK, (j + 1) * BLK)
        after = slice(j * BLK, SLOT)
        k, v = u(1, keys), u(2, keys)
        wide = jnp.concatenate([k, features(1, keys)], axis=0)
        probs, dscores = [], []
        for i in range(j, blocks):
            cols = slice(i * BLK, (i + 1) * BLK)
            query = jnp.concatenate([u(0, cols), features(0, cols)], axis=0)
            raw = dot_tn(wide, query) * SCORE_SCALE2 - lse[:, cols]
            prob = jnp.exp2(causal(raw) if i == j else raw)
            dprob = dot_tn(v, dctx[:, cols])
            probs.append(prob.astype(BF))
            dscores.append((prob * (dprob - delta[:, cols])).astype(BF))
        probs, dscores = jnp.concatenate(probs, axis=1), jnp.concatenate(dscores, axis=1)
        dq = dot_nn(k, dscores)
        if j == 0:
            dq_ref[...] = dq
        else:
            dq_ref[:, after] += dq
        out(1, keys, (dot_nt(u(0, after), dscores) * SCORE_SCALE).astype(BF))
        out(2, keys, dot_nt(dctx[:, after], probs).astype(BF))
    out(0, slice(0, SLOT), (dq_ref[...] * SCORE_SCALE).astype(BF))


BY_Y = (2, 2, 3, 3)


def norm_back(dn, values, gain):
    unit, scale = norm_parts(values)
    e = dn * gain
    back = scale * (
        e
        - jnp.mean(e, axis=-1, keepdims=True)
        - unit * jnp.mean(e * unit, axis=-1, keepdims=True)
    )
    return back, unit


def backward_kernel(custom, *refs):
    (gl_in, n1_in, u_in, ctx_in, lse_ref, feat_ref, ctxc_in, resid_in, wo_in, br_in, dn_in, gp_in, gf_in, gb_ref,
     wqk_in, wvo_in, tok_in, vec_ref), refs = refs[:18], refs[18:]
    given = None
    if custom:
        given, refs = (refs[:4], None, None, None), refs[4:]
    (mixed_out, ig_out), refs = refs[:2], refs[2:]
    if custom:
        totals, refs = refs[:4], refs[4:]
        (va_out, vb_out, norm_ref), refs = refs[:3], refs[3:]
        g01, g2o, refs = refs[0], refs[1], refs[2:]
        locals_, refs = (refs[:3], refs[3:6]), refs[6:]
        bufs, refs = [refs[5 * a : 5 * a + 5] for a in range(4)], refs[20:]
        last_bufs, last_loc, last_ss, last_rs, refs = refs[:6], *refs[6:9], refs[9:]
        (va, vb, near_a, far_a, near_b, far_b, near_s, far_s, square, lss, ss, rs, ass, ars, bss, brs, qss,
         qrs), refs = refs[:18], refs[18:]
    else:
        va, vb, g01, g2o, refs = *refs[:4], refs[4:]
    (gl_s, resid_s, dn_s, got_dn, br_s, got_br, mixed, low, dres, dctx, ctxc, wo, half_c, outgoing, u, ctx, n1,
     wqk, wvo, tok, du, dq, away, away_got, half, got, loc, ld, cs_s, cs_r, bs, xs, ws) = refs
    part = low
    dp, x, c = here()
    core = (dp, x * 2 + 1 - c)
    x_peer = (dp, (1 - x) * 2 + c)
    reduces = []
    if custom:
        greet(eight_peers() + neighbours()[0])
        shard_rows = totals[1].shape[0]
        half_rows = shard_rows // 2
        for a, grad in enumerate((gp_in, gf_in, g01, g2o)):
            rows = half_rows if a == 1 else shard_rows
            total = totals[1].at[pl.ds(0, half_rows)] if a == 1 else totals[a]
            local = locals_[a] if a < 2 else None
            loads = lss.at[a] if a < 2 else None
            came = given[a]
            reduces.append(
                Reduce(
                    grad, pl.ds(0, rows), BY_Y[a], local, came, total, bufs[a], loads, ss.at[a], rs.at[a]
                )
            )
        reduces.append(
            ReduceAlong(
                gf_in, half_rows, 32, totals[1].at[pl.ds(half_rows, half_rows)], last_bufs, last_loc, last_ss,
                last_rs,
            )
        )
    else:
        greet([core, x_peer, (dp, (1 - x) * 2 + 1 - c)])

    def step(number, what, *which):
        if custom:
            getattr(reduces[number], what)(*which)

    rows_all, width = low.shape
    own_rows = rows_all // 2
    n_chunks = rows_all // BLK
    order = [(1 - x) * 4 + i for i in range(HALF // BLK)] + [x * 2 + i for i in range(SLOT // BLK)]
    swaps = []
    for chunk in order:
        at = rows_at(chunk * BLK, BLK)
        swaps.append(remote(dn_in.at[at], got_dn.at[at], cs_s.at[chunk], cs_r.at[chunk], core))
    their = pl.ds(pl.multiple_of((1 - c) * own_rows, BLK), own_rows)
    mine = pl.ds(pl.multiple_of(c * own_rows, BLK), own_rows)
    branch = remote(br_in.at[their], got_br, bs.at[0], bs.at[1], core)

    def chunk_loads(n):
        at, slot = rows_at(order[n] * BLK, BLK), n % 2
        return [
            pltpu.make_async_copy(source.at[at], target.at[slot], ld.at[slot, k])
            for k, (source, target) in enumerate(
                ((resid_in, resid_s), (gl_in, gl_s), (dn_in, dn_s))
            )
        ]

    def load(number, source, target):
        copy = pltpu.make_async_copy(source, target, loc.at[number])
        copy.start()
        return copy

    loads = [chunk_loads(n) for n in range(n_chunks)]
    swaps[0].start()
    for n in range(2):
        for one in loads[n]:
            one.start()
    branch.start()
    for one in swaps[1:]:
        one.start()
    step(4, "start_along")
    step(0, "start_first")
    step(0, "start_early", 0)
    step(0, "start_early", 1)
    step(1, "start_first")
    br_load = load(0, br_in.at[mine], br_s)
    wo_load = load(1, wo_in, wo)
    ctxc_load = load(2, ctxc_in, ctxc)
    step(1, "start_early", 0)
    step(1, "start_early", 1)
    late = [
        load(3, u_in, u),
        load(4, ctx_in, ctx),
        load(5, n1_in, n1),
        load(6, wqk_in, wqk),
        load(7, wvo_in, wvo),
        load(8, tok_in, tok),
    ]

    @pl.when(c == x)
    def _():
        half[...] = jnp.zeros_like(half)

    va[...] = jnp.zeros_like(va)
    vb[...] = jnp.zeros_like(vb)
    for s in range(2):
        va[pl.ds(4 + c + 2 * s, 1), :] = gb_ref[s]
    branch.wait()
    br_load.wait()
    for n, chunk in enumerate(order):
        slot = n % 2
        for one in loads[n]:
            one.wait()
        swaps[n].wait()
        at = rows_at(chunk * BLK, BLK)
        dn = dn_s[slot].astype(F32) + got_dn[at, :].astype(F32)
        resid = resid_s[slot]
        back, unit = norm_back(dn, resid, vec_ref[2:3, :])
        grad = gl_s[slot].astype(F32)
        after = grad + back
        low[at, :] = after.astype(BF)

        @pl.when(chunk // (n_chunks // 2) == c)
        def _(chunk=chunk, dn=dn, resid=resid, unit=unit, grad=grad, after=after):
            here_at = rows_at((chunk - c * (n_chunks // 2)) * BLK, BLK)
            dres[here_at, :] = after
            branches = br_s[here_at, :].astype(F32) + got_br[here_at, :].astype(F32)
            mixed[here_at, :] = (resid + branches + vec_ref[7:8, :]).astype(BF)
            va[0:1, :] += jnp.sum(dn * unit, axis=0, keepdims=True)
            va[1:2, :] += jnp.sum(dn, axis=0, keepdims=True)
            va[2:3, :] += jnp.sum(after, axis=0, keepdims=True)
            va[3:4, :] += jnp.sum(grad, axis=0, keepdims=True)

        if n + 2 < n_chunks:
            for one in loads[n + 2]:
                one.start()
        if n == 1:
            wo_load.wait()
            for i in range(HALF // BLK):
                lanes = slice(i * BLK, (i + 1) * BLK)
                rows = low[rows_at((1 - x) * SLOT + i * BLK, BLK), :]
                outgoing[:, :, lanes] = (
                    dot_tt(wo[1 - x], rows).astype(BF).reshape(-1, HD, BLK)
                )
                dctx[2, :, :, rows_at(x * HALF + i * BLK, BLK)] = (
                    dot_tt(wo[x], rows).astype(BF).reshape(-1, HD, BLK)
                )
            cross_c = remote(outgoing, half_c, xs.at[0], xs.at[1], x_peer)
            cross_c.start()
            step(0, "start_second", 0)
            step(0, "start_second", 1)
    mixed_copy = pltpu.make_async_copy(mixed, mixed_out, ws.at[0])
    mixed_copy.start()
    if custom:
        early_sum = SumOverAll(va, near_a, far_a, ass, ars)
        early_sum.start()
    heads = u.shape[2]
    cols = heads * HD
    blocks = g2o.shape[1:4]
    ctxc_load.wait()
    for s in range(2):
        g2o[s, :, :, :, cols:] = dot_tt(low[...], ctxc[s]).astype(BF).reshape(*blocks, cols)
    for i in range(SLOT // BLK):
        lanes = slice(i * BLK, (i + 1) * BLK)
        rows = low[rows_at(x * HALF + i * BLK, BLK), :]
        for s in range(2):
            dctx[s, :, :, lanes] = dot_tt(wo[s], rows).astype(BF).reshape(-1, HD, BLK)
    step(1, "start_second", 0)
    step(1, "start_second", 1)
    late[0].wait()
    late[1].wait()

    def attend_back(group, which, begin, end):
        def unit(h, carry):
            def put(k, lanes, value):
                du[group, k, h, :, lanes] = value

            attend_back_unit(
                lambda k, lanes: u[group, k, h, :, lanes],
                put,
                lambda k, lanes: feat_ref[which, k, :, lanes],
                ctx[group, h],
                dctx[group, h],
                lse_ref[group, h],
                dq,
            )
            return carry

        lax.fori_loop(begin, end, unit, 0)

    full_rows = pl.ds(pl.multiple_of(x * SLOT, SLOT), SLOT)
    part_rows = pl.ds(pl.multiple_of((1 - x) * SLOT, SLOT), SLOT)
    everything = slice(0, SLOT)

    def of_group(group, k, lanes):
        value = du[group, k, :, :, lanes]
        return value.reshape(cols, value.shape[-1])

    def weight_grad(slot, which, with_part):
        def rows_of(group):
            value = du[group, :, heads - 1 :] if which else du[group, :, : heads - 1]
            return value.reshape(-1, SLOT)

        out = dot_tt(n1[full_rows, :], rows_of(slot))
        if with_part:
            out += dot_tt(n1[part_rows, :], rows_of(2))
        out = out.astype(BF)
        if which:
            g2o[slot, :, :, :, :cols] = out.reshape(*blocks, cols)
        else:
            g01[slot] = out.reshape(*blocks, 2 * cols)

    attend_back(1 - x, 0, 0, heads)
    for one in late[2:]:
        one.wait()
    for which in range(2):
        weight_grad(1 - x, which, False)
        step(2 + which, "start_first")
        step(2 + which, "start_early", 0)
    step(0, "start_third")
    cross_c.wait()
    dctx[2, :, :, pl.ds(pl.multiple_of((1 - x) * HALF, HALF), HALF)] = half_c[...]
    attend_back(2, 1, 0, heads)

    def back_through(group, lanes, slot):
        two = du[group, 0:2, :, :, lanes]
        two = two.reshape(2 * cols, two.shape[-1])
        out = dot_tt(two, whole_weight(wqk, slot))
        return out + dot_tt(of_group(group, 2, lanes), whole_weight(wvo, slot)[:, :cols])

    theirs = pl.ds(pl.multiple_of((1 - x) * HALF, HALF), HALF)
    away[...] = back_through(2, theirs, x).astype(BF).reshape(away.shape)
    swap_away = remote(away.at[1 - c], away_got, bs.at[4], bs.at[5], core)
    swap_away.start()
    step(1, "start_third")
    step(4, "start_first")
    swap_away.wait()
    away[c] = (away[c].astype(F32) + away_got[...].astype(F32)).astype(BF)
    cross = remote(away.at[c], half.at[c], xs.at[2], xs.at[3 + c], (dp, (1 - x) * 2 + x))
    cross.start()
    other = remote(away.at[1 - c], half.at[1 - c], xs.at[2], xs.at[4 - c], (dp, (1 - x) * 2 + x))
    attend_back(x, 0, 0, heads - 1)
    weight_grad(x, 0, True)
    step(2, "start_early", 1)
    step(2, "start_second", 1)
    step(2, "start_second", 0)
    step(4, "start_second")
    attend_back(x, 0, heads - 1, heads)
    weight_grad(x, 1, True)
    step(3, "start_early", 1)
    step(3, "start_second", 1)
    step(3, "start_second", 0)
    if custom:
        early_sum.middle()

    def bias_sums(group):
        sums = [
            jnp.sum(of_group(group, k, everything).astype(F32), axis=1, keepdims=True)
            for k in (0, 2)
        ]
        return jnp.concatenate(sums, axis=0)

    columns = [bias_sums(x) + bias_sums(2), bias_sums(1 - x)]
    as_rows = jnp.concatenate(columns + [jnp.zeros((2 * cols, 6), F32)], axis=1).T
    for n, slot in enumerate((x, 1 - x)):
        vb[pl.ds(2 + c + 2 * slot, 1), : 2 * cols] = as_rows[n : n + 1, :]

    def back_rows(start, count):
        return pl.ds(pl.multiple_of(start, HALF), count)

    for i in range(SLOT // HALF):
        lanes = slice(i * HALF, (i + 1) * HALF)
        back = back_through(0, lanes, 0) + back_through(1, lanes, 1)
        part[back_rows(x * HALF + i * HALF, HALF), :] = back.astype(BF)
    back = back_through(2, back_rows(x * HALF, HALF), x)
    part[back_rows((1 - x) * SLOT, HALF), :] = back.astype(BF)
    swap = remote(part.at[their], got, bs.at[2], bs.at[3], core)
    swap.start()
    step(2, "start_third")
    swap.wait()
    cross.wait_send()

    @pl.when(c == 1 - x)
    def _():
        cross.wait_recv()
        other.wait_recv()

    for r in range(own_rows // BLK):
        rows = slice(r * BLK, (r + 1) * BLK)
        wide = rows_at(c * own_rows + r * BLK, BLK)
        dn = part[wide, :].astype(F32) + got[rows, :].astype(F32)
        place = r - (1 - x)
        also = (c == 1 - x) & (place >= 0) & (place < 2)
        dn += jnp.where(also, half[jnp.clip(place, 0, 1)].astype(F32), 0.0)
        back, unit = norm_back(dn, tok[rows, :].astype(F32), vec_ref[0:1, :])
        mixed_copy.wait() if r == 0 else None
        mixed[rows, :] = (dres[rows, :] + back).astype(BF)
        vb[0:1, :] += jnp.sum(dn * unit, axis=0, keepdims=True)
        vb[1:2, :] += jnp.sum(dn, axis=0, keepdims=True)
    ig_copy = pltpu.make_async_copy(mixed, ig_out, ws.at[1])
    ig_copy.start()
    if custom:
        late_sum = SumOverAll(vb, near_b, far_b, bss, brs)
        late_sum.start()
        va_out[...] = early_sum.finish()
        step(3, "start_third")
        late_sum.middle()
        squares = functools.reduce(jnp.add, [one.finish() for one in reduces])
        square[...] = jnp.full(square.shape, squares, F32)
        norm = SumOverAll(square, near_s, far_s, qss, qrs)
        norm.start()
        vb_out[...] = late_sum.finish()
        vector_squares = jnp.sum(va_out[...] * va_out[...], keepdims=True)
        vector_squares += jnp.sum(vb_out[...] * vb_out[...], keepdims=True)
        norm.middle()
        norm_ref[...] = jnp.sqrt(norm.finish() + vector_squares)
    ig_copy.wait()


def backward(saved, weights, given, tokens, vectors):
    (gl, n1, u, ctx, lse, features, ctxc, resid, wo, br, dn, gp, gf, gb) = saved
    rows, width = tokens.shape
    chip = 2 * rows
    heads = u.shape[2]
    cols = heads * HD
    custom = lax.axis_size("dp") == 8
    dma = pltpu.SemaphoreType.DMA
    out_shape = [sds((rows, width), BF)] * 2
    out_specs = [ANY, ANY]
    if custom:
        hidden = gp.shape[-1]
        part_rows = width // 8
        shapes = [(part_rows, n) for n in (hidden, hidden, 2 * cols, 2 * cols)]
        gf = gf.reshape(gp.shape)
        out_shape += [sds(s, F32) for s in shapes]
        out_shape += [sds((8, width), F32)] * 2 + [sds((8, 128), F32)]
        out_specs += [VM] * 7
        scratch = [pltpu.VMEM((2, 4, 2) + s, BF) for s in shapes[2:]]
        half_rows = part_rows // 2
        pieces = [shapes[0], (half_rows, hidden), *shapes[2:]]
        scratch += [
            pltpu.VMEM((n,) + pieces[a], BF) for a in range(2) for n in (BY_Y[a], 4 - BY_Y[a], 4)
        ]
        scratch += [
            pltpu.VMEM((n,) + pieces[a], BF)
            for a in range(4)
            for n in (BY_Y[a], 4 - BY_Y[a], 4, 4, 3)
        ]
        scratch += [
            pltpu.VMEM((2, 2, half_rows, hidden), BF),
            pltpu.VMEM((3, 2, 2, half_rows, hidden), BF),
            pltpu.VMEM((32, hidden), BF),
            pltpu.VMEM((half_rows - 32, hidden), BF),
            pltpu.VMEM((half_rows, hidden), BF),
            pltpu.VMEM((half_rows, hidden), BF),
            dma,
            dma((9,)),
            dma((9,)),
        ]
        scratch += [
            *[pltpu.VMEM((8, width), F32)] * 2,
            *[pltpu.VMEM((8, 8, width), F32), pltpu.VMEM((4, 8, width), F32)] * 2,
            pltpu.VMEM((8, 8, 128), F32),
            pltpu.VMEM((4, 8, 128), F32),
            pltpu.VMEM((8, 128), F32),
            dma((2, 3)),
            dma((4, 9)),
            dma((4, 9)),
            *[dma((10,))] * 6,
        ]
    else:
        out_shape += [sds((8, width), F32)] * 2 + [sds((2, 1, 1, width, 2 * cols), BF)] * 2
        out_specs += [VM] * 4
        scratch = []
    scratch += [
        pltpu.VMEM((2, BLK, width), BF),
        pltpu.VMEM((2, BLK, width), F32),
        pltpu.VMEM((2, BLK, width), BF),
        pltpu.VMEM((chip, width), BF),
        pltpu.VMEM((rows, width), BF),
        pltpu.VMEM((rows, width), BF),
        pltpu.VMEM((rows, width), BF),
        pltpu.VMEM((chip, width), BF),
        pltpu.VMEM((rows, width), F32),
        pltpu.VMEM(ctx.shape, BF),
        pltpu.VMEM(ctxc.shape, BF),
        pltpu.VMEM(wo.shape, BF),
        pltpu.VMEM((heads, HD, HALF), BF),
        pltpu.VMEM((heads, HD, HALF), BF),
        pltpu.VMEM(u.shape, BF),
        pltpu.VMEM(ctx.shape, BF),
        pltpu.VMEM(n1.shape, BF),
        *[pltpu.VMEM(w.shape, BF) for w in weights],
        pltpu.VMEM((rows, width), BF),
        pltpu.VMEM(u.shape, BF),
        pltpu.VMEM((HD, SLOT), F32),
        pltpu.VMEM((2, BLK, width), BF),
        pltpu.VMEM((BLK, width), BF),
        pltpu.VMEM((2, BLK, width), BF),
        pltpu.VMEM((rows, width), BF),
        dma((9,)),
        dma((2, 3)),
        dma((chip // BLK,)),
        dma((chip // BLK,)),
        dma((6,)),
        dma((5,)),
        dma((2,)),
    ]
    return pl.pallas_call(
        functools.partial(backward_kernel, custom),
        out_shape=tuple(out_shape),
        in_specs=[ANY] * 4 + [VM, VM] + [ANY] * 7 + [VM] + [ANY] * 3 + [VM] + [ANY] * len(given),
        out_specs=tuple(out_specs),
        scratch_shapes=scratch,
        compiler_params=params(2),
        name="backward",
    )(gl, n1, u, ctx, lse, features, ctxc, resid, wo, br, dn, gp, gf, gb, *weights, tokens, vectors, *given)


def adamw_update(weight, moment_one, moment_two, gradient, step_rate, decay_rate):
    first_moment = DECAY_FIRST * moment_one + (1.0 - DECAY_FIRST) * gradient
    second_moment = DECAY_SECOND * moment_two + (1.0 - DECAY_SECOND) * gradient * gradient
    first_hat = first_moment / (1.0 - DECAY_FIRST**STEP)
    second_hat = second_moment / (1.0 - DECAY_SECOND**STEP)
    fresh_weight = weight - step_rate * (
        first_hat / (jnp.sqrt(second_hat) + ADAM_EPSILON) + decay_rate * weight
    )
    return (fresh_weight, first_moment, second_moment)


def update_kernel(*refs):
    (gp, gf, g01, g2o, va, vb, norm_ref), refs = refs[:7], refs[7:]
    kept, refs = refs[:2], refs[2:]
    cols = g2o.shape[1] // 2
    most = cols - HD
    old, new, norm_out, kept_out = refs[:18], refs[18:36], refs[36], refs[37:]
    norm_out[0, 0] = norm_ref[0, 0]
    for source, target in zip(kept, kept_out, strict=True):
        target[...] = source[...]
    factor = CLIP_NORM / jnp.maximum(norm_ref[0:1, 0:1], CLIP_NORM)

    def update(number, grad, index, rate, decay):
        values = [old[3 * number + m][index] for m in range(3)]
        fresh = adamw_update(*values, factor * grad, rate, decay)
        for m in range(3):
            new[3 * number + m][index] = fresh[m]

    for k in range(3):
        grad = [g01[:, k * most : (k + 1) * most], g2o[:, k * HD : (k + 1) * HD]]
        update(0, jnp.concatenate(grad, axis=1), k, RATE_MATRIX, WEIGHT_DECAY)
    for number, grad in ((1, g2o[:, cols:].T), (2, gf[...]), (3, gp[...])):
        update(number, grad, ..., RATE_MATRIX, WEIGHT_DECAY)
    width = va.shape[1]
    parts = old[15].shape[1] // width

    def heads(k):
        rows = [vb[2 + t : 3 + t, k * cols : (k + 1) * cols] for t in range(parts)]
        return jnp.concatenate(rows, axis=1)

    vector_grad = jnp.concatenate(
        [vb[0:2, :], va[0:2, :], heads(0), heads(1), va[2:4, :]], axis=0
    )
    update(4, vector_grad, ..., RATE_VECTOR, 0.0)
    for t in range(parts):
        lanes = slice(t * width, (t + 1) * width)
        update(5, va[4 + t : 5 + t, :], (slice(None), lanes), RATE_VECTOR, 0.0)


def update_all(totals, va, vb, norm, kept, states):
    return pl.pallas_call(
        update_kernel,
        out_shape=(
            *[sds(s.shape, F32) for s in states],
            sds((1, 1), F32),
            *[sds(k.shape, k.dtype) for k in kept],
        ),
        in_specs=[VM] * (9 + len(states)),
        out_specs=(*[VM] * len(states), pl.BlockSpec(memory_space=pltpu.SMEM), VM, VM),
        compiler_params=params(),
        name="update",
    )(*totals, va, vb, norm, *kept, *states)


def on_device(
    tokens,
    cotangent,
    segment_ids,
    valid,
    qkv_weight,
    qkv_moment1,
    qkv_moment2,
    out_weight,
    out_moment1,
    out_moment2,
    fc_weight,
    fc_moment1,
    fc_moment2,
    proj_weight,
    proj_moment1,
    proj_moment2,
    vector_params,
    vector_moment1,
    vector_moment2,
    fc_bias,
    fc_bias_moment1,
    fc_bias_moment2,
):
    custom = lax.axis_size("dp") == 8
    slot, swap = lax.axis_index("tensor") // 2, [(0, 2), (1, 3), (2, 0), (3, 1)]
    states = [jnp.transpose(s, (1, 0, 2)) for s in (qkv_weight, qkv_moment1, qkv_moment2)]
    states += [out_weight, out_moment1, out_moment2]
    states += [fc_weight, fc_moment1, fc_moment2]
    states += [s.T for s in (proj_weight, proj_moment1, proj_moment2)]
    states += [vector_params, vector_moment1, vector_moment2]
    states += [s[None] for s in (fc_bias, fc_bias_moment1, fc_bias_moment2)]
    shards = [states[0], states[3], states[6], states[9]]
    if not custom:
        parts = [
            jnp.concatenate([states[0][0], states[0][1]], axis=1),
            jnp.concatenate([states[0][2], shards[1].T], axis=1),
            *shards[2:],
        ]
        shards = []
        for part in parts:
            own = lax.all_gather(part.astype(BF), "dp", axis=0, tiled=True)
            other = lax.ppermute(own, "tensor", swap)
            shards.append(
                jnp.stack([jnp.where(slot == 0, own, other), jnp.where(slot == 0, other, own)])
            )
    saved, weights, given = forward(
        tokens,
        cotangent,
        valid,
        segment_ids,
        vector_params,
        states[15],
        shards,
    )
    outs = backward(saved, weights, given, tokens, vector_params)
    mixed, input_grad = outs[:2]
    if custom:
        totals, (va, vb, norm) = outs[2:6], outs[6:]
    else:
        va, vb, totals = *outs[2:4], []
        for g in [saved[11], saved[12], *outs[4:6]]:
            g = g.reshape(2, -1, g.shape[-1])
            mine = jnp.where(slot == 0, g[0], g[1])
            other = jnp.where(slot == 0, g[1], g[0])
            both = mine.astype(F32) + lax.ppermute(other, "tensor", swap).astype(F32)
            both = lax.psum_scatter(both.astype(BF), "dp", scatter_dimension=0, tiled=True)
            totals.append(both.astype(F32))
        squares = sum(jnp.sum(t * t) for t in totals)
        va, vb, squares = lax.psum((va, vb, squares), ("dp", "tensor"))
        squares += jnp.sum(va * va) + jnp.sum(vb * vb)
        norm = jnp.full((8, 128), jnp.sqrt(squares), F32)
    *new, grad_norm, mixed, input_grad = update_all(
        totals, va, vb, norm, (mixed, input_grad), states
    )
    new[:3] = [jnp.transpose(s, (1, 0, 2)) for s in new[:3]]
    new[9:12] = [s.T for s in new[9:12]]
    new[15:18] = [s[0] for s in new[15:18]]
    return (mixed, input_grad, grad_norm.reshape(()), *new)


def solution(mesh):
    rows = P(("dp", "tensor"), None)
    by_rows = [P("dp", None, "tensor")] * 3
    by_out = [P("tensor", "dp")] * 3
    by_fc = [P("dp", "tensor")] * 3
    weights = by_rows + by_out + by_fc + by_out
    return jax.shard_map(
        on_device,
        mesh=mesh,
        in_specs=(rows, rows, P("dp"), P(("dp", "tensor")), *weights, *[P()] * 6),
        out_specs=(rows, rows, P(), *weights, *[P()] * 6),
        check_vma=False,
    )
```
